32 devices in a mesh: dp: 16 (over z, y, x), mp: 2 (over core).
Axes of the slice: x: 2, y: 2, z: 4, core: 2. Of those that a mesh axis runs over, the one named last changes fastest.
Arguments:
- src_embed: bfloat16 [16384, 512], P('dp'), may hold values from -6 to 6
- tgt_embed: bfloat16 [16384, 512], P('dp'), may hold values from -6 to 6
- src_segment: int32 [16, 1024], P('dp'), may hold values from 0 to 15, never falling along the last dimension, each value on 1 to 128 neighbouring positions
- tgt_segment: int32 [16, 1024], P('dp'), may hold values from 0 to 15, never falling along the last dimension, each value on 1 to 128 neighbouring positions
- enc_qkv: bfloat16 [3, 512, 512], P(None, None, 'mp'), may hold values from -0.25 to 0.25
- enc_out_proj: bfloat16 [512, 512], P('mp'), may hold values from -0.75 to 0.75
- dec_qkv: bfloat16 [3, 512, 512], P(None, None, 'mp'), may hold values from -0.25 to 0.25
- dec_out_proj: bfloat16 [512, 512], P('mp'), may hold values from -0.75 to 0.75
- cross_query: bfloat16 [512, 512], P(None, 'mp'), may hold values from -0.25 to 0.25
- cross_kv: bfloat16 [2, 512, 512], P(None, None, 'mp'), may hold values from -0.25 to 0.25
- cross_out_proj: bfloat16 [512, 512], P('mp'), may hold values from -0.75 to 0.75
- ffn_up: bfloat16 [512, 2048], P(None, 'mp'), may hold values from -0.25 to 0.25
- ffn_down: bfloat16 [2048, 512], P('mp'), may hold values from -0.1875 to 0.1875
- norm_gain: float32 [5, 512], replicated, may hold values from 0.1 to 1.9
- norm_bias: float32 [5, 512], replicated, may hold values from -3 to 3
- enc_cotangent: bfloat16 [16384, 512], P(('dp', 'mp')), may hold values from -6 to 6
- dec_cotangent: bfloat16 [16384, 512], P(('dp', 'mp')), may hold values from -6 to 6
Outputs:
- enc_out: bfloat16 [16384, 512], P('dp')
- dec_out: bfloat16 [16384, 512], P('dp')
- src_grad: float32 [16384, 512], P(('dp', 'mp'))
- tgt_grad: float32 [16384, 512], P(('dp', 'mp'))
- enc_qkv_grad: float32 [3, 512, 512], P(None, None, 'mp')
- enc_out_proj_grad: float32 [512, 512], P('mp')
- dec_qkv_grad: float32 [3, 512, 512], P(None, None, 'mp')
- dec_out_proj_grad: float32 [512, 512], P('mp')
- cross_query_grad: float32 [512, 512], P(None, 'mp')
- cross_kv_grad: float32 [2, 512, 512], P(None, None, 'mp')
- cross_out_proj_grad: float32 [512, 512], P('mp')
- ffn_up_grad: float32 [512, 2048], P(None, 'mp')
- ffn_down_grad: float32 [2048, 512], P('mp')
- norm_gain_grad: float32 [5, 512], replicated
- norm_bias_grad: float32 [5, 512], replicated
The draws below stay inside these ranges and needn't reach their ends.
Inputs may be any that keep to these rules, and one draw needn't show every extreme that they name: `src_segment`: in every row the sentence numbers never fall, every number from 0 to 15 occurs, and a sentence holds 1 to 128 tokens. `tgt_segment`: in every row the sentence numbers never fall, every number from 0 to 15 occurs, and a sentence holds 1 to 128 tokens; target sentence s of a row pairs with source sentence s of the same row.
All inputs are finite; a program needn't handle non-finite values.
Results may differ from the reference program's by a relative error of at most 0.035.
Values may be sent and summed in bfloat16 or wider, within the bound.
No kernel may reach another device: no remote copies, remote signals or barrier semaphores. Data moves between devices by JAX's collectives and lax.ppermute only.
A program may use at most 192 MiB of HBM per device.

```python
import math
from functools import partial
import jax
import jax.numpy as jnp
import numpy as np
from jax import lax

D = 512
HEADS = 8
HDIM = 64
FF = 2048
ROW = 1024
SENTS = 16
MOST = 128
ROWS = 16
TOKENS = 16384


def shard_levels(rng, dims, shards, low, high):
    level, own = 1.0, jax.random.fold_in(rng, 6)
    for position, shards_of in shards:
        draws = jnp.exp(jax.random.uniform(jax.random.fold_in(own, position), (shards_of,), jnp.float32, low / len(shards), high / len(shards)))
        level = level * jnp.repeat(draws, dims[position] // shards_of).reshape([-1 if axis == position else 1 for axis in range(len(dims))])
    return level


def profile(amount, total, limit, skew):
    loads = [(1 << 20) // math.isqrt(grade ** skew) + 1 for grade in range(2, amount + 1)]
    surplus, counts = total - limit - (amount - 1), [1] * (amount - 1)
    while surplus > 0:
        movable = [i for i in range(amount - 1) if counts[i] < limit]
        pool, budget = sum([loads[i] for i in movable]), surplus
        for i in movable:
            extra = min(limit - counts[i], max(1, budget * loads[i] // pool), surplus)
            counts[i] = counts[i] + extra
            surplus = surplus - extra
    return np.array([limit] + counts)


def ragged(key, count, total, reach, lean):
    if count == 2:
        one = jax.random.randint(key, (), max(1, total - reach), min(reach, total - 1) + 1)
        return jnp.stack([one, total - one])
    tallies = jnp.asarray(profile(count, total, reach, lean), jnp.int32)
    twos = (count - 1) // 2
    source_of, sink = tallies[1:1 + 2 * twos:2], tallies[2:2 + 2 * twos:2]
    room = jnp.minimum(source_of - 1, reach - sink)
    moved = jax.random.randint(jax.random.fold_in(key, 1), (twos,), 0, 1 << 20) % (room + 1)
    tallies = tallies.at[1:1 + 2 * twos:2].set(source_of - moved).at[2:2 + 2 * twos:2].set(sink + moved)
    return tallies[jax.random.permutation(jax.random.fold_in(key, 2), count)]


def bell_draw(key, dims, spread, most, split=(), dtype=jnp.bfloat16):
    result = jax.random.normal(key, dims, jnp.float32) * spread
    if len(split) > 0:
        result = shard_levels(key, dims, split, -0.22, 0.18) * result
    return jnp.clip(result, min=-most, max=most).astype(dtype)


def setup_inputs(seed: int = 0) -> dict:
    seeds = jax.random.split(jax.random.key(seed), 18)
    src_embed = bell_draw(seeds[0], (TOKENS, D), 1.0, 6.0, ((0, 16),))
    tgt_embed = bell_draw(seeds[1], (TOKENS, D), 1.0, 6.0, ((0, 16),))
    src_segment = jax.vmap(lambda own: jnp.searchsorted(jnp.cumsum(ragged(own, SENTS, ROW, MOST, 1)), jnp.arange(ROW), side="right"))(jax.random.split(seeds[2], ROWS)).reshape((ROWS, ROW)).astype(jnp.int32)
    tgt_segment = jax.vmap(lambda own: jnp.searchsorted(jnp.cumsum(ragged(own, SENTS, ROW, MOST, 1)), jnp.arange(ROW), side="right"))(jax.random.split(seeds[3], ROWS)).reshape((ROWS, ROW)).astype(jnp.int32)
    enc_qkv = bell_draw(seeds[4], (3, D, D), D ** -0.5, 0.25, ((2, 2),))
    enc_out_proj = bell_draw(seeds[5], (D, D), (D // 8) ** -0.5, 0.75, ((0, 2),))
    dec_qkv = bell_draw(seeds[6], (3, D, D), D ** -0.5, 0.25, ((2, 2),))
    dec_out_proj = bell_draw(seeds[7], (D, D), (D // 8) ** -0.5, 0.75, ((0, 2),))
    cross_query = bell_draw(seeds[8], (D, D), D ** -0.5, 0.25, ((1, 2),))
    cross_kv = bell_draw(seeds[9], (2, D, D), D ** -0.5, 0.25, ((2, 2),))
    cross_out_proj = bell_draw(seeds[10], (D, D), (D // 8) ** -0.5, 0.75, ((0, 2),))
    ffn_up = bell_draw(seeds[11], (D, FF), D ** -0.5, 0.25, ((1, 2),))
    ffn_down = bell_draw(seeds[12], (FF, D), (FF // 2) ** -0.5, 0.1875, ((0, 2),))
    norm_gain = jnp.clip(1.0 + 0.18 * jax.random.normal(seeds[13], (5, D), jnp.float32), 0.1, 1.9)
    norm_bias = bell_draw(seeds[14], (5, D), 0.3, 3.0, (), jnp.float32)
    enc_cotangent = bell_draw(seeds[15], (TOKENS, D), 1.0, 6.0, ((0, 32),))
    dec_cotangent = bell_draw(seeds[16], (TOKENS, D), 1.0, 6.0, ((0, 32),))
    return {"src_embed": src_embed, "tgt_embed": tgt_embed, "src_segment": src_segment, "tgt_segment": tgt_segment, "enc_qkv": enc_qkv, "enc_out_proj": enc_out_proj, "dec_qkv": dec_qkv, "dec_out_proj": dec_out_proj, "cross_query": cross_query, "cross_kv": cross_kv, "cross_out_proj": cross_out_proj, "ffn_up": ffn_up, "ffn_down": ffn_down, "norm_gain": norm_gain, "norm_bias": norm_bias, "enc_cotangent": enc_cotangent, "dec_cotangent": dec_cotangent}


EPSILON = 1e-05
MASKED = -1e+30

@jax.custom_vjp
def low(v):
    return lax.optimization_barrier(v.astype(jnp.bfloat16)).astype(jnp.float32)

@jax.custom_vjp
def low_back(v):
    return v

def low_keep(v):
    return (low(v), None)

def low_pass(kept, grad):
    return (grad,)

def back_keep(v):
    return (v, None)

def back_low(kept, grad):
    return (low(grad),)
low.defvjp(low_keep, low_pass)
low_back.defvjp(back_keep, back_low)

def project(left, right):
    return jnp.dot(left, right, precision=lax.Precision.HIGHEST)

def layer_norm(stream, gain_row, shift_row):
    row_mean = lax.optimization_barrier(jnp.mean(stream, axis=-1, keepdims=True))
    centered = stream - row_mean
    variance = lax.optimization_barrier(jnp.mean(centered * centered, axis=-1, keepdims=True))
    return centered * lax.rsqrt(variance + EPSILON) * gain_row + shift_row

def attend_row(causal, row_inputs):
    queries, keys, values, query_marks, key_marks = row_inputs
    scores = jnp.einsum('qhd,khd->hqk', queries, keys, precision=lax.Precision.HIGHEST) * HDIM ** (-0.5)
    scores = low_back(scores)
    allowed = query_marks[:, None] == key_marks[None, :]
    if causal:
        places = jnp.arange(ROW)
        allowed = jnp.logical_and(allowed, places[:, None] >= places[None, :])
    scores = jnp.where(allowed[None], scores, MASKED)
    probabilities = low(jax.nn.softmax(scores, axis=-1))
    return jnp.einsum('hqk,khd->qhd', probabilities, values, precision=lax.Precision.HIGHEST)

def attention(query_side, key_side, w_query, w_key, w_value, w_out, query_marks, key_marks, causal):
    head_shape = (ROWS, ROW, HEADS, HDIM)
    queries = low_back(low(project(query_side, w_query))).reshape(head_shape)
    keys = low_back(low(project(key_side, w_key))).reshape(head_shape)
    values = low_back(low(project(key_side, w_value))).reshape(head_shape)
    mixed_heads = lax.map(jax.checkpoint(partial(attend_row, causal)), (queries, keys, values, query_marks, key_marks))
    mixed_flat = low_back(low(mixed_heads.reshape(TOKENS, D)))
    return low_back(project(mixed_flat, w_out))

def feed_forward(stream, ffn_up, ffn_down):
    hidden = low_back(project(low(stream), ffn_up))
    return low_back(project(low(jax.nn.gelu(hidden)), ffn_down))

def forward(src_segment, tgt_segment, src_embed, tgt_embed, enc_qkv, enc_out_proj, dec_qkv, dec_out_proj, cross_query, cross_kv, cross_out_proj, ffn_up, ffn_down, norm_gain, norm_bias):
    src_low = low(src_embed)
    stream_one = layer_norm(src_embed + attention(src_low, src_low, enc_qkv[0], enc_qkv[1], enc_qkv[2], enc_out_proj, src_segment, src_segment, False), norm_gain[0], norm_bias[0])
    encoded = layer_norm(stream_one + feed_forward(stream_one, ffn_up, ffn_down), norm_gain[1], norm_bias[1])
    tgt_low = low(tgt_embed)
    stream_two = layer_norm(tgt_embed + attention(tgt_low, tgt_low, dec_qkv[0], dec_qkv[1], dec_qkv[2], dec_out_proj, tgt_segment, tgt_segment, True), norm_gain[2], norm_bias[2])
    stream_three = layer_norm(stream_two + attention(low(stream_two), low(encoded), cross_query, cross_kv[0], cross_kv[1], cross_out_proj, tgt_segment, src_segment, False), norm_gain[3], norm_bias[3])
    decoded = layer_norm(stream_three + feed_forward(stream_three, ffn_up, ffn_down), norm_gain[4], norm_bias[4])
    return (encoded, decoded)

def reference(src_embed, tgt_embed, src_segment, tgt_segment, enc_qkv, enc_out_proj, dec_qkv, dec_out_proj, cross_query, cross_kv, cross_out_proj, ffn_up, ffn_down, norm_gain, norm_bias, enc_cotangent, dec_cotangent):
    floats = [array.astype(jnp.float32) for array in (src_embed, tgt_embed, enc_qkv, enc_out_proj, dec_qkv, dec_out_proj, cross_query, cross_kv, cross_out_proj, ffn_up, ffn_down, norm_gain, norm_bias)]
    outputs, pullback = jax.vjp(partial(forward, src_segment, tgt_segment), *floats)
    gradients = pullback((enc_cotangent.astype(jnp.float32), dec_cotangent.astype(jnp.float32)))
    return (outputs[0].astype(jnp.bfloat16), outputs[1].astype(jnp.bfloat16), gradients[0], gradients[1], gradients[2], gradients[3], gradients[4], gradients[5], gradients[6], gradients[7], gradients[8], gradients[9], gradients[10], gradients[11], gradients[12])
```

```python
import functools
import math

import jax
import jax.numpy as jnp
from jax import lax
from jax.experimental import pallas as pl
from jax.experimental.pallas import tpu as pltpu
from jax.sharding import PartitionSpec as P

HDIM = 64
SCALE = HDIM ** (-0.5)
EPSILON = 1e-05
MASKED = -1e30
BLOCK = 128
MOST = 128
QUAD = 4 * HDIM
F32 = jnp.float32
BF16 = jnp.bfloat16
VMEM_LIMIT = 56 * 1024 * 1024
GELU_IN = math.sqrt(2.0 / math.pi)
GELU_CUBE = 0.044715


def nn(left, right):
    return jnp.dot(left, right, preferred_element_type=F32)


def nt(left, right):
    return lax.dot_general(left, right, (((1,), (1,)), ((), ())), preferred_element_type=F32)


def tn(left, right):
    return lax.dot_general(left, right, (((0,), (0,)), ((), ())), preferred_element_type=F32)


def aligned(index, size=BLOCK):
    return pl.multiple_of(index, size)


def over_rows(rows, chunk, body, carry):
    return lax.fori_loop(
        0, rows // chunk, lambda i, kept: body(pl.ds(aligned(i * chunk, chunk), chunk), kept), carry
    )


def normalize(before):
    centered = before - jnp.mean(before, axis=-1, keepdims=True)
    variance = jnp.mean(centered * centered, axis=-1, keepdims=True)
    rate = lax.rsqrt(variance + EPSILON)
    return centered * rate, rate


def norm_backward(before, upstream, gain_row):
    normed, rate = normalize(before)
    scaled = upstream * gain_row
    first = jnp.mean(scaled, axis=-1, keepdims=True)
    second = jnp.mean(scaled * normed, axis=-1, keepdims=True)
    return rate * (scaled - first - normed * second), upstream * normed


def fold_rows(block):
    return jnp.sum(block.reshape(block.shape[0] // 8, 8, block.shape[1]), axis=0)


def gelu(hidden):
    inner = GELU_IN * (hidden + GELU_CUBE * hidden * hidden * hidden)
    return 0.5 * hidden * (1.0 + jnp.tanh(inner))


def gelu_both(hidden):
    square = hidden * hidden
    bent = jnp.tanh(GELU_IN * hidden * (1.0 + GELU_CUBE * square))
    half = 0.5 * (1.0 + bent)
    slope = half + 0.5 * hidden * (1.0 - bent * bent) * (GELU_IN * (1.0 + 3.0 * GELU_CUBE * square))
    return hidden * half, slope


def head_masks():
    lane = lax.broadcasted_iota(jnp.int32, (1, QUAD), 1)
    return [
        jnp.where((lane >= h * HDIM) & (lane < (h + 1) * HDIM), 1.0, 0.0).astype(BF16)
        for h in range(4)
    ]


def stack_heads(block, masks):
    return jnp.concatenate([block * mask for mask in masks], axis=0)


def window_bias(marks_ref, key_at, width, query_row, causal, key_start, query_start, skip):
    allowed = marks_ref[pl.ds(key_at, width), :] == query_row
    if causal or skip is not None:
        places = key_start + lax.broadcasted_iota(jnp.int32, (width, BLOCK), 0)
        if causal:
            queries = query_start + lax.broadcasted_iota(jnp.int32, (width, BLOCK), 1)
            allowed = allowed & (places <= queries)
        if skip is not None:
            allowed = allowed & (places >= skip)
    return jnp.where(allowed, 0.0, MASKED)


def project_heads(q_ref, k_ref, v_ref, queries, keys, w_query, w_key, w_value):
    for g in range(2):
        at = slice(g * QUAD, (g + 1) * QUAD)
        q_ref[:, at] = (nn(queries, w_query[g]) * SCALE).astype(BF16)
        k_ref[:, at] = nn(keys, w_key[g]).astype(BF16)
        v_ref[:, at] = nn(keys, w_value[g]).astype(BF16)


def self_window(core, block, causal):
    middle = block + core
    if causal:
        return aligned(jnp.maximum(middle - 1, 0) * BLOCK), 2 * BLOCK
    return aligned(jnp.clip(middle - 1, 0, 2) * BLOCK), 3 * BLOCK


def self_forward(core, tokens, q_ref, k_ref, vt_ref, marks_ref, query_marks, bias_ref, ot_ref, lse_ref, causal):
    own = q_ref.shape[0]
    masks = head_masks()
    window_start = core * (tokens - k_ref.shape[0])

    def one_block(block, carry):
        key_at, width = self_window(core, block, causal)
        rows = pl.ds(aligned(block * BLOCK), BLOCK)
        query_row = query_marks[:, pl.ds(aligned(core * own + block * BLOCK), BLOCK)]
        bias_ref[:width, :] = window_bias(
            marks_ref, key_at, width, query_row, causal, window_start + key_at, core * own + block * BLOCK, None
        )
        for g in range(2):
            at = slice(g * QUAD, (g + 1) * QUAD)
            stacked = stack_heads(q_ref[rows, at], masks)
            scores = nt(k_ref[pl.ds(key_at, width), at], stacked)
            for h in range(4):
                one = scores[:, h * BLOCK : (h + 1) * BLOCK] + bias_ref[:width, :]
                top = jnp.max(one, axis=0, keepdims=True)
                weights = jnp.exp(one - top)
                total = jnp.sum(weights, axis=0, keepdims=True)
                feature = g * QUAD + h * HDIM
                mixed = nn(vt_ref[feature : feature + HDIM, pl.ds(key_at, width)], weights.astype(BF16))
                ot_ref[feature : feature + HDIM, rows] = (mixed * (1.0 / total)).astype(BF16)
                lse_ref[g * 4 + h : g * 4 + h + 1, rows] = top + jnp.log(total)
        return carry

    lax.fori_loop(0, own // BLOCK, one_block, 0)


def backward_tile(
    rows, key_at, width, masks, q_ref, k_ref, v_ref, kt_ref, do_ref, bias_ref, lse_ref, delta_ref, dqt_ref, dk_ref, dv_ref, add
):
    keys = pl.ds(key_at, width)
    for g in range(2):
        at = slice(g * QUAD, (g + 1) * QUAD)
        q_stack = stack_heads(q_ref[rows, at], masks)
        do_stack = stack_heads(do_ref[rows, at], masks)
        scores = nt(k_ref[keys, at], q_stack)
        prob_grads = nt(v_ref[keys, at], do_stack)
        probs, score_grads = [], []
        for h in range(4):
            cols = slice(h * BLOCK, (h + 1) * BLOCK)
            head = g * 4 + h
            prob = jnp.exp(scores[:, cols] + bias_ref[:width, :] - lse_ref[head : head + 1, rows])
            score_grad = (prob * (prob_grads[:, cols] - delta_ref[head : head + 1, rows])).astype(BF16)
            probs.append(prob.astype(BF16))
            score_grads.append(score_grad)
            feature = g * QUAD + h * HDIM
            query_grad = nn(kt_ref[feature : feature + HDIM, keys], score_grad)
            if add:
                dqt_ref[feature : feature + HDIM, rows] += query_grad
            else:
                dqt_ref[feature : feature + HDIM, rows] = query_grad
        dv_ref[keys, at] += nn(jnp.concatenate(probs, axis=1), do_stack)
        dk_ref[keys, at] += nn(jnp.concatenate(score_grads, axis=1), q_stack)


def mixed_gradients(branch, ot_ref, w_out, do_ref, delta_ref):
    for g in range(2):
        do_ref[:, g * QUAD : (g + 1) * QUAD] = nt(branch, w_out[g][...]).astype(BF16)
        turned = nt(w_out[g][...], branch).astype(BF16).astype(F32)
        product = turned * ot_ref[g * QUAD : (g + 1) * QUAD, :].astype(F32)
        for h in range(4):
            delta_ref[g * 4 + h : g * 4 + h + 1, :] = jnp.sum(
                product[h * HDIM : (h + 1) * HDIM, :], axis=0, keepdims=True
            )


def spread_marks(marks_ref, column):
    marks_ref[...] = jnp.broadcast_to(column, marks_ref.shape)


def self_part_kernel(causal, encoder, norm_at, core_ref, *refs):
    if encoder:
        (x_ref, col_ref, row_ref, wqkv0, wqkv1, wo0, wo1, up0, up1, down0, down1, gain_ref, shift_ref,
         out_ref, z0_ref, z1_ref, x1_low, h_ref, q_ref, k_ref, v_ref, ot_ref, lse_ref,
         marks_ref, vt_ref, bias_ref, x1_ref, acc_ref) = refs
    else:
        (x_ref, col_ref, row_ref, wqkv0, wqkv1, wo0, wo1, gain_ref, shift_ref,
         x1_ref, x1_low, z0_ref, q_ref, k_ref, v_ref, ot_ref, lse_ref,
         marks_ref, vt_ref, bias_ref, acc_ref) = refs
    core = core_ref[0]
    tokens, own, window = x_ref.shape[0], q_ref.shape[0], k_ref.shape[0]
    start = aligned(core * (tokens - window))
    first = aligned(core * own)
    spread_marks(marks_ref, col_ref[pl.ds(start, window), :])
    keys = x_ref[pl.ds(start, window), :]
    queries = x_ref[pl.ds(first, own), :]
    wqkv = (wqkv0, wqkv1)
    project_heads(
        q_ref, k_ref, v_ref, queries, keys, [w[0] for w in wqkv], [w[1] for w in wqkv], [w[2] for w in wqkv]
    )
    vt_ref[...] = v_ref[...].T
    self_forward(core, tokens, q_ref, k_ref, vt_ref, marks_ref, row_ref, bias_ref, ot_ref, lse_ref, causal)
    acc_ref[...] = tn(ot_ref[:QUAD, :], wo0[...]) + tn(ot_ref[QUAD:, :], wo1[...])
    gain, shift = gain_ref[norm_at : norm_at + 1, :], shift_ref[norm_at : norm_at + 1, :]

    def first_norm(rows, carry):
        residual = x_ref[pl.ds(aligned(first + rows.start, rows.size), rows.size), :].astype(F32)
        before = residual + acc_ref[rows, :]
        z0_ref[rows, :] = before
        after = normalize(before)[0] * gain + shift
        x1_ref[rows, :] = after
        x1_low[rows, :] = after.astype(BF16)
        return carry

    over_rows(own, 64, first_norm, 0)
    if encoder:
        feed_forward(x1_low, (up0, up1), (down0, down1), h_ref, None, acc_ref)
        gain, shift = gain_ref[norm_at + 1 : norm_at + 2, :], shift_ref[norm_at + 1 : norm_at + 2, :]

        def second_norm(rows, carry):
            before = x1_ref[rows, :] + acc_ref[rows, :]
            z1_ref[rows, :] = before
            out_ref[rows, :] = (normalize(before)[0] * gain + shift).astype(BF16)
            return carry

        over_rows(own, 64, second_norm, 0)


def feed_forward(low_ref, ups, downs, h_ref, a_ref, acc_ref):
    width = 512
    half = ups[0].shape[1]
    for g in range(2):
        for j in range(half // width):
            cols = slice(j * width, (j + 1) * width)
            to = slice(g * half + j * width, g * half + (j + 1) * width)
            hidden = nn(low_ref[...], ups[g][:, cols])
            h_ref[:, to] = hidden.astype(h_ref.dtype)
            active = gelu(hidden).astype(BF16)
            if a_ref is not None:
                a_ref[:, to] = active
            term = nn(active, downs[g][cols, :])
            if g == 0 and j == 0:
                acc_ref[...] = term
            else:
                acc_ref[...] += term


def cross_kernel(
    core_ref, src_marks, tgt_marks,
    x2_ref, own_ref, other_ref, cot_ref, col_ref, row_ref, cq0, cq1, ckv0, ckv1, co0, co1, up0, up1, down0, down1,
    gain_ref, shift_ref,
    enc_ref, dec_ref, x3_low, a_ref, dh_ref, dy_ref, denc_own, denc_other, g2_ref, dcq0, dcq1, dckv0, dckv1, dco0, dco1,
    norms_ref,
    q_ref, k_ref, v_ref, turn_ref, marks_ref, bias_ref, ot_ref, lse_ref, x3_ref, z3_ref, z4_ref, acc_ref, h_ref,
    do_ref, delta_ref, dqt_ref, dk_ref, dv_ref,
):
    core = core_ref[0]
    own, tokens = x2_ref.shape[0], enc_ref.shape[0]
    first = aligned(core * own)
    second = aligned((1 - core) * own)
    width = 3 * BLOCK
    last_start = tokens - width
    enc_ref[pl.ds(first, own), :] = own_ref[...]
    enc_ref[pl.ds(second, own), :] = other_ref[...]
    spread_marks(marks_ref, col_ref[...])
    project_heads(
        q_ref, k_ref, v_ref, x2_ref[...].astype(BF16), enc_ref[...],
        [cq0[...], cq1[...]], [ckv0[0], ckv1[0]], [ckv0[1], ckv1[1]],
    )
    turn_ref[...] = v_ref[...].T
    masks = head_masks()
    steps = max(1, math.ceil(math.log2(tokens + 1)))

    def bound(mark, past):
        def step(i, pair):
            low, high = pair
            middle = (low + high) // 2
            value = src_marks[0, jnp.minimum(middle, tokens - 1)]
            below = (low < high) & ((value < mark) | (past & (value == mark)))
            above = (low < high) & jnp.logical_not(below)
            return jnp.where(below, middle + 1, low), jnp.where(above, middle, high)

        return lax.fori_loop(0, steps, step, (jnp.int32(0), jnp.int32(tokens)))[0]

    def key_range(block):
        head = first + block * BLOCK
        low = bound(tgt_marks[0, head], jnp.bool_(False)) // BLOCK * BLOCK
        high = bound(tgt_marks[0, head + BLOCK - 1], jnp.bool_(True))
        return low, (high - low + width - 1) // width

    def set_bias(block, low, i):
        nominal = low + i * width
        key_at = aligned(jnp.minimum(nominal, last_start))
        query_row = row_ref[:, pl.ds(aligned(first + block * BLOCK), BLOCK)]
        bias_ref[...] = window_bias(marks_ref, key_at, width, query_row, False, key_at, 0, nominal)
        return key_at

    def forward_block(block, carry):
        rows = pl.ds(aligned(block * BLOCK), BLOCK)
        low, count = key_range(block)
        acc_ref[...] = jnp.zeros(acc_ref.shape, F32)

        def one_window(i, state):
            tops, totals = state
            key_at = set_bias(block, low, i)
            new_tops, new_totals = [], []
            for g in range(2):
                at = slice(g * QUAD, (g + 1) * QUAD)
                stacked = stack_heads(q_ref[rows, at], masks)
                scores = nt(k_ref[pl.ds(key_at, width), at], stacked)
                for h in range(4):
                    head = g * 4 + h
                    one = scores[:, h * BLOCK : (h + 1) * BLOCK] + bias_ref[...]
                    top = jnp.maximum(tops[head], jnp.max(one, axis=0, keepdims=True))
                    weights = jnp.exp(one - top)
                    fade = jnp.exp(tops[head] - top)
                    new_tops.append(top)
                    new_totals.append(totals[head] * fade + jnp.sum(weights, axis=0, keepdims=True))
                    feature = head * HDIM
                    mixed = nn(turn_ref[feature : feature + HDIM, pl.ds(key_at, width)], weights.astype(BF16))
                    acc_ref[feature : feature + HDIM, :BLOCK] = (
                        acc_ref[feature : feature + HDIM, :BLOCK] * fade + mixed
                    )
            return tuple(new_tops), tuple(new_totals)

        start_top = tuple(jnp.full((1, BLOCK), 2 * MASKED, F32) for _ in range(8))
        start_total = tuple(jnp.zeros((1, BLOCK), F32) for _ in range(8))
        tops, totals = lax.fori_loop(0, count, one_window, (start_top, start_total))
        for head in range(8):
            feature = head * HDIM
            ot_ref[feature : feature + HDIM, rows] = (
                acc_ref[feature : feature + HDIM, :BLOCK] * (1.0 / totals[head])
            ).astype(BF16)
            lse_ref[head : head + 1, rows] = tops[head] + jnp.log(totals[head])
        return carry

    lax.fori_loop(0, own // BLOCK, forward_block, 0)
    acc_ref[...] = tn(ot_ref[:QUAD, :], co0[...]) + tn(ot_ref[QUAD:, :], co1[...])
    gain, shift = gain_ref[3:4, :], shift_ref[3:4, :]

    def third_norm(rows, carry):
        before = x2_ref[rows, :] + acc_ref[rows, :]
        z3_ref[rows, :] = before
        after = normalize(before)[0] * gain + shift
        x3_ref[rows, :] = after
        x3_low[rows, :] = after.astype(BF16)
        return carry

    over_rows(own, 64, third_norm, 0)
    ups, downs = (up0, up1), (down0, down1)
    feed_forward(x3_low, ups, downs, h_ref, a_ref, acc_ref)
    last_gain, last_shift = gain_ref[4:5, :], shift_ref[4:5, :]

    def fourth_norm(rows, sums):
        before = x3_ref[rows, :] + acc_ref[rows, :]
        dec_ref[rows, :] = (normalize(before)[0] * last_gain + last_shift).astype(BF16)
        upstream = cot_ref[rows, :].astype(F32)
        grad, gain_terms = norm_backward(before, upstream, last_gain)
        z4_ref[rows, :] = grad
        dy_ref[rows, :] = grad.astype(BF16)
        return sums[0] + fold_rows(gain_terms), sums[1] + fold_rows(upstream)

    zeros = jnp.zeros((8, x2_ref.shape[1]), F32)
    gain_four, shift_four = over_rows(own, 64, fourth_norm, (zeros, zeros))
    feed_backward(dy_ref, ups, downs, h_ref, dh_ref, z4_ref)

    def third_back(rows, sums):
        upstream = z4_ref[rows, :]
        grad, gain_terms = norm_backward(z3_ref[rows, :], upstream, gain)
        x3_ref[rows, :] = grad
        return sums[0] + fold_rows(gain_terms), sums[1] + fold_rows(upstream)

    gain_three, shift_three = over_rows(own, 64, third_back, (zeros, zeros))
    for row, part in enumerate((gain_three, gain_four, shift_three, shift_four)):
        norms_ref[row : row + 1, :] = jnp.sum(part, axis=0, keepdims=True)
    branch = x3_ref[...].astype(BF16)
    mixed_gradients(branch, ot_ref, (co0, co1), do_ref, delta_ref)
    dco0[...] = nn(ot_ref[:QUAD, :], branch).astype(BF16)
    dco1[...] = nn(ot_ref[QUAD:, :], branch).astype(BF16)
    turn_ref[...] = k_ref[...].T
    dk_ref[...] = jnp.zeros(dk_ref.shape, F32)
    dv_ref[...] = jnp.zeros(dv_ref.shape, F32)
    dqt_ref[...] = jnp.zeros(dqt_ref.shape, F32)

    def backward_block(block, carry):
        rows = pl.ds(aligned(block * BLOCK), BLOCK)
        low, count = key_range(block)

        def one_window(i, inner):
            key_at = set_bias(block, low, i)
            backward_tile(
                rows, key_at, width, masks, q_ref, k_ref, v_ref, turn_ref, do_ref, bias_ref, lse_ref, delta_ref,
                dqt_ref, dk_ref, dv_ref, True,
            )
            return inner

        return lax.fori_loop(0, count, one_window, carry)

    lax.fori_loop(0, own // BLOCK, backward_block, 0)
    dq = (dqt_ref[...] * SCALE).T.astype(BF16)
    key_grad = dk_ref[...].astype(BF16)
    value_grad = dv_ref[...].astype(BF16)
    query_turned = x2_ref[...].T.astype(BF16)
    enc_turned = enc_ref[...].T
    for g, (dcq, dckv) in enumerate(((dcq0, dckv0), (dcq1, dckv1))):
        at = slice(g * QUAD, (g + 1) * QUAD)
        dcq[...] = nn(query_turned, dq[:, at]).astype(BF16)
        dckv[0] = nn(enc_turned, key_grad[:, at]).astype(BF16)
        dckv[1] = nn(enc_turned, value_grad[:, at]).astype(BF16)
    g2_ref[...] = x3_ref[...] + nt(dq[:, :QUAD], cq0[...]) + nt(dq[:, QUAD:], cq1[...])
    dk_ref[...] = (
        nt(key_grad[:, :QUAD], ckv0[0])
        + nt(key_grad[:, QUAD:], ckv1[0])
        + nt(value_grad[:, :QUAD], ckv0[1])
        + nt(value_grad[:, QUAD:], ckv1[1])
    )
    denc_own[...] = dk_ref[pl.ds(first, own), :]
    denc_other[...] = dk_ref[pl.ds(second, own), :].astype(BF16)


def feed_backward(dy_ref, ups, downs, h_ref, dh_ref, acc_ref):
    width = 512
    half = ups[0].shape[1]
    for g in range(2):
        for j in range(half // width):
            cols = slice(j * width, (j + 1) * width)
            to = slice(g * half + j * width, g * half + (j + 1) * width)
            active_grad = nt(dy_ref[...], downs[g][cols, :])
            slope = gelu_both(h_ref[:, to])[1]
            hidden_grad = (active_grad * slope).astype(BF16)
            dh_ref[:, to] = hidden_grad
            acc_ref[...] += nt(hidden_grad, ups[g][:, cols])


def encoder_feed_kernel(
    z1_ref, cot_ref, denc_own, denc_recv, x1_low, h_ref, x3_low, dh3_ref, a3_ref, dy3_ref,
    up0, up1, down0, down1, gain_ref,
    g0_ref, dup0, dup1, ddown0, ddown1, norms_ref,
    dy_ref, turned_ref,
):
    own = z1_ref.shape[0]
    gain = gain_ref[1:2, :]

    def back(rows, sums):
        upstream = cot_ref[rows, :].astype(F32) + denc_own[rows, :] + denc_recv[rows, :].astype(F32)
        grad, gain_terms = norm_backward(z1_ref[rows, :], upstream, gain)
        g0_ref[rows, :] = grad
        dy_ref[rows, :] = grad.astype(BF16)
        return sums[0] + fold_rows(gain_terms), sums[1] + fold_rows(upstream)

    zeros = jnp.zeros((8, z1_ref.shape[1]), F32)
    for row, part in enumerate(over_rows(own, 64, back, (zeros, zeros))):
        norms_ref[row : row + 1, :] = jnp.sum(part, axis=0, keepdims=True)
    turned_ref[0] = x1_low[...].T
    turned_ref[1] = x3_low[...].T
    width = 512
    half = up0.shape[1]
    for g, (up, down, dup, ddown) in enumerate(((up0, down0, dup0, ddown0), (up1, down1, dup1, ddown1))):
        for j in range(half // width):
            cols = slice(j * width, (j + 1) * width)
            to = slice(g * half + j * width, g * half + (j + 1) * width)
            active, slope = gelu_both(h_ref[:, to].astype(F32))
            hidden_grad = (nt(dy_ref[...], down[cols, :]) * slope).astype(BF16)
            g0_ref[...] += nt(hidden_grad, up[:, cols])
            dup[:, cols] = (nn(turned_ref[0], hidden_grad) + nn(turned_ref[1], dh3_ref[:, to])).astype(BF16)
            ddown[cols, :] = (tn(active.astype(BF16), dy_ref[...]) + tn(a3_ref[:, to], dy3_ref[...])).astype(BF16)


def self_back_kernel(causal, norm_at, core_ref, *refs):
    (x_ref, col_ref, row_ref, z_ref, up_ref, q_ref, k_ref, v_ref, ot_ref, lse_ref, wqkv0, wqkv1, wo0, wo1, gain_ref,
     dx_ref, halo_ref, dqkv0, dqkv1, dwo0, dwo1, norms_ref,
     marks_ref, bias_ref, kt_ref, do_ref, delta_ref, dqt_ref, dk_ref, dv_ref, xt_ref) = refs
    core = core_ref[0]
    tokens, own, window = x_ref.shape[0], q_ref.shape[0], k_ref.shape[0]
    start = aligned(core * (tokens - window))
    first = aligned(core * own)
    gain = gain_ref[norm_at : norm_at + 1, :]

    def back(rows, sums):
        upstream = up_ref[rows, :]
        grad, gain_terms = norm_backward(z_ref[rows, :], upstream, gain)
        dx_ref[rows, :] = grad
        return sums[0] + fold_rows(gain_terms), sums[1] + fold_rows(upstream)

    zeros = jnp.zeros((8, z_ref.shape[1]), F32)
    for row, part in enumerate(over_rows(own, 64, back, (zeros, zeros))):
        norms_ref[row : row + 1, :] = jnp.sum(part, axis=0, keepdims=True)
    branch = dx_ref[...].astype(BF16)
    mixed_gradients(branch, ot_ref, (wo0, wo1), do_ref, delta_ref)
    dwo0[...] = nn(ot_ref[:QUAD, :], branch).astype(BF16)
    dwo1[...] = nn(ot_ref[QUAD:, :], branch).astype(BF16)
    kt_ref[...] = k_ref[...].T
    spread_marks(marks_ref, col_ref[pl.ds(start, window), :])
    dk_ref[...] = jnp.zeros(dk_ref.shape, F32)
    dv_ref[...] = jnp.zeros(dv_ref.shape, F32)
    masks = head_masks()

    def one_block(block, carry):
        rows = pl.ds(aligned(block * BLOCK), BLOCK)
        key_at, width = self_window(core, block, causal)
        query_row = row_ref[:, pl.ds(aligned(first + block * BLOCK), BLOCK)]
        bias_ref[:width, :] = window_bias(
            marks_ref, key_at, width, query_row, causal, start + key_at, first + block * BLOCK, None
        )
        backward_tile(
            rows, key_at, width, masks, q_ref, k_ref, v_ref, kt_ref, do_ref, bias_ref, lse_ref, delta_ref,
            dqt_ref, dk_ref, dv_ref, False,
        )
        return carry

    lax.fori_loop(0, own // BLOCK, one_block, 0)
    dq = (dqt_ref[...] * SCALE).T.astype(BF16)
    key_grad = dk_ref[...].astype(BF16)
    value_grad = dv_ref[...].astype(BF16)
    xt_ref[...] = x_ref[pl.ds(start, window), :].T
    query_turned = x_ref[pl.ds(first, own), :].T
    for g, dqkv in enumerate((dqkv0, dqkv1)):
        at = slice(g * QUAD, (g + 1) * QUAD)
        dqkv[0] = nn(query_turned, dq[:, at]).astype(BF16)
        dqkv[1] = nn(xt_ref[...], key_grad[:, at]).astype(BF16)
        dqkv[2] = nn(xt_ref[...], value_grad[:, at]).astype(BF16)
    dk_ref[...] = (
        nt(key_grad[:, :QUAD], wqkv0[1])
        + nt(key_grad[:, QUAD:], wqkv1[1])
        + nt(value_grad[:, :QUAD], wqkv0[2])
        + nt(value_grad[:, QUAD:], wqkv1[2])
    )
    dx_ref[...] = (
        dx_ref[...]
        + nt(dq[:, :QUAD], wqkv0[0])
        + nt(dq[:, QUAD:], wqkv1[0])
        + dk_ref[pl.ds(aligned(core * (window - own)), own), :]
    )
    halo_ref[...] = dk_ref[pl.ds(aligned((1 - core) * own), window - own), :].astype(BF16)


def call(kernel, name, inputs, outs, scratch, smem=1):
    memory = [pl.BlockSpec(memory_space=pltpu.SMEM)] * smem
    memory += [pl.BlockSpec(memory_space=pltpu.VMEM)] * (len(inputs) - smem)
    return pl.pallas_call(
        kernel,
        out_shape=[jax.ShapeDtypeStruct(shape, dtype) for shape, dtype in outs],
        in_specs=memory,
        out_specs=[pl.BlockSpec(memory_space=pltpu.VMEM)] * len(outs),
        scratch_shapes=[pltpu.VMEM(shape, dtype) for shape, dtype in scratch],
        compiler_params=pltpu.CompilerParams(vmem_limit_bytes=VMEM_LIMIT),
        name=name,
    )(*inputs)


def on_device(
    src_embed, tgt_embed, src_segment, tgt_segment, enc_qkv, enc_out_proj, dec_qkv, dec_out_proj, cross_query,
    cross_kv, cross_out_proj, ffn_up, ffn_down, norm_gain, norm_bias, enc_cotangent, dec_cotangent,
):
    tokens, model = src_embed.shape
    own = tokens // lax.axis_size("mp")
    window = own + MOST
    hidden = 2 * ffn_up.shape[1]
    quad = enc_qkv.shape[2]
    position = lax.axis_index("mp")
    core = position.astype(jnp.int32).reshape(1)
    pairs = [(0, 1), (1, 0)]

    def swap(tree):
        return jax.tree.map(lambda a: lax.ppermute(a, "mp", pairs), tree)

    enc_other = swap((enc_qkv, enc_out_proj))
    ffn_other = swap((ffn_up, ffn_down))
    dec_other = swap((dec_qkv, dec_out_proj))
    cross_other = swap((cross_query, cross_kv, cross_out_proj))
    src_column = src_segment.reshape(tokens, 1)
    tgt_column = tgt_segment.reshape(tokens, 1)

    def rows(count, dtype):
        return ((count, model), dtype)

    kept = [rows(own, BF16), rows(window, BF16), rows(window, BF16), ((model, own), BF16), ((8, own), F32)]
    forward_scratch = [((window, BLOCK), jnp.int32), ((model, window), BF16), ((3 * BLOCK, BLOCK), F32)]
    encoder = call(
        functools.partial(self_part_kernel, False, True, 0),
        "encoder_forward",
        (core, src_embed, src_column, src_segment, enc_qkv, enc_other[0], enc_out_proj, enc_other[1],
         ffn_up, ffn_other[0], ffn_down, ffn_other[1], norm_gain, norm_bias),
        [rows(own, BF16), rows(own, F32), rows(own, F32), rows(own, BF16), ((own, hidden), BF16)] + kept,
        forward_scratch + [rows(own, F32), rows(own, F32)],
    )
    enc_own, z0, z1, x1_low, h1 = encoder[:5]
    enc_kept = encoder[5:]
    enc_swapped = swap(enc_own)
    decoder = call(
        functools.partial(self_part_kernel, True, False, 2),
        "decoder_self_forward",
        (core, tgt_embed, tgt_column, tgt_segment, dec_qkv, dec_other[0], dec_out_proj, dec_other[1],
         norm_gain, norm_bias),
        [rows(own, F32), rows(own, BF16), rows(own, F32)] + kept,
        forward_scratch + [rows(own, F32)],
    )
    x2, x2_low, z2 = decoder[:3]
    dec_kept = decoder[3:]
    quads = ((model, quad), BF16)
    pair = ((2, model, quad), BF16)
    triple = ((3, model, quad), BF16)
    out_half = ((quad, model), BF16)
    crossed = call(
        cross_kernel,
        "cross_and_decoder_feed",
        (core, src_segment, tgt_segment,
         x2, enc_own, enc_swapped, dec_cotangent, src_column, tgt_segment, cross_query, cross_other[0],
         cross_kv, cross_other[1], cross_out_proj, cross_other[2],
         ffn_up, ffn_other[0], ffn_down, ffn_other[1], norm_gain, norm_bias),
        [rows(tokens, BF16), rows(own, BF16), rows(own, BF16), ((own, hidden), BF16), ((own, hidden), BF16),
         rows(own, BF16), rows(own, F32), rows(own, BF16), rows(own, F32),
         quads, quads, pair, pair, out_half, out_half, rows(4, F32)],
        [rows(own, BF16), rows(tokens, BF16), rows(tokens, BF16), ((model, tokens), BF16),
         ((tokens, BLOCK), jnp.int32), ((3 * BLOCK, BLOCK), F32), ((model, own), BF16), ((8, own), F32),
         rows(own, F32), rows(own, F32), rows(own, F32), rows(own, F32), ((own, hidden), F32),
         rows(own, BF16), ((8, own), F32), ((model, own), F32), rows(tokens, F32), rows(tokens, F32)],
        smem=3,
    )
    (encoded, dec_own, x3_low, a3, dh3, dy3, denc_own, denc_other, g2,
     dcq0, dcq1, dckv0, dckv1, dco0, dco1, cross_norms) = crossed
    denc_recv = swap(denc_other)
    dec_swapped = swap(dec_own)
    cross_recv = swap((dcq1, dckv1, dco1))
    back_outs = [rows(own, F32), rows(window - own, BF16), triple, triple, out_half, out_half, rows(2, F32)]
    back_scratch = [
        ((window, BLOCK), jnp.int32), ((3 * BLOCK, BLOCK), F32), ((model, window), BF16), rows(own, BF16),
        ((8, own), F32), ((model, own), F32), rows(window, F32), rows(window, F32), ((model, window), BF16),
    ]
    tgt_own, tgt_halo, ddqkv0, ddqkv1, ddo0, ddo1, dec_norms = call(
        functools.partial(self_back_kernel, True, 2),
        "decoder_self_backward",
        (core, tgt_embed, tgt_column, tgt_segment, z2, g2, *dec_kept,
         dec_qkv, dec_other[0], dec_out_proj, dec_other[1], norm_gain),
        back_outs, back_scratch,
    )
    tgt_recv = swap(tgt_halo)
    dec_recv = swap((ddqkv1, ddo1))
    g0, dup0, dup1, ddown0, ddown1, feed_norms = call(
        encoder_feed_kernel,
        "encoder_feed_backward",
        (z1, enc_cotangent, denc_own, denc_recv, x1_low, h1, x3_low, dh3, a3, dy3,
         ffn_up, ffn_other[0], ffn_down, ffn_other[1], norm_gain),
        [rows(own, F32), ((model, hidden // 2), BF16), ((model, hidden // 2), BF16),
         ((hidden // 2, model), BF16), ((hidden // 2, model), BF16), rows(2, F32)],
        [rows(own, BF16), ((2, model, own), BF16)],
        smem=0,
    )
    feed_recv = swap((dup1, ddown1))
    src_own, src_halo, deqkv0, deqkv1, deo0, deo1, enc_norms = call(
        functools.partial(self_back_kernel, False, 0),
        "encoder_self_backward",
        (core, src_embed, src_column, src_segment, z0, g0, *enc_kept,
         enc_qkv, enc_other[0], enc_out_proj, enc_other[1], norm_gain),
        back_outs, back_scratch,
    )
    src_recv = swap(src_halo)
    enc_recv = swap((deqkv1, deo1))
    norms = jnp.concatenate(
        [enc_norms[0:1], feed_norms[0:1], dec_norms[0:1], cross_norms[0:2],
         enc_norms[1:2], feed_norms[1:2], dec_norms[1:2], cross_norms[2:4]]
    )
    norms_low = norms.astype(BF16)
    norm_sum = (norms + swap(norms_low).astype(F32)).astype(BF16)

    def total(mine, received):
        return lax.psum(jax.tree.map(lambda a, b: a + b, mine, received), "dp")

    cross_sums = total((dcq0, dckv0, dco0), cross_recv)
    dec_sums = total((ddqkv0, ddo0), dec_recv)
    feed_sums = total((dup0, ddown0), feed_recv)
    enc_sums = lax.psum(
        (deqkv0 + enc_recv[0], deo0 + enc_recv[1], norm_sum), "dp"
    )

    def whole(mine, received):
        return jnp.where(
            position == 0, jnp.concatenate([mine, received]), jnp.concatenate([received, mine])
        )

    halo_at = (1 - position) * (own - (window - own))

    def with_halo(grad, received):
        part = lax.dynamic_slice_in_dim(grad, halo_at, window - own, 0) + received.astype(F32)
        return lax.dynamic_update_slice_in_dim(grad, part, halo_at, 0)

    wide = lambda a: a.astype(F32)
    return (
        encoded,
        whole(dec_own, dec_swapped),
        with_halo(src_own, src_recv),
        with_halo(tgt_own, tgt_recv),
        wide(enc_sums[0]),
        wide(enc_sums[1]),
        wide(dec_sums[0]),
        wide(dec_sums[1]),
        wide(cross_sums[0]),
        wide(cross_sums[1]),
        wide(cross_sums[2]),
        wide(feed_sums[0]),
        wide(feed_sums[1]),
        wide(enc_sums[2][:5]),
        wide(enc_sums[2][5:]),
    )


def solution(mesh):
    in_specs = (
        P("dp", None), P("dp", None), P("dp", None), P("dp", None),
        P(None, None, "mp"), P("mp", None), P(None, None, "mp"), P("mp", None),
        P(None, "mp"), P(None, None, "mp"), P("mp", None), P(None, "mp"), P("mp", None),
        P(), P(), P(("dp", "mp"), None), P(("dp", "mp"), None),
    )
    out_specs = (
        P("dp", None), P("dp", None), P(("dp", "mp"), None), P(("dp", "mp"), None),
        P(None, None, "mp"), P("mp", None), P(None, None, "mp"), P("mp", None),
        P(None, "mp"), P(None, None, "mp"), P("mp", None), P(None, "mp"), P("mp", None),
        P(), P(),
    )
    return jax.shard_map(on_device, mesh=mesh, in_specs=in_specs, out_specs=out_specs, check_vma=False)
```

```python
import functools
import math

import jax
import jax.numpy as jnp
from jax import lax
from jax.experimental import pallas as pl
from jax.experimental.pallas import tpu as pltpu
from jax.sharding import PartitionSpec as P

HDIM = 64
SCALE = HDIM ** (-0.5)
EPSILON = 1e-05
MASKED = -1e30
BLOCK = 128
MOST = 128
QUAD = 4 * HDIM
UNITS = 4
TILE = 16
F32 = jnp.float32
BF16 = jnp.bfloat16
VMEM_LIMIT = 56 * 1024 * 1024
GELU_IN = math.sqrt(2.0 / math.pi)
GELU_CUBE = 0.044715


def nn(left, right):
    return jnp.dot(left, right, preferred_element_type=F32)


def nt(left, right):
    return lax.dot_general(left, right, (((1,), (1,)), ((), ())), preferred_element_type=F32)


def tn(left, right):
    return lax.dot_general(left, right, (((0,), (0,)), ((), ())), preferred_element_type=F32)


def aligned(index, size=BLOCK):
    return pl.multiple_of(index, size)


def over_rows(rows, chunk, body, carry):
    return lax.fori_loop(
        0, rows // chunk, lambda i, kept: body(pl.ds(aligned(i * chunk, chunk), chunk), kept), carry
    )


def normalize(before):
    centered = before - jnp.mean(before, axis=-1, keepdims=True)
    variance = jnp.mean(centered * centered, axis=-1, keepdims=True)
    rate = lax.rsqrt(variance + EPSILON)
    return centered * rate, rate


def norm_backward(before, upstream, gain_row):
    normed, rate = normalize(before)
    scaled = upstream * gain_row
    first = jnp.mean(scaled, axis=-1, keepdims=True)
    second = jnp.mean(scaled * normed, axis=-1, keepdims=True)
    return rate * (scaled - first - normed * second), upstream * normed


def fold_rows(block):
    return jnp.sum(block.reshape(block.shape[0] // 8, 8, block.shape[1]), axis=0)


def gelu(hidden):
    inner = GELU_IN * (hidden + GELU_CUBE * hidden * hidden * hidden)
    return 0.5 * hidden * (1.0 + jnp.tanh(inner))


def gelu_both(hidden):
    square = hidden * hidden
    bent = jnp.tanh(GELU_IN * hidden * (1.0 + GELU_CUBE * square))
    half = 0.5 * (1.0 + bent)
    slope = half + 0.5 * hidden * (1.0 - bent * bent) * (GELU_IN * (1.0 + 3.0 * GELU_CUBE * square))
    return hidden * half, slope


def head_masks():
    lane = lax.broadcasted_iota(jnp.int32, (1, QUAD), 1)
    return [
        jnp.where((lane >= h * HDIM) & (lane < (h + 1) * HDIM), 1.0, 0.0).astype(BF16)
        for h in range(4)
    ]


def stack_heads(block, masks):
    return jnp.concatenate([block * mask for mask in masks], axis=0)


def window_bias(marks_ref, key_at, width, query_row, causal, key_start, query_start, skip):
    allowed = marks_ref[pl.ds(key_at, width), :] == query_row
    if causal or skip is not None:
        places = key_start + lax.broadcasted_iota(jnp.int32, (width, BLOCK), 0)
        if causal:
            queries = query_start + lax.broadcasted_iota(jnp.int32, (width, BLOCK), 1)
            allowed = allowed & (places <= queries)
        if skip is not None:
            allowed = allowed & (places >= skip)
    return jnp.where(allowed, 0.0, MASKED)


def project_heads(q_ref, k_ref, v_ref, queries, keys, w_query, w_key, w_value):
    for g in range(2):
        at = slice(g * QUAD, (g + 1) * QUAD)
        q_ref[:, at] = (nn(queries, w_query[g]) * SCALE).astype(BF16)
        k_ref[:, at] = nn(keys, w_key[g]).astype(BF16)
        v_ref[:, at] = nn(keys, w_value[g]).astype(BF16)


def self_window(core, block, causal):
    middle = block + core
    if causal:
        return aligned(jnp.maximum(middle - 1, 0) * BLOCK), 2 * BLOCK
    return aligned(jnp.clip(middle - 1, 0, 2) * BLOCK), 3 * BLOCK


def self_forward(core, tokens, q_ref, k_ref, vt_ref, marks_ref, query_marks, bias_ref, ot_ref, lse_ref, causal):
    own = q_ref.shape[0]
    masks = head_masks()
    window_start = core * (tokens - k_ref.shape[0])

    def one_block(block, carry):
        key_at, width = self_window(core, block, causal)
        rows = pl.ds(aligned(block * BLOCK), BLOCK)
        query_row = query_marks[:, pl.ds(aligned(core * own + block * BLOCK), BLOCK)]
        bias_ref[:width, :] = window_bias(
            marks_ref, key_at, width, query_row, causal, window_start + key_at, core * own + block * BLOCK, None
        )
        for g in range(2):
            at = slice(g * QUAD, (g + 1) * QUAD)
            stacked = stack_heads(q_ref[rows, at], masks)
            scores = nt(k_ref[pl.ds(key_at, width), at], stacked)
            for h in range(4):
                one = scores[:, h * BLOCK : (h + 1) * BLOCK] + bias_ref[:width, :]
                top = jnp.max(one, axis=0, keepdims=True)
                weights = jnp.exp(one - top)
                total = jnp.sum(weights, axis=0, keepdims=True)
                feature = g * QUAD + h * HDIM
                mixed = nn(vt_ref[feature : feature + HDIM, pl.ds(key_at, width)], weights.astype(BF16))
                ot_ref[feature : feature + HDIM, rows] = (mixed * (1.0 / total)).astype(BF16)
                lse_ref[g * 4 + h : g * 4 + h + 1, rows] = top + jnp.log(total)
        return carry

    lax.fori_loop(0, own // BLOCK, one_block, 0)


def backward_tile(
    rows, key_at, width, masks, q_ref, k_ref, v_ref, kt_ref, do_ref, bias_ref, lse_ref, delta_ref, dqt_ref, dk_ref, dv_ref, add
):
    keys = pl.ds(key_at, width)
    for g in range(2):
        at = slice(g * QUAD, (g + 1) * QUAD)
        q_stack = stack_heads(q_ref[rows, at], masks)
        do_stack = stack_heads(do_ref[rows, at], masks)
        scores = nt(k_ref[keys, at], q_stack)
        prob_grads = nt(v_ref[keys, at], do_stack)
        probs, score_grads = [], []
        for h in range(4):
            cols = slice(h * BLOCK, (h + 1) * BLOCK)
            head = g * 4 + h
            prob = jnp.exp(scores[:, cols] + bias_ref[:width, :] - lse_ref[head : head + 1, rows])
            score_grad = (prob * (prob_grads[:, cols] - delta_ref[head : head + 1, rows])).astype(BF16)
            probs.append(prob.astype(BF16))
            score_grads.append(score_grad)
            feature = g * QUAD + h * HDIM
            query_grad = nn(kt_ref[feature : feature + HDIM, keys], score_grad)
            if add:
                dqt_ref[feature : feature + HDIM, rows] += query_grad
            else:
                dqt_ref[feature : feature + HDIM, rows] = query_grad
        dv_ref[keys, at] += nn(jnp.concatenate(probs, axis=1), do_stack)
        dk_ref[keys, at] += nn(jnp.concatenate(score_grads, axis=1), q_stack)


def mixed_gradients(branch, ot_ref, w_out, do_ref, delta_ref):
    for g in range(2):
        do_ref[:, g * QUAD : (g + 1) * QUAD] = nt(branch, w_out[g][...]).astype(BF16)
        turned = nt(w_out[g][...], branch).astype(BF16).astype(F32)
        product = turned * ot_ref[g * QUAD : (g + 1) * QUAD, :].astype(F32)
        for h in range(4):
            delta_ref[g * 4 + h : g * 4 + h + 1, :] = jnp.sum(
                product[h * HDIM : (h + 1) * HDIM, :], axis=0, keepdims=True
            )


def spread_marks(marks_ref, row):
    marks_ref[...] = jnp.broadcast_to(row, (marks_ref.shape[1], marks_ref.shape[0])).T


def core_and_place(ids_ref):
    return ids_ref[0], ids_ref[1]


def slot(core, place, shard, bits):
    apart = place ^ shard
    first, second = apart & 1, (apart >> 1) & 1
    index = jnp.where(core == 0, 2 * first + second, 2 * second + first)
    for k in range(2, bits):
        index = 2 * index + ((apart >> k) & 1)
    return index


def pack(out_ref, core, place, unit, value):
    shards = out_ref.shape[0]
    rows = UNITS * value.shape[0] // shards
    per_unit = shards // UNITS
    for i in range(per_unit):
        at = slot(core, place, unit * per_unit + i, shards.bit_length() - 1)
        out_ref[pl.ds(at, 1), :rows, :] = value[i * rows : (i + 1) * rows][None]


def pack_columns(out_ref, core, place, unit, value):
    pack(out_ref, core, place, unit, jnp.concatenate([value[:, :QUAD], value[:, QUAD:]], axis=0))


def norm_rows(shards):
    return -(-20 // shards)


def pack_norms(out_ref, core, place, parts):
    shards, tall, width = out_ref.shape
    each = norm_rows(shards)
    halves = [part[:, half * width : (half + 1) * width] for part in parts for half in range(2)]
    blank = jnp.zeros((1, width), F32)
    halves += [blank] * (shards * each - len(halves))
    for i in range(shards):
        block = jnp.concatenate(halves[i * each : (i + 1) * each] + [blank] * (TILE - each), axis=0)
        out_ref[pl.ds(slot(core, place, i, shards.bit_length() - 1), 1), tall - TILE :, :] = block.astype(BF16)[None]


def finish_kernel(kind, ids_ref, *refs):
    core, place = core_and_place(ids_ref)
    gathered, sem = refs[-2:]
    shards = gathered.shape[0]
    each = UNITS * 2 * QUAD // shards
    per_unit = shards // UNITS
    count = len(refs) - 2 - {"self": 4, "cross": 3, "up": 1, "down": 1}[kind]
    parts, outs = refs[:count], refs[count:-2]
    size = shards // count
    copies = [
        pltpu.make_async_copy(part, gathered.at[pl.ds(i * size, size)], sem.at[i]) for i, part in enumerate(parts)
    ]
    for copy in copies:
        copy.start()
    for copy in copies:
        copy.wait()
    for shard in range(shards):
        unit, at = shard // per_unit, shard % per_unit * each
        where = slot(core, place, shard, shards.bit_length() - 1)
        value = gathered[pl.ds(where, 1), :each, :][0].astype(F32)
        rows = slice(at, at + each)
        if kind == "up":
            outs[0][rows, unit * QUAD : (unit + 1) * QUAD] = value
        elif kind == "down":
            down = slice(unit // 2 * 2 * QUAD + at, unit // 2 * 2 * QUAD + at + each)
            outs[0][down, unit % 2 * QUAD : (unit % 2 + 1) * QUAD] = value
        elif unit == 3:
            half = at // QUAD
            outs[2 if kind == "cross" else 1][at - half * QUAD : at - half * QUAD + each, half * QUAD : (half + 1) * QUAD] = value
        elif kind == "self":
            outs[0][unit, rows, :] = value
        elif unit == 0:
            outs[0][rows, :] = value
        else:
            outs[1][unit - 1, rows, :] = value
        if kind == "self" and gathered.shape[1] > each:
            norms = gathered[pl.ds(where, 1), each:, :][0].astype(F32)
            many = norm_rows(shards)
            for i in range(many):
                row, half = divmod(shard * many + i, 2)
                if row < 10:
                    outs[2 + row // 5][row % 5 : row % 5 + 1, half * QUAD : (half + 1) * QUAD] = norms[i : i + 1, :]


def self_part_kernel(causal, encoder, norm_at, ids_ref, *refs):
    if encoder:
        (x_ref, row_ref, wqkv0, wqkv1, wo0, wo1, up0, up1, down0, down1, gain_ref, shift_ref,
         out_ref, z0_ref, z1_ref, x1_low, h_ref, q_ref, k_ref, v_ref, ot_ref, lse_ref,
         marks_ref, vt_ref, bias_ref, x1_ref, acc_ref) = refs
    else:
        (x_ref, row_ref, wqkv0, wqkv1, wo0, wo1, gain_ref, shift_ref,
         x1_ref, x1_low, z0_ref, q_ref, k_ref, v_ref, ot_ref, lse_ref,
         marks_ref, vt_ref, bias_ref, acc_ref) = refs
    core, place = core_and_place(ids_ref)
    tokens, own, window = x_ref.shape[0], q_ref.shape[0], k_ref.shape[0]
    start = aligned(core * (tokens - window))
    first = aligned(core * own)
    spread_marks(marks_ref, row_ref[:, pl.ds(start, window)])
    keys = x_ref[pl.ds(start, window), :]
    queries = x_ref[pl.ds(first, own), :]
    wqkv = (wqkv0, wqkv1)
    project_heads(
        q_ref, k_ref, v_ref, queries, keys, [w[0] for w in wqkv], [w[1] for w in wqkv], [w[2] for w in wqkv]
    )
    vt_ref[...] = v_ref[...].T
    self_forward(core, tokens, q_ref, k_ref, vt_ref, marks_ref, row_ref, bias_ref, ot_ref, lse_ref, causal)
    acc_ref[...] = tn(ot_ref[:QUAD, :], wo0[...]) + tn(ot_ref[QUAD:, :], wo1[...])
    gain, shift = gain_ref[norm_at : norm_at + 1, :], shift_ref[norm_at : norm_at + 1, :]

    def first_norm(rows, carry):
        residual = x_ref[pl.ds(aligned(first + rows.start, rows.size), rows.size), :].astype(F32)
        before = residual + acc_ref[rows, :]
        z0_ref[rows, :] = before
        after = normalize(before)[0] * gain + shift
        x1_ref[rows, :] = after
        x1_low[rows, :] = after.astype(BF16)
        return carry

    over_rows(own, 64, first_norm, 0)
    if encoder:
        feed_forward(x1_low, (up0, up1), (down0, down1), h_ref, None, acc_ref)
        gain, shift = gain_ref[norm_at + 1 : norm_at + 2, :], shift_ref[norm_at + 1 : norm_at + 2, :]

        def second_norm(rows, carry):
            before = x1_ref[rows, :] + acc_ref[rows, :]
            z1_ref[rows, :] = before
            out_ref[rows, :] = (normalize(before)[0] * gain + shift).astype(BF16)
            return carry

        over_rows(own, 64, second_norm, 0)


def feed_forward(low_ref, ups, downs, h_ref, a_ref, acc_ref):
    width = 512
    half = ups[0].shape[1]
    for g in range(2):
        for j in range(half // width):
            cols = slice(j * width, (j + 1) * width)
            to = slice(g * half + j * width, g * half + (j + 1) * width)
            hidden = nn(low_ref[...], ups[g][:, cols])
            h_ref[:, to] = hidden.astype(h_ref.dtype)
            active = gelu(hidden).astype(BF16)
            if a_ref is not None:
                a_ref[:, to] = active
            term = nn(active, downs[g][cols, :])
            if g == 0 and j == 0:
                acc_ref[...] = term
            else:
                acc_ref[...] += term


def cross_kernel(
    ids_ref, src_marks, tgt_marks,
    x2_ref, own_ref, other_ref, cot_ref, src_row, row_ref, cq0, cq1, ckv0, ckv1, co0, co1, up0, up1, down0, down1,
    gain_ref, shift_ref,
    enc_ref, dec_ref, x3_low, a_ref, dh_ref, dy_ref, denc_own, denc_other, g2_ref, pack0, pack1, norms_ref,
    q_ref, k_ref, v_ref, turn_ref, marks_ref, bias_ref, ot_ref, lse_ref, x3_ref, z3_ref, z4_ref, acc_ref, h_ref,
    do_ref, delta_ref, dqt_ref, dk_ref, dv_ref,
):
    core, place = core_and_place(ids_ref)
    own, tokens = x2_ref.shape[0], enc_ref.shape[0]
    first = aligned(core * own)
    second = aligned((1 - core) * own)
    width = 3 * BLOCK
    last_start = tokens - width
    enc_ref[pl.ds(first, own), :] = own_ref[...]
    enc_ref[pl.ds(second, own), :] = other_ref[...]
    spread_marks(marks_ref, src_row[...])
    project_heads(
        q_ref, k_ref, v_ref, x2_ref[...].astype(BF16), enc_ref[...],
        [cq0[...], cq1[...]], [ckv0[0], ckv1[0]], [ckv0[1], ckv1[1]],
    )
    turn_ref[...] = v_ref[...].T
    masks = head_masks()
    steps = max(1, math.ceil(math.log2(tokens + 1)))

    def bound(mark, past):
        def step(i, pair):
            low, high = pair
            middle = (low + high) // 2
            value = src_marks[0, jnp.minimum(middle, tokens - 1)]
            below = (low < high) & ((value < mark) | (past & (value == mark)))
            above = (low < high) & jnp.logical_not(below)
            return jnp.where(below, middle + 1, low), jnp.where(above, middle, high)

        return lax.fori_loop(0, steps, step, (jnp.int32(0), jnp.int32(tokens)))[0]

    def key_range(block):
        head = first + block * BLOCK
        low = bound(tgt_marks[0, head], jnp.bool_(False)) // BLOCK * BLOCK
        high = bound(tgt_marks[0, head + BLOCK - 1], jnp.bool_(True))
        return low, (high - low + width - 1) // width

    def set_bias(block, low, i):
        nominal = low + i * width
        key_at = aligned(jnp.minimum(nominal, last_start))
        query_row = row_ref[:, pl.ds(aligned(first + block * BLOCK), BLOCK)]
        bias_ref[...] = window_bias(marks_ref, key_at, width, query_row, False, key_at, 0, nominal)
        return key_at

    def forward_block(block, carry):
        rows = pl.ds(aligned(block * BLOCK), BLOCK)
        low, count = key_range(block)
        acc_ref[...] = jnp.zeros(acc_ref.shape, F32)

        def one_window(i, state):
            tops, totals = state
            key_at = set_bias(block, low, i)
            new_tops, new_totals = [], []
            for g in range(2):
                at = slice(g * QUAD, (g + 1) * QUAD)
                stacked = stack_heads(q_ref[rows, at], masks)
                scores = nt(k_ref[pl.ds(key_at, width), at], stacked)
                for h in range(4):
                    head = g * 4 + h
                    one = scores[:, h * BLOCK : (h + 1) * BLOCK] + bias_ref[...]
                    top = jnp.maximum(tops[head], jnp.max(one, axis=0, keepdims=True))
                    weights = jnp.exp(one - top)
                    fade = jnp.exp(tops[head] - top)
                    new_tops.append(top)
                    new_totals.append(totals[head] * fade + jnp.sum(weights, axis=0, keepdims=True))
                    feature = head * HDIM
                    mixed = nn(turn_ref[feature : feature + HDIM, pl.ds(key_at, width)], weights.astype(BF16))
                    acc_ref[feature : feature + HDIM, :BLOCK] = (
                        acc_ref[feature : feature + HDIM, :BLOCK] * fade + mixed
                    )
            return tuple(new_tops), tuple(new_totals)

        start_top = tuple(jnp.full((1, BLOCK), 2 * MASKED, F32) for _ in range(8))
        start_total = tuple(jnp.zeros((1, BLOCK), F32) for _ in range(8))
        tops, totals = lax.fori_loop(0, count, one_window, (start_top, start_total))
        for head in range(8):
            feature = head * HDIM
            ot_ref[feature : feature + HDIM, rows] = (
                acc_ref[feature : feature + HDIM, :BLOCK] * (1.0 / totals[head])
            ).astype(BF16)
            lse_ref[head : head + 1, rows] = tops[head] + jnp.log(totals[head])
        return carry

    lax.fori_loop(0, own // BLOCK, forward_block, 0)
    acc_ref[...] = tn(ot_ref[:QUAD, :], co0[...]) + tn(ot_ref[QUAD:, :], co1[...])
    gain, shift = gain_ref[3:4, :], shift_ref[3:4, :]

    def third_norm(rows, carry):
        before = x2_ref[rows, :] + acc_ref[rows, :]
        z3_ref[rows, :] = before
        after = normalize(before)[0] * gain + shift
        x3_ref[rows, :] = after
        x3_low[rows, :] = after.astype(BF16)
        return carry

    over_rows(own, 64, third_norm, 0)
    ups, downs = (up0, up1), (down0, down1)
    feed_forward(x3_low, ups, downs, h_ref, a_ref, acc_ref)
    last_gain, last_shift = gain_ref[4:5, :], shift_ref[4:5, :]

    def fourth_norm(rows, sums):
        before = x3_ref[rows, :] + acc_ref[rows, :]
        dec_ref[rows, :] = (normalize(before)[0] * last_gain + last_shift).astype(BF16)
        upstream = cot_ref[rows, :].astype(F32)
        grad, gain_terms = norm_backward(before, upstream, last_gain)
        z4_ref[rows, :] = grad
        dy_ref[rows, :] = grad.astype(BF16)
        return sums[0] + fold_rows(gain_terms), sums[1] + fold_rows(upstream)

    zeros = jnp.zeros((8, x2_ref.shape[1]), F32)
    gain_four, shift_four = over_rows(own, 64, fourth_norm, (zeros, zeros))
    feed_backward(dy_ref, ups, downs, h_ref, dh_ref, z4_ref)

    def third_back(rows, sums):
        upstream = z4_ref[rows, :]
        grad, gain_terms = norm_backward(z3_ref[rows, :], upstream, gain)
        x3_ref[rows, :] = grad
        return sums[0] + fold_rows(gain_terms), sums[1] + fold_rows(upstream)

    gain_three, shift_three = over_rows(own, 64, third_back, (zeros, zeros))
    for row, part in enumerate((gain_three, gain_four, shift_three, shift_four)):
        norms_ref[row : row + 1, :] = jnp.sum(part, axis=0, keepdims=True)
    branch = x3_ref[...].astype(BF16)
    mixed_gradients(branch, ot_ref, (co0, co1), do_ref, delta_ref)
    packs = ((pack0, core), (pack1, 1 - core))
    for g, (packed, side) in enumerate(packs):
        pack_columns(packed, side, place, 3, nn(ot_ref[g * QUAD : (g + 1) * QUAD, :], branch).astype(BF16))
    turn_ref[...] = k_ref[...].T
    dk_ref[...] = jnp.zeros(dk_ref.shape, F32)
    dv_ref[...] = jnp.zeros(dv_ref.shape, F32)
    dqt_ref[...] = jnp.zeros(dqt_ref.shape, F32)

    def backward_block(block, carry):
        rows = pl.ds(aligned(block * BLOCK), BLOCK)
        low, count = key_range(block)

        def one_window(i, inner):
            key_at = set_bias(block, low, i)
            backward_tile(
                rows, key_at, width, masks, q_ref, k_ref, v_ref, turn_ref, do_ref, bias_ref, lse_ref, delta_ref,
                dqt_ref, dk_ref, dv_ref, True,
            )
            return inner

        return lax.fori_loop(0, count, one_window, carry)

    lax.fori_loop(0, own // BLOCK, backward_block, 0)
    dq = (dqt_ref[...] * SCALE).T.astype(BF16)
    key_grad = dk_ref[...].astype(BF16)
    value_grad = dv_ref[...].astype(BF16)
    query_turned = x2_ref[...].T.astype(BF16)
    enc_turned = enc_ref[...].T
    for g, (packed, side) in enumerate(packs):
        at = slice(g * QUAD, (g + 1) * QUAD)
        pack(packed, side, place, 0, nn(query_turned, dq[:, at]).astype(BF16))
        pack(packed, side, place, 1, nn(enc_turned, key_grad[:, at]).astype(BF16))
        pack(packed, side, place, 2, nn(enc_turned, value_grad[:, at]).astype(BF16))
    g2_ref[...] = x3_ref[...] + nt(dq[:, :QUAD], cq0[...]) + nt(dq[:, QUAD:], cq1[...])
    dk_ref[...] = (
        nt(key_grad[:, :QUAD], ckv0[0])
        + nt(key_grad[:, QUAD:], ckv1[0])
        + nt(value_grad[:, :QUAD], ckv0[1])
        + nt(value_grad[:, QUAD:], ckv1[1])
    )
    denc_own[...] = dk_ref[pl.ds(first, own), :]
    denc_other[...] = dk_ref[pl.ds(second, own), :].astype(BF16)


def feed_backward(dy_ref, ups, downs, h_ref, dh_ref, acc_ref):
    width = 512
    half = ups[0].shape[1]
    for g in range(2):
        for j in range(half // width):
            cols = slice(j * width, (j + 1) * width)
            to = slice(g * half + j * width, g * half + (j + 1) * width)
            active_grad = nt(dy_ref[...], downs[g][cols, :])
            slope = gelu_both(h_ref[:, to])[1]
            hidden_grad = (active_grad * slope).astype(BF16)
            dh_ref[:, to] = hidden_grad
            acc_ref[...] += nt(hidden_grad, ups[g][:, cols])


def feed_chunks(half, width=512):
    for g in range(2):
        for j in range(half // width):
            yield g, j, slice(j * width, (j + 1) * width), slice(g * half + j * width, g * half + (j + 1) * width)


def feed_down_kernel(
    ids_ref,
    z1_ref, cot_ref, denc_own, denc_recv, h_ref, a3_ref, dy3_ref, gain_ref,
    dz_ref, dy_ref, pack0, pack1, norms_ref,
):
    core, place = core_and_place(ids_ref)
    own = z1_ref.shape[0]
    gain = gain_ref[1:2, :]

    def back(rows, sums):
        upstream = cot_ref[rows, :].astype(F32) + denc_own[rows, :] + denc_recv[rows, :].astype(F32)
        grad, gain_terms = norm_backward(z1_ref[rows, :], upstream, gain)
        dz_ref[rows, :] = grad
        dy_ref[rows, :] = grad.astype(BF16)
        return sums[0] + fold_rows(gain_terms), sums[1] + fold_rows(upstream)

    zeros = jnp.zeros((8, z1_ref.shape[1]), F32)
    for row, part in enumerate(over_rows(own, 64, back, (zeros, zeros))):
        norms_ref[row : row + 1, :] = jnp.sum(part, axis=0, keepdims=True)
    packs = ((pack0, core), (pack1, 1 - core))
    for g, j, cols, to in feed_chunks(h_ref.shape[1] // 2):
        active = gelu(h_ref[:, to].astype(F32)).astype(BF16)
        down_grad = (tn(active, dy_ref[...]) + tn(a3_ref[:, to], dy3_ref[...])).astype(BF16)
        packed, side = packs[g]
        pack(packed, side, place, 2 * j, down_grad[:, :QUAD])
        pack(packed, side, place, 2 * j + 1, down_grad[:, QUAD:])


def feed_up_kernel(
    ids_ref,
    dz_ref, dy_ref, x1_low, h_ref, x3_low, dh3_ref, up0, up1, down0, down1,
    g0_ref, pack0, pack1,
    turned_ref,
):
    core, place = core_and_place(ids_ref)
    turned_ref[0] = x1_low[...].T
    turned_ref[1] = x3_low[...].T
    g0_ref[...] = dz_ref[...]
    packs = ((pack0, core, up0, down0), (pack1, 1 - core, up1, down1))
    for g, j, cols, to in feed_chunks(h_ref.shape[1] // 2):
        packed, side, up, down = packs[g]
        slope = gelu_both(h_ref[:, to].astype(F32))[1]
        hidden_grad = (nt(dy_ref[...], down[cols, :]) * slope).astype(BF16)
        g0_ref[...] += nt(hidden_grad, up[:, cols])
        up_grad = (nn(turned_ref[0], hidden_grad) + nn(turned_ref[1], dh3_ref[:, to])).astype(BF16)
        pack(packed, side, place, 2 * j, up_grad[:, :QUAD])
        pack(packed, side, place, 2 * j + 1, up_grad[:, QUAD:])


def self_back_kernel(causal, norm_at, ids_ref, *refs):
    others = ()
    if not causal:
        others, refs = refs[:3], refs[3:]
    (x_ref, row_ref, z_ref, up_ref, q_ref, k_ref, v_ref, ot_ref, lse_ref, wqkv0, wqkv1, wo0, wo1, gain_ref,
     dx_ref, halo_ref, pack0, pack1, norms_ref,
     marks_ref, bias_ref, kt_ref, do_ref, delta_ref, dqt_ref, dk_ref, dv_ref, xt_ref) = refs
    core, place = core_and_place(ids_ref)
    tokens, own, window = x_ref.shape[0], q_ref.shape[0], k_ref.shape[0]
    start = aligned(core * (tokens - window))
    first = aligned(core * own)
    gain = gain_ref[norm_at : norm_at + 1, :]

    def back(rows, sums):
        upstream = up_ref[rows, :]
        grad, gain_terms = norm_backward(z_ref[rows, :], upstream, gain)
        dx_ref[rows, :] = grad
        return sums[0] + fold_rows(gain_terms), sums[1] + fold_rows(upstream)

    zeros = jnp.zeros((8, z_ref.shape[1]), F32)
    for row, part in enumerate(over_rows(own, 64, back, (zeros, zeros))):
        norms_ref[row : row + 1, :] = jnp.sum(part, axis=0, keepdims=True)
    branch = dx_ref[...].astype(BF16)
    mixed_gradients(branch, ot_ref, (wo0, wo1), do_ref, delta_ref)
    packs = ((pack0, core), (pack1, 1 - core))
    for g, (packed, side) in enumerate(packs):
        pack_columns(packed, side, place, 3, nn(ot_ref[g * QUAD : (g + 1) * QUAD, :], branch).astype(BF16))
    if not causal:
        feed_norms, dec_norms, cross_norms = others
        gains = [norms_ref[0:1, :], feed_norms[0:1, :], dec_norms[0:1, :], cross_norms[0:1, :], cross_norms[1:2, :]]
        shifts = [norms_ref[1:2, :], feed_norms[1:2, :], dec_norms[1:2, :], cross_norms[2:3, :], cross_norms[3:4, :]]
        for packed, side in packs:
            pack_norms(packed, side, place, gains + shifts)
    kt_ref[...] = k_ref[...].T
    spread_marks(marks_ref, row_ref[:, pl.ds(start, window)])
    dk_ref[...] = jnp.zeros(dk_ref.shape, F32)
    dv_ref[...] = jnp.zeros(dv_ref.shape, F32)
    masks = head_masks()

    def one_block(block, carry):
        rows = pl.ds(aligned(block * BLOCK), BLOCK)
        key_at, width = self_window(core, block, causal)
        query_row = row_ref[:, pl.ds(aligned(first + block * BLOCK), BLOCK)]
        bias_ref[:width, :] = window_bias(
            marks_ref, key_at, width, query_row, causal, start + key_at, first + block * BLOCK, None
        )
        backward_tile(
            rows, key_at, width, masks, q_ref, k_ref, v_ref, kt_ref, do_ref, bias_ref, lse_ref, delta_ref,
            dqt_ref, dk_ref, dv_ref, False,
        )
        return carry

    lax.fori_loop(0, own // BLOCK, one_block, 0)
    dq = (dqt_ref[...] * SCALE).T.astype(BF16)
    key_grad = dk_ref[...].astype(BF16)
    value_grad = dv_ref[...].astype(BF16)
    xt_ref[...] = x_ref[pl.ds(start, window), :].T
    query_turned = x_ref[pl.ds(first, own), :].T
    for g, (packed, side) in enumerate(packs):
        at = slice(g * QUAD, (g + 1) * QUAD)
        pack(packed, side, place, 0, nn(query_turned, dq[:, at]).astype(BF16))
        pack(packed, side, place, 1, nn(xt_ref[...], key_grad[:, at]).astype(BF16))
        pack(packed, side, place, 2, nn(xt_ref[...], value_grad[:, at]).astype(BF16))
    dk_ref[...] = (
        nt(key_grad[:, :QUAD], wqkv0[1])
        + nt(key_grad[:, QUAD:], wqkv1[1])
        + nt(value_grad[:, :QUAD], wqkv0[2])
        + nt(value_grad[:, QUAD:], wqkv1[2])
    )
    dx_ref[...] = (
        dx_ref[...]
        + nt(dq[:, :QUAD], wqkv0[0])
        + nt(dq[:, QUAD:], wqkv1[0])
        + dk_ref[pl.ds(aligned(core * (window - own)), own), :]
    )
    halo_ref[...] = dk_ref[pl.ds(aligned((1 - core) * own), window - own), :].astype(BF16)


def call(kernel, name, inputs, outs, scratch, smem=1):
    memory = [pl.BlockSpec(memory_space=pltpu.SMEM)] * smem
    memory += [pl.BlockSpec(memory_space=pltpu.VMEM)] * (len(inputs) - smem)
    return pl.pallas_call(
        kernel,
        out_shape=[jax.ShapeDtypeStruct(shape, dtype) for shape, dtype in outs],
        in_specs=memory,
        out_specs=[pl.BlockSpec(memory_space=pltpu.VMEM)] * len(outs),
        scratch_shapes=[pltpu.VMEM(shape, dtype) for shape, dtype in scratch],
        compiler_params=pltpu.CompilerParams(vmem_limit_bytes=VMEM_LIMIT),
        name=name,
    )(*inputs)


def exchange(array, step, dp, mp):
    pairs = []
    for place in range(dp):
        for core in range(mp):
            bit = (1 - step if core else step) if step < 2 else step
            pairs.append((place * mp + core, (place ^ (1 << bit)) * mp + core))
    return lax.ppermute(array, ("dp", "mp"), pairs)


class Sum:
    def __init__(self, mine, other, dp, mp, kind):
        self.dp, self.mp, self.kind = dp, mp, kind
        self.bits = dp.bit_length() - 1
        self.step = 0
        self.keep, self.sent = mine, lax.ppermute(other, "mp", [(0, 1), (1, 0)])
        self.parts = None

    def advance(self):
        if self.parts is None:
            half = self.keep.shape[0] // 2
            if half:
                give = self.keep[half:] + self.sent[half:]
                self.keep = self.keep[:half] + self.sent[:half]
                give, self.keep = lax.optimization_barrier((give, self.keep))
                self.sent = exchange(give, self.step, self.dp, self.mp)
                self.step += 1
                return True
            self.parts = [self.keep + self.sent]
            self.arriving = []
        else:
            self.parts = self.parts + self.arriving
        if self.step == 0:
            return False
        self.step -= 1
        if len(self.parts) > 2:
            self.parts = [jnp.concatenate(self.parts)]
        self.arriving = [exchange(part, self.step, self.dp, self.mp) for part in self.parts]
        return True

    def state(self):
        return (self.keep, self.parts) if self.parts else (self.keep,)


def on_device(
    src_embed, tgt_embed, src_segment, tgt_segment, enc_qkv, enc_out_proj, dec_qkv, dec_out_proj, cross_query,
    cross_kv, cross_out_proj, ffn_up, ffn_down, norm_gain, norm_bias, enc_cotangent, dec_cotangent,
):
    dp, mp = lax.axis_size("dp"), lax.axis_size("mp")
    tokens, model = src_embed.shape
    own = tokens // mp
    window = own + MOST
    half = ffn_up.shape[1]
    hidden = 2 * half
    position = lax.axis_index("mp")
    ids = jnp.stack([position, lax.axis_index("dp")]).astype(jnp.int32)
    pairs = [(0, 1), (1, 0)]

    def swap(tree):
        return jax.tree.map(lambda a: lax.ppermute(a, "mp", pairs), tree)

    enc_other = swap((enc_qkv, enc_out_proj))
    ffn_other = swap((ffn_up, ffn_down))
    dec_other = swap((dec_qkv, dec_out_proj))
    cross_other = swap((cross_query, cross_kv, cross_out_proj))

    def rows(count, dtype):
        return ((count, model), dtype)

    kept = [rows(own, BF16), rows(window, BF16), rows(window, BF16), ((model, own), BF16), ((8, own), F32)]
    forward_scratch = [((window, BLOCK), jnp.int32), ((model, window), BF16), ((3 * BLOCK, BLOCK), F32)]
    encoder = call(
        functools.partial(self_part_kernel, False, True, 0),
        "encoder_forward",
        (ids, src_embed, src_segment, enc_qkv, enc_other[0], enc_out_proj, enc_other[1],
         ffn_up, ffn_other[0], ffn_down, ffn_other[1], norm_gain, norm_bias),
        [rows(own, BF16), rows(own, F32), rows(own, F32), rows(own, BF16), ((own, hidden), BF16)] + kept,
        forward_scratch + [rows(own, F32), rows(own, F32)],
    )
    enc_own, z0, z1, x1_low, h1 = encoder[:5]
    enc_kept = encoder[5:]
    enc_swapped = swap(enc_own)
    decoder = call(
        functools.partial(self_part_kernel, True, False, 2),
        "decoder_self_forward",
        (ids, tgt_embed, tgt_segment, dec_qkv, dec_other[0], dec_out_proj, dec_other[1], norm_gain, norm_bias),
        [rows(own, F32), rows(own, BF16), rows(own, F32)] + kept,
        forward_scratch + [rows(own, F32)],
    )
    x2, x2_low, z2 = decoder[:3]
    dec_kept = decoder[3:]
    pack_rows = UNITS * 2 * QUAD // dp
    packed = ((dp, pack_rows, QUAD), BF16)
    packed_norms = ((dp, pack_rows + TILE, QUAD), BF16)
    crossed = call(
        cross_kernel,
        "cross_and_decoder_feed",
        (ids, src_segment, tgt_segment,
         x2, enc_own, enc_swapped, dec_cotangent, src_segment, tgt_segment, cross_query, cross_other[0],
         cross_kv, cross_other[1], cross_out_proj, cross_other[2],
         ffn_up, ffn_other[0], ffn_down, ffn_other[1], norm_gain, norm_bias),
        [rows(tokens, BF16), rows(own, BF16), rows(own, BF16), ((own, hidden), BF16), ((own, hidden), BF16),
         rows(own, BF16), rows(own, F32), rows(own, BF16), rows(own, F32), packed, packed, rows(4, F32)],
        [rows(own, BF16), rows(tokens, BF16), rows(tokens, BF16), ((model, tokens), BF16),
         ((tokens, BLOCK), jnp.int32), ((3 * BLOCK, BLOCK), F32), ((model, own), BF16), ((8, own), F32),
         rows(own, F32), rows(own, F32), rows(own, F32), rows(own, F32), ((own, hidden), F32),
         rows(own, BF16), ((8, own), F32), ((model, own), F32), rows(tokens, F32), rows(tokens, F32)],
        smem=3,
    )
    (encoded, dec_own, x3_low, a3, dh3, dy3, denc_own, denc_other, g2, cross0, cross1, cross_norms) = crossed
    denc_recv = swap(denc_other)
    dec_swapped = swap(dec_own)
    sums = [Sum(cross0, cross1, dp, mp, "cross")]

    def advance(gate):
        for group in sums:
            group.advance()
        states = [group.state() for group in sums]
        gate, states = lax.optimization_barrier((gate, states))
        for group, state in zip(sums, states):
            group.keep = state[0]
            if len(state) > 1:
                group.parts = state[1]
        return gate

    back_scratch = [
        ((window, BLOCK), jnp.int32), ((3 * BLOCK, BLOCK), F32), ((model, window), BF16), rows(own, BF16),
        ((8, own), F32), ((model, own), F32), rows(window, F32), rows(window, F32), ((model, window), BF16),
    ]

    def back_outs(pack_shape):
        return [rows(own, F32), rows(window - own, BF16), pack_shape, pack_shape, rows(2, F32)]

    tgt_own, tgt_halo, dec0, dec1, dec_norms = call(
        functools.partial(self_back_kernel, True, 2),
        "decoder_self_backward",
        (ids, tgt_embed, tgt_segment, z2, g2, *dec_kept,
         dec_qkv, dec_other[0], dec_out_proj, dec_other[1], norm_gain),
        back_outs(packed), back_scratch,
    )
    tgt_recv = swap(tgt_halo)
    z1 = advance(z1)
    sums.append(Sum(dec0, dec1, dp, mp, "self"))
    dz1, dy1, down0, down1, feed_norms = call(
        feed_down_kernel,
        "encoder_feed_down_backward",
        (ids, z1, enc_cotangent, denc_own, denc_recv, h1, a3, dy3, norm_gain),
        [rows(own, F32), rows(own, BF16), packed, packed, rows(2, F32)], [],
    )
    dy1 = advance(dy1)
    sums.append(Sum(down0, down1, dp, mp, "down"))
    g0, up0, up1 = call(
        feed_up_kernel,
        "encoder_feed_up_backward",
        (ids, dz1, dy1, x1_low, h1, x3_low, dh3, ffn_up, ffn_other[0], ffn_down, ffn_other[1]),
        [rows(own, F32), packed, packed], [((2, model, own), BF16)],
    )
    g0 = advance(g0)
    sums.append(Sum(up0, up1, dp, mp, "up"))
    src_own, src_halo, enc0, enc1, enc_norms = call(
        functools.partial(self_back_kernel, False, 0),
        "encoder_self_backward",
        (ids, feed_norms, dec_norms, cross_norms, src_embed, src_segment, z0, g0, *enc_kept,
         enc_qkv, enc_other[0], enc_out_proj, enc_other[1], norm_gain),
        back_outs(packed_norms), back_scratch,
    )
    src_recv = swap(src_halo)
    sums.append(Sum(enc0, enc1, dp, mp, "self"))

    def whole(mine, received):
        return jnp.where(
            position == 0, jnp.concatenate([mine, received]), jnp.concatenate([received, mine])
        )

    halo_at = (1 - position) * (own - (window - own))

    def with_halo(grad, received):
        part = lax.dynamic_slice_in_dim(grad, halo_at, window - own, 0) + received.astype(F32)
        return lax.dynamic_update_slice_in_dim(grad, part, halo_at, 0)

    square = ((2 * QUAD, QUAD), F32)
    out_half = ((QUAD, model), F32)
    norm_out = ((5, model), F32)
    out_shapes = {
        "cross": [square, ((2, model, QUAD), F32), out_half],
        "self": [((3, model, QUAD), F32), out_half],
        "down": [((half, model), F32)],
        "up": [((model, half), F32)],
    }
    moving = list(sums)
    while moving:
        moving = [group for group in moving if group.advance()]
    results = []
    for i, group in enumerate(sums):
        last = i == len(sums) - 1
        outs = out_shapes[group.kind] + ([norm_out] * 2 if last else [])
        if group.kind == "self" and not last:
            outs = outs + [((8, BLOCK), F32)] * 2
        results.append(finish(group, ids, outs))
    cross_out, dec_out, down_out, up_out, enc_out = results
    return (
        encoded,
        whole(dec_own, dec_swapped),
        with_halo(src_own, src_recv),
        with_halo(tgt_own, tgt_recv),
        enc_out[0],
        enc_out[1],
        dec_out[0],
        dec_out[1],
        cross_out[0],
        cross_out[1],
        cross_out[2],
        up_out[0],
        down_out[0],
        enc_out[2],
        enc_out[3],
    )


def finish(group, ids, outs):
    parts = group.parts
    shape = (sum(part.shape[0] for part in parts),) + parts[0].shape[1:]
    return pl.pallas_call(
        functools.partial(finish_kernel, group.kind),
        out_shape=[jax.ShapeDtypeStruct(shape, dtype) for shape, dtype in outs],
        in_specs=[pl.BlockSpec(memory_space=pltpu.SMEM)] + [pl.BlockSpec(memory_space=pl.ANY)] * len(parts),
        out_specs=[pl.BlockSpec(memory_space=pltpu.VMEM)] * len(outs),
        scratch_shapes=[pltpu.VMEM(shape, BF16), pltpu.SemaphoreType.DMA((len(parts),))],
        compiler_params=pltpu.CompilerParams(vmem_limit_bytes=VMEM_LIMIT),
        name="finish_" + group.kind,
    )(ids, *parts)


def solution(mesh):
    in_specs = (
        P("dp", None), P("dp", None), P("dp", None), P("dp", None),
        P(None, None, "mp"), P("mp", None), P(None, None, "mp"), P("mp", None),
        P(None, "mp"), P(None, None, "mp"), P("mp", None), P(None, "mp"), P("mp", None),
        P(), P(), P(("dp", "mp"), None), P(("dp", "mp"), None),
    )
    out_specs = (
        P("dp", None), P("dp", None), P(("dp", "mp"), None), P(("dp", "mp"), None),
        P(None, None, "mp"), P("mp", None), P(None, None, "mp"), P("mp", None),
        P(None, "mp"), P(None, None, "mp"), P("mp", None), P(None, "mp"), P("mp", None),
        P(), P(),
    )
    return jax.shard_map(on_device, mesh=mesh, in_specs=in_specs, out_specs=out_specs, check_vma=False)
```

```python
import functools
import math
from types import SimpleNamespace

import jax
import jax.numpy as jnp
from jax import lax
from jax.experimental import pallas as pl
from jax.experimental.pallas import tpu as pltpu
from jax.sharding import PartitionSpec as P

HDIM = 64
SCALE = HDIM ** (-0.5)
EPSILON = 1e-05
MASKED = -1e30
BLOCK = 128
MOST = 128
QUAD = 4 * HDIM
UNITS = 4
TILE = 16
FEED = 512
F32 = jnp.float32
BF16 = jnp.bfloat16
VMEM_LIMIT = 56 * 1024 * 1024
GELU_IN = math.sqrt(2.0 / math.pi)
GELU_CUBE = 0.044715


def nn(left, right):
    return jnp.dot(left, right, preferred_element_type=F32)


def nt(left, right):
    return lax.dot_general(left, right, (((1,), (1,)), ((), ())), preferred_element_type=F32)


def tn(left, right):
    return lax.dot_general(left, right, (((0,), (0,)), ((), ())), preferred_element_type=F32)


def aligned(index, size=BLOCK):
    return pl.multiple_of(index, size)


def over_rows(rows, chunk, body, carry, unroll=4):
    return lax.fori_loop(
        0,
        rows // chunk,
        lambda i, kept: body(pl.ds(aligned(i * chunk, chunk), chunk), kept),
        carry,
        unroll=min(unroll, rows // chunk),
    )


def normalize(before):
    centered = before - jnp.mean(before, axis=-1, keepdims=True)
    variance = jnp.mean(centered * centered, axis=-1, keepdims=True)
    rate = lax.rsqrt(variance + EPSILON)
    return centered * rate, rate


def norm_backward(before, upstream, gain_row):
    normed, rate = normalize(before)
    scaled = upstream * gain_row
    first = jnp.mean(scaled, axis=-1, keepdims=True)
    second = jnp.mean(scaled * normed, axis=-1, keepdims=True)
    return rate * (scaled - first - normed * second), upstream * normed


def fold_rows(block):
    return jnp.sum(block.reshape(block.shape[0] // 8, 8, block.shape[1]), axis=0)


def gelu(hidden):
    inner = GELU_IN * hidden * (1.0 + GELU_CUBE * hidden * hidden)
    return 0.5 * hidden * (1.0 + jnp.tanh(inner))


def gelu_both(hidden):
    square = hidden * hidden
    bent = jnp.tanh(GELU_IN * hidden * (1.0 + GELU_CUBE * square))
    half = 0.5 * (1.0 + bent)
    slope = half + 0.5 * hidden * (1.0 - bent * bent) * (GELU_IN * (1.0 + 3.0 * GELU_CUBE * square))
    return hidden * half, slope


def head_masks():
    lane = lax.broadcasted_iota(jnp.int32, (1, QUAD), 1)
    return [
        jnp.where((lane >= h * HDIM) & (lane < (h + 1) * HDIM), 1.0, 0.0).astype(BF16)
        for h in range(4)
    ]


def stack_heads(block, masks):
    return jnp.concatenate([block * mask for mask in masks], axis=0)


def quad(g):
    return slice(g * QUAD, (g + 1) * QUAD)


def bias_for(marks_ref, key_at, width, query_row, causal=False, key_start=0, query_start=0):
    allowed = marks_ref[pl.ds(key_at, width), :] == query_row
    if causal:
        places = key_start + lax.broadcasted_iota(jnp.int32, (width, BLOCK), 0)
        queries = query_start + lax.broadcasted_iota(jnp.int32, (width, BLOCK), 1)
        allowed = allowed & (places <= queries)
    return jnp.where(allowed, 0.0, MASKED)


def self_window(core, block, causal):
    middle = block + core
    if causal:
        return aligned(jnp.maximum(middle - 1, 0) * BLOCK), 2 * BLOCK
    return aligned(jnp.clip(middle - 1, 0, 2) * BLOCK), 3 * BLOCK


def set_self_bias(bias_ref, core, tokens, marks_ref, row_ref, causal):
    window, own = marks_ref.shape[0], row_ref.shape[1] // 2
    start = core * (tokens - window)
    spots = []
    for block in range(own // BLOCK):
        key_at, width = self_window(core, block, causal)
        first = aligned(core * own + block * BLOCK)
        bias_ref[block, :width, :] = bias_for(
            marks_ref, key_at, width, row_ref[:, pl.ds(first, BLOCK)], causal, start + key_at, first
        )
        spots.append((key_at, width))
    return spots


def quad_forward(spots, q_ref, k_ref, vt_ref, bias_ref, ot_ref, lse_ref, masks):
    for block, (key_at, width) in enumerate(spots):
        rows = slice(block * BLOCK, (block + 1) * BLOCK)
        scores = nt(k_ref[pl.ds(key_at, width), :], stack_heads(q_ref[rows, :], masks))
        for h in range(4):
            one = scores[:, h * BLOCK : (h + 1) * BLOCK] + bias_ref[block, :width, :]
            top = jnp.max(one, axis=0, keepdims=True)
            weights = jnp.exp(one - top)
            total = jnp.sum(weights, axis=0, keepdims=True)
            features = slice(h * HDIM, (h + 1) * HDIM)
            mixed = nn(vt_ref[features, pl.ds(key_at, width)], weights.astype(BF16))
            ot_ref[features, rows] = (mixed * (1.0 / total)).astype(BF16)
            lse_ref[h : h + 1, rows] = top + jnp.log(total)


def backward_tile(
    g, rows, key_at, bias, masks, q_ref, k_ref, v_ref, kt_ref, do_ref, lse_ref, delta_ref, dqt_ref, dk_ref, dv_ref, add
):
    keys = pl.ds(key_at, bias.shape[0])
    q_stack = stack_heads(q_ref[rows, :], masks)
    do_stack = stack_heads(do_ref[rows, quad(g)], masks)
    scores = nt(k_ref[keys, :], q_stack)
    prob_grads = nt(v_ref[keys, :], do_stack)
    probs, score_grads = [], []
    for h in range(4):
        cols = slice(h * BLOCK, (h + 1) * BLOCK)
        head = g * 4 + h
        prob = jnp.exp(scores[:, cols] + bias - lse_ref[h : h + 1, rows])
        score_grad = (prob * (prob_grads[:, cols] - delta_ref[head : head + 1, rows])).astype(BF16)
        probs.append(prob.astype(BF16))
        score_grads.append(score_grad)
        features = slice(head * HDIM, (head + 1) * HDIM)
        query_grad = nn(kt_ref[features, keys], score_grad)
        if add:
            dqt_ref[features, rows] += query_grad
        else:
            dqt_ref[features, rows] = query_grad
    dv_ref[keys, quad(g)] += nn(jnp.concatenate(probs, axis=1), do_stack)
    dk_ref[keys, quad(g)] += nn(jnp.concatenate(score_grads, axis=1), q_stack)


def mixed_gradients(branch, ot_refs, w_out, do_ref, delta_ref):
    for g in range(2):
        do_ref[:, quad(g)] = nt(branch, w_out[g][...]).astype(BF16)
        turned = nt(w_out[g][...], branch).astype(BF16).astype(F32)
        product = turned * ot_refs[g][...].astype(F32)
        for h in range(4):
            delta_ref[g * 4 + h : g * 4 + h + 1, :] = jnp.sum(
                product[h * HDIM : (h + 1) * HDIM, :], axis=0, keepdims=True
            )


def spread_marks(marks_ref, row):
    marks_ref[...] = jnp.broadcast_to(row, (marks_ref.shape[1], marks_ref.shape[0])).T


def slot(core, place, shard, bits):
    apart = place ^ shard
    first, second = apart & 1, (apart >> 1) & 1
    index = jnp.where(core == 0, 2 * first + second, 2 * second + first)
    for k in range(2, bits):
        index = 2 * index + ((apart >> k) & 1)
    return index


def pack(out_ref, core, place, unit, value):
    shards = out_ref.shape[0]
    rows = UNITS * value.shape[0] // shards
    per_unit = shards // UNITS
    for i in range(per_unit):
        at = slot(core, place, unit * per_unit + i, shards.bit_length() - 1)
        out_ref[pl.ds(at, 1), :rows, :] = value[i * rows : (i + 1) * rows][None]


def pack_columns(out_ref, core, place, unit, value):
    pack(out_ref, core, place, unit, jnp.concatenate([value[:, :QUAD], value[:, QUAD:]], axis=0))


def norm_rows(shards):
    return -(-20 // shards)


def pack_norms(out_ref, core, place, parts):
    shards, tall, width = out_ref.shape
    each = norm_rows(shards)
    halves = [part[:, half * width : (half + 1) * width] for part in parts for half in range(2)]
    blank = jnp.zeros((1, width), F32)
    halves += [blank] * (shards * each - len(halves))
    for i in range(shards):
        block = jnp.concatenate(halves[i * each : (i + 1) * each] + [blank] * (TILE - each), axis=0)
        out_ref[pl.ds(slot(core, place, i, shards.bit_length() - 1), 1), tall - TILE :, :] = block.astype(BF16)[None]


def prepare_quad(x_ref, w_ref, core, q_ref, k_ref, v_ref, vt_ref):
    tokens, own, window = x_ref.shape[0], q_ref.shape[0], k_ref.shape[0]
    keys = x_ref[pl.ds(aligned(core * (tokens - window)), window), :]
    q_ref[...] = (nn(x_ref[pl.ds(aligned(core * own), own), :], w_ref[0]) * SCALE).astype(BF16)
    k_ref[...] = nn(keys, w_ref[1]).astype(BF16)
    v_ref[...] = nn(keys, w_ref[2]).astype(BF16)
    vt_ref[...] = v_ref[...].T


def own_heads_kernel(r):
    core = r.ids[0]
    masks = head_masks()
    for side, causal in (("src", False), ("tgt", True)):
        x_ref, row_ref = r.get(side), r.get(side + "_row")
        k_ref = r.out(side + "_k")
        start = aligned(core * (x_ref.shape[0] - k_ref.shape[0]))
        spread_marks(r.marks, row_ref[:, pl.ds(start, k_ref.shape[0])])
        bias_ref, vt_ref = getattr(r, side + "_bias"), getattr(r, side + "_vt")
        spots = set_self_bias(bias_ref, core, x_ref.shape[0], r.marks, row_ref, causal)
        q_ref, v_ref = r.out(side + "_q"), r.out(side + "_v")
        prepare_quad(x_ref, r.get(side + "_w"), core, q_ref, k_ref, v_ref, vt_ref)
        for key in ("_q", "_k", "_v"):
            r.send(side + key)
        quad_forward(spots, q_ref, k_ref, vt_ref, bias_ref, r.out(side + "_ot"), r.out(side + "_lse"), masks)
        r.send(side + "_ot")
        r.send(side + "_lse")


def other_heads(r, causal):
    core = r.ids[0]
    x_ref, row_ref, k_ref = r.get("x"), r.get("row"), r.out("k")
    start = aligned(core * (x_ref.shape[0] - k_ref.shape[0]))
    spread_marks(r.marks, row_ref[:, pl.ds(start, k_ref.shape[0])])
    spots = set_self_bias(r.bias, core, x_ref.shape[0], r.marks, row_ref, causal)
    q_ref, v_ref, ot_ref = r.out("q"), r.out("v"), r.out("ot")
    prepare_quad(x_ref, r.get("w"), core, q_ref, k_ref, v_ref, r.vt)
    for key in ("q", "k", "v"):
        r.send(key)
    quad_forward(spots, q_ref, k_ref, r.vt, r.bias, ot_ref, r.out("lse"), head_masks())
    r.send("lse")
    r.send("ot")
    r.acc[...] = tn(r.get("ot0")[...], r.get("wo0")[...]) + tn(ot_ref[...], r.get("wo1")[...])


def norm_forward(r, at, residual, before_ref, after_ref, low_ref):
    gain, shift = r.get("gain")[at : at + 1, :], r.get("shift")[at : at + 1, :]

    def body(rows, carry):
        before = residual(rows) + r.acc[rows, :]
        if before_ref is not None:
            before_ref[rows, :] = before
        after = normalize(before)[0] * gain + shift
        if after_ref is not None:
            after_ref[rows, :] = after
        if low_ref is not None:
            low_ref[rows, :] = after.astype(BF16)
        return carry

    over_rows(r.acc.shape[0], 32, body, 0)


def own_row_reader(x_ref, core, own):
    first = core * own
    return lambda rows: x_ref[pl.ds(aligned(first + rows.start, rows.size), rows.size), :].astype(F32)


def encoder_kernel(r):
    other_heads(r, False)
    x1_low = r.out("x1_low")
    norm_forward(r, 0, own_row_reader(r.get("x"), r.ids[0], r.acc.shape[0]), r.out("z0"), r.x1, x1_low)
    r.send("z0")
    r.send("x1_low")
    feed_forward(x1_low, *feed_weights(r), r.out("h"), None, r.acc)
    r.send("h")
    norm_forward(r, 1, lambda rows: r.x1[rows, :], r.out("z1"), None, r.out("enc"))


def decoder_kernel(r):
    other_heads(r, True)
    norm_forward(r, 2, own_row_reader(r.get("x"), r.ids[0], r.acc.shape[0]), r.out("z2"), r.out("x2"), None)


def feed_weights(r):
    return (r.get("up0"), r.get("up1")), (r.get("down0"), r.get("down1"))


def feed_chunks(half):
    for g in range(2):
        for j in range(half // FEED):
            yield g, j, slice(j * FEED, (j + 1) * FEED), slice(g * half + j * FEED, g * half + (j + 1) * FEED)


def feed_forward(low_ref, ups, downs, h_ref, a_ref, acc_ref):
    for g, j, cols, to in feed_chunks(ups[0].shape[1]):
        hidden = nn(low_ref[...], ups[g][:, cols])
        h_ref[:, to] = hidden.astype(h_ref.dtype)
        active = gelu(hidden).astype(BF16)
        if a_ref is not None:
            a_ref[:, to] = active
        term = nn(active, downs[g][cols, :])
        if g == 0 and j == 0:
            acc_ref[...] = term
        else:
            acc_ref[...] += term


def feed_backward(dy_ref, ups, downs, h_ref, dh_ref, acc_ref):
    for g, j, cols, to in feed_chunks(ups[0].shape[1]):
        active_grad = nt(dy_ref[...], downs[g][cols, :])
        slope = gelu_both(h_ref[:, to])[1]
        hidden_grad = (active_grad * slope).astype(BF16)
        dh_ref[:, to] = hidden_grad
        acc_ref[...] += nt(hidden_grad, ups[g][:, cols])


def norm_back(r, gain_row, before, upstream, outs):
    def body(rows, sums):
        above = upstream(rows)
        grad, gain_terms = norm_backward(before(rows), above, gain_row)
        for ref in outs:
            ref[rows, :] = grad.astype(ref.dtype)
        return sums[0] + fold_rows(gain_terms), sums[1] + fold_rows(above)

    zeros = jnp.zeros((8, outs[0].shape[1]), F32)
    gains, shifts = over_rows(outs[0].shape[0], 32, body, (zeros, zeros))
    return jnp.sum(gains, axis=0, keepdims=True), jnp.sum(shifts, axis=0, keepdims=True)


def cross_kernel(r):
    core, place = r.ids[0], r.ids[1]
    x2_ref, enc_ref = r.get("x2"), r.out("enc")
    own, tokens = x2_ref.shape[0], enc_ref.shape[0]
    blocks = own // BLOCK
    first, second = aligned(core * own), aligned((1 - core) * own)
    width = 3 * BLOCK
    enc_ref[pl.ds(first, own), :] = r.get("enc_own")[...]
    enc_ref[pl.ds(second, own), :] = r.get("enc_other")[...]
    r.send("enc")
    spread_marks(r.marks, r.get("src_row")[...])
    steps = tokens.bit_length()

    def bound(mark, past):
        def step(i, pair):
            low, high = pair
            middle = (low + high) // 2
            value = r.src_marks[0, jnp.minimum(middle, tokens - 1)]
            below = (low < high) & ((value < mark) | (past & (value == mark)))
            above = (low < high) & jnp.logical_not(below)
            return jnp.where(below, middle + 1, low), jnp.where(above, middle, high)

        return lax.fori_loop(0, steps, step, (jnp.int32(0), jnp.int32(tokens)))[0]

    row_ref = r.get("tgt_row")
    query_rows, spots, more = [], [], []
    for block in range(blocks):
        head = first + block * BLOCK
        low = bound(r.tgt_marks[0, head], jnp.bool_(False)) // BLOCK
        high = (bound(r.tgt_marks[0, head + BLOCK - 1], jnp.bool_(True)) + BLOCK - 1) // BLOCK
        key_at = aligned(jnp.minimum(low, (tokens - width) // BLOCK) * BLOCK)
        query_rows.append(row_ref[:, pl.ds(aligned(head), BLOCK)])
        spots.append(key_at)
        more.append((key_at // BLOCK + 3, high))
        r.bias[block] = bias_for(r.marks, key_at, width, query_rows[block])
    masks = head_masks()
    x2_low = x2_ref[...].astype(BF16)
    for g in range(2):
        r.q[g] = (nn(x2_low, r.get(f"cq{g}")[...]) * SCALE).astype(BF16)
        r.k[g] = nn(enc_ref[...], r.get(f"ckv{g}")[0]).astype(BF16)
        r.v[g] = nn(enc_ref[...], r.get(f"ckv{g}")[1]).astype(BF16)
        r.turn[quad(g), :] = r.v[g].T

    def weigh(g, h, scores, bias, key_at, keys_width, top):
        one = scores[:, h * BLOCK : (h + 1) * BLOCK] + bias
        new_top = jnp.max(one, axis=0, keepdims=True)
        if top is not None:
            new_top = jnp.maximum(top, new_top)
        weights = jnp.exp(one - new_top)
        features = slice(g * QUAD + h * HDIM, g * QUAD + (h + 1) * HDIM)
        mixed = nn(r.turn[features, pl.ds(key_at, keys_width)], weights.astype(BF16))
        return new_top, jnp.sum(weights, axis=0, keepdims=True), mixed, features

    for block in range(blocks):
        rows = slice(block * BLOCK, (block + 1) * BLOCK)
        for g in range(2):
            scores = nt(r.k[g, pl.ds(spots[block], width), :], stack_heads(r.q[g, rows, :], masks))
            for h in range(4):
                top, total, mixed, features = weigh(g, h, scores, r.bias[block], spots[block], width, None)
                r.mix[features, rows] = mixed
                r.tops[g * 4 + h : g * 4 + h + 1, rows] = top
                r.totals[g * 4 + h : g * 4 + h + 1, rows] = total

    for block in range(blocks):
        rows = slice(block * BLOCK, (block + 1) * BLOCK)

        def extra(i, carry, block=block, rows=rows):
            key_at = aligned(i * BLOCK)
            bias = bias_for(r.marks, key_at, BLOCK, query_rows[block])
            for g in range(2):
                scores = nt(r.k[g, pl.ds(key_at, BLOCK), :], stack_heads(r.q[g, rows, :], masks))
                for h in range(4):
                    at = slice(g * 4 + h, g * 4 + h + 1)
                    old = r.tops[at, rows]
                    top, total, mixed, features = weigh(g, h, scores, bias, key_at, BLOCK, old)
                    fade = jnp.exp(old - top)
                    r.mix[features, rows] = r.mix[features, rows] * fade + mixed
                    r.tops[at, rows] = top
                    r.totals[at, rows] = r.totals[at, rows] * fade + total
            return carry

        lax.fori_loop(*more[block], extra, 0)
    for head in range(8):
        features = slice(head * HDIM, (head + 1) * HDIM)
        at = slice(head, head + 1)
        r.ot[features, :] = (r.mix[features, :] * (1.0 / r.totals[at, :])).astype(BF16)
        r.lse[head // 4, head % 4 : head % 4 + 1, :] = r.tops[at, :] + jnp.log(r.totals[at, :])
    outs = (r.get("co0"), r.get("co1"))
    r.acc[...] = tn(r.ot[:QUAD, :], outs[0][...]) + tn(r.ot[QUAD:, :], outs[1][...])
    x3_low = r.out("x3_low")
    norm_forward(r, 3, lambda rows: x2_ref[rows, :], r.z3, r.x3, x3_low)
    r.send("x3_low")
    ups, downs = feed_weights(r)
    feed_forward(x3_low, ups, downs, r.h, r.out("a"), r.acc)
    r.send("a")
    gain_ref, shift_ref, cot_ref, dec_ref, dy_ref = (
        r.get("gain"), r.get("shift"), r.get("cot"), r.out("dec"), r.out("dy")
    )
    last_gain, last_shift = gain_ref[4:5, :], shift_ref[4:5, :]

    def fourth_norm(rows, sums):
        before = r.x3[rows, :] + r.acc[rows, :]
        normed, rate = normalize(before)
        dec_ref[rows, :] = (normed * last_gain + last_shift).astype(BF16)
        upstream = cot_ref[rows, :].astype(F32)
        scaled = upstream * last_gain
        mean_one = jnp.mean(scaled, axis=-1, keepdims=True)
        mean_two = jnp.mean(scaled * normed, axis=-1, keepdims=True)
        grad = rate * (scaled - mean_one - normed * mean_two)
        r.z4[rows, :] = grad
        dy_ref[rows, :] = grad.astype(BF16)
        return sums[0] + fold_rows(upstream * normed), sums[1] + fold_rows(upstream)

    zeros = jnp.zeros((8, x2_ref.shape[1]), F32)
    gain_four, shift_four = over_rows(own, 32, fourth_norm, (zeros, zeros))
    r.send("dec")
    r.send("dy")
    feed_backward(dy_ref, ups, downs, r.h, r.out("dh"), r.z4)
    r.send("dh")
    gain_three, shift_three = norm_back(
        r, gain_ref[3:4, :], lambda rows: r.z3[rows, :], lambda rows: r.z4[rows, :], (r.x3, r.low)
    )
    norms = r.out("norms")
    norms[0:1, :] = gain_three
    norms[1:2, :] = jnp.sum(gain_four, axis=0, keepdims=True)
    norms[2:3, :] = shift_three
    norms[3:4, :] = jnp.sum(shift_four, axis=0, keepdims=True)
    branch = r.low[...]
    ots = (r.ot.at[:QUAD], r.ot.at[QUAD:])
    mixed_gradients(branch, ots, outs, r.do, r.delta)
    packs = ((r.out("pack0"), core), (r.out("pack1"), 1 - core))
    for g, (packed, side) in enumerate(packs):
        pack_columns(packed, side, place, 3, nn(ots[g][...], branch).astype(BF16))
        r.turn[quad(g), :] = r.k[g].T
    r.dk[...] = jnp.zeros(r.dk.shape, F32)
    r.dv[...] = jnp.zeros(r.dv.shape, F32)

    def tile(block, g, key_at, bias, add):
        backward_tile(
            g, slice(block * BLOCK, (block + 1) * BLOCK), key_at, bias, masks, r.q.at[g], r.k.at[g], r.v.at[g],
            r.turn, r.do, r.lse.at[g], r.delta, r.dqt, r.dk, r.dv, add,
        )

    for block in range(blocks):
        for g in range(2):
            tile(block, g, spots[block], r.bias[block], False)
    for block in range(blocks):

        def extra_back(i, carry, block=block):
            key_at = aligned(i * BLOCK)
            bias = bias_for(r.marks, key_at, BLOCK, query_rows[block])
            for g in range(2):
                tile(block, g, key_at, bias, True)
            return carry

        lax.fori_loop(*more[block], extra_back, 0)
    dq = (r.dqt[...] * SCALE).T.astype(BF16)
    key_grad = r.dk[...].astype(BF16)
    value_grad = r.dv[...].astype(BF16)
    query_turned = x2_ref[...].T.astype(BF16)
    enc_turned = enc_ref[...].T
    for g in (1, 0):
        packed, side = packs[g]
        pack(packed, side, place, 0, nn(query_turned, dq[:, quad(g)]).astype(BF16))
        pack(packed, side, place, 1, nn(enc_turned, key_grad[:, quad(g)]).astype(BF16))
        pack(packed, side, place, 2, nn(enc_turned, value_grad[:, quad(g)]).astype(BF16))
        r.send(f"pack{g}")
    r.dk[...] = sum(
        nt(grad[:, quad(g)], r.get(f"ckv{g}")[i]) for i, grad in enumerate((key_grad, value_grad)) for g in range(2)
    )
    r.out("denc_other")[...] = r.dk[pl.ds(second, own), :].astype(BF16)
    r.send("denc_other")
    r.out("denc_own")[...] = r.dk[pl.ds(first, own), :]
    r.send("denc_own")
    r.out("g2")[...] = r.x3[...] + sum(nt(dq[:, quad(g)], r.get(f"cq{g}")[...]) for g in range(2))


def feed_down_kernel(r):
    core, place = r.ids[0], r.ids[1]
    cot_ref, own_ref, recv_ref, z1_ref = r.get("cot"), r.get("denc_own"), r.get("denc_recv"), r.get("z1")
    dy_ref = r.out("dy")
    gain, shift = norm_back(
        r,
        r.get("gain")[1:2, :],
        lambda rows: z1_ref[rows, :],
        lambda rows: cot_ref[rows, :].astype(F32) + own_ref[rows, :] + recv_ref[rows, :].astype(F32),
        (r.out("dz"), dy_ref),
    )
    r.out("norms")[0:1, :] = gain
    r.out("norms")[1:2, :] = shift
    r.send("dz")
    r.send("dy")
    h_ref, a3_ref, dy3_ref = r.get("h"), r.get("a3"), r.get("dy3")
    packs = ((r.out("pack0"), core), (r.out("pack1"), 1 - core))
    for g, j, cols, to in reversed(list(feed_chunks(h_ref.shape[1] // 2))):
        active = gelu(h_ref[:, to].astype(F32)).astype(BF16)
        down_grad = (tn(active, dy_ref[...]) + tn(a3_ref[:, to], dy3_ref[...])).astype(BF16)
        packed, side = packs[g]
        pack(packed, side, place, 2 * j, down_grad[:, :QUAD])
        pack(packed, side, place, 2 * j + 1, down_grad[:, QUAD:])
        if j == 0:
            r.send(f"pack{g}")


def feed_up_kernel(r):
    core, place = r.ids[0], r.ids[1]
    dy_ref, h_ref, dh3_ref, g0_ref = r.get("dy"), r.get("h"), r.get("dh3"), r.out("g0")
    r.turned[0] = r.get("x1_low")[...].T
    r.turned[1] = r.get("x3_low")[...].T
    g0_ref[...] = r.get("dz")[...]
    ups, downs = feed_weights(r)
    packs = ((r.out("pack0"), core), (r.out("pack1"), 1 - core))
    for g, j, cols, to in reversed(list(feed_chunks(h_ref.shape[1] // 2))):
        packed, side = packs[g]
        slope = gelu_both(h_ref[:, to].astype(F32))[1]
        hidden_grad = (nt(dy_ref[...], downs[g][cols, :]) * slope).astype(BF16)
        g0_ref[...] += nt(hidden_grad, ups[g][:, cols])
        up_grad = (nn(r.turned[0], hidden_grad) + nn(r.turned[1], dh3_ref[:, to])).astype(BF16)
        pack(packed, side, place, 2 * j, up_grad[:, :QUAD])
        pack(packed, side, place, 2 * j + 1, up_grad[:, QUAD:])
        if j == 0:
            r.send(f"pack{g}")


def self_back_kernel(causal, norm_at, r):
    core, place = r.ids[0], r.ids[1]
    z_ref, up_ref, x_ref, row_ref = r.get("z"), r.get("up"), r.get("x"), r.get("row")
    tokens, own = x_ref.shape[0], z_ref.shape[0]
    window = r.marks.shape[0]
    start, first = aligned(core * (tokens - window)), aligned(core * own)
    spread_marks(r.marks, row_ref[:, pl.ds(start, window)])
    spots = set_self_bias(r.bias, core, tokens, r.marks, row_ref, causal)
    dx_ref, norms = r.out("dx"), r.out("norms")
    gain, shift = norm_back(
        r,
        r.get("gain")[norm_at : norm_at + 1, :],
        lambda rows: z_ref[rows, :],
        lambda rows: up_ref[rows, :],
        (dx_ref, r.low),
    )
    norms[0:1, :] = gain
    norms[1:2, :] = shift
    branch = r.low[...]
    ots = (r.get("ot0"), r.get("ot1"))
    mixed_gradients(branch, ots, (r.get("wo0"), r.get("wo1")), r.do, r.delta)
    packs = ((r.out("pack0"), core), (r.out("pack1"), 1 - core))
    for g, (packed, side) in enumerate(packs):
        pack_columns(packed, side, place, 3, nn(ots[g][...], branch).astype(BF16))
        if not causal:
            others = [r.get("feed_norms"), r.get("dec_norms"), r.get("cross_norms")]
            rows = [(norms, 0), (others[0], 0), (others[1], 0), (others[2], 0), (others[2], 1)]
            rows += [(norms, 1), (others[0], 1), (others[1], 1), (others[2], 2), (others[2], 3)]
            pack_norms(packed, side, place, [ref[at : at + 1, :] for ref, at in rows])
    masks = head_masks()
    r.dk[...] = jnp.zeros(r.dk.shape, F32)
    r.dv[...] = jnp.zeros(r.dv.shape, F32)
    for g in range(2):
        r.kt[quad(g), :] = r.get(f"k{g}")[...].T
        for key in ("q", "v", "lse"):
            r.get(f"{key}{g}")
    for block, (key_at, width) in enumerate(spots):
        for g in range(2):
            backward_tile(
                g, slice(block * BLOCK, (block + 1) * BLOCK), key_at, r.bias[block, :width, :], masks,
                r.get(f"q{g}"), r.get(f"k{g}"), r.get(f"v{g}"), r.kt, r.do, r.get(f"lse{g}"), r.delta,
                r.dqt, r.dk, r.dv, False,
            )
    dq = (r.dqt[...] * SCALE).T.astype(BF16)
    key_grad = r.dk[...].astype(BF16)
    value_grad = r.dv[...].astype(BF16)
    keys_turned = x_ref[pl.ds(start, window), :].T
    query_turned = x_ref[pl.ds(first, own), :].T
    for g in (1, 0):
        packed, side = packs[g]
        pack(packed, side, place, 0, nn(query_turned, dq[:, quad(g)]).astype(BF16))
        pack(packed, side, place, 1, nn(keys_turned, key_grad[:, quad(g)]).astype(BF16))
        pack(packed, side, place, 2, nn(keys_turned, value_grad[:, quad(g)]).astype(BF16))
        r.send(f"pack{g}")
    w = (r.get("w0"), r.get("w1"))
    r.dk[...] = sum(
        nt(grad[:, quad(g)], w[g][i]) for i, grad in ((1, key_grad), (2, value_grad)) for g in range(2)
    )
    r.out("halo")[...] = r.dk[pl.ds(aligned((1 - core) * own), window - own), :].astype(BF16)
    r.send("halo")
    dx_ref[...] = (
        dx_ref[...]
        + nt(dq[:, :QUAD], w[0][0])
        + nt(dq[:, QUAD:], w[1][0])
        + r.dk[pl.ds(aligned(core * (window - own)), own), :]
    )


class Refs:
    def __init__(self, smem, ins, outs, scratch):
        for name, ref in list(smem.items()) + list(scratch.items()):
            setattr(self, name, ref)
        self.ins, self.outs = ins, outs
        self.waited, self.sent = set(), set()
        for copy, ref in ins.values():
            copy.start()

    def get(self, name):
        copy, ref = self.ins[name]
        if name not in self.waited:
            self.waited.add(name)
            copy.wait()
        return ref

    def out(self, name):
        return self.outs[name][1]

    def send(self, name):
        self.sent.add(name)
        self.outs[name][0].start()

    def close(self):
        for name in self.ins:
            self.get(name)
        for name in self.outs:
            if name not in self.sent:
                self.send(name)
        for copy, ref in self.outs.values():
            copy.wait()


def call(kernel, name, smem, ins, outs, scratch, cost):
    n_smem, n_in, n_out, n_scratch = len(smem), len(ins), len(outs), len(scratch)

    def body(*refs):
        smem_refs = refs[:n_smem]
        refs = refs[n_smem:]
        in_refs, out_refs, refs = refs[:n_in], refs[n_in : n_in + n_out], refs[n_in + n_out :]
        in_vmem, out_vmem, refs = refs[:n_in], refs[n_in : n_in + n_out], refs[n_in + n_out :]
        in_sem, out_sem = refs[-2:]
        copies_in = {
            key: (pltpu.make_async_copy(in_refs[i], in_vmem[i], in_sem.at[i]), in_vmem[i])
            for i, key in enumerate(ins)
        }
        copies_out = {
            key: (pltpu.make_async_copy(out_vmem[i], out_refs[i], out_sem.at[i]), out_vmem[i])
            for i, key in enumerate(outs)
        }
        held = Refs(dict(zip(smem, smem_refs)), copies_in, copies_out, dict(zip(scratch, refs)))
        kernel(held)
        held.close()

    results = pl.pallas_call(
        body,
        out_shape=[jax.ShapeDtypeStruct(*out) for out in outs.values()],
        in_specs=[pl.BlockSpec(memory_space=pltpu.SMEM)] * n_smem + [pl.BlockSpec(memory_space=pl.ANY)] * n_in,
        out_specs=[pl.BlockSpec(memory_space=pl.ANY)] * n_out,
        scratch_shapes=[pltpu.VMEM(array.shape, array.dtype) for array in ins.values()]
        + [pltpu.VMEM(*out) for out in outs.values()]
        + [pltpu.VMEM(*one) for one in scratch.values()]
        + [pltpu.SemaphoreType.DMA((n_in,)), pltpu.SemaphoreType.DMA((n_out,))],
        compiler_params=pltpu.CompilerParams(vmem_limit_bytes=VMEM_LIMIT),
        cost_estimate=pl.CostEstimate(flops=cost * 10**9, transcendentals=0, bytes_accessed=cost * 10**6),
        name=name,
    )(*smem.values(), *ins.values())
    return SimpleNamespace(**dict(zip(outs, results)))


def finish_kernel(kind, ids_ref, *refs):
    core, place = ids_ref[0], ids_ref[1]
    gathered, sem = refs[-2:]
    shards = gathered.shape[0]
    each = UNITS * 2 * QUAD // shards
    per_unit = shards // UNITS
    n_outs = {"enc": 4, "dec": 2, "cross": 3, "up": 1, "down": 1}[kind]
    count = len(refs) - 2 - n_outs
    parts, outs = refs[:count], refs[count:-2]
    copies, at = [], 0
    for i, part in enumerate(parts):
        copies.append(pltpu.make_async_copy(part, gathered.at[pl.ds(at, part.shape[0])], sem.at[i]))
        at += part.shape[0]
    for copy in copies:
        copy.start()
    for copy in copies:
        copy.wait()
    for shard in range(shards):
        unit, at = shard // per_unit, shard % per_unit * each
        where = slot(core, place, shard, shards.bit_length() - 1)
        value = gathered[pl.ds(where, 1), :each, :][0].astype(F32)
        rows = slice(at, at + each)
        if kind == "up":
            outs[0][rows, quad(unit)] = value
        elif kind == "down":
            down = unit // 2 * 2 * QUAD + at
            outs[0][down : down + each, quad(unit % 2)] = value
        elif unit == 3:
            half = at // QUAD
            out = outs[2 if kind == "cross" else 1]
            out[at - half * QUAD : at - half * QUAD + each, quad(half)] = value
        elif kind != "cross":
            outs[0][unit, rows, :] = value
        elif unit == 0:
            outs[0][rows, :] = value
        else:
            outs[1][unit - 1, rows, :] = value
        if kind == "enc":
            norms = gathered[pl.ds(where, 1), each:, :][0].astype(F32)
            many = norm_rows(shards)
            for i in range(many):
                row, half = divmod(shard * many + i, 2)
                if row < 10:
                    outs[2 + row // 5][row % 5 : row % 5 + 1, quad(half)] = norms[i : i + 1, :]


def finish(group, ids, outs):
    parts = group.parts
    shape = (sum(part.shape[0] for part in parts),) + parts[0].shape[1:]
    return pl.pallas_call(
        functools.partial(finish_kernel, group.kind),
        out_shape=[jax.ShapeDtypeStruct(shape, dtype) for shape, dtype in outs],
        in_specs=[pl.BlockSpec(memory_space=pltpu.SMEM)] + [pl.BlockSpec(memory_space=pl.ANY)] * len(parts),
        out_specs=[pl.BlockSpec(memory_space=pltpu.VMEM)] * len(outs),
        scratch_shapes=[pltpu.VMEM(shape, BF16), pltpu.SemaphoreType.DMA((len(parts),))],
        compiler_params=pltpu.CompilerParams(vmem_limit_bytes=VMEM_LIMIT),
        cost_estimate=pl.CostEstimate(flops=2 * 10**9, transcendentals=0, bytes_accessed=2 * 10**6),
        name="finish_" + group.kind,
    )(ids, *parts)


def exchange(array, step, dp, mp):
    pairs = []
    for place in range(dp):
        for core in range(mp):
            bit = (1 - step if core else step) if step < 2 else step
            pairs.append((place * mp + core, (place ^ (1 << bit)) * mp + core))
    return lax.ppermute(array, ("dp", "mp"), pairs)


class Sum:
    def __init__(self, mine, other, dp, mp, kind):
        self.dp, self.mp, self.kind = dp, mp, kind
        self.bits = dp.bit_length() - 1
        self.step = 0
        self.keep, self.sent = mine, lax.ppermute(other, "mp", [(0, 1), (1, 0)])
        self.parts = None

    def advance(self):
        if self.parts is None:
            half = self.keep.shape[0] // 2
            if half:
                give = self.keep[half:] + self.sent[half:]
                self.keep = self.keep[:half] + self.sent[:half]
                give, self.keep = lax.optimization_barrier((give, self.keep))
                self.sent = exchange(give, self.step, self.dp, self.mp)
                self.step += 1
                return True
            self.parts = [self.keep + self.sent]
            self.arriving = []
        else:
            self.parts = self.parts + self.arriving
        if self.step == 0:
            return False
        self.step -= 1
        if len(self.parts) > 2:
            self.parts = [jnp.concatenate(self.parts)]
        self.arriving = [exchange(part, self.step, self.dp, self.mp) for part in self.parts]
        return True


def tie(gate, groups):
    states = [group.parts if group.parts else [group.keep] for group in groups]
    gate, states = lax.optimization_barrier((gate, states))
    for group, state in zip(groups, states):
        if group.parts:
            group.parts = state
        else:
            group.keep = state[0]
    return gate


def on_device(
    src_embed, tgt_embed, src_segment, tgt_segment, enc_qkv, enc_out_proj, dec_qkv, dec_out_proj, cross_query,
    cross_kv, cross_out_proj, ffn_up, ffn_down, norm_gain, norm_bias, enc_cotangent, dec_cotangent,
):
    dp, mp = lax.axis_size("dp"), lax.axis_size("mp")
    tokens, model = src_embed.shape
    own = tokens // mp
    window = own + MOST
    half = ffn_up.shape[1]
    hidden = 2 * half
    position = lax.axis_index("mp")
    ids = jnp.stack([position, lax.axis_index("dp")]).astype(jnp.int32)
    pairs = [(0, 1), (1, 0)]

    def swap(tree):
        return jax.tree.map(lambda a: lax.ppermute(a, "mp", pairs), tree)

    enc_w1, enc_o1 = swap((enc_qkv, enc_out_proj))
    up1, down1 = swap((ffn_up, ffn_down))
    dec_w1, dec_o1 = swap((dec_qkv, dec_out_proj))
    cross_q1, cross_kv1, cross_o1 = swap((cross_query, cross_kv, cross_out_proj))
    feed = {"up0": ffn_up, "up1": up1, "down0": ffn_down, "down1": down1}

    def rows(count, dtype):
        return ((count, model), dtype)

    blocks = own // BLOCK
    q_shape, k_shape, ot_shape, lse_shape = ((own, QUAD), BF16), ((window, QUAD), BF16), ((QUAD, own), BF16), ((4, own), F32)
    vt_shape, marks, bias = ((QUAD, window), BF16), ((window, BLOCK), jnp.int32), ((blocks, 3 * BLOCK, BLOCK), F32)
    heads = {"q": q_shape, "k": k_shape, "v": k_shape, "ot": ot_shape, "lse": lse_shape}
    norm_in = {"gain": norm_gain, "shift": norm_bias}
    first = call(
        own_heads_kernel, "own_heads", {"ids": ids},
        {"src_row": src_segment, "src": src_embed, "src_w": enc_qkv,
         "tgt_row": tgt_segment, "tgt": tgt_embed, "tgt_w": dec_qkv},
        {f"{side}_{key}": shape for side in ("src", "tgt") for key, shape in heads.items()},
        {"marks": marks, "src_bias": bias, "tgt_bias": bias, "src_vt": vt_shape, "tgt_vt": vt_shape}, cost=8,
    )
    encoder = call(
        encoder_kernel, "encoder_forward", {"ids": ids},
        {"row": src_segment, "x": src_embed, "w": enc_w1, "ot0": first.src_ot, "wo0": enc_out_proj, "wo1": enc_o1,
         **norm_in, "up0": ffn_up, "down0": ffn_down, "up1": up1, "down1": down1},
        {**heads, "z0": rows(own, F32), "x1_low": rows(own, BF16), "h": ((own, hidden), BF16),
         "z1": rows(own, F32), "enc": rows(own, BF16)},
        {"marks": marks, "bias": bias, "vt": vt_shape, "x1": rows(own, F32), "acc": rows(own, F32)}, cost=12,
    )
    enc_swapped = swap(encoder.enc)
    decoder = call(
        decoder_kernel, "decoder_self_forward", {"ids": ids},
        {"row": tgt_segment, "x": tgt_embed, "w": dec_w1, "ot0": first.tgt_ot, "wo0": dec_out_proj, "wo1": dec_o1,
         **norm_in},
        {**heads, "z2": rows(own, F32), "x2": rows(own, F32)},
        {"marks": marks, "bias": bias, "vt": vt_shape, "acc": rows(own, F32)}, cost=6,
    )
    pack_rows = UNITS * 2 * QUAD // dp
    packed = ((dp, pack_rows, QUAD), BF16)
    packed_norms = ((dp, pack_rows + TILE, QUAD), BF16)
    crossed = call(
        cross_kernel, "cross_and_decoder_feed",
        {"ids": ids, "src_marks": src_segment, "tgt_marks": tgt_segment},
        {"src_row": src_segment, "tgt_row": tgt_segment, "enc_own": encoder.enc, "enc_other": enc_swapped,
         "x2": decoder.x2, "cq0": cross_query, "ckv0": cross_kv, "cq1": cross_q1, "ckv1": cross_kv1,
         "co0": cross_out_proj, "co1": cross_o1, **norm_in, **feed, "cot": dec_cotangent},
        {"enc": rows(tokens, BF16), "x3_low": rows(own, BF16), "a": ((own, hidden), BF16), "dec": rows(own, BF16),
         "dy": rows(own, BF16), "dh": ((own, hidden), BF16), "norms": rows(4, F32), "pack0": packed, "pack1": packed,
         "denc_other": rows(own, BF16), "denc_own": rows(own, F32), "g2": rows(own, F32)},
        {"marks": ((tokens, BLOCK), jnp.int32), "bias": bias, "q": ((2, own, QUAD), BF16),
         "k": ((2, tokens, QUAD), BF16), "v": ((2, tokens, QUAD), BF16), "turn": ((model, tokens), BF16),
         "mix": ((model, own), F32), "tops": ((8, own), F32), "totals": ((8, own), F32), "lse": ((2, 4, own), F32),
         "ot": ((model, own), BF16), "acc": rows(own, F32), "x3": rows(own, F32), "z3": rows(own, F32),
         "z4": rows(own, F32), "h": ((own, hidden), F32), "low": rows(own, BF16), "do": rows(own, BF16),
         "delta": ((8, own), F32), "dqt": ((model, own), F32), "dk": rows(tokens, F32), "dv": rows(tokens, F32)},
        cost=28,
    )
    denc_recv = swap(crossed.denc_other)
    dec_swapped = swap(crossed.dec)
    cross_sum = Sum(crossed.pack0, crossed.pack1, dp, mp, "cross")

    def self_backward(causal, at, name, side, x, row, z, up, w0, w1, o0, o1, others, pack_shape):
        ins = {"row": row, "gain": norm_gain, "z": z, "up": up, "x": x}
        ins |= {"ot0": getattr(first, side + "_ot"), "ot1": others.ot, "wo0": o0, "wo1": o1}
        for key in ("k", "q", "v", "lse"):
            ins |= {key + "0": getattr(first, f"{side}_{key}"), key + "1": getattr(others, key)}
        ins |= {"w0": w0, "w1": w1}
        if not causal:
            ins |= {"feed_norms": downed.norms, "dec_norms": dec_back.norms, "cross_norms": crossed.norms}
        return call(
            functools.partial(self_back_kernel, causal, at), name, {"ids": ids}, ins,
            {"dx": rows(own, F32), "halo": rows(window - own, BF16), "pack0": pack_shape, "pack1": pack_shape,
             "norms": rows(2, F32)},
            {"marks": marks, "bias": bias, "low": rows(own, BF16), "do": rows(own, BF16), "delta": ((8, own), F32),
             "kt": ((model, window), BF16), "dqt": ((model, own), F32), "dk": rows(window, F32), "dv": rows(window, F32)},
            cost=11,
        )

    dec_back = self_backward(
        True, 2, "decoder_self_backward", "tgt", tgt_embed, tgt_segment, decoder.z2, crossed.g2,
        dec_qkv, dec_w1, dec_out_proj, dec_o1, decoder, packed,
    )
    tgt_recv = swap(dec_back.halo)
    cross_sum.advance()
    z1 = tie(encoder.z1, [cross_sum])
    dec_sum = Sum(dec_back.pack0, dec_back.pack1, dp, mp, "dec")
    downed = call(
        feed_down_kernel, "encoder_feed_down_backward", {"ids": ids},
        {"cot": enc_cotangent, "denc_own": crossed.denc_own, "denc_recv": denc_recv, "z1": z1, "gain": norm_gain,
         "h": encoder.h, "a3": crossed.a, "dy3": crossed.dy},
        {"dz": rows(own, F32), "dy": rows(own, BF16), "norms": rows(2, F32), "pack0": packed, "pack1": packed},
        {}, cost=7,
    )
    cross_sum.advance()
    dec_sum.advance()
    dy1 = tie(downed.dy, [cross_sum, dec_sum])
    down_sum = Sum(downed.pack0, downed.pack1, dp, mp, "down")
    upped = call(
        feed_up_kernel, "encoder_feed_up_backward", {"ids": ids},
        {"x1_low": encoder.x1_low, "x3_low": crossed.x3_low, "dz": downed.dz, "dy": dy1, "h": encoder.h,
         "dh3": crossed.dh, **feed},
        {"g0": rows(own, F32), "pack0": packed, "pack1": packed},
        {"turned": ((2, model, own), BF16)}, cost=8,
    )
    cross_sum.advance()
    dec_sum.advance()
    down_sum.advance()
    g0 = tie(upped.g0, [cross_sum, dec_sum, down_sum])
    up_sum = Sum(upped.pack0, upped.pack1, dp, mp, "up")
    enc_back = self_backward(
        False, 0, "encoder_self_backward", "src", src_embed, src_segment, encoder.z0, g0,
        enc_qkv, enc_w1, enc_out_proj, enc_o1, encoder, packed_norms,
    )
    src_recv = swap(enc_back.halo)
    enc_sum = Sum(enc_back.pack0, enc_back.pack1, dp, mp, "enc")
    sums = [cross_sum, dec_sum, down_sum, up_sum, enc_sum]

    def whole(mine, received):
        return jnp.where(
            position == 0, jnp.concatenate([mine, received]), jnp.concatenate([received, mine])
        )

    halo_at = (1 - position) * (own - (window - own))

    def with_halo(grad, received):
        part = lax.dynamic_slice_in_dim(grad, halo_at, window - own, 0) + received.astype(F32)
        return lax.dynamic_update_slice_in_dim(grad, part, halo_at, 0)

    square, out_half, triple = ((model, QUAD), F32), ((QUAD, model), F32), ((3, model, QUAD), F32)
    out_shapes = {
        "cross": [square, ((2, model, QUAD), F32), out_half],
        "dec": [triple, out_half],
        "enc": [triple, out_half, rows(5, F32), rows(5, F32)],
        "down": [rows(half, F32)],
        "up": [((model, half), F32)],
    }
    moving = list(sums)
    while moving:
        moving = [group for group in moving if group.advance()]
    cross_out, dec_out, down_out, up_out, enc_out = [finish(group, ids, out_shapes[group.kind]) for group in sums]
    return (
        crossed.enc,
        whole(crossed.dec, dec_swapped),
        with_halo(enc_back.dx, src_recv),
        with_halo(dec_back.dx, tgt_recv),
        enc_out[0],
        enc_out[1],
        dec_out[0],
        dec_out[1],
        cross_out[0],
        cross_out[1],
        cross_out[2],
        up_out[0],
        down_out[0],
        enc_out[2],
        enc_out[3],
    )


def solution(mesh):
    in_specs = (
        P("dp", None), P("dp", None), P("dp", None), P("dp", None),
        P(None, None, "mp"), P("mp", None), P(None, None, "mp"), P("mp", None),
        P(None, "mp"), P(None, None, "mp"), P("mp", None), P(None, "mp"), P("mp", None),
        P(), P(), P(("dp", "mp"), None), P(("dp", "mp"), None),
    )
    out_specs = (
        P("dp", None), P("dp", None), P(("dp", "mp"), None), P(("dp", "mp"), None),
        P(None, None, "mp"), P("mp", None), P(None, None, "mp"), P("mp", None),
        P(None, "mp"), P(None, None, "mp"), P("mp", None), P(None, "mp"), P("mp", None),
        P(), P(),
    )
    return jax.shard_map(on_device, mesh=mesh, in_specs=in_specs, out_specs=out_specs, check_vma=False)
```

```python
import functools
import math
from types import SimpleNamespace

import jax
import jax.numpy as jnp
from jax import lax
from jax.experimental import pallas as pl
from jax.experimental.pallas import tpu as pltpu
from jax.sharding import PartitionSpec as P

HDIM = 64
SCALE = HDIM ** (-0.5)
EPSILON = 1e-05
MASKED = -1e30
BLOCK = 128
MOST = 128
QUAD = 4 * HDIM
UNITS = 4
TILE = 16
FEED = 512
CROSS_FLIP, DEC_FLIP, FEED_FLIP, ENC_FLIP = 0, 1, 0, 1
F32 = jnp.float32
BF16 = jnp.bfloat16
VMEM_LIMIT = 56 * 1024 * 1024
GELU_IN = math.sqrt(2.0 / math.pi)
GELU_CUBE = 0.044715


def nn(left, right):
    return jnp.dot(left, right, preferred_element_type=F32)


def nt(left, right):
    return lax.dot_general(left, right, (((1,), (1,)), ((), ())), preferred_element_type=F32)


def tn(left, right):
    return lax.dot_general(left, right, (((0,), (0,)), ((), ())), preferred_element_type=F32)


def aligned(index, size=BLOCK):
    return pl.multiple_of(index, size)


def over_rows(rows, chunk, body, carry, unroll=4):
    return lax.fori_loop(
        0,
        rows // chunk,
        lambda i, kept: body(pl.ds(aligned(i * chunk, chunk), chunk), kept),
        carry,
        unroll=min(unroll, rows // chunk),
    )


def normalize(before):
    centered = before - jnp.mean(before, axis=-1, keepdims=True)
    variance = jnp.mean(centered * centered, axis=-1, keepdims=True)
    rate = lax.rsqrt(variance + EPSILON)
    return centered * rate, rate


def norm_backward(before, upstream, gain_row):
    normed, rate = normalize(before)
    scaled = upstream * gain_row
    first = jnp.mean(scaled, axis=-1, keepdims=True)
    second = jnp.mean(scaled * normed, axis=-1, keepdims=True)
    return rate * (scaled - first - normed * second), upstream * normed


def fold_rows(block):
    return jnp.sum(block.reshape(block.shape[0] // 8, 8, block.shape[1]), axis=0)


def gelu(hidden):
    inner = GELU_IN * hidden * (1.0 + GELU_CUBE * hidden * hidden)
    return 0.5 * hidden * (1.0 + jnp.tanh(inner))


def gelu_both(hidden):
    square = hidden * hidden
    bent = jnp.tanh(GELU_IN * hidden * (1.0 + GELU_CUBE * square))
    half = 0.5 * (1.0 + bent)
    slope = half + 0.5 * hidden * (1.0 - bent * bent) * (GELU_IN * (1.0 + 3.0 * GELU_CUBE * square))
    return hidden * half, slope


def head_masks():
    lane = lax.broadcasted_iota(jnp.int32, (1, QUAD), 1)
    return [
        jnp.where((lane >= h * HDIM) & (lane < (h + 1) * HDIM), 1.0, 0.0).astype(BF16)
        for h in range(4)
    ]


def stack_heads(block, masks):
    return jnp.concatenate([block * mask for mask in masks], axis=0)


def quad(g):
    return slice(g * QUAD, (g + 1) * QUAD)


def bias_for(marks_ref, key_at, width, query_row, causal=False, key_start=0, query_start=0):
    allowed = marks_ref[pl.ds(key_at, width), :] == query_row
    if causal:
        places = key_start + lax.broadcasted_iota(jnp.int32, (width, BLOCK), 0)
        queries = query_start + lax.broadcasted_iota(jnp.int32, (width, BLOCK), 1)
        allowed = allowed & (places <= queries)
    return jnp.where(allowed, 0.0, MASKED)


def self_window(core, block, causal):
    middle = block + core
    if causal:
        return aligned(jnp.maximum(middle - 1, 0) * BLOCK), 2 * BLOCK
    return aligned(jnp.clip(middle - 1, 0, 2) * BLOCK), 3 * BLOCK


def set_self_bias(bias_ref, core, tokens, marks_ref, row_ref, causal):
    window, own = marks_ref.shape[0], row_ref.shape[1] // 2
    start = core * (tokens - window)
    spots = []
    for block in range(own // BLOCK):
        key_at, width = self_window(core, block, causal)
        first = aligned(core * own + block * BLOCK)
        bias_ref[block, :width, :] = bias_for(
            marks_ref, key_at, width, row_ref[:, pl.ds(first, BLOCK)], causal, start + key_at, first
        )
        spots.append((key_at, width))
    return spots


def quad_forward(spots, q_ref, k_ref, vt_ref, bias_ref, ot_ref, lse_ref, masks):
    for block, (key_at, width) in enumerate(spots):
        rows = slice(block * BLOCK, (block + 1) * BLOCK)
        scores = nt(k_ref[pl.ds(key_at, width), :], stack_heads(q_ref[rows, :], masks))
        for h in range(4):
            one = scores[:, h * BLOCK : (h + 1) * BLOCK] + bias_ref[block, :width, :]
            top = jnp.max(one, axis=0, keepdims=True)
            weights = jnp.exp(one - top)
            total = jnp.sum(weights, axis=0, keepdims=True)
            features = slice(h * HDIM, (h + 1) * HDIM)
            mixed = nn(vt_ref[features, pl.ds(key_at, width)], weights.astype(BF16))
            ot_ref[features, rows] = (mixed * (1.0 / total)).astype(BF16)
            lse_ref[h : h + 1, rows] = top + jnp.log(total)


def backward_tile(
    g, rows, key_at, bias, masks, q_ref, k_ref, v_ref, kt_ref, do_ref, lse_ref, delta_ref, dqt_ref, dk_ref, dv_ref, add
):
    keys = pl.ds(key_at, bias.shape[0])
    q_stack = stack_heads(q_ref[rows, :], masks)
    do_stack = stack_heads(do_ref[rows, quad(g)], masks)
    scores = nt(k_ref[keys, :], q_stack)
    prob_grads = nt(v_ref[keys, :], do_stack)
    probs, score_grads = [], []
    for h in range(4):
        cols = slice(h * BLOCK, (h + 1) * BLOCK)
        head = g * 4 + h
        prob = jnp.exp(scores[:, cols] + bias - lse_ref[h : h + 1, rows])
        score_grad = (prob * (prob_grads[:, cols] - delta_ref[head : head + 1, rows])).astype(BF16)
        probs.append(prob.astype(BF16))
        score_grads.append(score_grad)
        features = slice(head * HDIM, (head + 1) * HDIM)
        query_grad = nn(kt_ref[features, keys], score_grad)
        if add:
            dqt_ref[features, rows] += query_grad
        else:
            dqt_ref[features, rows] = query_grad
    dv_ref[keys, quad(g)] += nn(jnp.concatenate(probs, axis=1), do_stack)
    dk_ref[keys, quad(g)] += nn(jnp.concatenate(score_grads, axis=1), q_stack)


def mixed_gradients(branch, ot_refs, w_out, do_ref, delta_ref):
    for g in range(2):
        do_ref[:, quad(g)] = nt(branch, w_out[g][...]).astype(BF16)
        turned = nt(w_out[g][...], branch).astype(BF16).astype(F32)
        product = turned * ot_refs[g][...].astype(F32)
        for h in range(4):
            delta_ref[g * 4 + h : g * 4 + h + 1, :] = jnp.sum(
                product[h * HDIM : (h + 1) * HDIM, :], axis=0, keepdims=True
            )


def spread_marks(marks_ref, row):
    marks_ref[...] = jnp.broadcast_to(row, (marks_ref.shape[1], marks_ref.shape[0])).T


def slot(side, place, shard):
    apart = place ^ shard
    first, second = apart & 1, (apart >> 1) & 1
    return jnp.where(side == 0, 2 * first + second, 2 * second + first)


def pack(out_ref, side, place, unit, value, at=0):
    out_ref[pl.ds(slot(side, place & 3, unit), 1), at : at + value.shape[0], :] = value.astype(BF16)[None]


def as_unit(value):
    return jnp.concatenate([value[:, :QUAD], value[:, QUAD:]], axis=0).astype(BF16)


def pack_norms(out_ref, side, place, parts):
    shards, tall, width = out_ref.shape
    halves = [part[:, half * width : (half + 1) * width] for part in parts for half in range(2)]
    each = len(halves) // shards
    blank = jnp.zeros((TILE - each, width), F32)
    for i in range(shards):
        pack(out_ref, side, place, i, jnp.concatenate(halves[i * each : (i + 1) * each] + [blank], axis=0), tall - TILE)


def prepare_quad(x_ref, w_ref, core, q_ref, k_ref, v_ref, vt_ref):
    tokens, own, window = x_ref.shape[0], q_ref.shape[0], k_ref.shape[0]
    keys = x_ref[pl.ds(aligned(core * (tokens - window)), window), :]
    q_ref[...] = (nn(x_ref[pl.ds(aligned(core * own), own), :], w_ref[0]) * SCALE).astype(BF16)
    k_ref[...] = nn(keys, w_ref[1]).astype(BF16)
    v_ref[...] = nn(keys, w_ref[2]).astype(BF16)
    vt_ref[...] = v_ref[...].T


def own_heads_kernel(r):
    core = r.ids[0]
    masks = head_masks()
    for side, causal in (("src", False), ("tgt", True)):
        x_ref, row_ref = r.get(side), r.get(side + "_row")
        k_ref = r.out(side + "_k")
        start = aligned(core * (x_ref.shape[0] - k_ref.shape[0]))
        spread_marks(r.marks, row_ref[:, pl.ds(start, k_ref.shape[0])])
        bias_ref, vt_ref = getattr(r, side + "_bias"), getattr(r, side + "_vt")
        spots = set_self_bias(bias_ref, core, x_ref.shape[0], r.marks, row_ref, causal)
        q_ref, v_ref = r.out(side + "_q"), r.out(side + "_v")
        prepare_quad(x_ref, r.get(side + "_w"), core, q_ref, k_ref, v_ref, vt_ref)
        for key in ("_q", "_k", "_v"):
            r.send(side + key)
        quad_forward(spots, q_ref, k_ref, vt_ref, bias_ref, r.out(side + "_ot"), r.out(side + "_lse"), masks)
        r.send(side + "_ot")
        r.send(side + "_lse")


def other_heads(r, causal):
    core = r.ids[0]
    x_ref, row_ref, k_ref = r.get("x"), r.get("row"), r.out("k")
    start = aligned(core * (x_ref.shape[0] - k_ref.shape[0]))
    spread_marks(r.marks, row_ref[:, pl.ds(start, k_ref.shape[0])])
    spots = set_self_bias(r.bias, core, x_ref.shape[0], r.marks, row_ref, causal)
    q_ref, v_ref, ot_ref = r.out("q"), r.out("v"), r.out("ot")
    prepare_quad(x_ref, r.get("w"), core, q_ref, k_ref, v_ref, r.vt)
    for key in ("q", "k", "v"):
        r.send(key)
    quad_forward(spots, q_ref, k_ref, r.vt, r.bias, ot_ref, r.out("lse"), head_masks())
    r.send("lse")
    r.send("ot")
    r.acc[...] = tn(r.get("ot0")[...], r.get("wo0")[...]) + tn(ot_ref[...], r.get("wo1")[...])


def norm_forward(r, at, residual, before_ref, after_ref, low_ref):
    gain, shift = r.get("gain")[at : at + 1, :], r.get("shift")[at : at + 1, :]

    def body(rows, carry):
        before = residual(rows) + r.acc[rows, :]
        if before_ref is not None:
            before_ref[rows, :] = before
        after = normalize(before)[0] * gain + shift
        if after_ref is not None:
            after_ref[rows, :] = after
        if low_ref is not None:
            low_ref[rows, :] = after.astype(BF16)
        return carry

    over_rows(r.acc.shape[0], 32, body, 0)


def own_row_reader(x_ref, core, own):
    first = core * own
    return lambda rows: x_ref[pl.ds(aligned(first + rows.start, rows.size), rows.size), :].astype(F32)


def encoder_kernel(r):
    other_heads(r, False)
    x1_low = r.out("x1_low")
    norm_forward(r, 0, own_row_reader(r.get("x"), r.ids[0], r.acc.shape[0]), r.out("z0"), r.x1, x1_low)
    r.send("z0")
    r.send("x1_low")
    feed_forward(x1_low, *feed_weights(r), (r.out("h0"), r.out("h1")), None, r.acc)
    r.send("h0")
    r.send("h1")
    norm_forward(r, 1, lambda rows: r.x1[rows, :], r.out("z1"), None, r.out("enc"))


def decoder_kernel(r):
    other_heads(r, True)
    norm_forward(r, 2, own_row_reader(r.get("x"), r.ids[0], r.acc.shape[0]), r.out("z2"), r.out("x2"), None)


def feed_weights(r):
    return (r.get("up0"), r.get("up1")), (r.get("down0"), r.get("down1"))


def feed_chunks(half):
    return [(j, slice(j * FEED, (j + 1) * FEED)) for j in range(half // FEED)]


def feed_forward(low_ref, ups, downs, h_refs, a_refs, acc_ref):
    for g in range(2):
        for j, cols in feed_chunks(ups[0].shape[1]):
            hidden = nn(low_ref[...], ups[g][:, cols])
            h_refs[g][:, cols] = hidden.astype(h_refs[g].dtype)
            active = gelu(hidden).astype(BF16)
            if a_refs is not None:
                a_refs[g][:, cols] = active
            term = nn(active, downs[g][cols, :])
            if g == 0 and j == 0:
                acc_ref[...] = term
            else:
                acc_ref[...] += term


def feed_backward(dy_ref, ups, downs, h_refs, dh_refs, acc_ref):
    for g in range(2):
        for j, cols in feed_chunks(ups[0].shape[1]):
            active_grad = nt(dy_ref[...], downs[g][cols, :])
            slope = gelu_both(h_refs[g][:, cols])[1]
            hidden_grad = (active_grad * slope).astype(BF16)
            dh_refs[g][:, cols] = hidden_grad
            acc_ref[...] += nt(hidden_grad, ups[g][:, cols])


def norm_back(r, gain_row, before, upstream, outs):
    def body(rows, sums):
        above = upstream(rows)
        grad, gain_terms = norm_backward(before(rows), above, gain_row)
        for ref in outs:
            ref[rows, :] = grad.astype(ref.dtype)
        return sums[0] + fold_rows(gain_terms), sums[1] + fold_rows(above)

    zeros = jnp.zeros((8, outs[0].shape[1]), F32)
    gains, shifts = over_rows(outs[0].shape[0], 32, body, (zeros, zeros))
    return jnp.sum(gains, axis=0, keepdims=True), jnp.sum(shifts, axis=0, keepdims=True)


def cross_kernel(r):
    core, place = r.ids[0], r.ids[1]
    x2_ref, enc_ref = r.get("x2"), r.out("enc")
    own, tokens = x2_ref.shape[0], enc_ref.shape[0]
    blocks = own // BLOCK
    first, second = aligned(core * own), aligned((1 - core) * own)
    width = 3 * BLOCK
    enc_ref[pl.ds(first, own), :] = r.get("enc_own")[...]
    enc_ref[pl.ds(second, own), :] = r.get("enc_other")[...]
    r.send("enc")
    spread_marks(r.marks, r.get("src_row")[...])
    steps = tokens.bit_length()

    def bound(mark, past):
        def step(i, pair):
            low, high = pair
            middle = (low + high) // 2
            value = r.src_marks[0, jnp.minimum(middle, tokens - 1)]
            below = (low < high) & ((value < mark) | (past & (value == mark)))
            above = (low < high) & jnp.logical_not(below)
            return jnp.where(below, middle + 1, low), jnp.where(above, middle, high)

        return lax.fori_loop(0, steps, step, (jnp.int32(0), jnp.int32(tokens)))[0]

    row_ref = r.get("tgt_row")
    query_rows, spots, more = [], [], []
    for block in range(blocks):
        head = first + block * BLOCK
        low = bound(r.tgt_marks[0, head], jnp.bool_(False)) // BLOCK
        high = (bound(r.tgt_marks[0, head + BLOCK - 1], jnp.bool_(True)) + BLOCK - 1) // BLOCK
        key_at = aligned(jnp.minimum(low, (tokens - width) // BLOCK) * BLOCK)
        query_rows.append(row_ref[:, pl.ds(aligned(head), BLOCK)])
        spots.append(key_at)
        more.append((key_at // BLOCK + 3, high))
        r.bias[block] = bias_for(r.marks, key_at, width, query_rows[block])
    masks = head_masks()
    x2_low = x2_ref[...].astype(BF16)
    for g in range(2):
        r.q[g] = (nn(x2_low, r.get(f"cq{g}")[...]) * SCALE).astype(BF16)
        r.k[g] = nn(enc_ref[...], r.get(f"ckv{g}")[0]).astype(BF16)
        r.v[g] = nn(enc_ref[...], r.get(f"ckv{g}")[1]).astype(BF16)
        r.turn[quad(g), :] = r.v[g].T

    def weigh(g, h, scores, bias, key_at, keys_width, top):
        one = scores[:, h * BLOCK : (h + 1) * BLOCK] + bias
        new_top = jnp.max(one, axis=0, keepdims=True)
        if top is not None:
            new_top = jnp.maximum(top, new_top)
        weights = jnp.exp(one - new_top)
        features = slice(g * QUAD + h * HDIM, g * QUAD + (h + 1) * HDIM)
        mixed = nn(r.turn[features, pl.ds(key_at, keys_width)], weights.astype(BF16))
        return new_top, jnp.sum(weights, axis=0, keepdims=True), mixed, features

    for block in range(blocks):
        rows = slice(block * BLOCK, (block + 1) * BLOCK)
        for g in range(2):
            scores = nt(r.k[g, pl.ds(spots[block], width), :], stack_heads(r.q[g, rows, :], masks))
            for h in range(4):
                top, total, mixed, features = weigh(g, h, scores, r.bias[block], spots[block], width, None)
                r.mix[features, rows] = mixed
                r.tops[g * 4 + h : g * 4 + h + 1, rows] = top
                r.totals[g * 4 + h : g * 4 + h + 1, rows] = total

    for block in range(blocks):
        rows = slice(block * BLOCK, (block + 1) * BLOCK)

        def extra(i, carry, block=block, rows=rows):
            key_at = aligned(i * BLOCK)
            bias = bias_for(r.marks, key_at, BLOCK, query_rows[block])
            for g in range(2):
                scores = nt(r.k[g, pl.ds(key_at, BLOCK), :], stack_heads(r.q[g, rows, :], masks))
                for h in range(4):
                    at = slice(g * 4 + h, g * 4 + h + 1)
                    old = r.tops[at, rows]
                    top, total, mixed, features = weigh(g, h, scores, bias, key_at, BLOCK, old)
                    fade = jnp.exp(old - top)
                    r.mix[features, rows] = r.mix[features, rows] * fade + mixed
                    r.tops[at, rows] = top
                    r.totals[at, rows] = r.totals[at, rows] * fade + total
            return carry

        lax.fori_loop(*more[block], extra, 0)
    for head in range(8):
        features = slice(head * HDIM, (head + 1) * HDIM)
        at = slice(head, head + 1)
        r.ot[features, :] = (r.mix[features, :] * (1.0 / r.totals[at, :])).astype(BF16)
        r.lse[head // 4, head % 4 : head % 4 + 1, :] = r.tops[at, :] + jnp.log(r.totals[at, :])
    outs = (r.get("co0"), r.get("co1"))
    r.acc[...] = tn(r.ot[:QUAD, :], outs[0][...]) + tn(r.ot[QUAD:, :], outs[1][...])
    x3_low = r.out("x3_low")
    norm_forward(r, 3, lambda rows: x2_ref[rows, :], r.z3, r.x3, x3_low)
    r.send("x3_low")
    ups, downs = feed_weights(r)
    hs = (r.h.at[0], r.h.at[1])
    feed_forward(x3_low, ups, downs, hs, (r.out("a0"), r.out("a1")), r.acc)
    r.send("a0")
    r.send("a1")
    gain_ref, shift_ref, cot_ref, dec_ref, dy_ref = (
        r.get("gain"), r.get("shift"), r.get("cot"), r.out("dec"), r.out("dy")
    )
    last_gain, last_shift = gain_ref[4:5, :], shift_ref[4:5, :]

    def fourth_norm(rows, sums):
        before = r.x3[rows, :] + r.acc[rows, :]
        normed, rate = normalize(before)
        dec_ref[rows, :] = (normed * last_gain + last_shift).astype(BF16)
        upstream = cot_ref[rows, :].astype(F32)
        scaled = upstream * last_gain
        mean_one = jnp.mean(scaled, axis=-1, keepdims=True)
        mean_two = jnp.mean(scaled * normed, axis=-1, keepdims=True)
        grad = rate * (scaled - mean_one - normed * mean_two)
        r.z4[rows, :] = grad
        dy_ref[rows, :] = grad.astype(BF16)
        return sums[0] + fold_rows(upstream * normed), sums[1] + fold_rows(upstream)

    zeros = jnp.zeros((8, x2_ref.shape[1]), F32)
    gain_four, shift_four = over_rows(own, 32, fourth_norm, (zeros, zeros))
    r.send("dec")
    r.send("dy")
    feed_backward(dy_ref, ups, downs, hs, (r.out("dh0"), r.out("dh1")), r.z4)
    r.send("dh0")
    r.send("dh1")
    gain_three, shift_three = norm_back(
        r, gain_ref[3:4, :], lambda rows: r.z3[rows, :], lambda rows: r.z4[rows, :], (r.out("dz"), r.low)
    )
    r.send("dz")
    norms = r.out("norms")
    norms[0:1, :] = gain_three
    norms[1:2, :] = jnp.sum(gain_four, axis=0, keepdims=True)
    norms[2:3, :] = shift_three
    norms[3:4, :] = jnp.sum(shift_four, axis=0, keepdims=True)
    branch = r.low[...]
    ots = (r.ot.at[:QUAD], r.ot.at[QUAD:])
    mixed_gradients(branch, ots, outs, r.do, r.delta)
    packed, side = r.out("pack1"), 1 - core ^ CROSS_FLIP
    r.out("unit")[...] = as_unit(nn(ots[0][...], branch))
    pack(packed, side, place, 3, as_unit(nn(ots[1][...], branch)))
    for g in range(2):
        r.turn[quad(g), :] = r.k[g].T
    r.dk[...] = jnp.zeros(r.dk.shape, F32)
    r.dv[...] = jnp.zeros(r.dv.shape, F32)

    def tile(block, g, key_at, bias, add):
        backward_tile(
            g, slice(block * BLOCK, (block + 1) * BLOCK), key_at, bias, masks, r.q.at[g], r.k.at[g], r.v.at[g],
            r.turn, r.do, r.lse.at[g], r.delta, r.dqt, r.dk, r.dv, add,
        )

    for block in range(blocks):
        for g in range(2):
            tile(block, g, spots[block], r.bias[block], False)
    for block in range(blocks):

        def extra_back(i, carry, block=block):
            key_at = aligned(i * BLOCK)
            bias = bias_for(r.marks, key_at, BLOCK, query_rows[block])
            for g in range(2):
                tile(block, g, key_at, bias, True)
            return carry

        lax.fori_loop(*more[block], extra_back, 0)
    head_gradients(r)
    pack(packed, side, place, 0, tn(x2_ref[...].astype(BF16), r.out("dq1")[...]))
    enc_turned = enc_ref[...].T
    pack(packed, side, place, 1, nn(enc_turned, r.out("dk1")[...]))
    pack(packed, side, place, 2, nn(enc_turned, r.out("dv1")[...]))


def head_gradients(r):
    for g in (1, 0):
        r.out(f"dq{g}")[...] = (r.dqt[quad(g), :] * SCALE).T.astype(BF16)
        r.out(f"dk{g}")[...] = r.dk[:, quad(g)].astype(BF16)
        r.out(f"dv{g}")[...] = r.dv[:, quad(g)].astype(BF16)
        for key in ("dq", "dk", "dv"):
            r.send(f"{key}{g}")


def key_stream_gradient(r, weights, keys=("dk", "dv")):
    return sum(nt(r.get(f"{keys[i]}{g}")[...], weights[g][i]) for i in range(2) for g in range(2))


def cross_second_kernel(r):
    core, place = r.ids[0], r.ids[1]
    packed, side = r.out("pack0"), core ^ CROSS_FLIP
    enc_turned = r.get("enc")[...].T
    pack(packed, side, place, 1, nn(enc_turned, r.get("dk0")[...]))
    pack(packed, side, place, 2, nn(enc_turned, r.get("dv0")[...]))
    x2_low = r.get("x2")[...].astype(BF16)
    pack(packed, side, place, 0, tn(x2_low, r.get("dq0")[...]))
    pack(packed, side, place, 3, r.get("unit")[...])
    r.send("pack0")
    own = x2_low.shape[0]
    weights = [(r.get(f"ckv{g}")[0], r.get(f"ckv{g}")[1]) for g in range(2)]
    r.denc[...] = key_stream_gradient(r, weights)
    r.out("denc_other")[...] = r.denc[pl.ds(aligned((1 - core) * own), own), :].astype(BF16)
    r.send("denc_other")
    r.out("denc_own")[...] = r.denc[pl.ds(aligned(core * own), own), :]
    r.send("denc_own")
    r.out("g2")[...] = r.get("dz")[...] + sum(nt(r.get(f"dq{g}")[...], r.get(f"cq{g}")[...]) for g in range(2))


def feed_gradients(r, dy_ref, acc_ref, packed, side, place):
    h_ref, dh_ref, a_ref, dy3_ref = r.get("h"), r.get("dh"), r.get("a"), r.get("dy3")
    up_ref, down_ref = r.get("up"), r.get("down")
    turned_one, turned_three = r.get("x1_low")[...].T, r.get("x3_low")[...].T
    for j, cols in feed_chunks(h_ref.shape[1]):
        active, slope = gelu_both(h_ref[:, cols].astype(F32))
        hidden_grad = (nt(dy_ref[...], down_ref[cols, :]) * slope).astype(BF16)
        acc_ref[...] += nt(hidden_grad, up_ref[:, cols])
        up_grad = nn(turned_one, hidden_grad) + nn(turned_three, dh_ref[:, cols])
        down_grad = tn(active.astype(BF16), dy_ref[...]) + tn(a_ref[:, cols], dy3_ref[...])
        for b in range(2):
            pack(packed, side, place, 2 * j + b, up_grad[:, quad(b)])
            pack(packed, side, place, 2 * j + b, down_grad[:, quad(b)], FEED)


def feed_other_kernel(r):
    cot_ref, own_ref, recv_ref, z1_ref = r.get("cot"), r.get("denc_own"), r.get("denc_recv"), r.get("z1")
    dy_ref, acc_ref = r.out("dy"), r.out("g0")
    gain, shift = norm_back(
        r,
        r.get("gain")[1:2, :],
        lambda rows: z1_ref[rows, :],
        lambda rows: cot_ref[rows, :].astype(F32) + own_ref[rows, :] + recv_ref[rows, :].astype(F32),
        (acc_ref, dy_ref),
    )
    r.out("norms")[0:1, :] = gain
    r.out("norms")[1:2, :] = shift
    r.send("dy")
    feed_gradients(r, dy_ref, acc_ref, r.out("pack1"), 1 - r.ids[0] ^ FEED_FLIP, r.ids[1])


def feed_own_kernel(r):
    acc_ref = r.out("g0")
    acc_ref[...] = r.get("dz")[...]
    feed_gradients(r, r.get("dy"), acc_ref, r.out("pack0"), r.ids[0] ^ FEED_FLIP, r.ids[1])


def norm_parts(norms, r):
    feed, dec, cross = r.get("feed_norms"), r.get("dec_norms"), r.get("cross_norms")
    rows = [(norms, 0), (feed, 0), (dec, 0), (cross, 0), (cross, 1)]
    rows += [(norms, 1), (feed, 1), (dec, 1), (cross, 2), (cross, 3)]
    return [ref[at : at + 1, :] for ref, at in rows]


def self_back_kernel(causal, norm_at, flip, r):
    core, place = r.ids[0], r.ids[1]
    z_ref, up_ref, x_ref, row_ref = r.get("z"), r.get("up"), r.get("x"), r.get("row")
    tokens, own = x_ref.shape[0], z_ref.shape[0]
    window = r.marks.shape[0]
    start, first = aligned(core * (tokens - window)), aligned(core * own)
    spread_marks(r.marks, row_ref[:, pl.ds(start, window)])
    spots = set_self_bias(r.bias, core, tokens, r.marks, row_ref, causal)
    norms = r.out("norms")
    gain, shift = norm_back(
        r,
        r.get("gain")[norm_at : norm_at + 1, :],
        lambda rows: z_ref[rows, :],
        lambda rows: up_ref[rows, :],
        (r.out("dz"), r.low),
    )
    norms[0:1, :] = gain
    norms[1:2, :] = shift
    r.send("dz")
    branch = r.low[...]
    ots = (r.get("ot0"), r.get("ot1"))
    mixed_gradients(branch, ots, (r.get("wo0"), r.get("wo1")), r.do, r.delta)
    packed, side = r.out("pack1"), 1 - core ^ flip
    r.out("unit")[...] = as_unit(nn(ots[0][...], branch))
    r.send("unit")
    pack(packed, side, place, 3, as_unit(nn(ots[1][...], branch)))
    if not causal:
        pack_norms(packed, side, place, norm_parts(norms, r))
    masks = head_masks()
    r.dk[...] = jnp.zeros(r.dk.shape, F32)
    r.dv[...] = jnp.zeros(r.dv.shape, F32)
    for g in range(2):
        r.kt[quad(g), :] = r.get(f"k{g}")[...].T
        for key in ("q", "v", "lse"):
            r.get(f"{key}{g}")
    for block, (key_at, width) in enumerate(spots):
        for g in range(2):
            backward_tile(
                g, slice(block * BLOCK, (block + 1) * BLOCK), key_at, r.bias[block, :width, :], masks,
                r.get(f"q{g}"), r.get(f"k{g}"), r.get(f"v{g}"), r.kt, r.do, r.get(f"lse{g}"), r.delta,
                r.dqt, r.dk, r.dv, False,
            )
    head_gradients(r)
    keys_turned = x_ref[pl.ds(start, window), :].T
    pack(packed, side, place, 0, tn(x_ref[pl.ds(first, own), :], r.out("dq1")[...]))
    pack(packed, side, place, 1, nn(keys_turned, r.out("dk1")[...]))
    pack(packed, side, place, 2, nn(keys_turned, r.out("dv1")[...]))


def self_back_own_kernel(causal, flip, r):
    core, place = r.ids[0], r.ids[1]
    packed, side = r.out("pack0"), core ^ flip
    x_ref = r.get("x")
    own, window = r.get("dq0").shape[0], r.get("dk0").shape[0]
    keys_turned = x_ref[pl.ds(aligned(core * (x_ref.shape[0] - window)), window), :].T
    pack(packed, side, place, 0, tn(x_ref[pl.ds(aligned(core * own), own), :], r.get("dq0")[...]))
    pack(packed, side, place, 1, nn(keys_turned, r.get("dk0")[...]))
    pack(packed, side, place, 2, nn(keys_turned, r.get("dv0")[...]))
    pack(packed, side, place, 3, r.get("unit")[...])
    if not causal:
        pack_norms(packed, side, place, norm_parts(r.get("norms"), r))


def stream_gradient_kernel(r):
    core = r.ids[0]
    dz_ref, own, window = r.get("dz"), r.get("dq0").shape[0], r.get("dk0").shape[0]
    w = (r.get("w0"), r.get("w1"))
    r.near[...] = key_stream_gradient(r, [(w[g][1], w[g][2]) for g in range(2)])
    r.out("halo")[...] = r.near[pl.ds(aligned((1 - core) * own), window - own), :].astype(BF16)
    r.send("halo")
    r.out("dx")[...] = (
        dz_ref[...]
        + sum(nt(r.get(f"dq{g}")[...], w[g][0]) for g in range(2))
        + r.near[pl.ds(aligned(core * (window - own)), own), :]
    )


class Refs:
    def __init__(self, smem, ins, outs, scratch):
        for name, ref in list(smem.items()) + list(scratch.items()):
            setattr(self, name, ref)
        self.ins, self.outs = ins, outs
        self.waited, self.sent = set(), set()
        for copy, ref in ins.values():
            copy.start()

    def get(self, name):
        copy, ref = self.ins[name]
        if name not in self.waited:
            self.waited.add(name)
            copy.wait()
        return ref

    def out(self, name):
        return self.outs[name][1]

    def send(self, name):
        self.sent.add(name)
        self.outs[name][0].start()

    def close(self):
        for name in self.ins:
            self.get(name)
        for name in self.outs:
            if name not in self.sent:
                self.send(name)
        for copy, ref in self.outs.values():
            copy.wait()


def call(kernel, name, smem, ins, outs, scratch, cost):
    n_smem, n_in, n_out, n_scratch = len(smem), len(ins), len(outs), len(scratch)

    def body(*refs):
        smem_refs = refs[:n_smem]
        refs = refs[n_smem:]
        in_refs, out_refs, refs = refs[:n_in], refs[n_in : n_in + n_out], refs[n_in + n_out :]
        in_vmem, out_vmem, refs = refs[:n_in], refs[n_in : n_in + n_out], refs[n_in + n_out :]
        in_sem, out_sem = refs[-2:]
        copies_in = {
            key: (pltpu.make_async_copy(in_refs[i], in_vmem[i], in_sem.at[i]), in_vmem[i])
            for i, key in enumerate(ins)
        }
        copies_out = {
            key: (pltpu.make_async_copy(out_vmem[i], out_refs[i], out_sem.at[i]), out_vmem[i])
            for i, key in enumerate(outs)
        }
        held = Refs(dict(zip(smem, smem_refs)), copies_in, copies_out, dict(zip(scratch, refs)))
        kernel(held)
        held.close()

    results = pl.pallas_call(
        body,
        out_shape=[jax.ShapeDtypeStruct(*out) for out in outs.values()],
        in_specs=[pl.BlockSpec(memory_space=pltpu.SMEM)] * n_smem + [pl.BlockSpec(memory_space=pl.ANY)] * n_in,
        out_specs=[pl.BlockSpec(memory_space=pl.ANY)] * n_out,
        scratch_shapes=[pltpu.VMEM(array.shape, array.dtype) for array in ins.values()]
        + [pltpu.VMEM(*out) for out in outs.values()]
        + [pltpu.VMEM(*one) for one in scratch.values()]
        + [pltpu.SemaphoreType.DMA((n_in,)), pltpu.SemaphoreType.DMA((n_out,))],
        compiler_params=pltpu.CompilerParams(vmem_limit_bytes=VMEM_LIMIT),
        cost_estimate=pl.CostEstimate(flops=cost * 10**9, transcendentals=0, bytes_accessed=cost * 10**6),
        name=name,
    )(*smem.values(), *ins.values())
    return SimpleNamespace(**dict(zip(outs, results)))


def finish_kernel(kind, flip, ids_ref, *refs):
    side, place = ids_ref[0] ^ flip, ids_ref[1] & 3
    gathered, sem = refs[-2:]
    n_outs = {"enc": 4, "dec": 2, "cross": 3, "feed": 2}[kind]
    count = len(refs) - 2 - n_outs
    parts, outs = refs[:count], refs[count:-2]
    copies, at = [], 0
    for i, part in enumerate(parts):
        copies.append(pltpu.make_async_copy(part, gathered.at[pl.ds(at, part.shape[0])], sem.at[i]))
        at += part.shape[0]
    for copy in copies:
        copy.start()
    for copy in copies:
        copy.wait()
    tall = 2 * QUAD
    for unit in range(UNITS):
        where = pl.ds(slot(side, place, unit), 1)
        value = gathered[where, :tall, :][0].astype(F32)
        if kind == "feed":
            outs[0][:, quad(unit)] = value
            at = unit // 2 * tall
            outs[1][at : at + tall, quad(unit % 2)] = gathered[where, tall:, :][0].astype(F32)
        elif unit == 3:
            out = outs[2 if kind == "cross" else 1]
            for half in range(2):
                out[:, quad(half)] = value[half * QUAD : (half + 1) * QUAD]
        elif kind != "cross":
            outs[0][unit] = value
        elif unit == 0:
            outs[0][...] = value
        else:
            outs[1][unit - 1] = value
        if kind == "enc":
            norms = gathered[where, tall:, :][0].astype(F32)
            for i in range(5):
                row, half = divmod(unit * 5 + i, 2)
                outs[2 + row // 5][row % 5 : row % 5 + 1, quad(half)] = norms[i : i + 1, :]


def finish(group, ids, outs):
    parts = [group.whole, group.near] + group.far
    shape = (UNITS,) + parts[0].shape[1:]
    return pl.pallas_call(
        functools.partial(finish_kernel, group.kind, group.flip),
        out_shape=[jax.ShapeDtypeStruct(*out) for out in outs],
        in_specs=[pl.BlockSpec(memory_space=pltpu.SMEM)] + [pl.BlockSpec(memory_space=pl.ANY)] * len(parts),
        out_specs=[pl.BlockSpec(memory_space=pltpu.VMEM)] * len(outs),
        scratch_shapes=[pltpu.VMEM(shape, BF16), pltpu.SemaphoreType.DMA((len(parts),))],
        compiler_params=pltpu.CompilerParams(vmem_limit_bytes=VMEM_LIMIT),
        cost_estimate=pl.CostEstimate(flops=2 * 10**9, transcendentals=0, bytes_accessed=2 * 10**6),
        name="finish_" + group.kind,
    )(ids, *parts)


class Sum:
    def __init__(self, kind, flip, dp, mp):
        self.kind, self.flip, self.dp, self.mp = kind, flip, dp, mp

    def cross_over(self, array, step):
        pairs = []
        for place in range(self.dp):
            for core in range(self.mp):
                bit = step ^ core ^ self.flip
                pairs.append((place * self.mp + core, (place ^ (1 << bit)) * self.mp + core))
        return lax.ppermute(array, ("dp", "mp"), pairs)

    def swap(self, other):
        self.sent = lax.ppermute(other, "mp", [(0, 1), (1, 0)])

    def halve(self, mine=None):
        mine = self.keep if mine is None else mine
        half = mine.shape[0] // 2
        return [mine[half:] + self.sent[half:], mine[:half] + self.sent[:half]]

    def send_half(self, parts, step):
        self.keep = parts[1]
        self.sent = self.cross_over(parts[0], step)

    def last_sum(self):
        return self.keep + self.sent

    def total(self, part):
        groups = [[low + 4 * i for i in range(self.dp // 4)] for low in range(4)]
        self.whole = lax.psum(part, "dp", axis_index_groups=groups)

    def double(self):
        self.near = self.cross_over(self.whole, 1)
        self.far = []

    def double_again(self, parts):
        self.far += [self.cross_over(part, 0) for part in parts]

    def both(self):
        return jnp.concatenate([self.whole, self.near])


def together(*values):
    return lax.optimization_barrier(values)


def on_device(
    src_embed, tgt_embed, src_segment, tgt_segment, enc_qkv, enc_out_proj, dec_qkv, dec_out_proj, cross_query,
    cross_kv, cross_out_proj, ffn_up, ffn_down, norm_gain, norm_bias, enc_cotangent, dec_cotangent,
):
    dp, mp = lax.axis_size("dp"), lax.axis_size("mp")
    tokens, model = src_embed.shape
    own = tokens // mp
    window = own + MOST
    half = ffn_up.shape[1]
    hidden = 2 * half
    position = lax.axis_index("mp")
    ids = jnp.stack([position, lax.axis_index("dp")]).astype(jnp.int32)
    pairs = [(0, 1), (1, 0)]

    def swap(tree):
        return jax.tree.map(lambda a: lax.ppermute(a, "mp", pairs), tree)

    enc_w1, enc_o1 = swap((enc_qkv, enc_out_proj))
    up1, down1 = swap((ffn_up, ffn_down))
    dec_w1, dec_o1 = swap((dec_qkv, dec_out_proj))
    cross_q1, cross_kv1, cross_o1 = swap((cross_query, cross_kv, cross_out_proj))
    feed = {"up0": ffn_up, "up1": up1, "down0": ffn_down, "down1": down1}

    def rows(count, dtype):
        return ((count, model), dtype)

    blocks = own // BLOCK
    q_shape, k_shape, ot_shape, lse_shape = ((own, QUAD), BF16), ((window, QUAD), BF16), ((QUAD, own), BF16), ((4, own), F32)
    vt_shape, marks, bias = ((QUAD, window), BF16), ((window, BLOCK), jnp.int32), ((blocks, 3 * BLOCK, BLOCK), F32)
    heads = {"q": q_shape, "k": k_shape, "v": k_shape, "ot": ot_shape, "lse": lse_shape}
    wide = ((own, half), BF16)
    norm_in = {"gain": norm_gain, "shift": norm_bias}
    first = call(
        own_heads_kernel, "own_heads", {"ids": ids},
        {"src_row": src_segment, "src": src_embed, "src_w": enc_qkv,
         "tgt_row": tgt_segment, "tgt": tgt_embed, "tgt_w": dec_qkv},
        {f"{side}_{key}": shape for side in ("src", "tgt") for key, shape in heads.items()},
        {"marks": marks, "src_bias": bias, "tgt_bias": bias, "src_vt": vt_shape, "tgt_vt": vt_shape}, cost=8,
    )
    encoder = call(
        encoder_kernel, "encoder_forward", {"ids": ids},
        {"row": src_segment, "x": src_embed, "w": enc_w1, "ot0": first.src_ot, "wo0": enc_out_proj, "wo1": enc_o1,
         **norm_in, "up0": ffn_up, "down0": ffn_down, "up1": up1, "down1": down1},
        {**heads, "z0": rows(own, F32), "x1_low": rows(own, BF16), "h0": wide, "h1": wide,
         "z1": rows(own, F32), "enc": rows(own, BF16)},
        {"marks": marks, "bias": bias, "vt": vt_shape, "x1": rows(own, F32), "acc": rows(own, F32)}, cost=12,
    )
    enc_swapped = swap(encoder.enc)
    decoder = call(
        decoder_kernel, "decoder_self_forward", {"ids": ids},
        {"row": tgt_segment, "x": tgt_embed, "w": dec_w1, "ot0": first.tgt_ot, "wo0": dec_out_proj, "wo1": dec_o1,
         **norm_in},
        {**heads, "z2": rows(own, F32), "x2": rows(own, F32)},
        {"marks": marks, "bias": bias, "vt": vt_shape, "acc": rows(own, F32)}, cost=6,
    )
    packed = ((UNITS, 2 * QUAD, QUAD), BF16)
    packed_feed = ((UNITS, 4 * QUAD, QUAD), BF16)
    packed_norms = ((UNITS, 2 * QUAD + TILE, QUAD), BF16)
    unit = ((2 * QUAD, QUAD), BF16)
    cross_key = ((tokens, QUAD), BF16)
    crossed = call(
        cross_kernel, "cross_and_decoder_feed",
        {"ids": ids, "src_marks": src_segment, "tgt_marks": tgt_segment},
        {"src_row": src_segment, "tgt_row": tgt_segment, "enc_own": encoder.enc, "enc_other": enc_swapped,
         "x2": decoder.x2, "cq0": cross_query, "ckv0": cross_kv, "cq1": cross_q1, "ckv1": cross_kv1,
         "co0": cross_out_proj, "co1": cross_o1, **norm_in, **feed, "cot": dec_cotangent},
        {"enc": rows(tokens, BF16), "x3_low": rows(own, BF16), "a0": wide, "a1": wide, "dec": rows(own, BF16),
         "dy": rows(own, BF16), "dh0": wide, "dh1": wide, "norms": rows(4, F32), "pack1": packed, "unit": unit,
         "dz": rows(own, F32), "dq0": q_shape, "dq1": q_shape, "dk0": cross_key, "dk1": cross_key, "dv0": cross_key,
         "dv1": cross_key},
        {"marks": ((tokens, BLOCK), jnp.int32), "bias": bias, "q": ((2, own, QUAD), BF16),
         "k": ((2, tokens, QUAD), BF16), "v": ((2, tokens, QUAD), BF16), "turn": ((model, tokens), BF16),
         "mix": ((model, own), F32), "tops": ((8, own), F32), "totals": ((8, own), F32), "lse": ((2, 4, own), F32),
         "ot": ((model, own), BF16), "acc": rows(own, F32), "x3": rows(own, F32), "z3": rows(own, F32),
         "z4": rows(own, F32), "h": ((2, own, half), F32), "low": rows(own, BF16), "do": rows(own, BF16),
         "delta": ((8, own), F32), "dqt": ((model, own), F32), "dk": rows(tokens, F32), "dv": rows(tokens, F32)},
        cost=28,
    )
    cross_sum = Sum("cross", CROSS_FLIP, dp, mp)
    dec_sum = Sum("dec", DEC_FLIP, dp, mp)
    feed_sum = Sum("feed", FEED_FLIP, dp, mp)
    enc_sum = Sum("enc", ENC_FLIP, dp, mp)
    cross_sum.swap(crossed.pack1)
    heads_back = {f"{key}{g}": getattr(crossed, f"{key}{g}") for key in ("dk", "dv", "dq") for g in range(2)}
    crossed_more = call(
        cross_second_kernel, "cross_second", {"ids": ids},
        {"enc": crossed.enc, **heads_back, "x2": decoder.x2, "unit": crossed.unit, "ckv0": cross_kv, "ckv1": cross_kv1,
         "dz": crossed.dz, "cq0": cross_query, "cq1": cross_q1},
        {"pack0": packed, "denc_other": rows(own, BF16), "denc_own": rows(own, F32), "g2": rows(own, F32)},
        {"denc": rows(tokens, F32)}, cost=6,
    )
    def self_backward(causal, at, flip, name, side, x, row, z, up, w0, w1, o0, o1, others, pack_shape, more):
        ins = {"row": row, "gain": norm_gain, "z": z, "up": up, "x": x}
        ins |= {"ot0": getattr(first, side + "_ot"), "ot1": others.ot, "wo0": o0, "wo1": o1}
        for key in ("k", "q", "v", "lse"):
            ins |= {key + "0": getattr(first, f"{side}_{key}"), key + "1": getattr(others, key)}
        return call(
            functools.partial(self_back_kernel, causal, at, flip), name, {"ids": ids}, ins | more,
            {"dz": rows(own, F32), "pack1": pack_shape, "unit": unit, "norms": rows(2, F32), "dq0": q_shape,
             "dq1": q_shape, "dk0": k_shape, "dk1": k_shape, "dv0": k_shape, "dv1": k_shape},
            {"marks": marks, "bias": bias, "low": rows(own, BF16), "do": rows(own, BF16), "delta": ((8, own), F32),
             "kt": ((model, window), BF16), "dqt": ((model, own), F32), "dk": rows(window, F32), "dv": rows(window, F32)},
            cost=11,
        )

    def self_backward_own(causal, flip, name, x, back, gate, pack_shape, more):
        return call(
            functools.partial(self_back_own_kernel, causal, flip), name, {"ids": ids},
            {"x": x, "dq0": back.dq0, "dk0": back.dk0, "dv0": back.dv0, "unit": gate} | more,
            {"pack0": pack_shape}, {}, cost=3,
        ).pack0

    def stream_gradient(name, back, w0, w1, gate):
        ins = {"dz": gate, "w0": w0, "w1": w1}
        ins |= {f"{key}{g}": getattr(back, f"{key}{g}") for key in ("dk", "dv", "dq") for g in range(2)}
        return call(
            stream_gradient_kernel, name, {"ids": ids}, ins,
            {"halo": rows(window - own, BF16), "dx": rows(own, F32)}, {"near": rows(window, F32)}, cost=3,
        )

    square, out_half, triple = ((model, QUAD), F32), ((QUAD, model), F32), ((3, model, QUAD), F32)
    out_shapes = {
        "cross": [square, ((2, model, QUAD), F32), out_half],
        "dec": [triple, out_half],
        "feed": [((model, half), F32), rows(half, F32)],
        "enc": [triple, out_half, rows(5, F32), rows(5, F32)],
    }
    gate, give, keep, denc_other = together(
        crossed_more.g2, *cross_sum.halve(crossed_more.pack0), crossed_more.denc_other
    )
    cross_sum.send_half((give, keep), 0)
    denc_recv = swap(denc_other)
    dec_back = self_backward(
        True, 2, DEC_FLIP, "decoder_self_backward", "tgt", tgt_embed, tgt_segment, decoder.z2, gate,
        dec_qkv, dec_w1, dec_out_proj, dec_o1, decoder, packed, {},
    )
    gate, give, keep, other = together(dec_back.unit, *cross_sum.halve(), dec_back.pack1)
    cross_sum.send_half((give, keep), 1)
    dec_sum.swap(other)
    dec_pack = self_backward_own(True, DEC_FLIP, "decoder_self_own", tgt_embed, dec_back, gate, packed, {})
    gate, give, keep, denc_recv = together(encoder.z1, *dec_sum.halve(dec_pack), denc_recv)
    dec_sum.send_half((give, keep), 0)
    feed_in = {"x1_low": encoder.x1_low, "x3_low": crossed.x3_low, "dy3": crossed.dy}
    fed = call(
        feed_other_kernel, "encoder_feed_other", {"ids": ids},
        {"cot": enc_cotangent, "denc_own": crossed_more.denc_own, "denc_recv": denc_recv, "z1": gate,
         "gain": norm_gain, "h": encoder.h1, "down": down1, "up": up1, "dh": crossed.dh1, "a": crossed.a1, **feed_in},
        {"dy": rows(own, BF16), "norms": rows(2, F32), "pack1": packed_feed, "g0": rows(own, F32)}, {}, cost=10,
    )
    gate, give, keep, part, other = together(fed.dy, *dec_sum.halve(), cross_sum.last_sum(), fed.pack1)
    cross_sum.total(part)
    dec_sum.send_half((give, keep), 1)
    feed_sum.swap(other)
    fed_own = call(
        feed_own_kernel, "encoder_feed_own", {"ids": ids},
        {"dz": fed.g0, "dy": gate, "h": encoder.h0, "down": ffn_down, "up": ffn_up, "dh": crossed.dh0,
         "a": crossed.a0, **feed_in},
        {"g0": rows(own, F32), "pack0": packed_feed}, {}, cost=9,
    )
    gate, give, keep, part, cross_sum.whole = together(
        fed_own.g0, *feed_sum.halve(fed_own.pack0), dec_sum.last_sum(), cross_sum.whole
    )
    feed_sum.send_half((give, keep), 0)
    dec_sum.total(part)
    cross_sum.double()
    norms_before = {"feed_norms": fed.norms, "dec_norms": dec_back.norms, "cross_norms": crossed.norms}
    enc_back = self_backward(
        False, 0, ENC_FLIP, "encoder_self_backward", "src", src_embed, src_segment, encoder.z0, gate,
        enc_qkv, enc_w1, enc_out_proj, enc_o1, encoder, packed_norms, norms_before,
    )
    gate, other, cross_sum.near, dec_sum.whole = together(
        enc_back.unit, enc_back.pack1, cross_sum.near, dec_sum.whole
    )
    enc_sum.swap(other)
    cross_sum.double_again([cross_sum.both()])
    dec_sum.double()
    enc_pack = self_backward_own(
        False, ENC_FLIP, "encoder_self_own", src_embed, enc_back, gate, packed_norms,
        {"norms": enc_back.norms, **norms_before},
    )
    gate, gate_two, give, keep, feed_give, feed_keep = together(
        enc_back.dz, dec_back.dz, *enc_sum.halve(enc_pack), *feed_sum.halve()
    )
    enc_sum.send_half((give, keep), 0)
    feed_sum.send_half((feed_give, feed_keep), 1)
    src_side = stream_gradient("src_gradient", enc_back, enc_qkv, enc_w1, gate)
    src_halo, dec_sum.near, gate_two, dec_own = together(src_side.halo, dec_sum.near, gate_two, crossed.dec)
    dec_sum.double_again([dec_sum.both()])
    src_recv = swap(src_halo)
    dec_swapped = swap(dec_own)
    tgt_side = stream_gradient("tgt_gradient", dec_back, dec_qkv, dec_w1, gate_two)
    give, keep, part, tgt_halo, cross_sum.far[0] = together(
        *enc_sum.halve(), feed_sum.last_sum(), tgt_side.halo, cross_sum.far[0]
    )
    feed_sum.total(part)
    enc_sum.send_half((give, keep), 1)
    tgt_recv = swap(tgt_halo)
    cross_out = finish(cross_sum, ids, out_shapes["cross"])
    feed_sum.whole, part, dec_sum.far[0] = together(feed_sum.whole, enc_sum.last_sum(), dec_sum.far[0])
    enc_sum.total(part)
    feed_sum.double()
    feed_sum.double_again([feed_sum.whole])
    dec_out = finish(dec_sum, ids, out_shapes["dec"])
    feed_sum.near, enc_sum.whole = together(feed_sum.near, enc_sum.whole)
    feed_sum.double_again([feed_sum.near])
    enc_sum.double()
    enc_sum.double_again([enc_sum.whole])
    enc_sum.double_again([enc_sum.near])
    feed_out = finish(feed_sum, ids, out_shapes["feed"])
    enc_out = finish(enc_sum, ids, out_shapes["enc"])

    def whole(mine, received):
        return jnp.where(
            position == 0, jnp.concatenate([mine, received]), jnp.concatenate([received, mine])
        )

    halo_at = (1 - position) * (own - (window - own))

    def with_halo(grad, received):
        part = lax.dynamic_slice_in_dim(grad, halo_at, window - own, 0) + received.astype(F32)
        return lax.dynamic_update_slice_in_dim(grad, part, halo_at, 0)

    return (
        crossed.enc,
        whole(crossed.dec, dec_swapped),
        with_halo(src_side.dx, src_recv),
        with_halo(tgt_side.dx, tgt_recv),
        enc_out[0],
        enc_out[1],
        dec_out[0],
        dec_out[1],
        cross_out[0],
        cross_out[1],
        cross_out[2],
        feed_out[0],
        feed_out[1],
        enc_out[2],
        enc_out[3],
    )


def solution(mesh):
    in_specs = (
        P("dp", None), P("dp", None), P("dp", None), P("dp", None),
        P(None, None, "mp"), P("mp", None), P(None, None, "mp"), P("mp", None),
        P(None, "mp"), P(None, None, "mp"), P("mp", None), P(None, "mp"), P("mp", None),
        P(), P(), P(("dp", "mp"), None), P(("dp", "mp"), None),
    )
    out_specs = (
        P("dp", None), P("dp", None), P(("dp", "mp"), None), P(("dp", "mp"), None),
        P(None, None, "mp"), P("mp", None), P(None, None, "mp"), P("mp", None),
        P(None, "mp"), P(None, None, "mp"), P("mp", None), P(None, "mp"), P("mp", None),
        P(), P(),
    )
    return jax.shard_map(on_device, mesh=mesh, in_specs=in_specs, out_specs=out_specs, check_vma=False)
```

```python
import functools
import math
from types import SimpleNamespace

import jax
import jax.numpy as jnp
from jax import lax
from jax.experimental import pallas as pl
from jax.experimental.pallas import tpu as pltpu
from jax.sharding import PartitionSpec as P

HDIM = 64
SCALE = HDIM ** (-0.5)
EPSILON = 1e-05
MASKED = -1e30
BLOCK = 128
MOST = 128
QUAD = 4 * HDIM
UNITS = 4
TILE = 16
FEED = 512
SHARDS = 8
CROSS_BITS = ((0, 2, 3, 1), (1, 2, 3, 0))
FEED_BITS = ((0, 1, 2, 3), (1, 0, 2, 3))
DEC_BITS = ((1, 2, 3, 0), (0, 2, 3, 1))
ENC_BITS = ((1, 0, 2, 3), (0, 1, 2, 3))
F32 = jnp.float32
BF16 = jnp.bfloat16
VMEM_LIMIT = 56 * 1024 * 1024
GELU_IN = math.sqrt(2.0 / math.pi)
GELU_CUBE = 0.044715


def nn(left, right):
    return jnp.dot(left, right, preferred_element_type=F32)


def nt(left, right):
    return lax.dot_general(left, right, (((1,), (1,)), ((), ())), preferred_element_type=F32)


def tn(left, right):
    return lax.dot_general(left, right, (((0,), (0,)), ((), ())), preferred_element_type=F32)


def aligned(index, size=BLOCK):
    return pl.multiple_of(index, size)


def over_rows(rows, chunk, body, carry, unroll=4):
    return lax.fori_loop(
        0,
        rows // chunk,
        lambda i, kept: body(pl.ds(aligned(i * chunk, chunk), chunk), kept),
        carry,
        unroll=min(unroll, rows // chunk),
    )


def normalize(before):
    centered = before - jnp.mean(before, axis=-1, keepdims=True)
    variance = jnp.mean(centered * centered, axis=-1, keepdims=True)
    rate = lax.rsqrt(variance + EPSILON)
    return centered * rate, rate


def norm_backward(before, upstream, gain_row):
    normed, rate = normalize(before)
    scaled = upstream * gain_row
    first = jnp.mean(scaled, axis=-1, keepdims=True)
    second = jnp.mean(scaled * normed, axis=-1, keepdims=True)
    return rate * (scaled - first - normed * second), upstream * normed


def fold_rows(block):
    return jnp.sum(block.reshape(block.shape[0] // 8, 8, block.shape[1]), axis=0)


def gelu(hidden):
    inner = GELU_IN * hidden * (1.0 + GELU_CUBE * hidden * hidden)
    return 0.5 * hidden * (1.0 + jnp.tanh(inner))


def gelu_both(hidden):
    square = hidden * hidden
    bent = jnp.tanh(GELU_IN * hidden * (1.0 + GELU_CUBE * square))
    half = 0.5 * (1.0 + bent)
    slope = half + 0.5 * hidden * (1.0 - bent * bent) * (GELU_IN * (1.0 + 3.0 * GELU_CUBE * square))
    return hidden * half, slope


def head_masks():
    lane = lax.broadcasted_iota(jnp.int32, (1, QUAD), 1)
    return [
        jnp.where((lane >= h * HDIM) & (lane < (h + 1) * HDIM), 1.0, 0.0).astype(BF16)
        for h in range(4)
    ]


def stack_heads(block, masks):
    return jnp.concatenate([block * mask for mask in masks], axis=0)


def quad(g):
    return slice(g * QUAD, (g + 1) * QUAD)


def bias_for(marks_ref, key_at, width, query_row, causal=False, key_start=0, query_start=0):
    allowed = marks_ref[pl.ds(key_at, width), :] == query_row
    if causal:
        places = key_start + lax.broadcasted_iota(jnp.int32, (width, BLOCK), 0)
        queries = query_start + lax.broadcasted_iota(jnp.int32, (width, BLOCK), 1)
        allowed = allowed & (places <= queries)
    return jnp.where(allowed, 0.0, MASKED)


def self_window(core, block, causal):
    middle = block + core
    if causal:
        return aligned(jnp.maximum(middle - 1, 0) * BLOCK), 2 * BLOCK
    return aligned(jnp.clip(middle - 1, 0, 2) * BLOCK), 3 * BLOCK


def set_self_bias(bias_ref, core, tokens, marks_ref, row_ref, causal):
    window, own = marks_ref.shape[0], row_ref.shape[1] // 2
    start = core * (tokens - window)
    spots = []
    for block in range(own // BLOCK):
        key_at, width = self_window(core, block, causal)
        first = aligned(core * own + block * BLOCK)
        bias_ref[block, :width, :] = bias_for(
            marks_ref, key_at, width, row_ref[:, pl.ds(first, BLOCK)], causal, start + key_at, first
        )
        spots.append((key_at, width))
    return spots


def quad_forward(spots, q_ref, k_ref, vt_ref, bias_ref, ot_ref, lse_ref, masks):
    def score(block):
        rows, (key_at, width) = slice(block * BLOCK, (block + 1) * BLOCK), spots[block]
        return nt(k_ref[pl.ds(key_at, width), :], stack_heads(q_ref[rows, :], masks))

    ahead = score(0)
    for block, (key_at, width) in enumerate(spots):
        rows = slice(block * BLOCK, (block + 1) * BLOCK)
        scores, ahead = ahead, score(block + 1) if block + 1 < len(spots) else None
        for h in range(4):
            one = scores[:, h * BLOCK : (h + 1) * BLOCK] + bias_ref[block, :width, :]
            top = jnp.max(one, axis=0, keepdims=True)
            weights = jnp.exp(one - top)
            total = jnp.sum(weights, axis=0, keepdims=True)
            features = slice(h * HDIM, (h + 1) * HDIM)
            mixed = nn(vt_ref[features, pl.ds(key_at, width)], weights.astype(BF16))
            ot_ref[features, rows] = (mixed * (1.0 / total)).astype(BF16)
            lse_ref[h : h + 1, rows] = top + jnp.log(total)


def backward_tile(
    g, rows, key_at, bias, masks, q_ref, k_ref, v_ref, kt_ref, do_ref, lse_ref, delta_ref, dqt_ref, dk_ref, dv_ref, add
):
    keys = pl.ds(key_at, bias.shape[0])
    q_stack = stack_heads(q_ref[rows, :], masks)
    do_stack = stack_heads(do_ref[rows, quad(g)], masks)
    scores = nt(k_ref[keys, :], q_stack)
    prob_grads = nt(v_ref[keys, :], do_stack)
    probs, score_grads = [], []
    for h in range(4):
        cols = slice(h * BLOCK, (h + 1) * BLOCK)
        head = g * 4 + h
        prob = jnp.exp(scores[:, cols] + bias - lse_ref[h : h + 1, rows])
        score_grad = (prob * (prob_grads[:, cols] - delta_ref[head : head + 1, rows])).astype(BF16)
        probs.append(prob.astype(BF16))
        score_grads.append(score_grad)
        features = slice(head * HDIM, (head + 1) * HDIM)
        query_grad = nn(kt_ref[features, keys], score_grad)
        if add:
            dqt_ref[features, rows] += query_grad
        else:
            dqt_ref[features, rows] = query_grad
    dv_ref[keys, quad(g)] += nn(jnp.concatenate(probs, axis=1), do_stack)
    dk_ref[keys, quad(g)] += nn(jnp.concatenate(score_grads, axis=1), q_stack)


def mixed_gradients(branch, ot_refs, w_out, do_ref, delta_ref):
    for g in range(2):
        do_ref[:, quad(g)] = nt(branch, w_out[g][...]).astype(BF16)
        turned = nt(w_out[g][...], branch).astype(BF16).astype(F32)
        product = turned * ot_refs[g][...].astype(F32)
        for h in range(4):
            delta_ref[g * 4 + h : g * 4 + h + 1, :] = jnp.sum(
                product[h * HDIM : (h + 1) * HDIM, :], axis=0, keepdims=True
            )


def spread_marks(marks_ref, row):
    marks_ref[...] = jnp.broadcast_to(row, (marks_ref.shape[1], marks_ref.shape[0])).T


def label(bits, place):
    first, second, third = [(place >> bit) & 1 for bit in bits[:3]]
    return 4 * first + 2 * second + third


def own_label(bits, core, place):
    return jnp.where(core == 0, label(bits[0], place), label(bits[1], place))


def pack(out_ref, mark, unit, value, at=0):
    rows = value.shape[0] // 2
    for half in range(2):
        where = pl.ds(mark ^ (2 * unit + half), 1)
        out_ref[where, at : at + rows, :] = value[half * rows : (half + 1) * rows].astype(BF16)[None]


def as_unit(value):
    return jnp.concatenate([value[:, :QUAD], value[:, QUAD:]], axis=0).astype(BF16)


def pack_norms(out_ref, mark, parts):
    shards, tall, width = out_ref.shape
    halves = [part[:, half * width : (half + 1) * width] for part in parts for half in range(2)]
    each = norm_rows(shards)
    blank = jnp.zeros((1, width), F32)
    halves += [blank] * (shards * each - len(halves))
    for i in range(shards):
        block = jnp.concatenate(halves[i * each : (i + 1) * each] + [blank] * (TILE - each), axis=0)
        out_ref[pl.ds(mark ^ i, 1), tall - TILE :, :] = block.astype(BF16)[None]


def norm_rows(shards):
    return -(-20 // shards)


def prepare_quad(x_ref, w_ref, core, q_ref, k_ref, v_ref, vt_ref):
    tokens, own, window = x_ref.shape[0], q_ref.shape[0], k_ref.shape[0]
    keys = x_ref[pl.ds(aligned(core * (tokens - window)), window), :]
    q_ref[...] = (nn(x_ref[pl.ds(aligned(core * own), own), :], w_ref[0]) * SCALE).astype(BF16)
    k_ref[...] = nn(keys, w_ref[1]).astype(BF16)
    v_ref[...] = nn(keys, w_ref[2]).astype(BF16)
    vt_ref[...] = v_ref[...].T


def own_heads_kernel(r):
    core = r.ids[0]
    masks = head_masks()
    for side, causal in (("src", False), ("tgt", True)):
        x_ref, row_ref = r.get(side), r.get(side + "_row")
        k_ref = r.out(side + "_k")
        start = aligned(core * (x_ref.shape[0] - k_ref.shape[0]))
        spread_marks(r.marks, row_ref[:, pl.ds(start, k_ref.shape[0])])
        bias_ref, vt_ref = getattr(r, side + "_bias"), getattr(r, side + "_vt")
        spots = set_self_bias(bias_ref, core, x_ref.shape[0], r.marks, row_ref, causal)
        q_ref, v_ref = r.out(side + "_q"), r.out(side + "_v")
        prepare_quad(x_ref, r.get(side + "_w"), core, q_ref, k_ref, v_ref, vt_ref)
        for key in ("_q", "_k", "_v"):
            r.send(side + key)
        quad_forward(spots, q_ref, k_ref, vt_ref, bias_ref, r.out(side + "_ot"), r.out(side + "_lse"), masks)
        r.send(side + "_ot")
        r.send(side + "_lse")


def other_heads(r, causal):
    core = r.ids[0]
    x_ref, row_ref, k_ref = r.get("x"), r.get("row"), r.out("k")
    start = aligned(core * (x_ref.shape[0] - k_ref.shape[0]))
    spread_marks(r.marks, row_ref[:, pl.ds(start, k_ref.shape[0])])
    spots = set_self_bias(r.bias, core, x_ref.shape[0], r.marks, row_ref, causal)
    q_ref, v_ref, ot_ref = r.out("q"), r.out("v"), r.out("ot")
    prepare_quad(x_ref, r.get("w"), core, q_ref, k_ref, v_ref, r.vt)
    for key in ("q", "k", "v"):
        r.send(key)
    quad_forward(spots, q_ref, k_ref, r.vt, r.bias, ot_ref, r.out("lse"), head_masks())
    r.send("lse")
    r.send("ot")
    r.acc[...] = tn(r.get("ot0")[...], r.get("wo0")[...]) + tn(ot_ref[...], r.get("wo1")[...])


def norm_forward(r, at, residual, before_ref, after_ref, low_ref):
    gain, shift = r.get("gain")[at : at + 1, :], r.get("shift")[at : at + 1, :]

    def body(rows, carry):
        before = residual(rows) + r.acc[rows, :]
        if before_ref is not None:
            before_ref[rows, :] = before
        after = normalize(before)[0] * gain + shift
        if after_ref is not None:
            after_ref[rows, :] = after
        if low_ref is not None:
            low_ref[rows, :] = after.astype(BF16)
        return carry

    over_rows(r.acc.shape[0], 32, body, 0)


def own_row_reader(x_ref, core, own):
    first = core * own
    return lambda rows: x_ref[pl.ds(aligned(first + rows.start, rows.size), rows.size), :].astype(F32)


def encoder_kernel(r):
    other_heads(r, False)
    x1_low = r.out("x1_low")
    norm_forward(r, 0, own_row_reader(r.get("x"), r.ids[0], r.acc.shape[0]), r.out("z0"), r.x1, x1_low)
    r.send("z0")
    r.send("x1_low")
    feed_forward(x1_low, *feed_weights(r), (r.out("h0"), r.out("h1")), None, r.acc)
    r.send("h0")
    r.send("h1")
    norm_forward(r, 1, lambda rows: r.x1[rows, :], r.out("z1"), None, r.out("enc"))


def decoder_kernel(r):
    other_heads(r, True)
    norm_forward(r, 2, own_row_reader(r.get("x"), r.ids[0], r.acc.shape[0]), r.out("z2"), r.out("x2"), None)


def feed_weights(r):
    return (r.get("up0"), r.get("up1")), (r.get("down0"), r.get("down1"))


def feed_chunks(half):
    return [(j, slice(j * FEED, (j + 1) * FEED)) for j in range(half // FEED)]


def feed_forward(low_ref, ups, downs, h_refs, a_refs, acc_ref):
    chunks = [(g, cols) for g in range(2) for j, cols in feed_chunks(ups[0].shape[1])]
    ahead = nn(low_ref[...], ups[0][:, chunks[0][1]])
    for i, (g, cols) in enumerate(chunks):
        hidden = ahead
        if i + 1 < len(chunks):
            ahead = nn(low_ref[...], ups[chunks[i + 1][0]][:, chunks[i + 1][1]])
        h_refs[g][:, cols] = hidden.astype(h_refs[g].dtype)
        active = gelu(hidden).astype(BF16)
        if a_refs is not None:
            a_refs[g][:, cols] = active
        term = nn(active, downs[g][cols, :])
        if i == 0:
            acc_ref[...] = term
        else:
            acc_ref[...] += term


def feed_backward(dy_ref, ups, downs, h_refs, dh_refs, acc_ref):
    chunks = [(g, cols) for g in range(2) for j, cols in feed_chunks(ups[0].shape[1])]
    ahead = nt(dy_ref[...], downs[0][chunks[0][1], :])
    for i, (g, cols) in enumerate(chunks):
        active_grad = ahead
        if i + 1 < len(chunks):
            ahead = nt(dy_ref[...], downs[chunks[i + 1][0]][chunks[i + 1][1], :])
        slope = gelu_both(h_refs[g][:, cols])[1]
        hidden_grad = (active_grad * slope).astype(BF16)
        dh_refs[g][:, cols] = hidden_grad
        acc_ref[...] += nt(hidden_grad, ups[g][:, cols])


def norm_back(r, gain_row, before, upstream, outs):
    def body(rows, sums):
        above = upstream(rows)
        grad, gain_terms = norm_backward(before(rows), above, gain_row)
        for ref in outs:
            ref[rows, :] = grad.astype(ref.dtype)
        return sums[0] + fold_rows(gain_terms), sums[1] + fold_rows(above)

    zeros = jnp.zeros((8, outs[0].shape[1]), F32)
    gains, shifts = over_rows(outs[0].shape[0], 32, body, (zeros, zeros))
    return jnp.sum(gains, axis=0, keepdims=True), jnp.sum(shifts, axis=0, keepdims=True)


def cross_kernel(r):
    core, place = r.ids[0], r.ids[1]
    x2_ref, enc_ref = r.get("x2"), r.out("enc")
    own, tokens = x2_ref.shape[0], enc_ref.shape[0]
    blocks = own // BLOCK
    first, second = aligned(core * own), aligned((1 - core) * own)
    width = 3 * BLOCK
    enc_ref[pl.ds(first, own), :] = r.get("enc_own")[...]
    enc_ref[pl.ds(second, own), :] = r.get("enc_other")[...]
    r.send("enc")
    spread_marks(r.marks, r.get("src_row")[...])
    steps = tokens.bit_length()

    def bound(mark, past):
        def step(i, pair):
            low, high = pair
            middle = (low + high) // 2
            value = r.src_marks[0, jnp.minimum(middle, tokens - 1)]
            below = (low < high) & ((value < mark) | (past & (value == mark)))
            above = (low < high) & jnp.logical_not(below)
            return jnp.where(below, middle + 1, low), jnp.where(above, middle, high)

        return lax.fori_loop(0, steps, step, (jnp.int32(0), jnp.int32(tokens)))[0]

    row_ref = r.get("tgt_row")
    query_rows, spots, more = [], [], []
    for block in range(blocks):
        head = first + block * BLOCK
        low = bound(r.tgt_marks[0, head], jnp.bool_(False)) // BLOCK
        high = (bound(r.tgt_marks[0, head + BLOCK - 1], jnp.bool_(True)) + BLOCK - 1) // BLOCK
        key_at = aligned(jnp.minimum(low, (tokens - width) // BLOCK) * BLOCK)
        query_rows.append(row_ref[:, pl.ds(aligned(head), BLOCK)])
        spots.append(key_at)
        more.append((key_at // BLOCK + 3, high))
        r.bias[block] = bias_for(r.marks, key_at, width, query_rows[block])
    masks = head_masks()
    x2_low = x2_ref[...].astype(BF16)
    for g in range(2):
        r.q[g] = (nn(x2_low, r.get(f"cq{g}")[...]) * SCALE).astype(BF16)
        r.k[g] = nn(enc_ref[...], r.get(f"ckv{g}")[0]).astype(BF16)
        r.v[g] = nn(enc_ref[...], r.get(f"ckv{g}")[1]).astype(BF16)
        r.turn[quad(g), :] = r.v[g].T

    def weigh(g, h, scores, bias, key_at, keys_width, top):
        one = scores[:, h * BLOCK : (h + 1) * BLOCK] + bias
        new_top = jnp.max(one, axis=0, keepdims=True)
        if top is not None:
            new_top = jnp.maximum(top, new_top)
        weights = jnp.exp(one - new_top)
        features = slice(g * QUAD + h * HDIM, g * QUAD + (h + 1) * HDIM)
        mixed = nn(r.turn[features, pl.ds(key_at, keys_width)], weights.astype(BF16))
        return new_top, jnp.sum(weights, axis=0, keepdims=True), mixed, features

    def score(block, g):
        rows = slice(block * BLOCK, (block + 1) * BLOCK)
        return nt(r.k[g, pl.ds(spots[block], width), :], stack_heads(r.q[g, rows, :], masks))

    tiles = [(block, g) for block in range(blocks) for g in range(2)]
    ahead = score(*tiles[0])
    for i, (block, g) in enumerate(tiles):
        rows = slice(block * BLOCK, (block + 1) * BLOCK)
        scores, ahead = ahead, score(*tiles[i + 1]) if i + 1 < len(tiles) else None
        for h in range(4):
            top, total, mixed, features = weigh(g, h, scores, r.bias[block], spots[block], width, None)
            r.mix[features, rows] = mixed
            r.tops[g * 4 + h : g * 4 + h + 1, rows] = top
            r.totals[g * 4 + h : g * 4 + h + 1, rows] = total

    for block in range(blocks):
        rows = slice(block * BLOCK, (block + 1) * BLOCK)

        def extra(i, carry, block=block, rows=rows):
            key_at = aligned(i * BLOCK)
            bias = bias_for(r.marks, key_at, BLOCK, query_rows[block])
            for g in range(2):
                scores = nt(r.k[g, pl.ds(key_at, BLOCK), :], stack_heads(r.q[g, rows, :], masks))
                for h in range(4):
                    at = slice(g * 4 + h, g * 4 + h + 1)
                    old = r.tops[at, rows]
                    top, total, mixed, features = weigh(g, h, scores, bias, key_at, BLOCK, old)
                    fade = jnp.exp(old - top)
                    r.mix[features, rows] = r.mix[features, rows] * fade + mixed
                    r.tops[at, rows] = top
                    r.totals[at, rows] = r.totals[at, rows] * fade + total
            return carry

        lax.fori_loop(*more[block], extra, 0)
    for head in range(8):
        features = slice(head * HDIM, (head + 1) * HDIM)
        at = slice(head, head + 1)
        r.ot[features, :] = (r.mix[features, :] * (1.0 / r.totals[at, :])).astype(BF16)
        r.lse[head // 4, head % 4 : head % 4 + 1, :] = r.tops[at, :] + jnp.log(r.totals[at, :])
    outs = (r.get("co0"), r.get("co1"))
    r.acc[...] = tn(r.ot[:QUAD, :], outs[0][...]) + tn(r.ot[QUAD:, :], outs[1][...])
    x3_low = r.out("x3_low")
    norm_forward(r, 3, lambda rows: x2_ref[rows, :], r.z3, r.x3, x3_low)
    r.send("x3_low")
    ups, downs = feed_weights(r)
    hs = (r.h.at[0], r.h.at[1])
    feed_forward(x3_low, ups, downs, hs, (r.out("a0"), r.out("a1")), r.acc)
    r.send("a0")
    r.send("a1")
    gain_ref, shift_ref, cot_ref, dec_ref, dy_ref = (
        r.get("gain"), r.get("shift"), r.get("cot"), r.out("dec"), r.out("dy")
    )
    last_gain, last_shift = gain_ref[4:5, :], shift_ref[4:5, :]

    def fourth_norm(rows, sums):
        before = r.x3[rows, :] + r.acc[rows, :]
        normed, rate = normalize(before)
        dec_ref[rows, :] = (normed * last_gain + last_shift).astype(BF16)
        upstream = cot_ref[rows, :].astype(F32)
        scaled = upstream * last_gain
        mean_one = jnp.mean(scaled, axis=-1, keepdims=True)
        mean_two = jnp.mean(scaled * normed, axis=-1, keepdims=True)
        grad = rate * (scaled - mean_one - normed * mean_two)
        r.z4[rows, :] = grad
        dy_ref[rows, :] = grad.astype(BF16)
        return sums[0] + fold_rows(upstream * normed), sums[1] + fold_rows(upstream)

    zeros = jnp.zeros((8, x2_ref.shape[1]), F32)
    gain_four, shift_four = over_rows(own, 32, fourth_norm, (zeros, zeros))
    r.send("dec")
    r.send("dy")
    feed_backward(dy_ref, ups, downs, hs, (r.out("dh0"), r.out("dh1")), r.z4)
    r.send("dh0")
    r.send("dh1")
    gain_three, shift_three = norm_back(
        r, gain_ref[3:4, :], lambda rows: r.z3[rows, :], lambda rows: r.z4[rows, :], (r.out("dz"), r.low)
    )
    r.send("dz")
    norms = r.out("norms")
    norms[0:1, :] = gain_three
    norms[1:2, :] = jnp.sum(gain_four, axis=0, keepdims=True)
    norms[2:3, :] = shift_three
    norms[3:4, :] = jnp.sum(shift_four, axis=0, keepdims=True)
    branch = r.low[...]
    ots = (r.ot.at[:QUAD], r.ot.at[QUAD:])
    mixed_gradients(branch, ots, outs, r.do, r.delta)
    packed, mark = r.out("pack1"), own_label(CROSS_BITS, 1 - core, place)
    r.out("unit")[...] = as_unit(nn(ots[0][...], branch))
    r.send("unit")
    pack(packed, mark, 3, as_unit(nn(ots[1][...], branch)))
    for g in range(2):
        r.turn[quad(g), :] = r.k[g].T
    r.dk[...] = jnp.zeros(r.dk.shape, F32)
    r.dv[...] = jnp.zeros(r.dv.shape, F32)

    def tile(block, g, key_at, bias, add):
        backward_tile(
            g, slice(block * BLOCK, (block + 1) * BLOCK), key_at, bias, masks, r.q.at[g], r.k.at[g], r.v.at[g],
            r.turn, r.do, r.lse.at[g], r.delta, r.dqt, r.dk, r.dv, add,
        )

    for block in range(blocks):
        for g in range(2):
            tile(block, g, spots[block], r.bias[block], False)
    for block in range(blocks):

        def extra_back(i, carry, block=block):
            key_at = aligned(i * BLOCK)
            bias = bias_for(r.marks, key_at, BLOCK, query_rows[block])
            for g in range(2):
                tile(block, g, key_at, bias, True)
            return carry

        lax.fori_loop(*more[block], extra_back, 0)
    head_gradients(r)
    pack(packed, mark, 0, tn(x2_ref[...].astype(BF16), r.out("dq1")[...]))
    enc_turned = enc_ref[...].T
    pack(packed, mark, 1, nn(enc_turned, r.out("dk1")[...]))
    pack(packed, mark, 2, nn(enc_turned, r.out("dv1")[...]))
    r.send("pack1")
    r.dk[...] = sum(
        nt(r.out(f"{key}{g}")[...], r.get(f"ckv{g}")[i]) for i, key in enumerate(("dk", "dv")) for g in range(2)
    )
    r.out("denc_other")[...] = r.dk[pl.ds(second, own), :].astype(BF16)
    r.send("denc_other")
    r.out("denc_own")[...] = r.dk[pl.ds(first, own), :]


def head_gradients(r):
    for g in (1, 0):
        r.out(f"dq{g}")[...] = (r.dqt[quad(g), :] * SCALE).astype(BF16).T
        r.out(f"dk{g}")[...] = r.dk[:, quad(g)].astype(BF16)
        r.out(f"dv{g}")[...] = r.dv[:, quad(g)].astype(BF16)
        for key in ("dq", "dk", "dv"):
            r.send(f"{key}{g}")


def key_stream_gradient(r, weights, keys=("dk", "dv")):
    return sum(nt(r.get(f"{keys[i]}{g}")[...], weights[g][i]) for i in range(2) for g in range(2))


def cross_second_kernel(r):
    packed, mark = r.out("pack0"), own_label(CROSS_BITS, r.ids[0], r.ids[1])
    enc_turned = r.get("enc")[...].T
    pack(packed, mark, 1, nn(enc_turned, r.get("dk0")[...]))
    pack(packed, mark, 2, nn(enc_turned, r.get("dv0")[...]))
    pack(packed, mark, 0, tn(r.get("x2")[...].astype(BF16), r.get("dq0")[...]))
    pack(packed, mark, 3, r.get("unit")[...])
    r.send("pack0")
    r.out("g2")[...] = r.get("dz")[...] + sum(nt(r.get(f"dq{g}")[...], r.get(f"cq{g}")[...]) for g in range(2))


def feed_gradients(r, dy_ref, acc_ref, packed, mark):
    h_ref, dh_ref, a_ref, dy3_ref = r.get("h"), r.get("dh"), r.get("a"), r.get("dy3")
    up_ref, down_ref = r.get("up"), r.get("down")
    turned_one, turned_three = r.get("x1_low")[...].T, r.get("x3_low")[...].T
    for j, cols in feed_chunks(h_ref.shape[1]):
        active, slope = gelu_both(h_ref[:, cols].astype(F32))
        hidden_grad = (nt(dy_ref[...], down_ref[cols, :]) * slope).astype(BF16)
        acc_ref[...] += nt(hidden_grad, up_ref[:, cols])
        up_grad = nn(turned_one, hidden_grad) + nn(turned_three, dh_ref[:, cols])
        down_grad = tn(active.astype(BF16), dy_ref[...]) + tn(a_ref[:, cols], dy3_ref[...])
        for b in range(2):
            pack(packed, mark, 2 * j + b, up_grad[:, quad(b)])
            pack(packed, mark, 2 * j + b, down_grad[:, quad(b)], QUAD)


def feed_other_kernel(r):
    cot_ref, own_ref, recv_ref, z1_ref = r.get("cot"), r.get("denc_own"), r.get("denc_recv"), r.get("z1")
    dy_ref, acc_ref = r.out("dy"), r.out("g0")
    gain, shift = norm_back(
        r,
        r.get("gain")[1:2, :],
        lambda rows: z1_ref[rows, :],
        lambda rows: cot_ref[rows, :].astype(F32) + own_ref[rows, :] + recv_ref[rows, :].astype(F32),
        (acc_ref, dy_ref),
    )
    r.out("norms")[0:1, :] = gain
    r.out("norms")[1:2, :] = shift
    r.send("dy")
    feed_gradients(r, dy_ref, acc_ref, r.out("pack1"), own_label(FEED_BITS, 1 - r.ids[0], r.ids[1]))


def feed_own_kernel(r):
    acc_ref = r.out("g0")
    acc_ref[...] = r.get("dz")[...]
    feed_gradients(r, r.get("dy"), acc_ref, r.out("pack0"), own_label(FEED_BITS, r.ids[0], r.ids[1]))


def norm_parts(norms, r):
    feed, dec, cross = r.get("feed_norms"), r.get("dec_norms"), r.get("cross_norms")
    rows = [(norms, 0), (feed, 0), (dec, 0), (cross, 0), (cross, 1)]
    rows += [(norms, 1), (feed, 1), (dec, 1), (cross, 2), (cross, 3)]
    return [ref[at : at + 1, :] for ref, at in rows]


def self_back_kernel(causal, norm_at, bits, r):
    core, place = r.ids[0], r.ids[1]
    z_ref, up_ref, x_ref, row_ref = r.get("z"), r.get("up"), r.get("x"), r.get("row")
    tokens, own = x_ref.shape[0], z_ref.shape[0]
    window = r.marks.shape[0]
    start, first = aligned(core * (tokens - window)), aligned(core * own)
    spread_marks(r.marks, row_ref[:, pl.ds(start, window)])
    spots = set_self_bias(r.bias, core, tokens, r.marks, row_ref, causal)
    norms = r.out("norms")
    gain, shift = norm_back(
        r,
        r.get("gain")[norm_at : norm_at + 1, :],
        lambda rows: z_ref[rows, :],
        lambda rows: up_ref[rows, :],
        (r.out("dz"), r.low),
    )
    norms[0:1, :] = gain
    norms[1:2, :] = shift
    r.send("dz")
    branch = r.low[...]
    ots = (r.get("ot0"), r.get("ot1"))
    mixed_gradients(branch, ots, (r.get("wo0"), r.get("wo1")), r.do, r.delta)
    packed, mark = r.out("pack1"), own_label(bits, 1 - core, place)
    r.out("unit")[...] = as_unit(nn(ots[0][...], branch))
    r.send("unit")
    pack(packed, mark, 3, as_unit(nn(ots[1][...], branch)))
    if not causal:
        pack_norms(packed, mark, norm_parts(norms, r))
    masks = head_masks()
    r.dk[...] = jnp.zeros(r.dk.shape, F32)
    r.dv[...] = jnp.zeros(r.dv.shape, F32)
    for g in range(2):
        r.kt[quad(g), :] = r.get(f"k{g}")[...].T
        for key in ("q", "v", "lse"):
            r.get(f"{key}{g}")
    for block, (key_at, width) in enumerate(spots):
        for g in range(2):
            backward_tile(
                g, slice(block * BLOCK, (block + 1) * BLOCK), key_at, r.bias[block, :width, :], masks,
                r.get(f"q{g}"), r.get(f"k{g}"), r.get(f"v{g}"), r.kt, r.do, r.get(f"lse{g}"), r.delta,
                r.dqt, r.dk, r.dv, False,
            )
    head_gradients(r)
    keys_turned = x_ref[pl.ds(start, window), :].T
    pack(packed, mark, 0, tn(x_ref[pl.ds(first, own), :], r.out("dq1")[...]))
    pack(packed, mark, 1, nn(keys_turned, r.out("dk1")[...]))
    pack(packed, mark, 2, nn(keys_turned, r.out("dv1")[...]))


def self_back_own_kernel(causal, bits, r):
    core, place = r.ids[0], r.ids[1]
    packed, mark = r.out("pack0"), own_label(bits, core, place)
    x_ref = r.get("x")
    own, window = r.get("dq0").shape[0], r.get("dk0").shape[0]
    keys_turned = x_ref[pl.ds(aligned(core * (x_ref.shape[0] - window)), window), :].T
    pack(packed, mark, 0, tn(x_ref[pl.ds(aligned(core * own), own), :], r.get("dq0")[...]))
    pack(packed, mark, 1, nn(keys_turned, r.get("dk0")[...]))
    pack(packed, mark, 2, nn(keys_turned, r.get("dv0")[...]))
    pack(packed, mark, 3, r.get("unit")[...])
    if not causal:
        pack_norms(packed, mark, norm_parts(r.get("norms"), r))


def stream_gradient_kernel(r):
    core = r.ids[0]
    dz_ref, own, window = r.get("dz"), r.get("dq0").shape[0], r.get("dk0").shape[0]
    w = (r.get("w0"), r.get("w1"))
    r.near[...] = key_stream_gradient(r, [(w[g][1], w[g][2]) for g in range(2)])
    r.out("halo")[...] = r.near[pl.ds(aligned((1 - core) * own), window - own), :].astype(BF16)
    r.send("halo")
    r.out("dx")[...] = (
        dz_ref[...]
        + sum(nt(r.get(f"dq{g}")[...], w[g][0]) for g in range(2))
        + r.near[pl.ds(aligned(core * (window - own)), own), :]
    )


class Refs:
    def __init__(self, smem, ins, outs, scratch):
        for name, ref in list(smem.items()) + list(scratch.items()):
            setattr(self, name, ref)
        self.ins, self.outs = ins, outs
        self.waited, self.sent = set(), set()
        for copy, ref in ins.values():
            copy.start()

    def get(self, name):
        copy, ref = self.ins[name]
        if name not in self.waited:
            self.waited.add(name)
            copy.wait()
        return ref

    def out(self, name):
        return self.outs[name][1]

    def send(self, name):
        self.sent.add(name)
        self.outs[name][0].start()

    def close(self):
        for name in self.ins:
            self.get(name)
        for name in self.outs:
            if name not in self.sent:
                self.send(name)
        for copy, ref in self.outs.values():
            copy.wait()


def call(kernel, name, smem, ins, outs, scratch, cost):
    n_smem, n_in, n_out, n_scratch = len(smem), len(ins), len(outs), len(scratch)

    def body(*refs):
        smem_refs = refs[:n_smem]
        refs = refs[n_smem:]
        in_refs, out_refs, refs = refs[:n_in], refs[n_in : n_in + n_out], refs[n_in + n_out :]
        in_vmem, out_vmem, refs = refs[:n_in], refs[n_in : n_in + n_out], refs[n_in + n_out :]
        in_sem, out_sem = refs[-2:]
        copies_in = {
            key: (pltpu.make_async_copy(in_refs[i], in_vmem[i], in_sem.at[i]), in_vmem[i])
            for i, key in enumerate(ins)
        }
        copies_out = {
            key: (pltpu.make_async_copy(out_vmem[i], out_refs[i], out_sem.at[i]), out_vmem[i])
            for i, key in enumerate(outs)
        }
        held = Refs(dict(zip(smem, smem_refs)), copies_in, copies_out, dict(zip(scratch, refs)))
        kernel(held)
        held.close()

    results = pl.pallas_call(
        body,
        out_shape=[jax.ShapeDtypeStruct(*out) for out in outs.values()],
        in_specs=[pl.BlockSpec(memory_space=pltpu.SMEM)] * n_smem + [pl.BlockSpec(memory_space=pl.ANY)] * n_in,
        out_specs=[pl.BlockSpec(memory_space=pl.ANY)] * n_out,
        scratch_shapes=[pltpu.VMEM(array.shape, array.dtype) for array in ins.values()]
        + [pltpu.VMEM(*out) for out in outs.values()]
        + [pltpu.VMEM(*one) for one in scratch.values()]
        + [pltpu.SemaphoreType.DMA((n_in,)), pltpu.SemaphoreType.DMA((n_out,))],
        compiler_params=pltpu.CompilerParams(vmem_limit_bytes=VMEM_LIMIT),
        cost_estimate=pl.CostEstimate(flops=cost * 10**9, transcendentals=0, bytes_accessed=cost * 10**6),
        name=name,
    )(*smem.values(), *ins.values())
    return SimpleNamespace(**dict(zip(outs, results)))


def finish_kernel(kind, bits, ids_ref, *refs):
    mark = own_label(bits, ids_ref[0], ids_ref[1])
    gathered, sem = refs[-2:]
    n_outs = {"enc": 4, "dec": 2, "cross": 3, "feed": 2}[kind]
    count = len(refs) - 2 - n_outs
    parts, outs = refs[:count], refs[count:-2]
    copies, at = [], 0
    for i, part in enumerate(parts):
        copies.append(pltpu.make_async_copy(part, gathered.at[pl.ds(at, part.shape[0])], sem.at[i]))
        at += part.shape[0]
    for copy in copies:
        copy.start()
    for copy in copies:
        copy.wait()
    for shard in range(SHARDS):
        unit, half = divmod(shard, 2)
        rows = slice(half * QUAD, (half + 1) * QUAD)
        where = pl.ds(mark ^ shard, 1)
        value = gathered[where, :QUAD, :][0].astype(F32)
        if kind == "feed":
            outs[0][rows, quad(unit)] = value
            at = unit // 2 * 2 * QUAD + half * QUAD
            outs[1][at : at + QUAD, quad(unit % 2)] = gathered[where, QUAD:, :][0].astype(F32)
        elif unit == 3:
            outs[2 if kind == "cross" else 1][:, quad(half)] = value
        elif kind != "cross":
            outs[0][unit, rows, :] = value
        elif unit == 0:
            outs[0][rows, :] = value
        else:
            outs[1][unit - 1, rows, :] = value
        if kind == "enc":
            norms = gathered[where, QUAD:, :][0].astype(F32)
            many = norm_rows(SHARDS)
            for i in range(many):
                row, side = divmod(shard * many + i, 2)
                if row < 10:
                    outs[2 + row // 5][row % 5 : row % 5 + 1, quad(side)] = norms[i : i + 1, :]


def finish(group, ids, outs):
    parts = group.parts
    shape = (SHARDS,) + parts[0].shape[1:]
    return pl.pallas_call(
        functools.partial(finish_kernel, group.kind, group.bits),
        out_shape=[jax.ShapeDtypeStruct(*out) for out in outs],
        in_specs=[pl.BlockSpec(memory_space=pltpu.SMEM)] + [pl.BlockSpec(memory_space=pl.ANY)] * len(parts),
        out_specs=[pl.BlockSpec(memory_space=pltpu.VMEM)] * len(outs),
        scratch_shapes=[pltpu.VMEM(shape, BF16), pltpu.SemaphoreType.DMA((len(parts),))],
        compiler_params=pltpu.CompilerParams(vmem_limit_bytes=VMEM_LIMIT),
        cost_estimate=pl.CostEstimate(flops=2 * 10**9, transcendentals=0, bytes_accessed=2 * 10**6),
        name="finish_" + group.kind,
    )(ids, *parts)


class Sum:
    def __init__(self, kind, bits, dp, mp):
        self.kind, self.bits, self.dp, self.mp = kind, bits, dp, mp

    def hop(self, array, step):
        pairs = []
        for place in range(self.dp):
            for core in range(self.mp):
                bit = self.bits[core][step] if step < 4 else step
                pairs.append((place * self.mp + core, (place ^ (1 << bit)) * self.mp + core))
        return lax.ppermute(array, ("dp", "mp"), pairs)

    def swap(self, other):
        self.sent = lax.ppermute(other, "mp", [(0, 1), (1, 0)])

    def halve(self, mine=None):
        mine = self.keep if mine is None else mine
        half = mine.shape[0] // 2
        return [mine[half:] + self.sent[half:], mine[:half] + self.sent[:half]]

    def send_half(self, give, keep, step):
        self.keep = keep
        self.sent = self.hop(give, step)

    def last_sum(self):
        return self.keep + self.sent

    def exchange(self, part):
        step = 3
        while 2 << step < self.dp:
            part = part + self.hop(part, step)
            step += 1
        self.keep, self.sent = part, self.hop(part, step)

    def double(self, step, parts=None):
        self.parts = self.parts + [self.hop(part, step) for part in parts or [self.joined()]]

    def joined(self):
        return jnp.concatenate(self.parts) if len(self.parts) > 1 else self.parts[0]


def together(*values):
    return lax.optimization_barrier(values)


def on_device(
    src_embed, tgt_embed, src_segment, tgt_segment, enc_qkv, enc_out_proj, dec_qkv, dec_out_proj, cross_query,
    cross_kv, cross_out_proj, ffn_up, ffn_down, norm_gain, norm_bias, enc_cotangent, dec_cotangent,
):
    dp, mp = lax.axis_size("dp"), lax.axis_size("mp")
    tokens, model = src_embed.shape
    own = tokens // mp
    window = own + MOST
    half = ffn_up.shape[1]
    hidden = 2 * half
    position = lax.axis_index("mp")
    ids = jnp.stack([position, lax.axis_index("dp")]).astype(jnp.int32)
    pairs = [(0, 1), (1, 0)]

    def swap(tree):
        return jax.tree.map(lambda a: lax.ppermute(a, "mp", pairs), tree)

    enc_w1, enc_o1 = swap((enc_qkv, enc_out_proj))
    up1, down1 = swap((ffn_up, ffn_down))
    dec_w1, dec_o1 = swap((dec_qkv, dec_out_proj))
    cross_q1, cross_kv1, cross_o1 = swap((cross_query, cross_kv, cross_out_proj))
    feed = {"up0": ffn_up, "up1": up1, "down0": ffn_down, "down1": down1}

    def rows(count, dtype):
        return ((count, model), dtype)

    blocks = own // BLOCK
    q_shape, k_shape, ot_shape, lse_shape = ((own, QUAD), BF16), ((window, QUAD), BF16), ((QUAD, own), BF16), ((4, own), F32)
    vt_shape, marks, bias = ((QUAD, window), BF16), ((window, BLOCK), jnp.int32), ((blocks, 3 * BLOCK, BLOCK), F32)
    heads = {"q": q_shape, "k": k_shape, "v": k_shape, "ot": ot_shape, "lse": lse_shape}
    wide = ((own, half), BF16)
    norm_in = {"gain": norm_gain, "shift": norm_bias}
    first = call(
        own_heads_kernel, "own_heads", {"ids": ids},
        {"src_row": src_segment, "src": src_embed, "src_w": enc_qkv,
         "tgt_row": tgt_segment, "tgt": tgt_embed, "tgt_w": dec_qkv},
        {f"{side}_{key}": shape for side in ("src", "tgt") for key, shape in heads.items()},
        {"marks": marks, "src_bias": bias, "tgt_bias": bias, "src_vt": vt_shape, "tgt_vt": vt_shape}, cost=8,
    )
    encoder = call(
        encoder_kernel, "encoder_forward", {"ids": ids},
        {"row": src_segment, "x": src_embed, "w": enc_w1, "ot0": first.src_ot, "wo0": enc_out_proj, "wo1": enc_o1,
         **norm_in, "up0": ffn_up, "down0": ffn_down, "up1": up1, "down1": down1},
        {**heads, "z0": rows(own, F32), "x1_low": rows(own, BF16), "h0": wide, "h1": wide,
         "z1": rows(own, F32), "enc": rows(own, BF16)},
        {"marks": marks, "bias": bias, "vt": vt_shape, "x1": rows(own, F32), "acc": rows(own, F32)}, cost=12,
    )
    enc_swapped = swap(encoder.enc)
    decoder = call(
        decoder_kernel, "decoder_self_forward", {"ids": ids},
        {"row": tgt_segment, "x": tgt_embed, "w": dec_w1, "ot0": first.tgt_ot, "wo0": dec_out_proj, "wo1": dec_o1,
         **norm_in},
        {**heads, "z2": rows(own, F32), "x2": rows(own, F32)},
        {"marks": marks, "bias": bias, "vt": vt_shape, "acc": rows(own, F32)}, cost=6,
    )
    packed = ((SHARDS, QUAD, QUAD), BF16)
    packed_feed = ((SHARDS, 2 * QUAD, QUAD), BF16)
    packed_norms = ((SHARDS, QUAD + TILE, QUAD), BF16)
    unit = ((2 * QUAD, QUAD), BF16)
    cross_key = ((tokens, QUAD), BF16)
    crossed = call(
        cross_kernel, "cross_and_decoder_feed",
        {"ids": ids, "src_marks": src_segment, "tgt_marks": tgt_segment},
        {"src_row": src_segment, "tgt_row": tgt_segment, "enc_own": encoder.enc, "enc_other": enc_swapped,
         "x2": decoder.x2, "cq0": cross_query, "ckv0": cross_kv, "cq1": cross_q1, "ckv1": cross_kv1,
         "co0": cross_out_proj, "co1": cross_o1, **norm_in, **feed, "cot": dec_cotangent},
        {"enc": rows(tokens, BF16), "x3_low": rows(own, BF16), "a0": wide, "a1": wide, "dec": rows(own, BF16),
         "dy": rows(own, BF16), "dh0": wide, "dh1": wide, "norms": rows(4, F32), "pack1": packed, "unit": unit,
         "dz": rows(own, F32), "dq0": q_shape, "dq1": q_shape, "dk0": cross_key, "dk1": cross_key, "dv0": cross_key,
         "dv1": cross_key, "denc_other": rows(own, BF16), "denc_own": rows(own, F32)},
        {"marks": ((tokens, BLOCK), jnp.int32), "bias": bias, "q": ((2, own, QUAD), BF16),
         "k": ((2, tokens, QUAD), BF16), "v": ((2, tokens, QUAD), BF16), "turn": ((model, tokens), BF16),
         "mix": ((model, own), F32), "tops": ((8, own), F32), "totals": ((8, own), F32), "lse": ((2, 4, own), F32),
         "ot": ((model, own), BF16), "acc": rows(own, F32), "x3": rows(own, F32), "z3": rows(own, F32),
         "z4": rows(own, F32), "h": ((2, own, half), F32), "low": rows(own, BF16), "do": rows(own, BF16),
         "delta": ((8, own), F32), "dqt": ((model, own), F32), "dk": rows(tokens, F32), "dv": rows(tokens, F32)},
        cost=28,
    )
    cross_sum = Sum("cross", CROSS_BITS, dp, mp)
    dec_sum = Sum("dec", DEC_BITS, dp, mp)
    feed_sum = Sum("feed", FEED_BITS, dp, mp)
    enc_sum = Sum("enc", ENC_BITS, dp, mp)
    cross_sum.swap(crossed.pack1)
    denc_recv = swap(crossed.denc_other)
    crossed_more = call(
        cross_second_kernel, "cross_second", {"ids": ids},
        {"enc": crossed.enc, "dk0": crossed.dk0, "dv0": crossed.dv0, "x2": decoder.x2, "dq0": crossed.dq0,
         "unit": crossed.unit, "dz": crossed.dz, "dq1": crossed.dq1, "cq0": cross_query, "cq1": cross_q1},
        {"pack0": packed, "g2": rows(own, F32)}, {}, cost=4,
    )

    def self_backward(causal, at, bits, name, side, x, row, z, up, w0, w1, o0, o1, others, pack_shape, more):
        ins = {"row": row, "gain": norm_gain, "z": z, "up": up, "x": x}
        ins |= {"ot0": getattr(first, side + "_ot"), "ot1": others.ot, "wo0": o0, "wo1": o1}
        for key in ("k", "q", "v", "lse"):
            ins |= {key + "0": getattr(first, f"{side}_{key}"), key + "1": getattr(others, key)}
        return call(
            functools.partial(self_back_kernel, causal, at, bits), name, {"ids": ids}, ins | more,
            {"dz": rows(own, F32), "pack1": pack_shape, "unit": unit, "norms": rows(2, F32), "dq0": q_shape,
             "dq1": q_shape, "dk0": k_shape, "dk1": k_shape, "dv0": k_shape, "dv1": k_shape},
            {"marks": marks, "bias": bias, "low": rows(own, BF16), "do": rows(own, BF16), "delta": ((8, own), F32),
             "kt": ((model, window), BF16), "dqt": ((model, own), F32), "dk": rows(window, F32), "dv": rows(window, F32)},
            cost=11,
        )

    def self_backward_own(causal, bits, name, x, back, gate, pack_shape, more):
        return call(
            functools.partial(self_back_own_kernel, causal, bits), name, {"ids": ids},
            {"x": x, "dq0": back.dq0, "dk0": back.dk0, "dv0": back.dv0, "unit": gate} | more,
            {"pack0": pack_shape}, {}, cost=3,
        ).pack0

    def stream_gradient(name, back, w0, w1, gate):
        ins = {"dz": gate, "w0": w0, "w1": w1}
        ins |= {f"{key}{g}": getattr(back, f"{key}{g}") for key in ("dk", "dv", "dq") for g in range(2)}
        return call(
            stream_gradient_kernel, name, {"ids": ids}, ins,
            {"halo": rows(window - own, BF16), "dx": rows(own, F32)}, {"near": rows(window, F32)}, cost=3,
        )

    square, out_half, triple = ((model, QUAD), F32), ((QUAD, model), F32), ((3, model, QUAD), F32)
    out_shapes = {
        "cross": [square, ((2, model, QUAD), F32), out_half],
        "dec": [triple, out_half],
        "feed": [((model, half), F32), rows(half, F32)],
        "enc": [triple, out_half, rows(5, F32), rows(5, F32)],
    }
    gate, give, keep, denc_recv = together(encoder.z1, *cross_sum.halve(crossed_more.pack0), denc_recv)
    cross_sum.send_half(give, keep, 0)
    feed_in = {"x1_low": encoder.x1_low, "x3_low": crossed.x3_low, "dy3": crossed.dy}
    fed = call(
        feed_other_kernel, "encoder_feed_other", {"ids": ids},
        {"cot": enc_cotangent, "denc_own": crossed.denc_own, "denc_recv": denc_recv, "z1": gate,
         "gain": norm_gain, "h": encoder.h1, "down": down1, "up": up1, "dh": crossed.dh1, "a": crossed.a1, **feed_in},
        {"dy": rows(own, BF16), "norms": rows(2, F32), "pack1": packed_feed, "g0": rows(own, F32)}, {}, cost=10,
    )
    gate, give, keep, other = together(fed.dy, *cross_sum.halve(), fed.pack1)
    cross_sum.send_half(give, keep, 1)
    feed_sum.swap(other)
    fed_own = call(
        feed_own_kernel, "encoder_feed_own", {"ids": ids},
        {"dz": fed.g0, "dy": gate, "h": encoder.h0, "down": ffn_down, "up": ffn_up, "dh": crossed.dh0,
         "a": crossed.a0, **feed_in},
        {"g0": rows(own, F32), "pack0": packed_feed}, {}, cost=9,
    )
    gate, give, keep, feed_give, feed_keep = together(
        crossed_more.g2, *cross_sum.halve(), *feed_sum.halve(fed_own.pack0)
    )
    feed_sum.send_half(feed_give, feed_keep, 0)
    cross_sum.send_half(give, keep, 2)
    dec_back = self_backward(
        True, 2, DEC_BITS, "decoder_self_backward", "tgt", tgt_embed, tgt_segment, decoder.z2, gate,
        dec_qkv, dec_w1, dec_out_proj, dec_o1, decoder, packed, {},
    )
    gate, part, other = together(dec_back.unit, cross_sum.last_sum(), dec_back.pack1)
    cross_sum.exchange(part)
    dec_sum.swap(other)
    dec_pack = self_backward_own(True, DEC_BITS, "decoder_self_own", tgt_embed, dec_back, gate, packed, {})
    gate, cross_part, give, keep, dec_give, dec_keep = together(
        fed_own.g0, cross_sum.last_sum(), *feed_sum.halve(), *dec_sum.halve(dec_pack)
    )
    feed_sum.send_half(give, keep, 1)
    dec_sum.send_half(dec_give, dec_keep, 0)
    cross_sum.parts = [cross_part]
    cross_sum.double(2)
    norms_before = {"feed_norms": fed.norms, "dec_norms": dec_back.norms, "cross_norms": crossed.norms}
    enc_back = self_backward(
        False, 0, ENC_BITS, "encoder_self_backward", "src", src_embed, src_segment, encoder.z0, gate,
        enc_qkv, enc_w1, enc_out_proj, enc_o1, encoder, packed_norms, norms_before,
    )
    gate, other, give, keep, dec_give, dec_keep, *cross_sum.parts = together(
        enc_back.unit, enc_back.pack1, *feed_sum.halve(), *dec_sum.halve(), *cross_sum.parts
    )
    dec_sum.send_half(dec_give, dec_keep, 1)
    feed_sum.send_half(give, keep, 2)
    cross_sum.double(1)
    enc_sum.swap(other)
    enc_pack = self_backward_own(
        False, ENC_BITS, "encoder_self_own", src_embed, enc_back, gate, packed_norms,
        {"norms": enc_back.norms, **norms_before},
    )
    gate, enc_give, enc_keep, part, dec_give, dec_keep, *cross_sum.parts = together(
        enc_back.dz, *enc_sum.halve(enc_pack), feed_sum.last_sum(), *dec_sum.halve(), *cross_sum.parts
    )
    enc_sum.send_half(enc_give, enc_keep, 0)
    feed_sum.exchange(part)
    dec_sum.send_half(dec_give, dec_keep, 2)
    cross_sum.double(0)
    src_side = stream_gradient("src_gradient", enc_back, enc_qkv, enc_w1, gate)
    gate, src_halo, dec_own, enc_give, enc_keep, feed_part, dec_part = together(
        dec_back.dz, src_side.halo, crossed.dec, *enc_sum.halve(), feed_sum.last_sum(), dec_sum.last_sum()
    )
    enc_sum.send_half(enc_give, enc_keep, 1)
    feed_sum.parts = [feed_part]
    feed_sum.double(2)
    dec_sum.exchange(dec_part)
    src_recv = swap(src_halo)
    dec_swapped = swap(dec_own)
    tgt_side = stream_gradient("tgt_gradient", dec_back, dec_qkv, dec_w1, gate)
    tgt_halo, enc_give, enc_keep, dec_part, feed_zero, feed_one, *cross_sum.parts = together(
        tgt_side.halo, *enc_sum.halve(), dec_sum.last_sum(), *feed_sum.parts, *cross_sum.parts
    )
    enc_sum.send_half(enc_give, enc_keep, 2)
    feed_sum.parts = [feed_zero, feed_one]
    feed_sum.double(1)
    dec_sum.parts = [dec_part]
    dec_sum.double(2)
    tgt_recv = swap(tgt_halo)
    cross_out = finish(cross_sum, ids, out_shapes["cross"])
    enc_part, *parts = together(enc_sum.last_sum(), *dec_sum.parts, *feed_sum.parts)
    dec_sum.parts, feed_sum.parts = parts[:2], parts[2:]
    enc_sum.exchange(enc_part)
    feed_sum.double(0)
    dec_sum.double(1)
    enc_part, *dec_sum.parts = together(enc_sum.last_sum(), *dec_sum.parts)
    enc_sum.parts = [enc_part]
    enc_sum.double(2)
    dec_sum.double(0)
    enc_sum.double(1)
    enc_sum.double(0)
    feed_out = finish(feed_sum, ids, out_shapes["feed"])
    dec_out = finish(dec_sum, ids, out_shapes["dec"])
    enc_out = finish(enc_sum, ids, out_shapes["enc"])

    def whole(mine, received):
        return jnp.where(
            position == 0, jnp.concatenate([mine, received]), jnp.concatenate([received, mine])
        )

    halo_at = (1 - position) * (own - (window - own))

    def with_halo(grad, received):
        part = lax.dynamic_slice_in_dim(grad, halo_at, window - own, 0) + received.astype(F32)
        return lax.dynamic_update_slice_in_dim(grad, part, halo_at, 0)

    return (
        crossed.enc,
        whole(crossed.dec, dec_swapped),
        with_halo(src_side.dx, src_recv),
        with_halo(tgt_side.dx, tgt_recv),
        enc_out[0],
        enc_out[1],
        dec_out[0],
        dec_out[1],
        cross_out[0],
        cross_out[1],
        cross_out[2],
        feed_out[0],
        feed_out[1],
        enc_out[2],
        enc_out[3],
    )


def solution(mesh):
    in_specs = (
        P("dp", None), P("dp", None), P("dp", None), P("dp", None),
        P(None, None, "mp"), P("mp", None), P(None, None, "mp"), P("mp", None),
        P(None, "mp"), P(None, None, "mp"), P("mp", None), P(None, "mp"), P("mp", None),
        P(), P(), P(("dp", "mp"), None), P(("dp", "mp"), None),
    )
    out_specs = (
        P("dp", None), P("dp", None), P(("dp", "mp"), None), P(("dp", "mp"), None),
        P(None, None, "mp"), P("mp", None), P(None, None, "mp"), P("mp", None),
        P(None, "mp"), P(None, None, "mp"), P("mp", None), P(None, "mp"), P("mp", None),
        P(), P(),
    )
    return jax.shard_map(on_device, mesh=mesh, in_specs=in_specs, out_specs=out_specs, check_vma=False)
```

```python
import functools
import math
from types import SimpleNamespace

import jax
import jax.numpy as jnp
from jax import lax
from jax.experimental import pallas as pl
from jax.experimental.pallas import tpu as pltpu
from jax.sharding import PartitionSpec as P

HDIM = 64
SCALE = HDIM ** (-0.5)
EPSILON = 1e-05
MASKED = -1e30
BLOCK = 128
MOST = 128
QUAD = 4 * HDIM
UNITS = 4
TILE = 16
FEED = 512
SHARDS = 8
CROSS_BITS = ((0, 1, 2, 3), (1, 0, 2, 3))
FEED_BITS = ((0, 1, 2, 3), (1, 0, 2, 3))
DEC_BITS = ((1, 0, 2, 3), (0, 1, 2, 3))
ENC_BITS = ((1, 0, 2, 3), (0, 1, 2, 3))
PIECE = 32
F32 = jnp.float32
BF16 = jnp.bfloat16
VMEM_LIMIT = 56 * 1024 * 1024
GELU_IN = math.sqrt(2.0 / math.pi)
GELU_CUBE = 0.044715


def nn(left, right):
    return jnp.dot(left, right, preferred_element_type=F32)


def nt(left, right):
    return lax.dot_general(left, right, (((1,), (1,)), ((), ())), preferred_element_type=F32)


def tn(left, right):
    return lax.dot_general(left, right, (((0,), (0,)), ((), ())), preferred_element_type=F32)


def aligned(index, size=BLOCK):
    return pl.multiple_of(index, size)


def over_rows(rows, chunk, body, carry, unroll=4):
    return lax.fori_loop(
        0,
        rows // chunk,
        lambda i, kept: body(pl.ds(aligned(i * chunk, chunk), chunk), kept),
        carry,
        unroll=min(unroll, rows // chunk),
    )


def normalize(before):
    centered = before - jnp.mean(before, axis=-1, keepdims=True)
    variance = jnp.mean(centered * centered, axis=-1, keepdims=True)
    rate = lax.rsqrt(variance + EPSILON)
    return centered * rate, rate


def norm_backward(before, upstream, gain_row):
    normed, rate = normalize(before)
    scaled = upstream * gain_row
    first = jnp.mean(scaled, axis=-1, keepdims=True)
    second = jnp.mean(scaled * normed, axis=-1, keepdims=True)
    return rate * (scaled - first - normed * second), upstream * normed


def fold_rows(block):
    return jnp.sum(block.reshape(block.shape[0] // 8, 8, block.shape[1]), axis=0)


def gelu(hidden):
    inner = GELU_IN * hidden * (1.0 + GELU_CUBE * hidden * hidden)
    return 0.5 * hidden * (1.0 + jnp.tanh(inner))


def gelu_both(hidden):
    square = hidden * hidden
    bent = jnp.tanh(GELU_IN * hidden * (1.0 + GELU_CUBE * square))
    half = 0.5 * (1.0 + bent)
    slope = half + 0.5 * hidden * (1.0 - bent * bent) * (GELU_IN * (1.0 + 3.0 * GELU_CUBE * square))
    return hidden * half, slope


def head_masks():
    lane = lax.broadcasted_iota(jnp.int32, (1, QUAD), 1)
    return [
        jnp.where((lane >= h * HDIM) & (lane < (h + 1) * HDIM), 1.0, 0.0).astype(BF16)
        for h in range(4)
    ]


def stack_heads(block, masks):
    return jnp.concatenate([block * mask for mask in masks], axis=0)


def quad(g):
    return slice(g * QUAD, (g + 1) * QUAD)


def bias_for(marks_ref, key_at, width, query_row, causal=False, key_start=0, query_start=0):
    allowed = marks_ref[pl.ds(key_at, width), :] == query_row
    if causal:
        places = key_start + lax.broadcasted_iota(jnp.int32, (width, BLOCK), 0)
        queries = query_start + lax.broadcasted_iota(jnp.int32, (width, BLOCK), 1)
        allowed = allowed & (places <= queries)
    return jnp.where(allowed, 0.0, MASKED)


def self_window(core, block, causal):
    middle = block + core
    if causal:
        return aligned(jnp.maximum(middle - 1, 0) * BLOCK), 2 * BLOCK
    return aligned(jnp.clip(middle - 1, 0, 2) * BLOCK), 3 * BLOCK


def set_self_bias(bias_ref, core, tokens, marks_ref, row_ref, causal):
    window, own = marks_ref.shape[0], row_ref.shape[1] // 2
    start = core * (tokens - window)
    spots = []
    for block in range(own // BLOCK):
        key_at, width = self_window(core, block, causal)
        first = aligned(core * own + block * BLOCK)
        bias_ref[block, :width, :] = bias_for(
            marks_ref, key_at, width, row_ref[:, pl.ds(first, BLOCK)], causal, start + key_at, first
        )
        spots.append((key_at, width))
    return spots


def soft_weights(scores, h, bias, weights_ref, top=None):
    cols = slice(h * BLOCK, (h + 1) * BLOCK)
    pieces = [slice(at, at + BLOCK) for at in range(0, scores.shape[0], BLOCK)]
    masked = [scores[piece, cols] + bias(piece) for piece in pieces]
    tops = [jnp.max(one, axis=0, keepdims=True) for one in masked]
    top = functools.reduce(jnp.maximum, tops if top is None else tops + [top])
    total = None
    for piece, one in zip(pieces, masked):
        weights = jnp.exp(one - top)
        weights_ref[piece, cols] = weights.astype(BF16)
        term = jnp.sum(weights, axis=0, keepdims=True)
        total = term if total is None else total + term
    return top, total


def quad_forward(spots, q_ref, k_ref, vt_ref, bias_ref, ot_ref, lse_ref, masks, weights_ref):
    def score(block):
        rows, (key_at, width) = slice(block * BLOCK, (block + 1) * BLOCK), spots[block]
        return nt(k_ref[pl.ds(key_at, width), :], stack_heads(q_ref[rows, :], masks))

    ahead = score(0)
    for block, (key_at, width) in enumerate(spots):
        rows = slice(block * BLOCK, (block + 1) * BLOCK)
        scores, ahead = ahead, score(block + 1) if block + 1 < len(spots) else None
        for h in range(4):
            held = weights_ref.at[block % 2]
            top, total = soft_weights(scores, h, lambda piece: bias_ref[block, piece, :], held)
            features = slice(h * HDIM, (h + 1) * HDIM)
            mixed = nn(vt_ref[features, pl.ds(key_at, width)], held[:width, h * BLOCK : (h + 1) * BLOCK])
            ot_ref[features, rows] = (mixed * (1.0 / total)).astype(BF16)
            lse_ref[h : h + 1, rows] = top + jnp.log(total)


def backward_tile(
    g, rows, key_at, width, bias, masks, q_ref, k_ref, v_ref, kt_ref, do_ref, lse_ref, delta_ref, dqt_ref, dk_ref, dv_ref,
    prob_ref, grad_ref, add,
):
    keys = pl.ds(key_at, width)
    q_stack = stack_heads(q_ref[rows, :], masks)
    do_stack = stack_heads(do_ref[rows, quad(g)], masks)
    scores = nt(k_ref[keys, :], q_stack)
    prob_grads = nt(v_ref[keys, :], do_stack)
    for h in range(4):
        cols = slice(h * BLOCK, (h + 1) * BLOCK)
        head = g * 4 + h
        lse, delta = lse_ref[h : h + 1, rows], delta_ref[head : head + 1, rows]
        for at in range(0, width, BLOCK):
            piece = slice(at, at + BLOCK)
            prob = jnp.exp(scores[piece, cols] + bias(piece) - lse)
            prob_ref[piece, cols] = prob.astype(BF16)
            grad_ref[piece, cols] = (prob * (prob_grads[piece, cols] - delta)).astype(BF16)
        features = slice(head * HDIM, (head + 1) * HDIM)
        query_grad = nn(kt_ref[features, keys], grad_ref[:width, cols])
        if add:
            dqt_ref[features, rows] += query_grad
        else:
            dqt_ref[features, rows] = query_grad
    dv_ref[keys, quad(g)] += nn(prob_ref[:width, :], do_stack)
    dk_ref[keys, quad(g)] += nn(grad_ref[:width, :], q_stack)


def mixed_gradients(branch, ot_refs, w_out, do_ref, delta_ref):
    for g in range(2):
        do_ref[:, quad(g)] = nt(branch, w_out[g][...]).astype(BF16)
        turned = nt(w_out[g][...], branch).astype(BF16).astype(F32)
        product = turned * ot_refs[g][...].astype(F32)
        for h in range(4):
            delta_ref[g * 4 + h : g * 4 + h + 1, :] = jnp.sum(
                product[h * HDIM : (h + 1) * HDIM, :], axis=0, keepdims=True
            )


def spread_marks(marks_ref, row):
    marks_ref[...] = jnp.broadcast_to(row, (marks_ref.shape[1], marks_ref.shape[0])).T


def label(bits, place):
    first, second, third = [(place >> bit) & 1 for bit in bits[:3]]
    return 4 * first + 2 * second + third


def own_label(bits, core, place):
    return jnp.where(core == 0, label(bits[0], place), label(bits[1], place))


def pack(out_ref, mark, unit, value, at=0):
    rows = value.shape[0] // 2
    for half in range(2):
        where = pl.ds(mark ^ (2 * unit + half), 1)
        out_ref[where, at : at + rows, :] = value[half * rows : (half + 1) * rows].astype(BF16)[None]


def as_unit(value):
    return jnp.concatenate([value[:, :QUAD], value[:, QUAD:]], axis=0).astype(BF16)


def pack_norms(out_ref, mark, parts):
    shards, tall, width = out_ref.shape
    halves = [part[:, half * width : (half + 1) * width] for part in parts for half in range(2)]
    each = norm_rows(shards)
    blank = jnp.zeros((1, width), F32)
    halves += [blank] * (shards * each - len(halves))
    for i in range(shards):
        block = jnp.concatenate(halves[i * each : (i + 1) * each] + [blank] * (TILE - each), axis=0)
        out_ref[pl.ds(mark ^ i, 1), tall - TILE :, :] = block.astype(BF16)[None]


def norm_rows(shards):
    return -(-20 // shards)


def prepare_quad(x_ref, w_ref, core, q_ref, k_ref, v_ref, vt_ref):
    tokens, own, window = x_ref.shape[0], q_ref.shape[0], k_ref.shape[0]
    keys = x_ref[pl.ds(aligned(core * (tokens - window)), window), :]
    q_ref[...] = (nn(x_ref[pl.ds(aligned(core * own), own), :], w_ref[0]) * SCALE).astype(BF16)
    k_ref[...] = nn(keys, w_ref[1]).astype(BF16)
    v_ref[...] = nn(keys, w_ref[2]).astype(BF16)
    vt_ref[...] = v_ref[...].T


def own_heads_kernel(r):
    core = r.ids[0]
    masks = head_masks()
    for side, causal in (("src", False), ("tgt", True)):
        x_ref, row_ref = r.get(side), r.get(side + "_row")
        k_ref = r.out(side + "_k")
        start = aligned(core * (x_ref.shape[0] - k_ref.shape[0]))
        spread_marks(r.marks, row_ref[:, pl.ds(start, k_ref.shape[0])])
        bias_ref, vt_ref = getattr(r, side + "_bias"), getattr(r, side + "_vt")
        spots = set_self_bias(bias_ref, core, x_ref.shape[0], r.marks, row_ref, causal)
        q_ref, v_ref = r.out(side + "_q"), r.out(side + "_v")
        prepare_quad(x_ref, r.get(side + "_w"), core, q_ref, k_ref, v_ref, vt_ref)
        for key in ("_q", "_k", "_v"):
            r.send(side + key)
        quad_forward(
            spots, q_ref, k_ref, vt_ref, bias_ref, r.out(side + "_ot"), r.out(side + "_lse"), masks, r.weights
        )
        r.send(side + "_ot")
        r.send(side + "_lse")


def other_heads(r, causal):
    core = r.ids[0]
    x_ref, row_ref, k_ref = r.get("x"), r.get("row"), r.out("k")
    start = aligned(core * (x_ref.shape[0] - k_ref.shape[0]))
    spread_marks(r.marks, row_ref[:, pl.ds(start, k_ref.shape[0])])
    spots = set_self_bias(r.bias, core, x_ref.shape[0], r.marks, row_ref, causal)
    q_ref, v_ref, ot_ref = r.out("q"), r.out("v"), r.out("ot")
    prepare_quad(x_ref, r.get("w"), core, q_ref, k_ref, v_ref, r.vt)
    for key in ("q", "k", "v"):
        r.send(key)
    quad_forward(spots, q_ref, k_ref, r.vt, r.bias, ot_ref, r.out("lse"), head_masks(), r.weights)
    r.send("lse")
    r.send("ot")
    r.acc[...] = tn(r.get("ot0")[...], r.get("wo0")[...]) + tn(ot_ref[...], r.get("wo1")[...])


def norm_forward(r, at, residual, before_ref, after_ref, low_ref):
    gain, shift = r.get("gain")[at : at + 1, :], r.get("shift")[at : at + 1, :]

    def body(rows, carry):
        before = residual(rows) + r.acc[rows, :]
        if before_ref is not None:
            before_ref[rows, :] = before
        after = normalize(before)[0] * gain + shift
        if after_ref is not None:
            after_ref[rows, :] = after
        if low_ref is not None:
            low_ref[rows, :] = after.astype(BF16)
        return carry

    over_rows(r.acc.shape[0], 32, body, 0)


def own_row_reader(x_ref, core, own):
    first = core * own
    return lambda rows: x_ref[pl.ds(aligned(first + rows.start, rows.size), rows.size), :].astype(F32)


def encoder_kernel(r):
    other_heads(r, False)
    x1_low = r.out("x1_low")
    norm_forward(r, 0, own_row_reader(r.get("x"), r.ids[0], r.acc.shape[0]), r.out("z0"), r.x1, x1_low)
    r.send("z0")
    r.send("x1_low")
    feed_forward(x1_low, *feed_weights(r), (r.out("h0"), r.out("h1")), (r.a.at[0], r.a.at[1]), r.acc)
    r.send("h0")
    r.send("h1")
    norm_forward(r, 1, lambda rows: r.x1[rows, :], r.out("z1"), None, r.out("enc"))


def decoder_kernel(r):
    other_heads(r, True)
    norm_forward(r, 2, own_row_reader(r.get("x"), r.ids[0], r.acc.shape[0]), r.out("z2"), r.out("x2"), None)


def feed_weights(r):
    return (r.get("up0"), r.get("up1")), (r.get("down0"), r.get("down1"))


def feed_chunks(half):
    return [(j, slice(j * FEED, (j + 1) * FEED)) for j in range(half // FEED)]


def feed_forward(low_ref, ups, downs, h_refs, a_refs, acc_ref):
    chunks = [(g, cols) for g in range(2) for j, cols in feed_chunks(ups[0].shape[1])]
    ahead = nn(low_ref[...], ups[0][:, chunks[0][1]])
    for i, (g, cols) in enumerate(chunks):
        hidden = ahead
        if i + 1 < len(chunks):
            ahead = nn(low_ref[...], ups[chunks[i + 1][0]][:, chunks[i + 1][1]])
        for at in range(0, hidden.shape[0], PIECE):
            piece = slice(at, at + PIECE)
            h_refs[g][piece, cols] = hidden[piece].astype(h_refs[g].dtype)
            a_refs[g][piece, cols] = gelu(hidden[piece]).astype(BF16)
        term = nn(a_refs[g][:, cols], downs[g][cols, :])
        if i == 0:
            acc_ref[...] = term
        else:
            acc_ref[...] += term


def feed_backward(dy_ref, ups, downs, h_refs, dh_refs, acc_ref):
    chunks = [(g, cols) for g in range(2) for j, cols in feed_chunks(ups[0].shape[1])]
    ahead = nt(dy_ref[...], downs[0][chunks[0][1], :])
    for i, (g, cols) in enumerate(chunks):
        active_grad = ahead
        if i + 1 < len(chunks):
            ahead = nt(dy_ref[...], downs[chunks[i + 1][0]][chunks[i + 1][1], :])
        for at in range(0, active_grad.shape[0], PIECE):
            piece = slice(at, at + PIECE)
            slope = gelu_both(h_refs[g][piece, cols].astype(F32))[1]
            dh_refs[g][piece, cols] = (active_grad[piece] * slope).astype(BF16)
        acc_ref[...] += nt(dh_refs[g][:, cols], ups[g][:, cols])


def norm_back(r, gain_row, before, upstream, outs):
    def body(rows, sums):
        above = upstream(rows)
        grad, gain_terms = norm_backward(before(rows), above, gain_row)
        for ref in outs:
            ref[rows, :] = grad.astype(ref.dtype)
        return sums[0] + fold_rows(gain_terms), sums[1] + fold_rows(above)

    zeros = jnp.zeros((8, outs[0].shape[1]), F32)
    gains, shifts = over_rows(outs[0].shape[0], 32, body, (zeros, zeros))
    return jnp.sum(gains, axis=0, keepdims=True), jnp.sum(shifts, axis=0, keepdims=True)


def cross_kernel(r):
    core, place = r.ids[0], r.ids[1]
    x2_ref, enc_ref = r.get("x2"), r.out("enc")
    own, tokens = x2_ref.shape[0], enc_ref.shape[0]
    blocks = own // BLOCK
    first, second = aligned(core * own), aligned((1 - core) * own)
    width = 3 * BLOCK
    enc_ref[pl.ds(first, own), :] = r.get("enc_own")[...]
    enc_ref[pl.ds(second, own), :] = r.get("enc_other")[...]
    r.send("enc")
    spread_marks(r.marks, r.get("src_row")[...])
    steps = tokens.bit_length()

    def bound(mark, past):
        def step(i, pair):
            low, high = pair
            middle = (low + high) // 2
            value = r.src_marks[0, jnp.minimum(middle, tokens - 1)]
            below = (low < high) & ((value < mark) | (past & (value == mark)))
            above = (low < high) & jnp.logical_not(below)
            return jnp.where(below, middle + 1, low), jnp.where(above, middle, high)

        return lax.fori_loop(0, steps, step, (jnp.int32(0), jnp.int32(tokens)))[0]

    row_ref = r.get("tgt_row")
    query_rows, spots, more = [], [], []
    for block in range(blocks):
        head = first + block * BLOCK
        low = bound(r.tgt_marks[0, head], jnp.bool_(False)) // BLOCK
        high = (bound(r.tgt_marks[0, head + BLOCK - 1], jnp.bool_(True)) + BLOCK - 1) // BLOCK
        key_at = aligned(jnp.minimum(low, (tokens - width) // BLOCK) * BLOCK)
        query_rows.append(row_ref[:, pl.ds(aligned(head), BLOCK)])
        spots.append(key_at)
        more.append((key_at // BLOCK + 3, high))
        r.bias[block] = bias_for(r.marks, key_at, width, query_rows[block])
    masks = head_masks()
    x2_low = x2_ref[...].astype(BF16)
    for g in range(2):
        r.q[g] = (nn(x2_low, r.get(f"cq{g}")[...]) * SCALE).astype(BF16)
        r.k[g] = nn(enc_ref[...], r.get(f"ckv{g}")[0]).astype(BF16)
        r.v[g] = nn(enc_ref[...], r.get(f"ckv{g}")[1]).astype(BF16)
        r.turn[quad(g), :] = r.v[g].T

    def weigh(g, h, scores, bias, key_at, keys_width, top, held):
        new_top, total = soft_weights(scores, h, bias, held, top)
        features = slice(g * QUAD + h * HDIM, g * QUAD + (h + 1) * HDIM)
        mixed = nn(r.turn[features, pl.ds(key_at, keys_width)], held[:keys_width, h * BLOCK : (h + 1) * BLOCK])
        return new_top, total, mixed, features

    def score(block, g):
        rows = slice(block * BLOCK, (block + 1) * BLOCK)
        return nt(r.k[g, pl.ds(spots[block], width), :], stack_heads(r.q[g, rows, :], masks))

    tiles = [(block, g) for block in range(blocks) for g in range(2)]
    ahead = score(*tiles[0])
    for i, (block, g) in enumerate(tiles):
        rows = slice(block * BLOCK, (block + 1) * BLOCK)
        scores, ahead = ahead, score(*tiles[i + 1]) if i + 1 < len(tiles) else None
        for h in range(4):
            top, total, mixed, features = weigh(
                g, h, scores, lambda piece: r.bias[block, piece, :], spots[block], width, None, r.prob.at[g]
            )
            r.mix[features, rows] = mixed
            r.tops[g * 4 + h : g * 4 + h + 1, rows] = top
            r.totals[g * 4 + h : g * 4 + h + 1, rows] = total

    for block in range(blocks):
        rows = slice(block * BLOCK, (block + 1) * BLOCK)

        def extra(i, carry, block=block, rows=rows):
            key_at = aligned(i * BLOCK)
            bias = bias_for(r.marks, key_at, BLOCK, query_rows[block])
            for g in range(2):
                scores = nt(r.k[g, pl.ds(key_at, BLOCK), :], stack_heads(r.q[g, rows, :], masks))
                for h in range(4):
                    at = slice(g * 4 + h, g * 4 + h + 1)
                    old = r.tops[at, rows]
                    top, total, mixed, features = weigh(
                        g, h, scores, lambda piece: bias, key_at, BLOCK, old, r.prob.at[g]
                    )
                    fade = jnp.exp(old - top)
                    r.mix[features, rows] = r.mix[features, rows] * fade + mixed
                    r.tops[at, rows] = top
                    r.totals[at, rows] = r.totals[at, rows] * fade + total
            return carry

        lax.fori_loop(*more[block], extra, 0)
    for head in range(8):
        features = slice(head * HDIM, (head + 1) * HDIM)
        at = slice(head, head + 1)
        r.ot[features, :] = (r.mix[features, :] * (1.0 / r.totals[at, :])).astype(BF16)
        r.lse[head // 4, head % 4 : head % 4 + 1, :] = r.tops[at, :] + jnp.log(r.totals[at, :])
    outs = (r.get("co0"), r.get("co1"))
    r.acc[...] = tn(r.ot[:QUAD, :], outs[0][...]) + tn(r.ot[QUAD:, :], outs[1][...])
    x3_low = r.out("x3_low")
    norm_forward(r, 3, lambda rows: x2_ref[rows, :], r.z3, r.x3, x3_low)
    r.send("x3_low")
    ups, downs = feed_weights(r)
    hs = (r.h.at[0], r.h.at[1])
    feed_forward(x3_low, ups, downs, hs, (r.out("a0"), r.out("a1")), r.acc)
    r.send("a0")
    r.send("a1")
    gain_ref, shift_ref, cot_ref, dec_ref, dy_ref = (
        r.get("gain"), r.get("shift"), r.get("cot"), r.out("dec"), r.out("dy")
    )
    last_gain, last_shift = gain_ref[4:5, :], shift_ref[4:5, :]

    def fourth_norm(rows, sums):
        before = r.x3[rows, :] + r.acc[rows, :]
        normed, rate = normalize(before)
        dec_ref[rows, :] = (normed * last_gain + last_shift).astype(BF16)
        upstream = cot_ref[rows, :].astype(F32)
        scaled = upstream * last_gain
        mean_one = jnp.mean(scaled, axis=-1, keepdims=True)
        mean_two = jnp.mean(scaled * normed, axis=-1, keepdims=True)
        grad = rate * (scaled - mean_one - normed * mean_two)
        r.z4[rows, :] = grad
        dy_ref[rows, :] = grad.astype(BF16)
        return sums[0] + fold_rows(upstream * normed), sums[1] + fold_rows(upstream)

    zeros = jnp.zeros((8, x2_ref.shape[1]), F32)
    gain_four, shift_four = over_rows(own, 32, fourth_norm, (zeros, zeros))
    r.send("dec")
    r.send("dy")
    feed_backward(dy_ref, ups, downs, hs, (r.out("dh0"), r.out("dh1")), r.z4)
    r.send("dh0")
    r.send("dh1")
    gain_three, shift_three = norm_back(
        r, gain_ref[3:4, :], lambda rows: r.z3[rows, :], lambda rows: r.z4[rows, :], (r.out("dz"), r.low)
    )
    r.send("dz")
    norms = r.out("norms")
    norms[0:1, :] = gain_three
    norms[1:2, :] = jnp.sum(gain_four, axis=0, keepdims=True)
    norms[2:3, :] = shift_three
    norms[3:4, :] = jnp.sum(shift_four, axis=0, keepdims=True)
    branch = r.low[...]
    ots = (r.ot.at[:QUAD], r.ot.at[QUAD:])
    mixed_gradients(branch, ots, outs, r.do, r.delta)
    packed, mark = r.out("pack1"), own_label(CROSS_BITS, 1 - core, place)
    r.out("unit")[...] = as_unit(nn(ots[0][...], branch))
    r.send("unit")
    pack(packed, mark, 3, as_unit(nn(ots[1][...], branch)))
    for g in range(2):
        r.turn[quad(g), :] = r.k[g].T
    r.dk[...] = jnp.zeros(r.dk.shape, F32)
    r.dv[...] = jnp.zeros(r.dv.shape, F32)

    def tile(block, g, key_at, keys_width, bias, add):
        backward_tile(
            g, slice(block * BLOCK, (block + 1) * BLOCK), key_at, keys_width, bias, masks, r.q.at[g], r.k.at[g],
            r.v.at[g], r.turn, r.do, r.lse.at[g], r.delta, r.dqt, r.dk, r.dv, r.prob.at[g], r.grad.at[g], add,
        )

    for block in range(blocks):
        for g in range(2):
            tile(block, g, spots[block], width, lambda piece: r.bias[block, piece, :], False)
    for block in range(blocks):

        def extra_back(i, carry, block=block):
            key_at = aligned(i * BLOCK)
            bias = bias_for(r.marks, key_at, BLOCK, query_rows[block])
            for g in range(2):
                tile(block, g, key_at, BLOCK, lambda piece: bias, True)
            return carry

        lax.fori_loop(*more[block], extra_back, 0)
    head_gradients(r)
    pack(packed, mark, 0, tn(x2_ref[...].astype(BF16), r.out("dq1")[...]))
    enc_turned = enc_ref[...].T
    pack(packed, mark, 1, nn(enc_turned, r.out("dk1")[...]))
    pack(packed, mark, 2, nn(enc_turned, r.out("dv1")[...]))
    r.send("pack1")
    r.dk[...] = sum(
        nt(r.out(f"{key}{g}")[...], r.get(f"ckv{g}")[i]) for i, key in enumerate(("dk", "dv")) for g in range(2)
    )
    r.out("denc_other")[...] = r.dk[pl.ds(second, own), :].astype(BF16)
    r.send("denc_other")
    r.out("denc_own")[...] = r.dk[pl.ds(first, own), :]


def head_gradients(r):
    for g in (1, 0):
        r.out(f"dq{g}")[...] = (r.dqt[quad(g), :] * SCALE).astype(BF16).T
        r.out(f"dk{g}")[...] = r.dk[:, quad(g)].astype(BF16)
        r.out(f"dv{g}")[...] = r.dv[:, quad(g)].astype(BF16)
        for key in ("dq", "dk", "dv"):
            r.send(f"{key}{g}")


def key_stream_gradient(r, weights, keys=("dk", "dv")):
    return sum(nt(r.get(f"{keys[i]}{g}")[...], weights[g][i]) for i in range(2) for g in range(2))


def cross_second_kernel(r):
    packed, mark = r.out("pack0"), own_label(CROSS_BITS, r.ids[0], r.ids[1])
    enc_turned = r.get("enc")[...].T
    pack(packed, mark, 1, nn(enc_turned, r.get("dk0")[...]))
    pack(packed, mark, 2, nn(enc_turned, r.get("dv0")[...]))
    pack(packed, mark, 0, tn(r.get("x2")[...].astype(BF16), r.get("dq0")[...]))
    pack(packed, mark, 3, r.get("unit")[...])
    r.send("pack0")
    r.out("g2")[...] = r.get("dz")[...] + sum(nt(r.get(f"dq{g}")[...], r.get(f"cq{g}")[...]) for g in range(2))


def feed_gradients(r, dy_ref, acc_ref, turned, packed, mark):
    h_ref, dh_ref, a_ref = r.get("h"), r.get("dh"), r.get("a")
    up_ref, down_ref = r.get("up"), r.get("down")
    chunks = [cols for j, cols in feed_chunks(h_ref.shape[1])]
    ahead = nt(dy_ref[...], down_ref[chunks[0], :])
    for j, cols in enumerate(chunks):
        active_grad = ahead
        if j + 1 < len(chunks):
            ahead = nt(dy_ref[...], down_ref[chunks[j + 1], :])
        for at in range(0, active_grad.shape[0], PIECE):
            piece = slice(at, at + PIECE)
            active, slope = gelu_both(h_ref[piece, cols].astype(F32))
            r.active[piece, :] = active.astype(BF16)
            r.hidden_grad[piece, :] = (active_grad[piece] * slope).astype(BF16)
        acc_ref[...] += nt(r.hidden_grad[...], up_ref[:, cols])
        up_grad = nn(turned[0], r.hidden_grad[...]) + nn(turned[1], dh_ref[:, cols])
        down_grad = nn(turned[2], r.active[...]) + nn(turned[3], a_ref[:, cols])
        for b in range(2):
            pack(packed, mark, 2 * j + b, up_grad[:, quad(b)])
            pack(packed, mark, 2 * j + b, down_grad[:, quad(b)], QUAD)


def feed_other_kernel(r):
    cot_ref, own_ref, recv_ref, z1_ref = r.get("cot"), r.get("denc_own"), r.get("denc_recv"), r.get("z1")
    dy_ref, acc_ref, turned = r.out("dy"), r.out("g0"), r.out("turned")
    gain, shift = norm_back(
        r,
        r.get("gain")[1:2, :],
        lambda rows: z1_ref[rows, :],
        lambda rows: cot_ref[rows, :].astype(F32) + own_ref[rows, :] + recv_ref[rows, :].astype(F32),
        (acc_ref, dy_ref),
    )
    r.out("norms")[0:1, :] = gain
    r.out("norms")[1:2, :] = shift
    r.send("dy")
    for i, ref in enumerate((r.get("x1_low"), r.get("x3_low"), dy_ref, r.get("dy3"))):
        turned[i] = ref[...].T
    r.send("turned")
    feed_gradients(r, dy_ref, acc_ref, turned, r.out("pack1"), own_label(FEED_BITS, 1 - r.ids[0], r.ids[1]))


def feed_own_kernel(r):
    dy_ref, acc_ref = r.get("dy"), r.out("g0")
    acc_ref[...] = r.get("dz")[...]
    turned = r.get("turned")
    feed_gradients(r, dy_ref, acc_ref, turned, r.out("pack0"), own_label(FEED_BITS, r.ids[0], r.ids[1]))


def norm_parts(norms, r):
    feed, dec, cross = r.get("feed_norms"), r.get("dec_norms"), r.get("cross_norms")
    rows = [(norms, 0), (feed, 0), (dec, 0), (cross, 0), (cross, 1)]
    rows += [(norms, 1), (feed, 1), (dec, 1), (cross, 2), (cross, 3)]
    return [ref[at : at + 1, :] for ref, at in rows]


def self_back_kernel(causal, norm_at, bits, r):
    core, place = r.ids[0], r.ids[1]
    z_ref, up_ref, x_ref, row_ref = r.get("z"), r.get("up"), r.get("x"), r.get("row")
    tokens, own = x_ref.shape[0], z_ref.shape[0]
    window = r.marks.shape[0]
    start, first = aligned(core * (tokens - window)), aligned(core * own)
    spread_marks(r.marks, row_ref[:, pl.ds(start, window)])
    spots = set_self_bias(r.bias, core, tokens, r.marks, row_ref, causal)
    norms = r.out("norms")
    gain, shift = norm_back(
        r,
        r.get("gain")[norm_at : norm_at + 1, :],
        lambda rows: z_ref[rows, :],
        lambda rows: up_ref[rows, :],
        (r.out("dz"), r.low),
    )
    norms[0:1, :] = gain
    norms[1:2, :] = shift
    r.send("dz")
    branch = r.low[...]
    ots = (r.get("ot0"), r.get("ot1"))
    mixed_gradients(branch, ots, (r.get("wo0"), r.get("wo1")), r.do, r.delta)
    packed, mark = r.out("pack1"), own_label(bits, 1 - core, place)
    r.out("unit")[...] = as_unit(nn(ots[0][...], branch))
    r.send("unit")
    pack(packed, mark, 3, as_unit(nn(ots[1][...], branch)))
    if not causal:
        pack_norms(packed, mark, norm_parts(norms, r))
    masks = head_masks()
    r.dk[...] = jnp.zeros(r.dk.shape, F32)
    r.dv[...] = jnp.zeros(r.dv.shape, F32)
    for g in range(2):
        r.kt[quad(g), :] = r.get(f"k{g}")[...].T
        for key in ("q", "v", "lse"):
            r.get(f"{key}{g}")
    for block, (key_at, width) in enumerate(spots):
        for g in range(2):
            backward_tile(
                g, slice(block * BLOCK, (block + 1) * BLOCK), key_at, width, lambda piece: r.bias[block, piece, :],
                masks, r.get(f"q{g}"), r.get(f"k{g}"), r.get(f"v{g}"), r.kt, r.do, r.get(f"lse{g}"), r.delta,
                r.dqt, r.dk, r.dv, r.prob.at[g], r.grad.at[g], False,
            )
    head_gradients(r)
    keys_turned = x_ref[pl.ds(start, window), :].T
    pack(packed, mark, 0, tn(x_ref[pl.ds(first, own), :], r.out("dq1")[...]))
    pack(packed, mark, 1, nn(keys_turned, r.out("dk1")[...]))
    pack(packed, mark, 2, nn(keys_turned, r.out("dv1")[...]))


def self_back_own_kernel(causal, bits, r):
    core, place = r.ids[0], r.ids[1]
    packed, mark = r.out("pack0"), own_label(bits, core, place)
    x_ref = r.get("x")
    own, window = r.get("dq0").shape[0], r.get("dk0").shape[0]
    keys_turned = x_ref[pl.ds(aligned(core * (x_ref.shape[0] - window)), window), :].T
    pack(packed, mark, 0, tn(x_ref[pl.ds(aligned(core * own), own), :], r.get("dq0")[...]))
    pack(packed, mark, 1, nn(keys_turned, r.get("dk0")[...]))
    pack(packed, mark, 2, nn(keys_turned, r.get("dv0")[...]))
    pack(packed, mark, 3, r.get("unit")[...])
    if not causal:
        pack_norms(packed, mark, norm_parts(r.get("norms"), r))


def stream_gradient_kernel(r):
    core = r.ids[0]
    dz_ref, own, window = r.get("dz"), r.get("dq0").shape[0], r.get("dk0").shape[0]
    w = (r.get("w0"), r.get("w1"))
    r.near[...] = key_stream_gradient(r, [(w[g][1], w[g][2]) for g in range(2)])
    r.out("halo")[...] = r.near[pl.ds(aligned((1 - core) * own), window - own), :].astype(BF16)
    r.send("halo")
    r.out("dx")[...] = (
        dz_ref[...]
        + sum(nt(r.get(f"dq{g}")[...], w[g][0]) for g in range(2))
        + r.near[pl.ds(aligned(core * (window - own)), own), :]
    )


class Refs:
    def __init__(self, smem, ins, outs, scratch, early):
        for name, ref in list(smem.items()) + list(scratch.items()):
            setattr(self, name, ref)
        self.ins, self.outs = ins, outs
        self.waited, self.sent = set(), set()
        self.early, self.late = list(ins)[:early], list(ins)[early:]
        for name in self.early:
            ins[name][0].start()

    def get(self, name):
        copy, ref = self.ins[name]
        if name not in self.waited:
            if name in self.late:
                self.start_late()
            self.waited.add(name)
            copy.wait()
            if all(key in self.waited for key in self.early):
                self.start_late()
        return ref

    def start_late(self):
        for name in self.late:
            self.ins[name][0].start()
        self.late = []

    def out(self, name):
        return self.outs[name][1]

    def send(self, name):
        self.sent.add(name)
        self.outs[name][0].start()

    def close(self):
        for name in self.ins:
            self.get(name)
        for name in self.outs:
            if name not in self.sent:
                self.send(name)
        for copy, ref in self.outs.values():
            copy.wait()


def call(kernel, name, smem, ins, outs, scratch, cost, early=3):
    n_smem, n_in, n_out, n_scratch = len(smem), len(ins), len(outs), len(scratch)

    def body(*refs):
        smem_refs = refs[:n_smem]
        refs = refs[n_smem:]
        in_refs, out_refs, refs = refs[:n_in], refs[n_in : n_in + n_out], refs[n_in + n_out :]
        in_vmem, out_vmem, refs = refs[:n_in], refs[n_in : n_in + n_out], refs[n_in + n_out :]
        in_sem, out_sem = refs[-2:]
        copies_in = {
            key: (pltpu.make_async_copy(in_refs[i], in_vmem[i], in_sem.at[i]), in_vmem[i])
            for i, key in enumerate(ins)
        }
        copies_out = {
            key: (pltpu.make_async_copy(out_vmem[i], out_refs[i], out_sem.at[i]), out_vmem[i])
            for i, key in enumerate(outs)
        }
        held = Refs(dict(zip(smem, smem_refs)), copies_in, copies_out, dict(zip(scratch, refs)), early)
        kernel(held)
        held.close()

    results = pl.pallas_call(
        body,
        out_shape=[jax.ShapeDtypeStruct(*out) for out in outs.values()],
        in_specs=[pl.BlockSpec(memory_space=pltpu.SMEM)] * n_smem + [pl.BlockSpec(memory_space=pl.ANY)] * n_in,
        out_specs=[pl.BlockSpec(memory_space=pl.ANY)] * n_out,
        scratch_shapes=[pltpu.VMEM(array.shape, array.dtype) for array in ins.values()]
        + [pltpu.VMEM(*out) for out in outs.values()]
        + [pltpu.VMEM(*one) for one in scratch.values()]
        + [pltpu.SemaphoreType.DMA((n_in,)), pltpu.SemaphoreType.DMA((n_out,))],
        compiler_params=pltpu.CompilerParams(vmem_limit_bytes=VMEM_LIMIT),
        cost_estimate=pl.CostEstimate(flops=cost * 10**9, transcendentals=0, bytes_accessed=cost * 10**6),
        name=name,
    )(*smem.values(), *ins.values())
    return SimpleNamespace(**dict(zip(outs, results)))


def finish_kernel(kind, bits, ids_ref, *refs):
    mark = own_label(bits, ids_ref[0], ids_ref[1])
    gathered, sem = refs[-2:]
    n_outs = {"enc": 4, "dec": 2, "cross": 3, "feed": 2}[kind]
    count = len(refs) - 2 - n_outs
    parts, outs = refs[:count], refs[count:-2]
    copies, at = [], 0
    for i, part in enumerate(parts):
        copies.append(pltpu.make_async_copy(part, gathered.at[pl.ds(at, part.shape[0])], sem.at[i]))
        at += part.shape[0]
    for copy in copies:
        copy.start()
    for copy in copies:
        copy.wait()
    for shard in range(SHARDS):
        unit, half = divmod(shard, 2)
        rows = slice(half * QUAD, (half + 1) * QUAD)
        where = pl.ds(mark ^ shard, 1)
        value = gathered[where, :QUAD, :][0].astype(F32)
        if kind == "feed":
            outs[0][rows, quad(unit)] = value
            outs[1][quad(unit), rows] = gathered[where, QUAD:, :][0].T.astype(F32)
        elif unit == 3:
            outs[2 if kind == "cross" else 1][:, quad(half)] = value
        elif kind != "cross":
            outs[0][unit, rows, :] = value
        elif unit == 0:
            outs[0][rows, :] = value
        else:
            outs[1][unit - 1, rows, :] = value
        if kind == "enc":
            norms = gathered[where, QUAD:, :][0].astype(F32)
            many = norm_rows(SHARDS)
            for i in range(many):
                row, side = divmod(shard * many + i, 2)
                if row < 10:
                    outs[2 + row // 5][row % 5 : row % 5 + 1, quad(side)] = norms[i : i + 1, :]


def finish(group, ids, outs):
    parts = group.parts
    shape = (SHARDS,) + parts[0].shape[1:]
    return pl.pallas_call(
        functools.partial(finish_kernel, group.kind, group.bits),
        out_shape=[jax.ShapeDtypeStruct(*out) for out in outs],
        in_specs=[pl.BlockSpec(memory_space=pltpu.SMEM)] + [pl.BlockSpec(memory_space=pl.ANY)] * len(parts),
        out_specs=[pl.BlockSpec(memory_space=pltpu.VMEM)] * len(outs),
        scratch_shapes=[pltpu.VMEM(shape, BF16), pltpu.SemaphoreType.DMA((len(parts),))],
        compiler_params=pltpu.CompilerParams(vmem_limit_bytes=VMEM_LIMIT),
        cost_estimate=pl.CostEstimate(flops=2 * 10**9, transcendentals=0, bytes_accessed=2 * 10**6),
        name="finish_" + group.kind,
    )(ids, *parts)


class Sum:
    def __init__(self, kind, bits, dp, mp):
        self.kind, self.bits, self.dp, self.mp = kind, bits, dp, mp

    def hop(self, array, step):
        pairs = []
        for place in range(self.dp):
            for core in range(self.mp):
                bit = self.bits[core][step] if step < 4 else step
                pairs.append((place * self.mp + core, (place ^ (1 << bit)) * self.mp + core))
        return lax.ppermute(array, ("dp", "mp"), pairs)

    def swap(self, other):
        self.sent = lax.ppermute(other, "mp", [(0, 1), (1, 0)])

    def halve(self, mine=None):
        mine = self.keep if mine is None else mine
        half = mine.shape[0] // 2
        return [mine[half:] + self.sent[half:], mine[:half] + self.sent[:half]]

    def send_half(self, give, keep, step):
        self.keep = keep
        self.sent = self.hop(give, step)

    def last_sum(self):
        return self.keep + self.sent

    def exchange(self, part):
        step = 3
        while 2 << step < self.dp:
            part = part + self.hop(part, step)
            step += 1
        self.keep, self.sent = part, self.hop(part, step)

    def double(self, step, parts=None):
        self.parts = self.parts + [self.hop(part, step) for part in parts or [self.joined()]]

    def joined(self):
        return jnp.concatenate(self.parts) if len(self.parts) > 1 else self.parts[0]


def together(*values):
    return lax.optimization_barrier(values)


def on_device(
    src_embed, tgt_embed, src_segment, tgt_segment, enc_qkv, enc_out_proj, dec_qkv, dec_out_proj, cross_query,
    cross_kv, cross_out_proj, ffn_up, ffn_down, norm_gain, norm_bias, enc_cotangent, dec_cotangent,
):
    dp, mp = lax.axis_size("dp"), lax.axis_size("mp")
    tokens, model = src_embed.shape
    own = tokens // mp
    window = own + MOST
    half = ffn_up.shape[1]
    hidden = 2 * half
    position = lax.axis_index("mp")
    ids = jnp.stack([position, lax.axis_index("dp")]).astype(jnp.int32)
    pairs = [(0, 1), (1, 0)]

    def swap(tree):
        return jax.tree.map(lambda a: lax.ppermute(a, "mp", pairs), tree)

    enc_w1, enc_o1 = swap((enc_qkv, enc_out_proj))
    up1, down1 = swap((ffn_up, ffn_down))
    dec_w1, dec_o1 = swap((dec_qkv, dec_out_proj))
    cross_q1, cross_kv1, cross_o1 = swap((cross_query, cross_kv, cross_out_proj))
    feed = {"up0": ffn_up, "up1": up1, "down0": ffn_down, "down1": down1}

    def rows(count, dtype):
        return ((count, model), dtype)

    blocks = own // BLOCK
    q_shape, k_shape, ot_shape, lse_shape = ((own, QUAD), BF16), ((window, QUAD), BF16), ((QUAD, own), BF16), ((4, own), F32)
    vt_shape, marks, bias = ((QUAD, window), BF16), ((window, BLOCK), jnp.int32), ((blocks, 3 * BLOCK, BLOCK), F32)
    weights = ((2, 3 * BLOCK, 4 * BLOCK), BF16)
    heads = {"q": q_shape, "k": k_shape, "v": k_shape, "ot": ot_shape, "lse": lse_shape}
    wide = ((own, half), BF16)
    norm_in = {"gain": norm_gain, "shift": norm_bias}
    first = call(
        own_heads_kernel, "own_heads", {"ids": ids},
        {"src_row": src_segment, "src": src_embed, "src_w": enc_qkv,
         "tgt_row": tgt_segment, "tgt": tgt_embed, "tgt_w": dec_qkv},
        {f"{side}_{key}": shape for side in ("src", "tgt") for key, shape in heads.items()},
        {"marks": marks, "src_bias": bias, "tgt_bias": bias, "src_vt": vt_shape, "tgt_vt": vt_shape, "weights": weights},
        cost=8,
    )
    encoder = call(
        encoder_kernel, "encoder_forward", {"ids": ids},
        {"row": src_segment, "x": src_embed, "w": enc_w1, "ot0": first.src_ot, "wo0": enc_out_proj, "wo1": enc_o1,
         **norm_in, "up0": ffn_up, "down0": ffn_down, "up1": up1, "down1": down1},
        {**heads, "z0": rows(own, F32), "x1_low": rows(own, BF16), "h0": wide, "h1": wide,
         "z1": rows(own, F32), "enc": rows(own, BF16)},
        {"marks": marks, "bias": bias, "vt": vt_shape, "x1": rows(own, F32), "acc": rows(own, F32), "weights": weights,
         "a": ((2, own, half), BF16)},
        cost=12,
    )
    enc_swapped = swap(encoder.enc)
    decoder = call(
        decoder_kernel, "decoder_self_forward", {"ids": ids},
        {"row": tgt_segment, "x": tgt_embed, "w": dec_w1, "ot0": first.tgt_ot, "wo0": dec_out_proj, "wo1": dec_o1,
         **norm_in},
        {**heads, "z2": rows(own, F32), "x2": rows(own, F32)},
        {"marks": marks, "bias": bias, "vt": vt_shape, "acc": rows(own, F32), "weights": weights}, cost=6,
    )
    packed = ((SHARDS, QUAD, QUAD), BF16)
    packed_feed = ((SHARDS, 2 * QUAD, QUAD), BF16)
    packed_norms = ((SHARDS, QUAD + TILE, QUAD), BF16)
    unit = ((2 * QUAD, QUAD), BF16)
    cross_key = ((tokens, QUAD), BF16)
    crossed = call(
        cross_kernel, "cross_and_decoder_feed",
        {"ids": ids, "src_marks": src_segment, "tgt_marks": tgt_segment},
        {"src_row": src_segment, "tgt_row": tgt_segment, "enc_own": encoder.enc, "enc_other": enc_swapped,
         "x2": decoder.x2, "cq0": cross_query, "ckv0": cross_kv, "cq1": cross_q1, "ckv1": cross_kv1,
         "co0": cross_out_proj, "co1": cross_o1, **norm_in, **feed, "cot": dec_cotangent},
        {"enc": rows(tokens, BF16), "x3_low": rows(own, BF16), "a0": wide, "a1": wide, "dec": rows(own, BF16),
         "dy": rows(own, BF16), "dh0": wide, "dh1": wide, "norms": rows(4, F32), "pack1": packed, "unit": unit,
         "dz": rows(own, F32), "dq0": q_shape, "dq1": q_shape, "dk0": cross_key, "dk1": cross_key, "dv0": cross_key,
         "dv1": cross_key, "denc_other": rows(own, BF16), "denc_own": rows(own, F32)},
        {"marks": ((tokens, BLOCK), jnp.int32), "bias": bias, "q": ((2, own, QUAD), BF16),
         "k": ((2, tokens, QUAD), BF16), "v": ((2, tokens, QUAD), BF16), "turn": ((model, tokens), BF16),
         "mix": ((model, own), F32), "tops": ((8, own), F32), "totals": ((8, own), F32), "lse": ((2, 4, own), F32),
         "ot": ((model, own), BF16), "acc": rows(own, F32), "x3": rows(own, F32), "z3": rows(own, F32),
         "z4": rows(own, F32), "h": ((2, own, half), F32), "low": rows(own, BF16), "do": rows(own, BF16),
         "delta": ((8, own), F32), "dqt": ((model, own), F32), "dk": rows(tokens, F32), "dv": rows(tokens, F32), "prob": weights,
         "grad": weights},
        cost=28, early=6,
    )
    cross_sum = Sum("cross", CROSS_BITS, dp, mp)
    dec_sum = Sum("dec", DEC_BITS, dp, mp)
    feed_sum = Sum("feed", FEED_BITS, dp, mp)
    enc_sum = Sum("enc", ENC_BITS, dp, mp)
    cross_sum.swap(crossed.pack1)
    denc_recv = swap(crossed.denc_other)
    crossed_more = call(
        cross_second_kernel, "cross_second", {"ids": ids},
        {"enc": crossed.enc, "dk0": crossed.dk0, "dv0": crossed.dv0, "x2": decoder.x2, "dq0": crossed.dq0,
         "unit": crossed.unit, "dz": crossed.dz, "dq1": crossed.dq1, "cq0": cross_query, "cq1": cross_q1},
        {"pack0": packed, "g2": rows(own, F32)}, {}, cost=4,
    )

    def self_backward(causal, at, bits, name, side, x, row, z, up, w0, w1, o0, o1, others, pack_shape, more):
        ins = {"z": z, "up": up, "gain": norm_gain, "row": row, "x": x}
        ins |= {"ot0": getattr(first, side + "_ot"), "ot1": others.ot, "wo0": o0, "wo1": o1}
        for key in ("k", "q", "v", "lse"):
            ins |= {key + "0": getattr(first, f"{side}_{key}"), key + "1": getattr(others, key)}
        return call(
            functools.partial(self_back_kernel, causal, at, bits), name, {"ids": ids}, ins | more,
            {"dz": rows(own, F32), "pack1": pack_shape, "unit": unit, "norms": rows(2, F32), "dq0": q_shape,
             "dq1": q_shape, "dk0": k_shape, "dk1": k_shape, "dv0": k_shape, "dv1": k_shape},
            {"marks": marks, "bias": bias, "low": rows(own, BF16), "do": rows(own, BF16), "delta": ((8, own), F32),
             "kt": ((model, window), BF16), "dqt": ((model, own), F32), "dk": rows(window, F32), "dv": rows(window, F32),
             "prob": weights, "grad": weights},
            cost=11,
        )

    def self_backward_own(causal, bits, name, x, back, gate, pack_shape, more):
        return call(
            functools.partial(self_back_own_kernel, causal, bits), name, {"ids": ids},
            {"x": x, "dq0": back.dq0, "dk0": back.dk0, "dv0": back.dv0, "unit": gate} | more,
            {"pack0": pack_shape}, {}, cost=3,
        ).pack0

    def stream_gradient(name, back, w0, w1, gate):
        ins = {"dz": gate, "w0": w0, "w1": w1}
        ins |= {f"{key}{g}": getattr(back, f"{key}{g}") for key in ("dk", "dv", "dq") for g in range(2)}
        return call(
            stream_gradient_kernel, name, {"ids": ids}, ins,
            {"halo": rows(window - own, BF16), "dx": rows(own, F32)}, {"near": rows(window, F32)}, cost=3,
        )

    square, out_half, triple = ((model, QUAD), F32), ((QUAD, model), F32), ((3, model, QUAD), F32)
    out_shapes = {
        "cross": [square, ((2, model, QUAD), F32), out_half],
        "dec": [triple, out_half],
        "feed": [((model, half), F32), rows(half, F32)],
        "enc": [triple, out_half, rows(5, F32), rows(5, F32)],
    }
    gate, give, keep, denc_recv = together(encoder.z1, *cross_sum.halve(crossed_more.pack0), denc_recv)
    cross_sum.send_half(give, keep, 0)
    feed_scratch = {"active": ((own, FEED), BF16), "hidden_grad": ((own, FEED), BF16)}
    fed = call(
        feed_other_kernel, "encoder_feed_other", {"ids": ids},
        {"cot": enc_cotangent, "denc_own": crossed.denc_own, "denc_recv": denc_recv, "z1": gate,
         "gain": norm_gain, "x1_low": encoder.x1_low, "x3_low": crossed.x3_low, "dy3": crossed.dy, "down": down1,
         "h": encoder.h1, "up": up1, "dh": crossed.dh1, "a": crossed.a1},
        {"dy": rows(own, BF16), "norms": rows(2, F32), "turned": ((4, model, own), BF16), "pack1": packed_feed,
         "g0": rows(own, F32)},
        feed_scratch, cost=10, early=5,
    )
    gate, give, keep, other = together(fed.dy, *cross_sum.halve(), fed.pack1)
    cross_sum.send_half(give, keep, 1)
    feed_sum.swap(other)
    fed_own = call(
        feed_own_kernel, "encoder_feed_own", {"ids": ids},
        {"dy": gate, "down": ffn_down, "h": encoder.h0, "dz": fed.g0, "turned": fed.turned, "up": ffn_up,
         "dh": crossed.dh0, "a": crossed.a0},
        {"g0": rows(own, F32), "pack0": packed_feed}, feed_scratch, cost=9,
    )
    gate, give, keep, feed_give, feed_keep = together(
        crossed_more.g2, *cross_sum.halve(), *feed_sum.halve(fed_own.pack0)
    )
    feed_sum.send_half(feed_give, feed_keep, 0)
    cross_sum.send_half(give, keep, 2)
    dec_back = self_backward(
        True, 2, DEC_BITS, "decoder_self_backward", "tgt", tgt_embed, tgt_segment, decoder.z2, gate,
        dec_qkv, dec_w1, dec_out_proj, dec_o1, decoder, packed, {},
    )
    gate, part, other = together(dec_back.unit, cross_sum.last_sum(), dec_back.pack1)
    cross_sum.exchange(part)
    dec_sum.swap(other)
    dec_pack = self_backward_own(True, DEC_BITS, "decoder_self_own", tgt_embed, dec_back, gate, packed, {})
    gate, cross_part, give, keep, dec_give, dec_keep = together(
        fed_own.g0, cross_sum.last_sum(), *feed_sum.halve(), *dec_sum.halve(dec_pack)
    )
    feed_sum.send_half(give, keep, 1)
    dec_sum.send_half(dec_give, dec_keep, 0)
    cross_sum.parts = [cross_part]
    cross_sum.double(2)
    norms_before = {"feed_norms": fed.norms, "dec_norms": dec_back.norms, "cross_norms": crossed.norms}
    enc_back = self_backward(
        False, 0, ENC_BITS, "encoder_self_backward", "src", src_embed, src_segment, encoder.z0, gate,
        enc_qkv, enc_w1, enc_out_proj, enc_o1, encoder, packed_norms, norms_before,
    )
    gate, other, give, keep, dec_give, dec_keep, *cross_sum.parts = together(
        enc_back.unit, enc_back.pack1, *feed_sum.halve(), *dec_sum.halve(), *cross_sum.parts
    )
    dec_sum.send_half(dec_give, dec_keep, 1)
    feed_sum.send_half(give, keep, 2)
    cross_sum.double(1)
    enc_sum.swap(other)
    enc_pack = self_backward_own(
        False, ENC_BITS, "encoder_self_own", src_embed, enc_back, gate, packed_norms,
        {"norms": enc_back.norms, **norms_before},
    )
    gate, enc_give, enc_keep, part, dec_give, dec_keep, *cross_sum.parts = together(
        enc_back.dz, *enc_sum.halve(enc_pack), feed_sum.last_sum(), *dec_sum.halve(), *cross_sum.parts
    )
    enc_sum.send_half(enc_give, enc_keep, 0)
    feed_sum.exchange(part)
    dec_sum.send_half(dec_give, dec_keep, 2)
    cross_sum.double(0)
    src_side = stream_gradient("src_gradient", enc_back, enc_qkv, enc_w1, gate)
    gate, src_halo, dec_own, enc_give, enc_keep, feed_part, dec_part = together(
        dec_back.dz, src_side.halo, crossed.dec, *enc_sum.halve(), feed_sum.last_sum(), dec_sum.last_sum()
    )
    enc_sum.send_half(enc_give, enc_keep, 1)
    feed_sum.parts = [feed_part]
    feed_sum.double(2)
    dec_sum.exchange(dec_part)
    src_recv = swap(src_halo)
    dec_swapped = swap(dec_own)
    tgt_side = stream_gradient("tgt_gradient", dec_back, dec_qkv, dec_w1, gate)
    tgt_halo, enc_give, enc_keep, dec_part, feed_zero, feed_one, *cross_sum.parts = together(
        tgt_side.halo, *enc_sum.halve(), dec_sum.last_sum(), *feed_sum.parts, *cross_sum.parts
    )
    enc_sum.send_half(enc_give, enc_keep, 2)
    feed_sum.parts = [feed_zero, feed_one]
    feed_sum.double(1)
    dec_sum.parts = [dec_part]
    dec_sum.double(2)
    tgt_recv = swap(tgt_halo)
    cross_out = finish(cross_sum, ids, out_shapes["cross"])
    enc_part, *parts = together(enc_sum.last_sum(), *dec_sum.parts, *feed_sum.parts)
    dec_sum.parts, feed_sum.parts = parts[:2], parts[2:]
    enc_sum.exchange(enc_part)
    feed_sum.double(0)
    dec_sum.double(1)
    enc_part, *dec_sum.parts = together(enc_sum.last_sum(), *dec_sum.parts)
    enc_sum.parts = [enc_part]
    enc_sum.double(2)
    dec_sum.double(0)
    enc_sum.double(1)
    enc_sum.double(0)
    feed_out = finish(feed_sum, ids, out_shapes["feed"])
    dec_out = finish(dec_sum, ids, out_shapes["dec"])
    enc_out = finish(enc_sum, ids, out_shapes["enc"])

    def whole(mine, received):
        return jnp.where(
            position == 0, jnp.concatenate([mine, received]), jnp.concatenate([received, mine])
        )

    halo_at = (1 - position) * (own - (window - own))

    def with_halo(grad, received):
        part = lax.dynamic_slice_in_dim(grad, halo_at, window - own, 0) + received.astype(F32)
        return lax.dynamic_update_slice_in_dim(grad, part, halo_at, 0)

    return (
        crossed.enc,
        whole(crossed.dec, dec_swapped),
        with_halo(src_side.dx, src_recv),
        with_halo(tgt_side.dx, tgt_recv),
        enc_out[0],
        enc_out[1],
        dec_out[0],
        dec_out[1],
        cross_out[0],
        cross_out[1],
        cross_out[2],
        feed_out[0],
        feed_out[1],
        enc_out[2],
        enc_out[3],
    )


def solution(mesh):
    in_specs = (
        P("dp", None), P("dp", None), P("dp", None), P("dp", None),
        P(None, None, "mp"), P("mp", None), P(None, None, "mp"), P("mp", None),
        P(None, "mp"), P(None, None, "mp"), P("mp", None), P(None, "mp"), P("mp", None),
        P(), P(), P(("dp", "mp"), None), P(("dp", "mp"), None),
    )
    out_specs = (
        P("dp", None), P("dp", None), P(("dp", "mp"), None), P(("dp", "mp"), None),
        P(None, None, "mp"), P("mp", None), P(None, None, "mp"), P("mp", None),
        P(None, "mp"), P(None, None, "mp"), P("mp", None), P(None, "mp"), P("mp", None),
        P(), P(),
    )
    return jax.shard_map(on_device, mesh=mesh, in_specs=in_specs, out_specs=out_specs, check_vma=False)
```

```python
import functools
import math
from types import SimpleNamespace

import jax
import jax.numpy as jnp
from jax import lax
from jax.experimental import pallas as pl
from jax.experimental.pallas import tpu as pltpu
from jax.sharding import PartitionSpec as P

HDIM = 64
SCALE = HDIM ** (-0.5)
EPSILON = 1e-05
MASKED = -1e30
BLOCK = 128
MOST = 128
QUAD = 4 * HDIM
UNITS = 4
TILE = 16
FEED = 512
SHARDS = 8
CROSS_BITS = ((0, 1, 2, 3), (1, 0, 2, 3))
FEED_BITS = ((0, 1, 2, 3), (1, 0, 2, 3))
DEC_BITS = ((1, 0, 2, 3), (0, 1, 2, 3))
ENC_BITS = ((1, 0, 2, 3), (0, 1, 2, 3))
F32 = jnp.float32
BF16 = jnp.bfloat16
VMEM_LIMIT = 56 * 1024 * 1024
GELU_IN = math.sqrt(2.0 / math.pi)
GELU_CUBE = 0.044715


def nn(left, right):
    return jnp.dot(left, right, preferred_element_type=F32)


def nt(left, right):
    return lax.dot_general(left, right, (((1,), (1,)), ((), ())), preferred_element_type=F32)


def tn(left, right):
    return lax.dot_general(left, right, (((0,), (0,)), ((), ())), preferred_element_type=F32)


def aligned(index, size=BLOCK):
    return pl.multiple_of(index, size)


def over_rows(rows, chunk, body, carry, unroll=4):
    return lax.fori_loop(
        0,
        rows // chunk,
        lambda i, kept: body(pl.ds(aligned(i * chunk, chunk), chunk), kept),
        carry,
        unroll=min(unroll, rows // chunk),
    )


def normalize(before):
    centered = before - jnp.mean(before, axis=-1, keepdims=True)
    variance = jnp.mean(centered * centered, axis=-1, keepdims=True)
    rate = lax.rsqrt(variance + EPSILON)
    return centered * rate, rate


def norm_backward(before, upstream, gain_row):
    normed, rate = normalize(before)
    scaled = upstream * gain_row
    first = jnp.mean(scaled, axis=-1, keepdims=True)
    second = jnp.mean(scaled * normed, axis=-1, keepdims=True)
    return rate * (scaled - first - normed * second), upstream * normed


def fold_rows(block):
    return jnp.sum(block.reshape(block.shape[0] // 8, 8, block.shape[1]), axis=0)


def gelu(hidden):
    inner = GELU_IN * hidden * (1.0 + GELU_CUBE * hidden * hidden)
    return 0.5 * hidden * (1.0 + jnp.tanh(inner))


def gelu_both(hidden):
    square = hidden * hidden
    bent = jnp.tanh(GELU_IN * hidden * (1.0 + GELU_CUBE * square))
    half = 0.5 * (1.0 + bent)
    slope = half + 0.5 * hidden * (1.0 - bent * bent) * (GELU_IN * (1.0 + 3.0 * GELU_CUBE * square))
    return hidden * half, slope


def head_masks():
    lane = lax.broadcasted_iota(jnp.int32, (1, QUAD), 1)
    return [
        jnp.where((lane >= h * HDIM) & (lane < (h + 1) * HDIM), 1.0, 0.0).astype(BF16)
        for h in range(4)
    ]


def stack_heads(block, masks):
    return jnp.concatenate([block * mask for mask in masks], axis=0)


def quad(g):
    return slice(g * QUAD, (g + 1) * QUAD)


def bias_for(marks_ref, key_at, width, query_row, causal=False, key_start=0, query_start=0):
    allowed = marks_ref[pl.ds(key_at, width), :] == query_row
    if causal:
        places = key_start + lax.broadcasted_iota(jnp.int32, (width, BLOCK), 0)
        queries = query_start + lax.broadcasted_iota(jnp.int32, (width, BLOCK), 1)
        allowed = allowed & (places <= queries)
    return jnp.where(allowed, 0.0, MASKED)


def self_window(core, block, causal):
    middle = block + core
    if causal:
        return aligned(jnp.maximum(middle - 1, 0) * BLOCK), 2 * BLOCK
    return aligned(jnp.clip(middle - 1, 0, 2) * BLOCK), 3 * BLOCK


def set_self_bias(bias_ref, core, tokens, marks_ref, row_ref, causal):
    window, own = marks_ref.shape[0], row_ref.shape[1] // 2
    start = core * (tokens - window)
    spots = []
    for block in range(own // BLOCK):
        key_at, width = self_window(core, block, causal)
        first = aligned(core * own + block * BLOCK)
        bias_ref[block, :width, :] = bias_for(
            marks_ref, key_at, width, row_ref[:, pl.ds(first, BLOCK)], causal, start + key_at, first
        )
        spots.append((key_at, width))
    return spots


def soft_weights(scores, h, bias, top=None):
    one = scores[:, h * BLOCK : (h + 1) * BLOCK] + bias
    high = jnp.max(one, axis=0, keepdims=True)
    top = high if top is None else jnp.maximum(top, high)
    weights = jnp.exp(one - top)
    return top, jnp.sum(weights, axis=0, keepdims=True), weights.astype(BF16)


def quad_forward(spots, q_ref, k_ref, vt_ref, bias_ref, ot_ref, lse_ref, masks):
    def score(block):
        rows, (key_at, width) = slice(block * BLOCK, (block + 1) * BLOCK), spots[block]
        return nt(k_ref[pl.ds(key_at, width), :], stack_heads(q_ref[rows, :], masks))

    ahead = score(0)
    for block, (key_at, width) in enumerate(spots):
        rows = slice(block * BLOCK, (block + 1) * BLOCK)
        scores, ahead = ahead, score(block + 1) if block + 1 < len(spots) else None
        for h in range(4):
            top, total, weights = soft_weights(scores, h, bias_ref[block, :width, :])
            features = slice(h * HDIM, (h + 1) * HDIM)
            mixed = nn(vt_ref[features, pl.ds(key_at, width)], weights)
            ot_ref[features, rows] = (mixed * (1.0 / total)).astype(BF16)
            lse_ref[h : h + 1, rows] = top + jnp.log(total)


def backward_scores(g, rows, key_at, width, masks, q_ref, k_ref, v_ref, do_ref):
    keys = pl.ds(key_at, width)
    q_stack = stack_heads(q_ref[rows, :], masks)
    do_stack = stack_heads(do_ref[rows, quad(g)], masks)
    return q_stack, do_stack, nt(k_ref[keys, :], q_stack), nt(v_ref[keys, :], do_stack)


def backward_sums(g, rows, key_at, bias, scored, kt_ref, lse_ref, delta_ref, dqt_ref, dk_ref, dv_ref, add):
    q_stack, do_stack, scores, prob_grads = scored
    keys = pl.ds(key_at, bias.shape[0])
    probs, score_grads = [], []
    for h in range(4):
        cols = slice(h * BLOCK, (h + 1) * BLOCK)
        head = g * 4 + h
        prob = jnp.exp(scores[:, cols] + bias - lse_ref[h : h + 1, rows])
        score_grad = (prob * (prob_grads[:, cols] - delta_ref[head : head + 1, rows])).astype(BF16)
        probs.append(prob.astype(BF16))
        score_grads.append(score_grad)
    for h in range(4):
        features = slice((g * 4 + h) * HDIM, (g * 4 + h + 1) * HDIM)
        query_grad = nn(kt_ref[features, keys], score_grads[h])
        if add:
            dqt_ref[features, rows] += query_grad
        else:
            dqt_ref[features, rows] = query_grad
    dv_ref[keys, quad(g)] += nn(jnp.concatenate(probs, axis=1), do_stack)
    dk_ref[keys, quad(g)] += nn(jnp.concatenate(score_grads, axis=1), q_stack)


def mixed_gradients(branch, ot_refs, w_out, do_ref, delta_ref):
    for g in range(2):
        do_ref[:, quad(g)] = nt(branch, w_out[g][...]).astype(BF16)
        turned = nt(w_out[g][...], branch).astype(BF16).astype(F32)
        product = turned * ot_refs[g][...].astype(F32)
        for h in range(4):
            delta_ref[g * 4 + h : g * 4 + h + 1, :] = jnp.sum(
                product[h * HDIM : (h + 1) * HDIM, :], axis=0, keepdims=True
            )


def spread_marks(marks_ref, row):
    marks_ref[...] = jnp.broadcast_to(row, (marks_ref.shape[1], marks_ref.shape[0])).T


def label(bits, place):
    first, second, third = [(place >> bit) & 1 for bit in bits[:3]]
    return 4 * first + 2 * second + third


def own_label(bits, core, place):
    return jnp.where(core == 0, label(bits[0], place), label(bits[1], place))


def pack(out_ref, mark, unit, value, at=0):
    rows = value.shape[0] // 2
    for half in range(2):
        where = pl.ds(mark ^ (2 * unit + half), 1)
        out_ref[where, at : at + rows, :] = value[half * rows : (half + 1) * rows].astype(BF16)[None]


def as_unit(value):
    return jnp.concatenate([value[:, :QUAD], value[:, QUAD:]], axis=0).astype(BF16)


def pack_norms(out_ref, mark, parts):
    shards, tall, width = out_ref.shape
    halves = [part[:, half * width : (half + 1) * width] for part in parts for half in range(2)]
    each = norm_rows(shards)
    blank = jnp.zeros((1, width), F32)
    halves += [blank] * (shards * each - len(halves))
    for i in range(shards):
        block = jnp.concatenate(halves[i * each : (i + 1) * each] + [blank] * (TILE - each), axis=0)
        out_ref[pl.ds(mark ^ i, 1), tall - TILE :, :] = block.astype(BF16)[None]


def norm_rows(shards):
    return -(-20 // shards)


def prepare_quad(x_ref, w_ref, core, q_ref, k_ref, v_ref, vt_ref):
    tokens, own, window = x_ref.shape[0], q_ref.shape[0], k_ref.shape[0]
    keys = x_ref[pl.ds(aligned(core * (tokens - window)), window), :]
    q_ref[...] = (nn(x_ref[pl.ds(aligned(core * own), own), :], w_ref[0]) * SCALE).astype(BF16)
    k_ref[...] = nn(keys, w_ref[1]).astype(BF16)
    v_ref[...] = nn(keys, w_ref[2]).astype(BF16)
    vt_ref[...] = v_ref[...].T


def own_heads_kernel(r):
    core = r.ids[0]
    masks = head_masks()
    for side, causal in (("src", False), ("tgt", True)):
        x_ref, row_ref = r.get(side), r.get(side + "_row")
        k_ref = r.out(side + "_k")
        start = aligned(core * (x_ref.shape[0] - k_ref.shape[0]))
        spread_marks(r.marks, row_ref[:, pl.ds(start, k_ref.shape[0])])
        bias_ref, vt_ref = getattr(r, side + "_bias"), getattr(r, side + "_vt")
        spots = set_self_bias(bias_ref, core, x_ref.shape[0], r.marks, row_ref, causal)
        q_ref, v_ref = r.out(side + "_q"), r.out(side + "_v")
        prepare_quad(x_ref, r.get(side + "_w"), core, q_ref, k_ref, v_ref, vt_ref)
        for key in ("_q", "_k", "_v"):
            r.send(side + key)
        quad_forward(
            spots, q_ref, k_ref, vt_ref, bias_ref, r.out(side + "_ot"), r.out(side + "_lse"), masks
        )
        r.send(side + "_ot")
        r.send(side + "_lse")


def other_heads(r, causal):
    core = r.ids[0]
    x_ref, row_ref, k_ref = r.get("x"), r.get("row"), r.out("k")
    start = aligned(core * (x_ref.shape[0] - k_ref.shape[0]))
    spread_marks(r.marks, row_ref[:, pl.ds(start, k_ref.shape[0])])
    spots = set_self_bias(r.bias, core, x_ref.shape[0], r.marks, row_ref, causal)
    q_ref, v_ref, ot_ref = r.out("q"), r.out("v"), r.out("ot")
    prepare_quad(x_ref, r.get("w"), core, q_ref, k_ref, v_ref, r.vt)
    for key in ("q", "k", "v"):
        r.send(key)
    quad_forward(spots, q_ref, k_ref, r.vt, r.bias, ot_ref, r.out("lse"), head_masks())
    r.send("lse")
    r.send("ot")
    r.acc[...] = tn(r.get("ot0")[...], r.get("wo0")[...]) + tn(ot_ref[...], r.get("wo1")[...])


def norm_forward(r, at, residual, before_ref, after_ref, low_ref):
    gain, shift = r.get("gain")[at : at + 1, :], r.get("shift")[at : at + 1, :]

    def body(rows, carry):
        before = residual(rows) + r.acc[rows, :]
        if before_ref is not None:
            before_ref[rows, :] = before
        after = normalize(before)[0] * gain + shift
        if after_ref is not None:
            after_ref[rows, :] = after
        if low_ref is not None:
            low_ref[rows, :] = after.astype(BF16)
        return carry

    over_rows(r.acc.shape[0], 32, body, 0)


def own_row_reader(x_ref, core, own):
    first = core * own
    return lambda rows: x_ref[pl.ds(aligned(first + rows.start, rows.size), rows.size), :].astype(F32)


def encoder_kernel(r):
    other_heads(r, False)
    x1_low = r.out("x1_low")
    norm_forward(r, 0, own_row_reader(r.get("x"), r.ids[0], r.acc.shape[0]), r.out("z0"), r.x1, x1_low)
    r.send("z0")
    r.send("x1_low")
    feed_forward(x1_low, *feed_weights(r), (r.out("h0"), r.out("h1")), None, r.acc)
    r.send("h0")
    r.send("h1")
    norm_forward(r, 1, lambda rows: r.x1[rows, :], r.out("z1"), None, r.out("enc"))


def decoder_kernel(r):
    other_heads(r, True)
    norm_forward(r, 2, own_row_reader(r.get("x"), r.ids[0], r.acc.shape[0]), r.out("z2"), r.out("x2"), None)


def feed_weights(r):
    return (r.get("up0"), r.get("up1")), (r.get("down0"), r.get("down1"))


def feed_chunks(half):
    return [(j, slice(j * FEED, (j + 1) * FEED)) for j in range(half // FEED)]


def feed_forward(low_ref, ups, downs, h_refs, a_refs, acc_ref):
    chunks = [(g, cols) for g in range(2) for j, cols in feed_chunks(ups[0].shape[1])]
    ahead = nn(low_ref[...], ups[0][:, chunks[0][1]])
    for i, (g, cols) in enumerate(chunks):
        hidden = ahead
        if i + 1 < len(chunks):
            ahead = nn(low_ref[...], ups[chunks[i + 1][0]][:, chunks[i + 1][1]])
        h_refs[g][:, cols] = hidden.astype(h_refs[g].dtype)
        active = gelu(hidden).astype(BF16)
        if a_refs is not None:
            a_refs[g][:, cols] = active
        term = nn(active, downs[g][cols, :])
        if i == 0:
            acc_ref[...] = term
        else:
            acc_ref[...] += term


def feed_backward(dy_ref, ups, downs, h_refs, dh_refs, acc_ref):
    chunks = [(g, cols) for g in range(2) for j, cols in feed_chunks(ups[0].shape[1])]
    ahead = nt(dy_ref[...], downs[0][chunks[0][1], :])
    for i, (g, cols) in enumerate(chunks):
        active_grad = ahead
        if i + 1 < len(chunks):
            ahead = nt(dy_ref[...], downs[chunks[i + 1][0]][chunks[i + 1][1], :])
        hidden_grad = (active_grad * gelu_both(h_refs[g][:, cols])[1]).astype(BF16)
        dh_refs[g][:, cols] = hidden_grad
        acc_ref[...] += nt(hidden_grad, ups[g][:, cols])


def norm_back(r, gain_row, before, upstream, outs):
    def body(rows, sums):
        above = upstream(rows)
        grad, gain_terms = norm_backward(before(rows), above, gain_row)
        for ref in outs:
            ref[rows, :] = grad.astype(ref.dtype)
        return sums[0] + fold_rows(gain_terms), sums[1] + fold_rows(above)

    zeros = jnp.zeros((8, outs[0].shape[1]), F32)
    gains, shifts = over_rows(outs[0].shape[0], 32, body, (zeros, zeros))
    return jnp.sum(gains, axis=0, keepdims=True), jnp.sum(shifts, axis=0, keepdims=True)


def cross_kernel(r):
    core, place = r.ids[0], r.ids[1]
    x2_ref, enc_ref = r.get("x2"), r.out("enc")
    own, tokens = x2_ref.shape[0], enc_ref.shape[0]
    blocks = own // BLOCK
    first, second = aligned(core * own), aligned((1 - core) * own)
    width = 3 * BLOCK
    enc_ref[pl.ds(first, own), :] = r.get("enc_own")[...]
    enc_ref[pl.ds(second, own), :] = r.get("enc_other")[...]
    r.send("enc")
    spread_marks(r.marks, r.get("src_row")[...])
    steps = tokens.bit_length()

    def bound(mark, past):
        def step(i, pair):
            low, high = pair
            middle = (low + high) // 2
            value = r.src_marks[0, jnp.minimum(middle, tokens - 1)]
            below = (low < high) & ((value < mark) | (past & (value == mark)))
            above = (low < high) & jnp.logical_not(below)
            return jnp.where(below, middle + 1, low), jnp.where(above, middle, high)

        return lax.fori_loop(0, steps, step, (jnp.int32(0), jnp.int32(tokens)))[0]

    row_ref = r.get("tgt_row")
    query_rows, spots, more = [], [], []
    for block in range(blocks):
        head = first + block * BLOCK
        low = bound(r.tgt_marks[0, head], jnp.bool_(False)) // BLOCK
        high = (bound(r.tgt_marks[0, head + BLOCK - 1], jnp.bool_(True)) + BLOCK - 1) // BLOCK
        key_at = aligned(jnp.minimum(low, (tokens - width) // BLOCK) * BLOCK)
        query_rows.append(row_ref[:, pl.ds(aligned(head), BLOCK)])
        spots.append(key_at)
        more.append((key_at // BLOCK + 3, high))
        r.bias[block] = bias_for(r.marks, key_at, width, query_rows[block])
    masks = head_masks()
    x2_low = x2_ref[...].astype(BF16)
    for g in range(2):
        r.q[g] = (nn(x2_low, r.get(f"cq{g}")[...]) * SCALE).astype(BF16)
        r.k[g] = nn(enc_ref[...], r.get(f"ckv{g}")[0]).astype(BF16)
        r.v[g] = nn(enc_ref[...], r.get(f"ckv{g}")[1]).astype(BF16)
        r.turn[quad(g), :] = r.v[g].T

    def weigh(g, h, scores, bias, key_at, keys_width, top):
        new_top, total, weights = soft_weights(scores, h, bias, top)
        features = slice(g * QUAD + h * HDIM, g * QUAD + (h + 1) * HDIM)
        return new_top, total, nn(r.turn[features, pl.ds(key_at, keys_width)], weights), features

    def score(block, g):
        rows = slice(block * BLOCK, (block + 1) * BLOCK)
        return nt(r.k[g, pl.ds(spots[block], width), :], stack_heads(r.q[g, rows, :], masks))

    tiles = [(block, g) for block in range(blocks) for g in range(2)]
    ahead = score(*tiles[0])
    for i, (block, g) in enumerate(tiles):
        rows = slice(block * BLOCK, (block + 1) * BLOCK)
        scores, ahead = ahead, score(*tiles[i + 1]) if i + 1 < len(tiles) else None
        for h in range(4):
            top, total, mixed, features = weigh(g, h, scores, r.bias[block], spots[block], width, None)
            r.mix[features, rows] = mixed
            r.tops[g * 4 + h : g * 4 + h + 1, rows] = top
            r.totals[g * 4 + h : g * 4 + h + 1, rows] = total

    for block in range(blocks):
        rows = slice(block * BLOCK, (block + 1) * BLOCK)

        def extra(i, carry, block=block, rows=rows):
            key_at = aligned(i * BLOCK)
            bias = bias_for(r.marks, key_at, BLOCK, query_rows[block])
            for g in range(2):
                scores = nt(r.k[g, pl.ds(key_at, BLOCK), :], stack_heads(r.q[g, rows, :], masks))
                for h in range(4):
                    at = slice(g * 4 + h, g * 4 + h + 1)
                    old = r.tops[at, rows]
                    top, total, mixed, features = weigh(g, h, scores, bias, key_at, BLOCK, old)
                    fade = jnp.exp(old - top)
                    r.mix[features, rows] = r.mix[features, rows] * fade + mixed
                    r.tops[at, rows] = top
                    r.totals[at, rows] = r.totals[at, rows] * fade + total
            return carry

        lax.fori_loop(*more[block], extra, 0)
    for head in range(8):
        features = slice(head * HDIM, (head + 1) * HDIM)
        at = slice(head, head + 1)
        r.ot[features, :] = (r.mix[features, :] * (1.0 / r.totals[at, :])).astype(BF16)
        r.lse[head // 4, head % 4 : head % 4 + 1, :] = r.tops[at, :] + jnp.log(r.totals[at, :])
    outs = (r.get("co0"), r.get("co1"))
    r.acc[...] = tn(r.ot[:QUAD, :], outs[0][...]) + tn(r.ot[QUAD:, :], outs[1][...])
    x3_low = r.out("x3_low")
    norm_forward(r, 3, lambda rows: x2_ref[rows, :], r.z3, r.x3, x3_low)
    r.send("x3_low")
    ups, downs = feed_weights(r)
    hs = (r.h.at[0], r.h.at[1])
    feed_forward(x3_low, ups, downs, hs, (r.out("a0"), r.out("a1")), r.acc)
    r.send("a0")
    r.send("a1")
    gain_ref, shift_ref, cot_ref, dec_ref, dy_ref = (
        r.get("gain"), r.get("shift"), r.get("cot"), r.out("dec"), r.out("dy")
    )
    last_gain, last_shift = gain_ref[4:5, :], shift_ref[4:5, :]

    def fourth_norm(rows, sums):
        before = r.x3[rows, :] + r.acc[rows, :]
        normed, rate = normalize(before)
        dec_ref[rows, :] = (normed * last_gain + last_shift).astype(BF16)
        upstream = cot_ref[rows, :].astype(F32)
        scaled = upstream * last_gain
        mean_one = jnp.mean(scaled, axis=-1, keepdims=True)
        mean_two = jnp.mean(scaled * normed, axis=-1, keepdims=True)
        grad = rate * (scaled - mean_one - normed * mean_two)
        r.z4[rows, :] = grad
        dy_ref[rows, :] = grad.astype(BF16)
        return sums[0] + fold_rows(upstream * normed), sums[1] + fold_rows(upstream)

    zeros = jnp.zeros((8, x2_ref.shape[1]), F32)
    gain_four, shift_four = over_rows(own, 32, fourth_norm, (zeros, zeros))
    r.send("dec")
    r.send("dy")
    feed_backward(dy_ref, ups, downs, hs, (r.out("dh0"), r.out("dh1")), r.z4)
    r.send("dh0")
    r.send("dh1")
    gain_three, shift_three = norm_back(
        r, gain_ref[3:4, :], lambda rows: r.z3[rows, :], lambda rows: r.z4[rows, :], (r.dz, r.low)
    )
    norms = r.out("norms")
    norms[0:1, :] = gain_three
    norms[1:2, :] = jnp.sum(gain_four, axis=0, keepdims=True)
    norms[2:3, :] = shift_three
    norms[3:4, :] = jnp.sum(shift_four, axis=0, keepdims=True)
    branch = r.low[...]
    ots = (r.ot.at[:QUAD], r.ot.at[QUAD:])
    mixed_gradients(branch, ots, outs, r.do, r.delta)
    packs = pair_of_packs(r, CROSS_BITS)
    for g, (packed, mark) in enumerate(packs):
        pack(packed, mark, 3, as_unit(nn(ots[g][...], branch)))
        r.turn[quad(g), :] = r.k[g].T
    r.dk[...] = jnp.zeros(r.dk.shape, F32)
    r.dv[...] = jnp.zeros(r.dv.shape, F32)

    def back_scores(block, g, key_at, keys_width):
        rows = slice(block * BLOCK, (block + 1) * BLOCK)
        return backward_scores(g, rows, key_at, keys_width, masks, r.q.at[g], r.k.at[g], r.v.at[g], r.do)

    def back_sums(block, g, key_at, bias, scored, add):
        rows = slice(block * BLOCK, (block + 1) * BLOCK)
        backward_sums(
            g, rows, key_at, bias, scored, r.turn, r.lse.at[g], r.delta, r.dqt, r.dk, r.dv, add
        )

    ahead = back_scores(*tiles[0], spots[0], width)
    for i, (block, g) in enumerate(tiles):
        scored = ahead
        if i + 1 < len(tiles):
            ahead = back_scores(*tiles[i + 1], spots[tiles[i + 1][0]], width)
        back_sums(block, g, spots[block], r.bias[block], scored, False)
    for block in range(blocks):

        def extra_back(i, carry, block=block):
            key_at = aligned(i * BLOCK)
            bias = bias_for(r.marks, key_at, BLOCK, query_rows[block])
            for g in range(2):
                back_sums(block, g, key_at, bias, back_scores(block, g, key_at, BLOCK), True)
            return carry

        lax.fori_loop(*more[block], extra_back, 0)
    query_grad = (r.dqt[...] * SCALE).astype(BF16).T
    key_grad, value_grad = r.dk[...].astype(BF16), r.dv[...].astype(BF16)
    query_turned, enc_turned = x2_ref[...].astype(BF16).T, enc_ref[...].T
    for g in (1, 0):
        packed, mark = packs[g]
        pack(packed, mark, 0, nn(query_turned, query_grad[:, quad(g)]))
        pack(packed, mark, 1, nn(enc_turned, key_grad[:, quad(g)]))
        pack(packed, mark, 2, nn(enc_turned, value_grad[:, quad(g)]))
        r.send(f"pack{g}")
    r.dk[...] = sum(
        nt(grad[:, quad(g)], r.get(f"ckv{g}")[i]) for i, grad in enumerate((key_grad, value_grad)) for g in range(2)
    )
    r.out("denc_other")[...] = r.dk[pl.ds(second, own), :].astype(BF16)
    r.send("denc_other")
    r.out("denc_own")[...] = r.dk[pl.ds(first, own), :]
    r.send("denc_own")
    r.out("g2")[...] = r.dz[...] + sum(nt(query_grad[:, quad(g)], r.get(f"cq{g}")[...]) for g in range(2))


def pair_of_packs(r, bits):
    core, place = r.ids[0], r.ids[1]
    return (r.out("pack0"), own_label(bits, core, place)), (r.out("pack1"), own_label(bits, 1 - core, place))


def head_gradients(r):
    for g in (1, 0):
        r.out(f"dq{g}")[...] = (r.dqt[quad(g), :] * SCALE).astype(BF16).T
        r.out(f"dk{g}")[...] = r.dk[:, quad(g)].astype(BF16)
        r.out(f"dv{g}")[...] = r.dv[:, quad(g)].astype(BF16)
        for key in ("dq", "dk", "dv"):
            r.send(f"{key}{g}")


def key_stream_gradient(r, weights, keys=("dk", "dv")):
    return sum(nt(r.get(f"{keys[i]}{g}")[...], weights[g][i]) for i in range(2) for g in range(2))


def feed_back_kernel(r):
    cot_ref, own_ref, recv_ref, z1_ref = r.get("cot"), r.get("denc_own"), r.get("denc_recv"), r.get("z1")
    acc_ref, packs = r.out("g0"), pair_of_packs(r, FEED_BITS)
    gain, shift = norm_back(
        r,
        r.get("gain")[1:2, :],
        lambda rows: z1_ref[rows, :],
        lambda rows: cot_ref[rows, :].astype(F32) + own_ref[rows, :] + recv_ref[rows, :].astype(F32),
        (acc_ref, r.dy),
    )
    r.out("norms")[0:1, :] = gain
    r.out("norms")[1:2, :] = shift
    turned = [ref[...].T for ref in (r.get("x1_low"), r.get("x3_low"), r.dy, r.get("dy3"))]
    chunks = [(g, j, cols) for g in (1, 0) for j, cols in feed_chunks(r.get("h0").shape[1])]

    def active_grad(i):
        g, j, cols = chunks[i]
        return nt(r.dy[...], r.get(f"down{g}")[cols, :])

    ahead = active_grad(0)
    for i, (g, j, cols) in enumerate(chunks):
        above = ahead
        if i + 1 < len(chunks):
            ahead = active_grad(i + 1)
        active, slope = gelu_both(r.get(f"h{g}")[:, cols].astype(F32))
        hidden_grad, active = (above * slope).astype(BF16), active.astype(BF16)
        acc_ref[...] += nt(hidden_grad, r.get(f"up{g}")[:, cols])
        up_grad = nn(turned[0], hidden_grad) + nn(turned[1], r.get(f"dh{g}")[:, cols])
        down_grad = nn(turned[2], active) + nn(turned[3], r.get(f"a{g}")[:, cols])
        packed, mark = packs[g]
        for b in range(2):
            pack(packed, mark, 2 * j + b, up_grad[:, quad(b)])
            pack(packed, mark, 2 * j + b, down_grad[:, quad(b)], QUAD)
        if j == 1:
            r.send(f"pack{g}")


def norm_parts(norms, r):
    feed, dec, cross = r.get("feed_norms"), r.get("dec_norms"), r.get("cross_norms")
    rows = [(norms, 0), (feed, 0), (dec, 0), (cross, 0), (cross, 1)]
    rows += [(norms, 1), (feed, 1), (dec, 1), (cross, 2), (cross, 3)]
    return [ref[at : at + 1, :] for ref, at in rows]


def self_back_kernel(causal, norm_at, bits, r):
    core, place = r.ids[0], r.ids[1]
    z_ref, up_ref, x_ref, row_ref = r.get("z"), r.get("up"), r.get("x"), r.get("row")
    tokens, own = x_ref.shape[0], z_ref.shape[0]
    window = r.marks.shape[0]
    start, first = aligned(core * (tokens - window)), aligned(core * own)
    spread_marks(r.marks, row_ref[:, pl.ds(start, window)])
    spots = set_self_bias(r.bias, core, tokens, r.marks, row_ref, causal)
    norms = r.out("norms")
    gain, shift = norm_back(
        r,
        r.get("gain")[norm_at : norm_at + 1, :],
        lambda rows: z_ref[rows, :],
        lambda rows: up_ref[rows, :],
        (r.out("dz"), r.low),
    )
    norms[0:1, :] = gain
    norms[1:2, :] = shift
    r.send("dz")
    branch = r.low[...]
    ots = (r.get("ot0"), r.get("ot1"))
    mixed_gradients(branch, ots, (r.get("wo0"), r.get("wo1")), r.do, r.delta)
    packs = pair_of_packs(r, bits)
    for g, (packed, mark) in enumerate(packs):
        pack(packed, mark, 3, as_unit(nn(ots[g][...], branch)))
        if not causal:
            pack_norms(packed, mark, norm_parts(norms, r))
    masks = head_masks()
    r.dk[...] = jnp.zeros(r.dk.shape, F32)
    r.dv[...] = jnp.zeros(r.dv.shape, F32)
    for g in range(2):
        r.kt[quad(g), :] = r.get(f"k{g}")[...].T
        for key in ("q", "v", "lse"):
            r.get(f"{key}{g}")
    tiles = [(block, g) for block in range(len(spots)) for g in range(2)]

    def back_scores(block, g):
        rows = slice(block * BLOCK, (block + 1) * BLOCK)
        return backward_scores(g, rows, *spots[block], masks, r.get(f"q{g}"), r.get(f"k{g}"), r.get(f"v{g}"), r.do)

    ahead = back_scores(*tiles[0])
    for i, (block, g) in enumerate(tiles):
        rows, (key_at, width) = slice(block * BLOCK, (block + 1) * BLOCK), spots[block]
        scored = ahead
        if i + 1 < len(tiles):
            ahead = back_scores(*tiles[i + 1])
        backward_sums(
            g, rows, key_at, r.bias[block, :width, :], scored, r.kt, r.get(f"lse{g}"), r.delta, r.dqt, r.dk, r.dv, False
        )
    head_gradients(r)
    keys_turned, query_turned = x_ref[pl.ds(start, window), :].T, x_ref[pl.ds(first, own), :].T
    for g in (1, 0):
        packed, mark = packs[g]
        pack(packed, mark, 0, nn(query_turned, r.out(f"dq{g}")[...]))
        pack(packed, mark, 1, nn(keys_turned, r.out(f"dk{g}")[...]))
        pack(packed, mark, 2, nn(keys_turned, r.out(f"dv{g}")[...]))
        r.send(f"pack{g}")


def stream_gradient_kernel(r):
    core = r.ids[0]
    dz_ref, own, window = r.get("dz"), r.get("dq0").shape[0], r.get("dk0").shape[0]
    w = (r.get("w0"), r.get("w1"))
    r.near[...] = key_stream_gradient(r, [(w[g][1], w[g][2]) for g in range(2)])
    r.out("halo")[...] = r.near[pl.ds(aligned((1 - core) * own), window - own), :].astype(BF16)
    r.send("halo")
    r.out("dx")[...] = (
        dz_ref[...]
        + sum(nt(r.get(f"dq{g}")[...], w[g][0]) for g in range(2))
        + r.near[pl.ds(aligned(core * (window - own)), own), :]
    )


class Refs:
    def __init__(self, smem, ins, outs, scratch):
        for name, ref in list(smem.items()) + list(scratch.items()):
            setattr(self, name, ref)
        self.ins, self.outs = ins, outs
        self.waited, self.sent = set(), set()
        for copy, ref in ins.values():
            copy.start()

    def get(self, name):
        copy, ref = self.ins[name]
        if name not in self.waited:
            self.waited.add(name)
            copy.wait()
        return ref

    def out(self, name):
        return self.outs[name][1]

    def send(self, name):
        self.sent.add(name)
        self.outs[name][0].start()

    def close(self):
        for name in self.ins:
            self.get(name)
        for name in self.outs:
            if name not in self.sent:
                self.send(name)
        for copy, ref in self.outs.values():
            copy.wait()


def call(kernel, name, smem, ins, outs, scratch, cost):
    n_smem, n_in, n_out, n_scratch = len(smem), len(ins), len(outs), len(scratch)

    def body(*refs):
        smem_refs = refs[:n_smem]
        refs = refs[n_smem:]
        in_refs, out_refs, refs = refs[:n_in], refs[n_in : n_in + n_out], refs[n_in + n_out :]
        in_vmem, out_vmem, refs = refs[:n_in], refs[n_in : n_in + n_out], refs[n_in + n_out :]
        in_sem, out_sem = refs[-2:]
        copies_in = {
            key: (pltpu.make_async_copy(in_refs[i], in_vmem[i], in_sem.at[i]), in_vmem[i])
            for i, key in enumerate(ins)
        }
        copies_out = {
            key: (pltpu.make_async_copy(out_vmem[i], out_refs[i], out_sem.at[i]), out_vmem[i])
            for i, key in enumerate(outs)
        }
        held = Refs(dict(zip(smem, smem_refs)), copies_in, copies_out, dict(zip(scratch, refs)))
        kernel(held)
        held.close()

    results = pl.pallas_call(
        body,
        out_shape=[jax.ShapeDtypeStruct(*out) for out in outs.values()],
        in_specs=[pl.BlockSpec(memory_space=pltpu.SMEM)] * n_smem + [pl.BlockSpec(memory_space=pl.ANY)] * n_in,
        out_specs=[pl.BlockSpec(memory_space=pl.ANY)] * n_out,
        scratch_shapes=[pltpu.VMEM(array.shape, array.dtype) for array in ins.values()]
        + [pltpu.VMEM(*out) for out in outs.values()]
        + [pltpu.VMEM(*one) for one in scratch.values()]
        + [pltpu.SemaphoreType.DMA((n_in,)), pltpu.SemaphoreType.DMA((n_out,))],
        compiler_params=pltpu.CompilerParams(vmem_limit_bytes=VMEM_LIMIT),
        cost_estimate=pl.CostEstimate(flops=cost * 10**9, transcendentals=0, bytes_accessed=cost * 10**6),
        name=name,
    )(*smem.values(), *ins.values())
    return SimpleNamespace(**dict(zip(outs, results)))


def finish_kernel(kind, bits, ids_ref, *refs):
    mark = own_label(bits, ids_ref[0], ids_ref[1])
    gathered, sem = refs[-2:]
    n_outs = {"enc": 4, "dec": 2, "cross": 3, "feed": 2}[kind]
    count = len(refs) - 2 - n_outs
    parts, outs = refs[:count], refs[count:-2]
    copies, at = [], 0
    for i, part in enumerate(parts):
        copies.append(pltpu.make_async_copy(part, gathered.at[pl.ds(at, part.shape[0])], sem.at[i]))
        at += part.shape[0]
    for copy in copies:
        copy.start()
    for copy in copies:
        copy.wait()
    for shard in range(SHARDS):
        unit, half = divmod(shard, 2)
        rows = slice(half * QUAD, (half + 1) * QUAD)
        where = pl.ds(mark ^ shard, 1)
        value = gathered[where, :QUAD, :][0].astype(F32)
        if kind == "feed":
            outs[0][rows, quad(unit)] = value
            outs[1][quad(unit), rows] = gathered[where, QUAD:, :][0].T.astype(F32)
        elif unit == 3:
            outs[2 if kind == "cross" else 1][:, quad(half)] = value
        elif kind != "cross":
            outs[0][unit, rows, :] = value
        elif unit == 0:
            outs[0][rows, :] = value
        else:
            outs[1][unit - 1, rows, :] = value
        if kind == "enc":
            norms = gathered[where, QUAD:, :][0].astype(F32)
            many = norm_rows(SHARDS)
            for i in range(many):
                row, side = divmod(shard * many + i, 2)
                if row < 10:
                    outs[2 + row // 5][row % 5 : row % 5 + 1, quad(side)] = norms[i : i + 1, :]


def finish(group, ids, outs):
    parts = group.parts
    shape = (SHARDS,) + parts[0].shape[1:]
    return pl.pallas_call(
        functools.partial(finish_kernel, group.kind, group.bits),
        out_shape=[jax.ShapeDtypeStruct(*out) for out in outs],
        in_specs=[pl.BlockSpec(memory_space=pltpu.SMEM)] + [pl.BlockSpec(memory_space=pl.ANY)] * len(parts),
        out_specs=[pl.BlockSpec(memory_space=pltpu.VMEM)] * len(outs),
        scratch_shapes=[pltpu.VMEM(shape, BF16), pltpu.SemaphoreType.DMA((len(parts),))],
        compiler_params=pltpu.CompilerParams(vmem_limit_bytes=VMEM_LIMIT),
        cost_estimate=pl.CostEstimate(flops=2 * 10**9, transcendentals=0, bytes_accessed=2 * 10**6),
        name="finish_" + group.kind,
    )(ids, *parts)


class Sum:
    def __init__(self, kind, bits, dp, mp):
        self.kind, self.bits, self.dp, self.mp = kind, bits, dp, mp

    def hop(self, array, step):
        pairs = []
        for place in range(self.dp):
            for core in range(self.mp):
                bit = self.bits[core][step] if step < 4 else step
                pairs.append((place * self.mp + core, (place ^ (1 << bit)) * self.mp + core))
        return lax.ppermute(array, ("dp", "mp"), pairs)

    def swap(self, other):
        self.sent = lax.ppermute(other, "mp", [(0, 1), (1, 0)])

    def halve(self, mine=None):
        mine = self.keep if mine is None else mine
        half = mine.shape[0] // 2
        return [mine[half:] + self.sent[half:], mine[:half] + self.sent[:half]]

    def send_half(self, give, keep, step):
        self.keep = keep
        self.sent = self.hop(give, step)

    def last_sum(self):
        return self.keep + self.sent

    def exchange(self, part):
        step = 3
        while 2 << step < self.dp:
            part = part + self.hop(part, step)
            step += 1
        self.keep, self.sent = part, self.hop(part, step)

    def double(self, step, parts=None):
        self.parts = self.parts + [self.hop(part, step) for part in parts or [self.joined()]]

    def joined(self):
        return jnp.concatenate(self.parts) if len(self.parts) > 1 else self.parts[0]


def together(*values):
    return lax.optimization_barrier(values)


def on_device(
    src_embed, tgt_embed, src_segment, tgt_segment, enc_qkv, enc_out_proj, dec_qkv, dec_out_proj, cross_query,
    cross_kv, cross_out_proj, ffn_up, ffn_down, norm_gain, norm_bias, enc_cotangent, dec_cotangent,
):
    dp, mp = lax.axis_size("dp"), lax.axis_size("mp")
    tokens, model = src_embed.shape
    own = tokens // mp
    window = own + MOST
    half = ffn_up.shape[1]
    hidden = 2 * half
    position = lax.axis_index("mp")
    ids = jnp.stack([position, lax.axis_index("dp")]).astype(jnp.int32)
    pairs = [(0, 1), (1, 0)]

    def swap(tree):
        return jax.tree.map(lambda a: lax.ppermute(a, "mp", pairs), tree)

    enc_w1, enc_o1 = swap((enc_qkv, enc_out_proj))
    up1, down1 = swap((ffn_up, ffn_down))
    dec_w1, dec_o1 = swap((dec_qkv, dec_out_proj))
    cross_q1, cross_kv1, cross_o1 = swap((cross_query, cross_kv, cross_out_proj))
    feed = {"up0": ffn_up, "up1": up1, "down0": ffn_down, "down1": down1}

    def rows(count, dtype):
        return ((count, model), dtype)

    blocks = own // BLOCK
    q_shape, k_shape, ot_shape, lse_shape = ((own, QUAD), BF16), ((window, QUAD), BF16), ((QUAD, own), BF16), ((4, own), F32)
    vt_shape, marks, bias = ((QUAD, window), BF16), ((window, BLOCK), jnp.int32), ((blocks, 3 * BLOCK, BLOCK), F32)
    heads = {"q": q_shape, "k": k_shape, "v": k_shape, "ot": ot_shape, "lse": lse_shape}
    wide = ((own, half), BF16)
    norm_in = {"gain": norm_gain, "shift": norm_bias}
    first = call(
        own_heads_kernel, "own_heads", {"ids": ids},
        {"src_row": src_segment, "src": src_embed, "src_w": enc_qkv,
         "tgt_row": tgt_segment, "tgt": tgt_embed, "tgt_w": dec_qkv},
        {f"{side}_{key}": shape for side in ("src", "tgt") for key, shape in heads.items()},
        {"marks": marks, "src_bias": bias, "tgt_bias": bias, "src_vt": vt_shape, "tgt_vt": vt_shape},
        cost=8,
    )
    encoder = call(
        encoder_kernel, "encoder_forward", {"ids": ids},
        {"row": src_segment, "x": src_embed, "w": enc_w1, "ot0": first.src_ot, "wo0": enc_out_proj, "wo1": enc_o1,
         **norm_in, "up0": ffn_up, "down0": ffn_down, "up1": up1, "down1": down1},
        {**heads, "z0": rows(own, F32), "x1_low": rows(own, BF16), "h0": wide, "h1": wide,
         "z1": rows(own, F32), "enc": rows(own, BF16)},
        {"marks": marks, "bias": bias, "vt": vt_shape, "x1": rows(own, F32), "acc": rows(own, F32)},
        cost=12,
    )
    enc_swapped = swap(encoder.enc)
    decoder = call(
        decoder_kernel, "decoder_self_forward", {"ids": ids},
        {"row": tgt_segment, "x": tgt_embed, "w": dec_w1, "ot0": first.tgt_ot, "wo0": dec_out_proj, "wo1": dec_o1,
         **norm_in},
        {**heads, "z2": rows(own, F32), "x2": rows(own, F32)},
        {"marks": marks, "bias": bias, "vt": vt_shape, "acc": rows(own, F32)}, cost=6,
    )
    packed = ((SHARDS, QUAD, QUAD), BF16)
    packed_feed = ((SHARDS, 2 * QUAD, QUAD), BF16)
    packed_norms = ((SHARDS, QUAD + TILE, QUAD), BF16)
    crossed = call(
        cross_kernel, "cross_and_decoder_feed",
        {"ids": ids, "src_marks": src_segment, "tgt_marks": tgt_segment},
        {"src_row": src_segment, "tgt_row": tgt_segment, "enc_own": encoder.enc, "enc_other": enc_swapped,
         "x2": decoder.x2, "cq0": cross_query, "ckv0": cross_kv, "cq1": cross_q1, "ckv1": cross_kv1,
         "co0": cross_out_proj, "co1": cross_o1, **norm_in, **feed, "cot": dec_cotangent},
        {"enc": rows(tokens, BF16), "x3_low": rows(own, BF16), "a0": wide, "a1": wide, "dec": rows(own, BF16),
         "dy": rows(own, BF16), "dh0": wide, "dh1": wide, "norms": rows(4, F32), "pack0": packed, "pack1": packed,
         "denc_other": rows(own, BF16), "denc_own": rows(own, F32), "g2": rows(own, F32)},
        {"marks": ((tokens, BLOCK), jnp.int32), "bias": bias, "q": ((2, own, QUAD), BF16),
         "k": ((2, tokens, QUAD), BF16), "v": ((2, tokens, QUAD), BF16), "turn": ((model, tokens), BF16),
         "mix": ((model, own), F32), "tops": ((8, own), F32), "totals": ((8, own), F32), "lse": ((2, 4, own), F32),
         "ot": ((model, own), BF16), "acc": rows(own, F32), "x3": rows(own, F32), "z3": rows(own, F32),
         "z4": rows(own, F32), "dz": rows(own, F32), "h": ((2, own, half), F32), "low": rows(own, BF16), "do": rows(own, BF16),
         "delta": ((8, own), F32), "dqt": ((model, own), F32), "dk": rows(tokens, F32), "dv": rows(tokens, F32)},
        cost=30,
    )
    def whole(mine, received):
        return jnp.where(
            position == 0, jnp.concatenate([mine, received]), jnp.concatenate([received, mine])
        )

    cross_sum = Sum("cross", CROSS_BITS, dp, mp)
    dec_sum = Sum("dec", DEC_BITS, dp, mp)
    feed_sum = Sum("feed", FEED_BITS, dp, mp)
    enc_sum = Sum("enc", ENC_BITS, dp, mp)
    cross_sum.swap(crossed.pack1)
    denc_recv = swap(crossed.denc_other)
    def self_backward(causal, at, bits, name, side, x, row, z, up, w0, w1, o0, o1, others, pack_shape, more):
        ins = {"z": z, "up": up, "gain": norm_gain, "row": row, "x": x}
        ins |= {"ot0": getattr(first, side + "_ot"), "ot1": others.ot, "wo0": o0, "wo1": o1}
        for key in ("k", "q", "v", "lse"):
            ins |= {key + "0": getattr(first, f"{side}_{key}"), key + "1": getattr(others, key)}
        return call(
            functools.partial(self_back_kernel, causal, at, bits), name, {"ids": ids}, ins | more,
            {"dz": rows(own, F32), "pack0": pack_shape, "pack1": pack_shape, "norms": rows(2, F32), "dq0": q_shape,
             "dq1": q_shape, "dk0": k_shape, "dk1": k_shape, "dv0": k_shape, "dv1": k_shape},
            {"marks": marks, "bias": bias, "low": rows(own, BF16), "do": rows(own, BF16), "delta": ((8, own), F32),
             "kt": ((model, window), BF16), "dqt": ((model, own), F32), "dk": rows(window, F32), "dv": rows(window, F32)},
            cost=13,
        )

    def stream_gradient(name, back, w0, w1, gate):
        ins = {"dz": gate, "w0": w0, "w1": w1}
        ins |= {f"{key}{g}": getattr(back, f"{key}{g}") for key in ("dk", "dv", "dq") for g in range(2)}
        return call(
            stream_gradient_kernel, name, {"ids": ids}, ins,
            {"halo": rows(window - own, BF16), "dx": rows(own, F32)}, {"near": rows(window, F32)}, cost=3,
        )

    square, out_half, triple = ((model, QUAD), F32), ((QUAD, model), F32), ((3, model, QUAD), F32)
    out_shapes = {
        "cross": [square, ((2, model, QUAD), F32), out_half],
        "dec": [triple, out_half],
        "feed": [((model, half), F32), rows(half, F32)],
        "enc": [triple, out_half, rows(5, F32), rows(5, F32)],
    }
    gate, give, keep, denc_recv, dec_own = together(
        encoder.z1, *cross_sum.halve(crossed.pack0), denc_recv, crossed.dec
    )
    cross_sum.send_half(give, keep, 0)
    fed = call(
        feed_back_kernel, "encoder_feed_backward", {"ids": ids},
        {"cot": enc_cotangent, "denc_own": crossed.denc_own, "denc_recv": denc_recv, "z1": gate, "gain": norm_gain,
         "x1_low": encoder.x1_low, "x3_low": crossed.x3_low, "dy3": crossed.dy, "h0": encoder.h0, "down1": down1,
         "h1": encoder.h1, "up1": up1, "dh1": crossed.dh1, "a1": crossed.a1, "down0": ffn_down, "up0": ffn_up,
         "dh0": crossed.dh0, "a0": crossed.a0},
        {"norms": rows(2, F32), "pack0": packed_feed, "pack1": packed_feed, "g0": rows(own, F32)},
        {"dy": rows(own, BF16)}, cost=17,
    )
    give, keep, other = together(*cross_sum.halve(), fed.pack1)
    cross_sum.send_half(give, keep, 1)
    feed_sum.swap(other)
    dec_swapped = swap(dec_own)
    dec_whole = whole(crossed.dec, dec_swapped)
    gate, dec_whole, give, keep = together(crossed.g2, dec_whole, *feed_sum.halve(fed.pack0))
    feed_sum.send_half(give, keep, 0)
    dec_back = self_backward(
        True, 2, DEC_BITS, "decoder_self_backward", "tgt", tgt_embed, tgt_segment, decoder.z2, gate,
        dec_qkv, dec_w1, dec_out_proj, dec_o1, decoder, packed, {},
    )
    gate, give, keep, other = together(dec_back.dz, *cross_sum.halve(), dec_back.pack1)
    cross_sum.send_half(give, keep, 2)
    dec_sum.swap(other)
    tgt_side = stream_gradient("tgt_gradient", dec_back, dec_qkv, dec_w1, gate)
    gate, give, keep, dec_give, dec_keep, part = together(
        fed.g0, *feed_sum.halve(), *dec_sum.halve(dec_back.pack0), cross_sum.last_sum()
    )
    feed_sum.send_half(give, keep, 1)
    dec_sum.send_half(dec_give, dec_keep, 0)
    cross_sum.exchange(part)
    tgt_recv = swap(tgt_side.halo)
    enc_back = self_backward(
        False, 0, ENC_BITS, "encoder_self_backward", "src", src_embed, src_segment, encoder.z0, gate,
        enc_qkv, enc_w1, enc_out_proj, enc_o1, encoder, packed_norms,
        {"feed_norms": fed.norms, "dec_norms": dec_back.norms, "cross_norms": crossed.norms},
    )
    gate, other, give, keep, dec_give, dec_keep, part = together(
        enc_back.dz, enc_back.pack1, *feed_sum.halve(), *dec_sum.halve(), cross_sum.last_sum()
    )
    enc_sum.swap(other)
    dec_sum.send_half(dec_give, dec_keep, 1)
    feed_sum.send_half(give, keep, 2)
    cross_sum.parts = [part]
    cross_sum.double(2)
    src_side = stream_gradient("src_gradient", enc_back, enc_qkv, enc_w1, gate)
    src_halo, give, keep, part, dec_give, dec_keep, *cross_sum.parts = together(
        src_side.halo, *enc_sum.halve(enc_back.pack0), feed_sum.last_sum(), *dec_sum.halve(), *cross_sum.parts
    )
    enc_sum.send_half(give, keep, 0)
    feed_sum.exchange(part)
    dec_sum.send_half(dec_give, dec_keep, 2)
    cross_sum.double(1)
    src_recv = swap(src_halo)
    give, keep, dec_part, *cross_sum.parts = together(*enc_sum.halve(), dec_sum.last_sum(), *cross_sum.parts)
    enc_sum.send_half(give, keep, 1)
    cross_sum.double(0)
    dec_sum.exchange(dec_part)
    give, keep, part = together(*enc_sum.halve(), feed_sum.last_sum())
    enc_sum.send_half(give, keep, 2)
    feed_sum.parts = [part]
    feed_sum.double(2)
    part, dec_part, *feed_sum.parts = together(enc_sum.last_sum(), dec_sum.last_sum(), *feed_sum.parts)
    enc_sum.exchange(part)
    dec_sum.parts = [dec_part]
    dec_sum.double(2)
    feed_sum.double(1)
    cross_out = finish(cross_sum, ids, out_shapes["cross"])
    part, dec_zero, dec_one, *feed_sum.parts = together(enc_sum.last_sum(), *dec_sum.parts, *feed_sum.parts)
    enc_sum.parts, dec_sum.parts = [part], [dec_zero, dec_one]
    enc_sum.double(2)
    dec_sum.double(1)
    feed_sum.double(0)
    enc_zero, enc_one, *dec_sum.parts = together(*enc_sum.parts, *dec_sum.parts)
    enc_sum.parts = [enc_zero, enc_one]
    enc_sum.double(1)
    dec_sum.double(0)
    enc_sum.double(0)
    feed_out = finish(feed_sum, ids, out_shapes["feed"])
    dec_out = finish(dec_sum, ids, out_shapes["dec"])
    enc_out = finish(enc_sum, ids, out_shapes["enc"])

    halo_at = (1 - position) * (own - (window - own))

    def with_halo(grad, received):
        part = lax.dynamic_slice_in_dim(grad, halo_at, window - own, 0) + received.astype(F32)
        return lax.dynamic_update_slice_in_dim(grad, part, halo_at, 0)

    return (
        crossed.enc,
        dec_whole,
        with_halo(src_side.dx, src_recv),
        with_halo(tgt_side.dx, tgt_recv),
        enc_out[0],
        enc_out[1],
        dec_out[0],
        dec_out[1],
        cross_out[0],
        cross_out[1],
        cross_out[2],
        feed_out[0],
        feed_out[1],
        enc_out[2],
        enc_out[3],
    )


def solution(mesh):
    in_specs = (
        P("dp", None), P("dp", None), P("dp", None), P("dp", None),
        P(None, None, "mp"), P("mp", None), P(None, None, "mp"), P("mp", None),
        P(None, "mp"), P(None, None, "mp"), P("mp", None), P(None, "mp"), P("mp", None),
        P(), P(), P(("dp", "mp"), None), P(("dp", "mp"), None),
    )
    out_specs = (
        P("dp", None), P("dp", None), P(("dp", "mp"), None), P(("dp", "mp"), None),
        P(None, None, "mp"), P("mp", None), P(None, None, "mp"), P("mp", None),
        P(None, "mp"), P(None, None, "mp"), P("mp", None), P(None, "mp"), P("mp", None),
        P(), P(),
    )
    return jax.shard_map(on_device, mesh=mesh, in_specs=in_specs, out_specs=out_specs, check_vma=False)
```

```python
import functools
import math
from types import SimpleNamespace

import jax
import jax.numpy as jnp
from jax import lax
from jax.experimental import pallas as pl
from jax.experimental.pallas import tpu as pltpu
from jax.sharding import PartitionSpec as P

HDIM = 64
SCALE = HDIM ** (-0.5)
EPSILON = 1e-05
MASKED = -1e30
BLOCK = 128
MOST = 128
QUAD = 4 * HDIM
UNITS = 4
TILE = 16
FEED = 512
SHARDS = 8
CROSS_BITS = ((0, 1, 2, 3), (1, 0, 2, 3))
UP_BITS = ((0, 1, 2, 3), (1, 0, 2, 3))
DOWN_BITS = ((1, 0, 2, 3), (0, 1, 2, 3))
DEC_BITS = ((0, 1, 2, 3), (1, 0, 2, 3))
ENC_BITS = ((1, 0, 2, 3), (0, 1, 2, 3))
F32 = jnp.float32
BF16 = jnp.bfloat16
VMEM_LIMIT = 56 * 1024 * 1024
GELU_IN = math.sqrt(2.0 / math.pi)
GELU_CUBE = 0.044715


def nn(left, right):
    return jnp.dot(left, right, preferred_element_type=F32)


def nt(left, right):
    return lax.dot_general(left, right, (((1,), (1,)), ((), ())), preferred_element_type=F32)


def tn(left, right):
    return lax.dot_general(left, right, (((0,), (0,)), ((), ())), preferred_element_type=F32)


def aligned(index, size=BLOCK):
    return pl.multiple_of(index, size)


def over_rows(rows, chunk, body, carry, unroll=4):
    return lax.fori_loop(
        0,
        rows // chunk,
        lambda i, kept: body(pl.ds(aligned(i * chunk, chunk), chunk), kept),
        carry,
        unroll=min(unroll, rows // chunk),
    )


def normalize(before):
    centered = before - jnp.mean(before, axis=-1, keepdims=True)
    variance = jnp.mean(centered * centered, axis=-1, keepdims=True)
    rate = lax.rsqrt(variance + EPSILON)
    return centered * rate, rate


def norm_backward(before, upstream, gain_row):
    normed, rate = normalize(before)
    scaled = upstream * gain_row
    first = jnp.mean(scaled, axis=-1, keepdims=True)
    second = jnp.mean(scaled * normed, axis=-1, keepdims=True)
    return rate * (scaled - first - normed * second), upstream * normed


def fold_rows(block):
    return jnp.sum(block.reshape(block.shape[0] // 8, 8, block.shape[1]), axis=0)


def gelu(hidden):
    inner = GELU_IN * hidden * (1.0 + GELU_CUBE * hidden * hidden)
    return 0.5 * hidden * (1.0 + jnp.tanh(inner))


def gelu_both(hidden):
    square = hidden * hidden
    bent = jnp.tanh(GELU_IN * hidden * (1.0 + GELU_CUBE * square))
    half = 0.5 * (1.0 + bent)
    slope = half + 0.5 * hidden * (1.0 - bent * bent) * (GELU_IN * (1.0 + 3.0 * GELU_CUBE * square))
    return hidden * half, slope


def head_masks():
    lane = lax.broadcasted_iota(jnp.int32, (1, QUAD), 1)
    return [
        jnp.where((lane >= h * HDIM) & (lane < (h + 1) * HDIM), 1.0, 0.0).astype(BF16)
        for h in range(4)
    ]


def stack_heads(block, masks):
    return jnp.concatenate([block * mask for mask in masks], axis=0)


def quad(g):
    return slice(g * QUAD, (g + 1) * QUAD)


def bias_for(marks_ref, key_at, width, query_row, causal=False, key_start=0, query_start=0):
    allowed = marks_ref[pl.ds(key_at, width), :] == query_row
    if causal:
        places = key_start + lax.broadcasted_iota(jnp.int32, (width, BLOCK), 0)
        queries = query_start + lax.broadcasted_iota(jnp.int32, (width, BLOCK), 1)
        allowed = allowed & (places <= queries)
    return jnp.where(allowed, 0.0, MASKED)


def self_window(core, block, causal):
    middle = block + core
    if causal:
        return aligned(jnp.maximum(middle - 1, 0) * BLOCK), 2 * BLOCK
    return aligned(jnp.clip(middle - 1, 0, 2) * BLOCK), 3 * BLOCK


def set_self_bias(bias_ref, core, tokens, marks_ref, row_ref, causal):
    window, own = marks_ref.shape[0], row_ref.shape[1] // 2
    start = core * (tokens - window)
    spots = []
    for block in range(own // BLOCK):
        key_at, width = self_window(core, block, causal)
        first = aligned(core * own + block * BLOCK)
        bias_ref[block, :width, :] = bias_for(
            marks_ref, key_at, width, row_ref[:, pl.ds(first, BLOCK)], causal, start + key_at, first
        )
        spots.append((key_at, width))
    return spots


def soft_weights(scores, h, bias, top=None):
    one = scores[:, h * BLOCK : (h + 1) * BLOCK] + bias
    high = jnp.max(one, axis=0, keepdims=True)
    top = high if top is None else jnp.maximum(top, high)
    weights = jnp.exp(one - top)
    return top, jnp.sum(weights, axis=0, keepdims=True), weights.astype(BF16)


def quad_forward(spots, q_ref, k_ref, vt_ref, bias_ref, ot_ref, lse_ref, masks):
    def score(block):
        rows, (key_at, width) = slice(block * BLOCK, (block + 1) * BLOCK), spots[block]
        return nt(k_ref[pl.ds(key_at, width), :], stack_heads(q_ref[rows, :], masks))

    ahead = score(0)
    for block, (key_at, width) in enumerate(spots):
        rows = slice(block * BLOCK, (block + 1) * BLOCK)
        scores, ahead = ahead, score(block + 1) if block + 1 < len(spots) else None
        for h in range(4):
            top, total, weights = soft_weights(scores, h, bias_ref[block, :width, :])
            features = slice(h * HDIM, (h + 1) * HDIM)
            mixed = nn(vt_ref[features, pl.ds(key_at, width)], weights)
            ot_ref[features, rows] = (mixed * (1.0 / total)).astype(BF16)
            lse_ref[h : h + 1, rows] = top + jnp.log(total)


def backward_scores(g, rows, key_at, width, masks, q_ref, k_ref, v_ref, do_ref):
    keys = pl.ds(key_at, width)
    q_stack = stack_heads(q_ref[rows, :], masks)
    do_stack = stack_heads(do_ref[rows, quad(g)], masks)
    return q_stack, do_stack, nt(k_ref[keys, :], q_stack), nt(v_ref[keys, :], do_stack)


def backward_sums(g, rows, key_at, bias, scored, kt_ref, lse_ref, delta_ref, dqt_ref, dk_ref, dv_ref, add):
    q_stack, do_stack, scores, prob_grads = scored
    keys = pl.ds(key_at, bias.shape[0])
    probs, score_grads = [], []
    for h in range(4):
        cols = slice(h * BLOCK, (h + 1) * BLOCK)
        head = g * 4 + h
        prob = jnp.exp(scores[:, cols] + bias - lse_ref[h : h + 1, rows])
        score_grad = (prob * (prob_grads[:, cols] - delta_ref[head : head + 1, rows])).astype(BF16)
        probs.append(prob.astype(BF16))
        score_grads.append(score_grad)
    for h in range(4):
        features = slice((g * 4 + h) * HDIM, (g * 4 + h + 1) * HDIM)
        query_grad = nn(kt_ref[features, keys], score_grads[h])
        if add:
            dqt_ref[features, rows] += query_grad
        else:
            dqt_ref[features, rows] = query_grad
    dv_ref[keys, quad(g)] += nn(jnp.concatenate(probs, axis=1), do_stack)
    dk_ref[keys, quad(g)] += nn(jnp.concatenate(score_grads, axis=1), q_stack)


def mixed_gradients(branch, ot_refs, w_out, do_ref, delta_ref):
    for g in range(2):
        do_ref[:, quad(g)] = nt(branch, w_out[g][...]).astype(BF16)
        turned = nt(w_out[g][...], branch).astype(BF16).astype(F32)
        product = turned * ot_refs[g][...].astype(F32)
        for h in range(4):
            delta_ref[g * 4 + h : g * 4 + h + 1, :] = jnp.sum(
                product[h * HDIM : (h + 1) * HDIM, :], axis=0, keepdims=True
            )


def spread_marks(marks_ref, row):
    marks_ref[...] = jnp.broadcast_to(row, (marks_ref.shape[1], marks_ref.shape[0])).T


def label(bits, place):
    first, second, third = [(place >> bit) & 1 for bit in bits[:3]]
    return 4 * first + 2 * second + third


def own_label(bits, core, place):
    return jnp.where(core == 0, label(bits[0], place), label(bits[1], place))


def pack(out_ref, mark, unit, value, at=0):
    rows = value.shape[0] // 2
    for half in range(2):
        where = pl.ds(mark ^ (2 * unit + half), 1)
        out_ref[where, at : at + rows, :] = value[half * rows : (half + 1) * rows].astype(BF16)[None]


def as_unit(value):
    return jnp.concatenate([value[:, :QUAD], value[:, QUAD:]], axis=0).astype(BF16)


def pack_norms(out_ref, mark, parts):
    shards, tall, width = out_ref.shape
    halves = [part[:, half * width : (half + 1) * width] for part in parts for half in range(2)]
    each = norm_rows(shards)
    blank = jnp.zeros((1, width), F32)
    halves += [blank] * (shards * each - len(halves))
    for i in range(shards):
        block = jnp.concatenate(halves[i * each : (i + 1) * each] + [blank] * (TILE - each), axis=0)
        out_ref[pl.ds(mark ^ i, 1), tall - TILE :, :] = block.astype(BF16)[None]


def norm_rows(shards):
    return -(-20 // shards)


def prepare_quad(x_ref, w_ref, core, q_ref, k_ref, v_ref, vt_ref):
    tokens, own, window = x_ref.shape[0], q_ref.shape[0], k_ref.shape[0]
    keys = x_ref[pl.ds(aligned(core * (tokens - window)), window), :]
    q_ref[...] = (nn(x_ref[pl.ds(aligned(core * own), own), :], w_ref[0]) * SCALE).astype(BF16)
    k_ref[...] = nn(keys, w_ref[1]).astype(BF16)
    v_ref[...] = nn(keys, w_ref[2]).astype(BF16)
    vt_ref[...] = v_ref[...].T


def own_heads_kernel(r):
    core = r.ids[0]
    masks = head_masks()
    for side, causal in (("src", False), ("tgt", True)):
        x_ref, row_ref = r.get(side), r.get(side + "_row")
        k_ref = r.out(side + "_k")
        start = aligned(core * (x_ref.shape[0] - k_ref.shape[0]))
        spread_marks(r.marks, row_ref[:, pl.ds(start, k_ref.shape[0])])
        bias_ref, vt_ref = getattr(r, side + "_bias"), getattr(r, side + "_vt")
        spots = set_self_bias(bias_ref, core, x_ref.shape[0], r.marks, row_ref, causal)
        q_ref, v_ref = r.out(side + "_q"), r.out(side + "_v")
        prepare_quad(x_ref, r.get(side + "_w"), core, q_ref, k_ref, v_ref, vt_ref)
        for key in ("_q", "_k", "_v"):
            r.send(side + key)
        quad_forward(
            spots, q_ref, k_ref, vt_ref, bias_ref, r.out(side + "_ot"), r.out(side + "_lse"), masks
        )
        r.send(side + "_ot")
        r.send(side + "_lse")


def other_heads(r, causal):
    core = r.ids[0]
    x_ref, row_ref, k_ref = r.get("x"), r.get("row"), r.out("k")
    start = aligned(core * (x_ref.shape[0] - k_ref.shape[0]))
    spread_marks(r.marks, row_ref[:, pl.ds(start, k_ref.shape[0])])
    spots = set_self_bias(r.bias, core, x_ref.shape[0], r.marks, row_ref, causal)
    q_ref, v_ref, ot_ref = r.out("q"), r.out("v"), r.out("ot")
    prepare_quad(x_ref, r.get("w"), core, q_ref, k_ref, v_ref, r.vt)
    for key in ("q", "k", "v"):
        r.send(key)
    quad_forward(spots, q_ref, k_ref, r.vt, r.bias, ot_ref, r.out("lse"), head_masks())
    r.send("lse")
    r.send("ot")
    r.acc[...] = tn(r.get("ot0")[...], r.get("wo0")[...]) + tn(ot_ref[...], r.get("wo1")[...])


def norm_forward(r, at, residual, before_ref, after_ref, low_ref):
    gain, shift = r.get("gain")[at : at + 1, :], r.get("shift")[at : at + 1, :]

    def body(rows, carry):
        before = residual(rows) + r.acc[rows, :]
        if before_ref is not None:
            before_ref[rows, :] = before
        after = normalize(before)[0] * gain + shift
        if after_ref is not None:
            after_ref[rows, :] = after
        if low_ref is not None:
            low_ref[rows, :] = after.astype(BF16)
        return carry

    over_rows(r.acc.shape[0], 32, body, 0)


def own_row_reader(x_ref, core, own):
    first = core * own
    return lambda rows: x_ref[pl.ds(aligned(first + rows.start, rows.size), rows.size), :].astype(F32)


def encoder_kernel(r):
    other_heads(r, False)
    x1_low = r.out("x1_low")
    norm_forward(r, 0, own_row_reader(r.get("x"), r.ids[0], r.acc.shape[0]), r.out("z0"), r.x1, x1_low)
    r.send("z0")
    r.send("x1_low")
    feed_forward(x1_low, *feed_weights(r), (r.out("h0"), r.out("h1")), None, r.acc)
    r.send("h0")
    r.send("h1")
    norm_forward(r, 1, lambda rows: r.x1[rows, :], r.out("z1"), None, r.out("enc"))


def decoder_kernel(r):
    other_heads(r, True)
    norm_forward(r, 2, own_row_reader(r.get("x"), r.ids[0], r.acc.shape[0]), r.out("z2"), r.out("x2"), None)


def feed_weights(r):
    return (r.get("up0"), r.get("up1")), (r.get("down0"), r.get("down1"))


def feed_chunks(half):
    return [(j, slice(j * FEED, (j + 1) * FEED)) for j in range(half // FEED)]


def feed_forward(low_ref, ups, downs, h_refs, a_refs, acc_ref):
    chunks = [(g, cols) for g in range(2) for j, cols in feed_chunks(ups[0].shape[1])]
    ahead = nn(low_ref[...], ups[0][:, chunks[0][1]])
    for i, (g, cols) in enumerate(chunks):
        hidden = ahead
        if i + 1 < len(chunks):
            ahead = nn(low_ref[...], ups[chunks[i + 1][0]][:, chunks[i + 1][1]])
        h_refs[g][:, cols] = hidden.astype(h_refs[g].dtype)
        active = gelu(hidden).astype(BF16)
        if a_refs is not None:
            a_refs[g][:, cols] = active
        term = nn(active, downs[g][cols, :])
        if i == 0:
            acc_ref[...] = term
        else:
            acc_ref[...] += term


def feed_backward(dy_ref, ups, downs, h_refs, dh_refs, acc_ref):
    chunks = [(g, cols) for g in range(2) for j, cols in feed_chunks(ups[0].shape[1])]
    ahead = nt(dy_ref[...], downs[0][chunks[0][1], :])
    for i, (g, cols) in enumerate(chunks):
        active_grad = ahead
        if i + 1 < len(chunks):
            ahead = nt(dy_ref[...], downs[chunks[i + 1][0]][chunks[i + 1][1], :])
        hidden_grad = (active_grad * gelu_both(h_refs[g][:, cols])[1]).astype(BF16)
        dh_refs[g][:, cols] = hidden_grad
        acc_ref[...] += nt(hidden_grad, ups[g][:, cols])


def norm_back(r, gain_row, before, upstream, outs):
    def body(rows, sums):
        above = upstream(rows)
        grad, gain_terms = norm_backward(before(rows), above, gain_row)
        for ref in outs:
            ref[rows, :] = grad.astype(ref.dtype)
        return sums[0] + fold_rows(gain_terms), sums[1] + fold_rows(above)

    zeros = jnp.zeros((8, outs[0].shape[1]), F32)
    gains, shifts = over_rows(outs[0].shape[0], 32, body, (zeros, zeros))
    return jnp.sum(gains, axis=0, keepdims=True), jnp.sum(shifts, axis=0, keepdims=True)


def cross_kernel(r):
    core, place = r.ids[0], r.ids[1]
    x2_ref, enc_ref = r.get("x2"), r.out("enc")
    own, tokens = x2_ref.shape[0], enc_ref.shape[0]
    blocks = own // BLOCK
    first, second = aligned(core * own), aligned((1 - core) * own)
    width = 3 * BLOCK
    enc_ref[pl.ds(first, own), :] = r.get("enc_own")[...]
    enc_ref[pl.ds(second, own), :] = r.get("enc_other")[...]
    r.send("enc")
    spread_marks(r.marks, r.get("src_row")[...])
    steps = tokens.bit_length()

    def bound(mark, past):
        def step(i, pair):
            low, high = pair
            middle = (low + high) // 2
            value = r.src_marks[0, jnp.minimum(middle, tokens - 1)]
            below = (low < high) & ((value < mark) | (past & (value == mark)))
            above = (low < high) & jnp.logical_not(below)
            return jnp.where(below, middle + 1, low), jnp.where(above, middle, high)

        return lax.fori_loop(0, steps, step, (jnp.int32(0), jnp.int32(tokens)))[0]

    row_ref = r.get("tgt_row")
    query_rows, spots, more = [], [], []
    for block in range(blocks):
        head = first + block * BLOCK
        low = bound(r.tgt_marks[0, head], jnp.bool_(False)) // BLOCK
        high = (bound(r.tgt_marks[0, head + BLOCK - 1], jnp.bool_(True)) + BLOCK - 1) // BLOCK
        key_at = aligned(jnp.minimum(low, (tokens - width) // BLOCK) * BLOCK)
        query_rows.append(row_ref[:, pl.ds(aligned(head), BLOCK)])
        spots.append(key_at)
        more.append((key_at // BLOCK + 3, high))
        r.bias[block] = bias_for(r.marks, key_at, width, query_rows[block])
    masks = head_masks()
    x2_low = x2_ref[...].astype(BF16)
    for g in range(2):
        r.q[g] = (nn(x2_low, r.get(f"cq{g}")[...]) * SCALE).astype(BF16)
        r.k[g] = nn(enc_ref[...], r.get(f"ckv{g}")[0]).astype(BF16)
        r.v[g] = nn(enc_ref[...], r.get(f"ckv{g}")[1]).astype(BF16)
        r.turn[quad(g), :] = r.v[g].T

    def weigh(g, h, scores, bias, key_at, keys_width, top):
        new_top, total, weights = soft_weights(scores, h, bias, top)
        features = slice(g * QUAD + h * HDIM, g * QUAD + (h + 1) * HDIM)
        return new_top, total, nn(r.turn[features, pl.ds(key_at, keys_width)], weights), features

    def score(block, g):
        rows = slice(block * BLOCK, (block + 1) * BLOCK)
        return nt(r.k[g, pl.ds(spots[block], width), :], stack_heads(r.q[g, rows, :], masks))

    tiles = [(block, g) for block in range(blocks) for g in range(2)]
    ahead = score(*tiles[0])
    for i, (block, g) in enumerate(tiles):
        rows = slice(block * BLOCK, (block + 1) * BLOCK)
        scores, ahead = ahead, score(*tiles[i + 1]) if i + 1 < len(tiles) else None
        for h in range(4):
            top, total, mixed, features = weigh(g, h, scores, r.bias[block], spots[block], width, None)
            r.mix[features, rows] = mixed
            r.tops[g * 4 + h : g * 4 + h + 1, rows] = top
            r.totals[g * 4 + h : g * 4 + h + 1, rows] = total

    for block in range(blocks):
        rows = slice(block * BLOCK, (block + 1) * BLOCK)

        def extra(i, carry, block=block, rows=rows):
            key_at = aligned(i * BLOCK)
            bias = bias_for(r.marks, key_at, BLOCK, query_rows[block])
            for g in range(2):
                scores = nt(r.k[g, pl.ds(key_at, BLOCK), :], stack_heads(r.q[g, rows, :], masks))
                for h in range(4):
                    at = slice(g * 4 + h, g * 4 + h + 1)
                    old = r.tops[at, rows]
                    top, total, mixed, features = weigh(g, h, scores, bias, key_at, BLOCK, old)
                    fade = jnp.exp(old - top)
                    r.mix[features, rows] = r.mix[features, rows] * fade + mixed
                    r.tops[at, rows] = top
                    r.totals[at, rows] = r.totals[at, rows] * fade + total
            return carry

        lax.fori_loop(*more[block], extra, 0)
    for head in range(8):
        features = slice(head * HDIM, (head + 1) * HDIM)
        at = slice(head, head + 1)
        r.ot[features, :] = (r.mix[features, :] * (1.0 / r.totals[at, :])).astype(BF16)
        r.lse[head // 4, head % 4 : head % 4 + 1, :] = r.tops[at, :] + jnp.log(r.totals[at, :])
    outs = (r.get("co0"), r.get("co1"))
    r.acc[...] = tn(r.ot[:QUAD, :], outs[0][...]) + tn(r.ot[QUAD:, :], outs[1][...])
    x3_low = r.out("x3_low")
    norm_forward(r, 3, lambda rows: x2_ref[rows, :], r.z3, r.x3, x3_low)
    r.send("x3_low")
    ups, downs = feed_weights(r)
    hs = (r.h.at[0], r.h.at[1])
    feed_forward(x3_low, ups, downs, hs, (r.out("a0"), r.out("a1")), r.acc)
    r.send("a0")
    r.send("a1")
    gain_ref, shift_ref, cot_ref, dec_ref, dy_ref = (
        r.get("gain"), r.get("shift"), r.get("cot"), r.out("dec"), r.out("dy")
    )
    last_gain, last_shift = gain_ref[4:5, :], shift_ref[4:5, :]

    def fourth_norm(rows, sums):
        before = r.x3[rows, :] + r.acc[rows, :]
        normed, rate = normalize(before)
        dec_ref[rows, :] = (normed * last_gain + last_shift).astype(BF16)
        upstream = cot_ref[rows, :].astype(F32)
        scaled = upstream * last_gain
        mean_one = jnp.mean(scaled, axis=-1, keepdims=True)
        mean_two = jnp.mean(scaled * normed, axis=-1, keepdims=True)
        grad = rate * (scaled - mean_one - normed * mean_two)
        r.z4[rows, :] = grad
        dy_ref[rows, :] = grad.astype(BF16)
        return sums[0] + fold_rows(upstream * normed), sums[1] + fold_rows(upstream)

    zeros = jnp.zeros((8, x2_ref.shape[1]), F32)
    gain_four, shift_four = over_rows(own, 32, fourth_norm, (zeros, zeros))
    r.send("dec")
    r.send("dy")
    feed_backward(dy_ref, ups, downs, hs, (r.out("dh0"), r.out("dh1")), r.z4)
    r.send("dh0")
    r.send("dh1")
    gain_three, shift_three = norm_back(
        r, gain_ref[3:4, :], lambda rows: r.z3[rows, :], lambda rows: r.z4[rows, :], (r.dz, r.low)
    )
    norms = r.out("norms")
    norms[0:1, :] = gain_three
    norms[1:2, :] = jnp.sum(gain_four, axis=0, keepdims=True)
    norms[2:3, :] = shift_three
    norms[3:4, :] = jnp.sum(shift_four, axis=0, keepdims=True)
    branch = r.low[...]
    ots = (r.ot.at[:QUAD], r.ot.at[QUAD:])
    mixed_gradients(branch, ots, outs, r.do, r.delta)
    packs = pair_of_packs(r, CROSS_BITS)
    for g, (packed, mark) in enumerate(packs):
        pack(packed, mark, 3, as_unit(nn(ots[g][...], branch)))
        r.turn[quad(g), :] = r.k[g].T
    r.dk[...] = jnp.zeros(r.dk.shape, F32)
    r.dv[...] = jnp.zeros(r.dv.shape, F32)

    def back_scores(block, g, key_at, keys_width):
        rows = slice(block * BLOCK, (block + 1) * BLOCK)
        return backward_scores(g, rows, key_at, keys_width, masks, r.q.at[g], r.k.at[g], r.v.at[g], r.do)

    def back_sums(block, g, key_at, bias, scored, add):
        rows = slice(block * BLOCK, (block + 1) * BLOCK)
        backward_sums(
            g, rows, key_at, bias, scored, r.turn, r.lse.at[g], r.delta, r.dqt, r.dk, r.dv, add
        )

    ahead = back_scores(*tiles[0], spots[0], width)
    for i, (block, g) in enumerate(tiles):
        scored = ahead
        if i + 1 < len(tiles):
            ahead = back_scores(*tiles[i + 1], spots[tiles[i + 1][0]], width)
        back_sums(block, g, spots[block], r.bias[block], scored, False)
    for block in range(blocks):

        def extra_back(i, carry, block=block):
            key_at = aligned(i * BLOCK)
            bias = bias_for(r.marks, key_at, BLOCK, query_rows[block])
            for g in range(2):
                back_sums(block, g, key_at, bias, back_scores(block, g, key_at, BLOCK), True)
            return carry

        lax.fori_loop(*more[block], extra_back, 0)
    query_grad = (r.dqt[...] * SCALE).astype(BF16).T
    key_grad, value_grad = r.dk[...].astype(BF16), r.dv[...].astype(BF16)
    query_turned, enc_turned = x2_ref[...].astype(BF16).T, enc_ref[...].T
    for g in (1, 0):
        packed, mark = packs[g]
        pack(packed, mark, 0, nn(query_turned, query_grad[:, quad(g)]))
        pack(packed, mark, 1, nn(enc_turned, key_grad[:, quad(g)]))
        pack(packed, mark, 2, nn(enc_turned, value_grad[:, quad(g)]))
        r.send(f"pack{g}")
    r.dk[...] = sum(
        nt(grad[:, quad(g)], r.get(f"ckv{g}")[i]) for i, grad in enumerate((key_grad, value_grad)) for g in range(2)
    )
    r.out("denc_other")[...] = r.dk[pl.ds(second, own), :].astype(BF16)
    r.send("denc_other")
    r.out("denc_own")[...] = r.dk[pl.ds(first, own), :]
    r.send("denc_own")
    r.out("g2")[...] = r.dz[...] + sum(nt(query_grad[:, quad(g)], r.get(f"cq{g}")[...]) for g in range(2))


def pair_of_packs(r, bits, name="pack"):
    core, place = r.ids[0], r.ids[1]
    return [(r.out(f"{name}{g}"), own_label(bits, core ^ g, place)) for g in range(2)]


def head_gradients(r):
    for g in (1, 0):
        r.out(f"dq{g}")[...] = (r.dqt[quad(g), :] * SCALE).astype(BF16).T
        r.out(f"dk{g}")[...] = r.dk[:, quad(g)].astype(BF16)
        r.out(f"dv{g}")[...] = r.dv[:, quad(g)].astype(BF16)
        for key in ("dq", "dk", "dv"):
            r.send(f"{key}{g}")


def key_stream_gradient(r, weights, keys=("dk", "dv")):
    return sum(nt(r.get(f"{keys[i]}{g}")[...], weights[g][i]) for i in range(2) for g in range(2))


def feed_back_kernel(r):
    cot_ref, own_ref, recv_ref, z1_ref = r.get("cot"), r.get("denc_own"), r.get("denc_recv"), r.get("z1")
    acc_ref, ups, downs = r.out("g0"), pair_of_packs(r, UP_BITS, "up_pack"), pair_of_packs(r, DOWN_BITS, "down_pack")
    gain, shift = norm_back(
        r,
        r.get("gain")[1:2, :],
        lambda rows: z1_ref[rows, :],
        lambda rows: cot_ref[rows, :].astype(F32) + own_ref[rows, :] + recv_ref[rows, :].astype(F32),
        (acc_ref, r.dy),
    )
    r.out("norms")[0:1, :] = gain
    r.out("norms")[1:2, :] = shift
    turned = [ref[...].T for ref in (r.get("x1_low"), r.get("x3_low"), r.dy, r.get("dy3"))]
    chunks = [(g, j, cols) for g in (1, 0) for j, cols in feed_chunks(r.get("h0").shape[1])]

    def active_grad(i):
        g, j, cols = chunks[i]
        return nt(r.dy[...], r.get(f"down{g}")[cols, :])

    ahead = active_grad(0)
    for i, (g, j, cols) in enumerate(chunks):
        above = ahead
        if i + 1 < len(chunks):
            ahead = active_grad(i + 1)
        active, slope = gelu_both(r.get(f"h{g}")[:, cols].astype(F32))
        hidden_grad, active = (above * slope).astype(BF16), active.astype(BF16)
        acc_ref[...] += nt(hidden_grad, r.get(f"up{g}")[:, cols])
        up_grad = nn(turned[0], hidden_grad) + nn(turned[1], r.get(f"dh{g}")[:, cols])
        down_grad = nn(turned[2], active) + nn(turned[3], r.get(f"a{g}")[:, cols])
        for b in range(2):
            pack(*ups[g], 2 * j + b, up_grad[:, quad(b)])
            pack(*downs[g], 2 * j + b, down_grad[:, quad(b)])
        if j == 1:
            r.send(f"up_pack{g}")
            r.send(f"down_pack{g}")


def norm_parts(norms, r):
    feed, dec, cross = r.get("feed_norms"), r.get("dec_norms"), r.get("cross_norms")
    rows = [(norms, 0), (feed, 0), (dec, 0), (cross, 0), (cross, 1)]
    rows += [(norms, 1), (feed, 1), (dec, 1), (cross, 2), (cross, 3)]
    return [ref[at : at + 1, :] for ref, at in rows]


def self_back_kernel(causal, norm_at, bits, r):
    core, place = r.ids[0], r.ids[1]
    z_ref, up_ref, x_ref, row_ref = r.get("z"), r.get("up"), r.get("x"), r.get("row")
    tokens, own = x_ref.shape[0], z_ref.shape[0]
    window = r.marks.shape[0]
    start, first = aligned(core * (tokens - window)), aligned(core * own)
    spread_marks(r.marks, row_ref[:, pl.ds(start, window)])
    spots = set_self_bias(r.bias, core, tokens, r.marks, row_ref, causal)
    norms = r.out("norms")
    gain, shift = norm_back(
        r,
        r.get("gain")[norm_at : norm_at + 1, :],
        lambda rows: z_ref[rows, :],
        lambda rows: up_ref[rows, :],
        (r.out("dz"), r.low),
    )
    norms[0:1, :] = gain
    norms[1:2, :] = shift
    r.send("dz")
    branch = r.low[...]
    ots = (r.get("ot0"), r.get("ot1"))
    mixed_gradients(branch, ots, (r.get("wo0"), r.get("wo1")), r.do, r.delta)
    packs = pair_of_packs(r, bits)
    for g, (packed, mark) in enumerate(packs):
        pack(packed, mark, 3, as_unit(nn(ots[g][...], branch)))
        if not causal:
            pack_norms(packed, mark, norm_parts(norms, r))
    masks = head_masks()
    r.dk[...] = jnp.zeros(r.dk.shape, F32)
    r.dv[...] = jnp.zeros(r.dv.shape, F32)
    for g in range(2):
        r.kt[quad(g), :] = r.get(f"k{g}")[...].T
        for key in ("q", "v", "lse"):
            r.get(f"{key}{g}")
    tiles = [(block, g) for block in range(len(spots)) for g in range(2)]

    def back_scores(block, g):
        rows = slice(block * BLOCK, (block + 1) * BLOCK)
        return backward_scores(g, rows, *spots[block], masks, r.get(f"q{g}"), r.get(f"k{g}"), r.get(f"v{g}"), r.do)

    ahead = back_scores(*tiles[0])
    for i, (block, g) in enumerate(tiles):
        rows, (key_at, width) = slice(block * BLOCK, (block + 1) * BLOCK), spots[block]
        scored = ahead
        if i + 1 < len(tiles):
            ahead = back_scores(*tiles[i + 1])
        backward_sums(
            g, rows, key_at, r.bias[block, :width, :], scored, r.kt, r.get(f"lse{g}"), r.delta, r.dqt, r.dk, r.dv, False
        )
    head_gradients(r)
    keys_turned, query_turned = x_ref[pl.ds(start, window), :].T, x_ref[pl.ds(first, own), :].T
    for g in (1, 0):
        packed, mark = packs[g]
        pack(packed, mark, 0, nn(query_turned, r.out(f"dq{g}")[...]))
        pack(packed, mark, 1, nn(keys_turned, r.out(f"dk{g}")[...]))
        pack(packed, mark, 2, nn(keys_turned, r.out(f"dv{g}")[...]))
        r.send(f"pack{g}")


def stream_gradient_kernel(r):
    core = r.ids[0]
    dz_ref, own, window = r.get("dz"), r.get("dq0").shape[0], r.get("dk0").shape[0]
    w = (r.get("w0"), r.get("w1"))
    r.near[...] = key_stream_gradient(r, [(w[g][1], w[g][2]) for g in range(2)])
    r.out("halo")[...] = r.near[pl.ds(aligned((1 - core) * own), window - own), :].astype(BF16)
    r.send("halo")
    r.out("dx")[...] = (
        dz_ref[...]
        + sum(nt(r.get(f"dq{g}")[...], w[g][0]) for g in range(2))
        + r.near[pl.ds(aligned(core * (window - own)), own), :]
    )


class Refs:
    def __init__(self, smem, ins, outs, scratch):
        for name, ref in list(smem.items()) + list(scratch.items()):
            setattr(self, name, ref)
        self.ins, self.outs = ins, outs
        self.waited, self.sent = set(), set()
        for copy, ref in ins.values():
            copy.start()

    def get(self, name):
        copy, ref = self.ins[name]
        if name not in self.waited:
            self.waited.add(name)
            copy.wait()
        return ref

    def out(self, name):
        return self.outs[name][1]

    def send(self, name):
        self.sent.add(name)
        self.outs[name][0].start()

    def close(self):
        for name in self.ins:
            self.get(name)
        for name in self.outs:
            if name not in self.sent:
                self.send(name)
        for copy, ref in self.outs.values():
            copy.wait()


def call(kernel, name, smem, ins, outs, scratch, cost):
    n_smem, n_in, n_out, n_scratch = len(smem), len(ins), len(outs), len(scratch)

    def body(*refs):
        smem_refs = refs[:n_smem]
        refs = refs[n_smem:]
        in_refs, out_refs, refs = refs[:n_in], refs[n_in : n_in + n_out], refs[n_in + n_out :]
        in_vmem, out_vmem, refs = refs[:n_in], refs[n_in : n_in + n_out], refs[n_in + n_out :]
        in_sem, out_sem = refs[-2:]
        copies_in = {
            key: (pltpu.make_async_copy(in_refs[i], in_vmem[i], in_sem.at[i]), in_vmem[i])
            for i, key in enumerate(ins)
        }
        copies_out = {
            key: (pltpu.make_async_copy(out_vmem[i], out_refs[i], out_sem.at[i]), out_vmem[i])
            for i, key in enumerate(outs)
        }
        held = Refs(dict(zip(smem, smem_refs)), copies_in, copies_out, dict(zip(scratch, refs)))
        kernel(held)
        held.close()

    results = pl.pallas_call(
        body,
        out_shape=[jax.ShapeDtypeStruct(*out) for out in outs.values()],
        in_specs=[pl.BlockSpec(memory_space=pltpu.SMEM)] * n_smem + [pl.BlockSpec(memory_space=pl.ANY)] * n_in,
        out_specs=[pl.BlockSpec(memory_space=pl.ANY)] * n_out,
        scratch_shapes=[pltpu.VMEM(array.shape, array.dtype) for array in ins.values()]
        + [pltpu.VMEM(*out) for out in outs.values()]
        + [pltpu.VMEM(*one) for one in scratch.values()]
        + [pltpu.SemaphoreType.DMA((n_in,)), pltpu.SemaphoreType.DMA((n_out,))],
        compiler_params=pltpu.CompilerParams(vmem_limit_bytes=VMEM_LIMIT),
        cost_estimate=pl.CostEstimate(flops=cost * 10**9, transcendentals=0, bytes_accessed=cost * 10**6),
        name=name,
    )(*smem.values(), *ins.values())
    return SimpleNamespace(**dict(zip(outs, results)))


def finish_kernel(kind, bits, ids_ref, *refs):
    mark = own_label(bits, ids_ref[0], ids_ref[1])
    gathered, sem = refs[-2:]
    n_outs = {"enc": 4, "dec": 2, "cross": 3, "up": 1, "down": 1}[kind]
    count = len(refs) - 2 - n_outs
    parts, outs = refs[:count], refs[count:-2]
    copies, at = [], 0
    for i, part in enumerate(parts):
        copies.append(pltpu.make_async_copy(part, gathered.at[pl.ds(at, part.shape[0])], sem.at[i]))
        at += part.shape[0]
    for copy in copies:
        copy.start()
    for copy in copies:
        copy.wait()
    for shard in range(SHARDS):
        unit, half = divmod(shard, 2)
        rows = slice(half * QUAD, (half + 1) * QUAD)
        where = pl.ds(mark ^ shard, 1)
        value = gathered[where, :QUAD, :][0].astype(F32)
        if kind == "up":
            outs[0][rows, quad(unit)] = value
        elif kind == "down":
            outs[0][quad(unit), rows] = value.T
        elif unit == 3:
            outs[2 if kind == "cross" else 1][:, quad(half)] = value
        elif kind != "cross":
            outs[0][unit, rows, :] = value
        elif unit == 0:
            outs[0][rows, :] = value
        else:
            outs[1][unit - 1, rows, :] = value
        if kind == "enc":
            norms = gathered[where, QUAD:, :][0].astype(F32)
            many = norm_rows(SHARDS)
            for i in range(many):
                row, side = divmod(shard * many + i, 2)
                if row < 10:
                    outs[2 + row // 5][row % 5 : row % 5 + 1, quad(side)] = norms[i : i + 1, :]


def finish(group, ids, outs):
    parts = group.parts
    shape = (SHARDS,) + parts[0].shape[1:]
    return pl.pallas_call(
        functools.partial(finish_kernel, group.kind, group.bits),
        out_shape=[jax.ShapeDtypeStruct(*out) for out in outs],
        in_specs=[pl.BlockSpec(memory_space=pltpu.SMEM)] + [pl.BlockSpec(memory_space=pl.ANY)] * len(parts),
        out_specs=[pl.BlockSpec(memory_space=pltpu.VMEM)] * len(outs),
        scratch_shapes=[pltpu.VMEM(shape, BF16), pltpu.SemaphoreType.DMA((len(parts),))],
        compiler_params=pltpu.CompilerParams(vmem_limit_bytes=VMEM_LIMIT),
        cost_estimate=pl.CostEstimate(flops=2 * 10**9, transcendentals=0, bytes_accessed=2 * 10**6),
        name="finish_" + group.kind,
    )(ids, *parts)


class Sum:
    def __init__(self, kind, bits, dp, mp, mine, other):
        self.kind, self.bits, self.dp, self.mp = kind, bits, dp, mp
        self.phase, self.parts, self.outgoing = -1, [mine], [other]

    def hop(self, array, step):
        pairs = []
        for place in range(self.dp):
            for core in range(self.mp):
                bit = self.bits[core][step] if step < 4 else step
                pairs.append((place * self.mp + core, (place ^ (1 << bit)) * self.mp + core))
        return lax.ppermute(array, ("dp", "mp"), pairs)

    def launch(self):
        if self.phase < 0:
            self.flying = [lax.ppermute(self.outgoing[0], "mp", [(0, 1), (1, 0)])]
        elif self.phase <= 3:
            self.flying = [self.hop(self.outgoing[0], self.last if self.phase == 3 else self.phase)]
        else:
            self.flying = [self.hop(part, 6 - self.phase) for part in self.outgoing]

    def add_up(self):
        self.phase += 1
        if self.phase <= 2:
            mine, sent = self.parts[0], self.flying[0]
            half = mine.shape[0] // 2
            self.outgoing, self.parts = [mine[half:] + sent[half:]], [mine[:half] + sent[:half]]
        elif self.phase == 3:
            part, self.last = self.parts[0] + self.flying[0], 3
            while 2 << self.last < self.dp:
                part = part + self.hop(part, self.last)
                self.last += 1
            self.parts = self.outgoing = [part]
        elif self.phase == 4:
            self.parts = self.outgoing = [self.parts[0] + self.flying[0]]
        else:
            self.parts = self.parts + self.flying
            if self.phase < 7:
                self.outgoing = self.parts if self.phase == 5 and self.kind == "enc" else [jnp.concatenate(self.parts)]
        self.flying = []


def boundary(before, after, landing, launching=()):
    before, after, landing, launching = list(before), list(after), list(landing), list(launching)
    before, landed = lax.optimization_barrier((before, [group.flying for group in landing]))
    for group, flying in zip(landing, landed):
        group.flying = flying
        group.add_up()
    moving = landing + launching
    states = [(group.parts, group.outgoing) for group in moving]
    before, after, states = lax.optimization_barrier((before, after, states))
    for group, state in zip(moving, states):
        group.parts, group.outgoing = list(state[0]), list(state[1])
        if group.phase < 7:
            group.launch()
    return before, after


def on_device(
    src_embed, tgt_embed, src_segment, tgt_segment, enc_qkv, enc_out_proj, dec_qkv, dec_out_proj, cross_query,
    cross_kv, cross_out_proj, ffn_up, ffn_down, norm_gain, norm_bias, enc_cotangent, dec_cotangent,
):
    dp, mp = lax.axis_size("dp"), lax.axis_size("mp")
    tokens, model = src_embed.shape
    own = tokens // mp
    window = own + MOST
    half = ffn_up.shape[1]
    hidden = 2 * half
    position = lax.axis_index("mp")
    ids = jnp.stack([position, lax.axis_index("dp")]).astype(jnp.int32)
    pairs = [(0, 1), (1, 0)]

    def swap(tree):
        return jax.tree.map(lambda a: lax.ppermute(a, "mp", pairs), tree)

    enc_w1, enc_o1 = swap((enc_qkv, enc_out_proj))
    up1, down1 = swap((ffn_up, ffn_down))
    dec_w1, dec_o1 = swap((dec_qkv, dec_out_proj))
    cross_q1, cross_kv1, cross_o1 = swap((cross_query, cross_kv, cross_out_proj))
    feed = {"up0": ffn_up, "up1": up1, "down0": ffn_down, "down1": down1}

    def rows(count, dtype):
        return ((count, model), dtype)

    blocks = own // BLOCK
    q_shape, k_shape, ot_shape, lse_shape = ((own, QUAD), BF16), ((window, QUAD), BF16), ((QUAD, own), BF16), ((4, own), F32)
    vt_shape, marks, bias = ((QUAD, window), BF16), ((window, BLOCK), jnp.int32), ((blocks, 3 * BLOCK, BLOCK), F32)
    heads = {"q": q_shape, "k": k_shape, "v": k_shape, "ot": ot_shape, "lse": lse_shape}
    wide = ((own, half), BF16)
    norm_in = {"gain": norm_gain, "shift": norm_bias}
    first = call(
        own_heads_kernel, "own_heads", {"ids": ids},
        {"src_row": src_segment, "src": src_embed, "src_w": enc_qkv,
         "tgt_row": tgt_segment, "tgt": tgt_embed, "tgt_w": dec_qkv},
        {f"{side}_{key}": shape for side in ("src", "tgt") for key, shape in heads.items()},
        {"marks": marks, "src_bias": bias, "tgt_bias": bias, "src_vt": vt_shape, "tgt_vt": vt_shape},
        cost=8,
    )
    encoder = call(
        encoder_kernel, "encoder_forward", {"ids": ids},
        {"row": src_segment, "x": src_embed, "w": enc_w1, "ot0": first.src_ot, "wo0": enc_out_proj, "wo1": enc_o1,
         **norm_in, "up0": ffn_up, "down0": ffn_down, "up1": up1, "down1": down1},
        {**heads, "z0": rows(own, F32), "x1_low": rows(own, BF16), "h0": wide, "h1": wide,
         "z1": rows(own, F32), "enc": rows(own, BF16)},
        {"marks": marks, "bias": bias, "vt": vt_shape, "x1": rows(own, F32), "acc": rows(own, F32)},
        cost=12,
    )
    enc_swapped = swap(encoder.enc)
    decoder = call(
        decoder_kernel, "decoder_self_forward", {"ids": ids},
        {"row": tgt_segment, "x": tgt_embed, "w": dec_w1, "ot0": first.tgt_ot, "wo0": dec_out_proj, "wo1": dec_o1,
         **norm_in},
        {**heads, "z2": rows(own, F32), "x2": rows(own, F32)},
        {"marks": marks, "bias": bias, "vt": vt_shape, "acc": rows(own, F32)}, cost=6,
    )
    packed = ((SHARDS, QUAD, QUAD), BF16)
    packed_norms = ((SHARDS, QUAD + TILE, QUAD), BF16)
    crossed = call(
        cross_kernel, "cross_and_decoder_feed",
        {"ids": ids, "src_marks": src_segment, "tgt_marks": tgt_segment},
        {"src_row": src_segment, "tgt_row": tgt_segment, "enc_own": encoder.enc, "enc_other": enc_swapped,
         "x2": decoder.x2, "cq0": cross_query, "ckv0": cross_kv, "cq1": cross_q1, "ckv1": cross_kv1,
         "co0": cross_out_proj, "co1": cross_o1, **norm_in, **feed, "cot": dec_cotangent},
        {"enc": rows(tokens, BF16), "x3_low": rows(own, BF16), "a0": wide, "a1": wide, "dec": rows(own, BF16),
         "dy": rows(own, BF16), "dh0": wide, "dh1": wide, "norms": rows(4, F32), "pack0": packed, "pack1": packed,
         "denc_other": rows(own, BF16), "denc_own": rows(own, F32), "g2": rows(own, F32)},
        {"marks": ((tokens, BLOCK), jnp.int32), "bias": bias, "q": ((2, own, QUAD), BF16),
         "k": ((2, tokens, QUAD), BF16), "v": ((2, tokens, QUAD), BF16), "turn": ((model, tokens), BF16),
         "mix": ((model, own), F32), "tops": ((8, own), F32), "totals": ((8, own), F32), "lse": ((2, 4, own), F32),
         "ot": ((model, own), BF16), "acc": rows(own, F32), "x3": rows(own, F32), "z3": rows(own, F32),
         "z4": rows(own, F32), "dz": rows(own, F32), "h": ((2, own, half), F32), "low": rows(own, BF16), "do": rows(own, BF16),
         "delta": ((8, own), F32), "dqt": ((model, own), F32), "dk": rows(tokens, F32), "dv": rows(tokens, F32)},
        cost=30,
    )
    def whole(mine, received):
        return jnp.where(
            position == 0, jnp.concatenate([mine, received]), jnp.concatenate([received, mine])
        )

    def group(kind, bits, mine, other):
        return Sum(kind, bits, dp, mp, mine, other)

    def self_backward(causal, at, bits, name, side, x, row, z, up, w0, w1, o0, o1, others, pack_shape, more):
        ins = {"z": z, "up": up, "gain": norm_gain, "row": row, "x": x}
        ins |= {"ot0": getattr(first, side + "_ot"), "ot1": others.ot, "wo0": o0, "wo1": o1}
        for key in ("k", "q", "v", "lse"):
            ins |= {key + "0": getattr(first, f"{side}_{key}"), key + "1": getattr(others, key)}
        return call(
            functools.partial(self_back_kernel, causal, at, bits), name, {"ids": ids}, ins | more,
            {"dz": rows(own, F32), "pack0": pack_shape, "pack1": pack_shape, "norms": rows(2, F32), "dq0": q_shape,
             "dq1": q_shape, "dk0": k_shape, "dk1": k_shape, "dv0": k_shape, "dv1": k_shape},
            {"marks": marks, "bias": bias, "low": rows(own, BF16), "do": rows(own, BF16), "delta": ((8, own), F32),
             "kt": ((model, window), BF16), "dqt": ((model, own), F32), "dk": rows(window, F32), "dv": rows(window, F32)},
            cost=13,
        )

    def stream_gradient(name, back, w0, w1, gate):
        ins = {"dz": gate, "w0": w0, "w1": w1}
        ins |= {f"{key}{g}": getattr(back, f"{key}{g}") for key in ("dk", "dv", "dq") for g in range(2)}
        return call(
            stream_gradient_kernel, name, {"ids": ids}, ins,
            {"halo": rows(window - own, BF16), "dx": rows(own, F32)}, {"near": rows(window, F32)}, cost=3,
        )

    halo_at = (1 - position) * (own - (window - own))

    def with_halo(grad, received):
        part = lax.dynamic_slice_in_dim(grad, halo_at, window - own, 0) + received.astype(F32)
        return lax.dynamic_update_slice_in_dim(grad, part, halo_at, 0)

    square, out_half, triple = ((model, QUAD), F32), ((QUAD, model), F32), ((3, model, QUAD), F32)
    out_shapes = {
        "cross": [square, ((2, model, QUAD), F32), out_half],
        "dec": [triple, out_half],
        "up": [((model, half), F32)],
        "down": [rows(half, F32)],
        "enc": [triple, out_half, rows(5, F32), rows(5, F32)],
    }
    cross_sum = group("cross", CROSS_BITS, crossed.pack0, crossed.pack1)
    cross_sum.launch()
    denc_recv = swap(crossed.denc_other)
    (cross_norms,), (z1, denc_recv) = boundary([crossed.norms], [encoder.z1, denc_recv], [cross_sum])
    fed = call(
        feed_back_kernel, "encoder_feed_backward", {"ids": ids},
        {"cot": enc_cotangent, "denc_own": crossed.denc_own, "denc_recv": denc_recv, "z1": z1, "gain": norm_gain,
         "x1_low": encoder.x1_low, "x3_low": crossed.x3_low, "dy3": crossed.dy, "h0": encoder.h0, "down1": down1,
         "h1": encoder.h1, "up1": up1, "dh1": crossed.dh1, "a1": crossed.a1, "down0": ffn_down, "up0": ffn_up,
         "dh0": crossed.dh0, "a0": crossed.a0},
        {"norms": rows(2, F32), "up_pack0": packed, "up_pack1": packed, "down_pack0": packed, "down_pack1": packed,
         "g0": rows(own, F32)},
        {"dy": rows(own, BF16)}, cost=17,
    )
    up_sum = group("up", UP_BITS, fed.up_pack0, fed.up_pack1)
    down_sum = group("down", DOWN_BITS, fed.down_pack0, fed.down_pack1)
    (feed_norms,), () = boundary([fed.norms], [], [cross_sum], [up_sum, down_sum])
    (feed_norms,), (g2,) = boundary([feed_norms], [crossed.g2], [up_sum, down_sum])
    dec_back = self_backward(
        True, 2, DEC_BITS, "decoder_self_backward", "tgt", tgt_embed, tgt_segment, decoder.z2, g2,
        dec_qkv, dec_w1, dec_out_proj, dec_o1, decoder, packed, {},
    )
    dec_sum = group("dec", DEC_BITS, dec_back.pack0, dec_back.pack1)
    (dec_norms,), () = boundary([dec_back.norms], [], [cross_sum, up_sum, down_sum], [dec_sum])
    (dec_norms,), (g0,) = boundary([dec_norms], [fed.g0], [dec_sum])
    enc_back = self_backward(
        False, 0, ENC_BITS, "encoder_self_backward", "src", src_embed, src_segment, encoder.z0, g0,
        enc_qkv, enc_w1, enc_out_proj, enc_o1, encoder, packed_norms,
        {"feed_norms": feed_norms, "dec_norms": dec_norms, "cross_norms": cross_norms},
    )
    enc_sum = group("enc", ENC_BITS, enc_back.pack0, enc_back.pack1)
    (src_dz,), (src_dz_two,) = boundary(
        [enc_back.dz], [enc_back.dz], [cross_sum, up_sum, down_sum, dec_sum], [enc_sum]
    )
    src_side = stream_gradient("src_gradient", enc_back, enc_qkv, enc_w1, src_dz)
    (src_halo,), (tgt_dz,) = boundary([src_side.halo], [dec_back.dz], [enc_sum, cross_sum, up_sum, down_sum])
    tgt_side = stream_gradient("tgt_gradient", dec_back, dec_qkv, dec_w1, tgt_dz)
    (tgt_halo,), (dec_own, src_halo) = boundary(
        [tgt_side.halo], [crossed.dec, src_halo], [dec_sum, cross_sum, up_sum, down_sum]
    )
    src_recv, tgt_recv, dec_swapped = swap(src_halo), swap(tgt_halo), swap(dec_own)
    (dec_swapped,), () = boundary([dec_swapped], [], [enc_sum, cross_sum, up_sum])
    dec_whole = whole(crossed.dec, dec_swapped)
    (dec_whole,), (src_recv,) = boundary([dec_whole], [src_recv], [dec_sum, up_sum, enc_sum, down_sum])
    src_grad = with_halo(src_side.dx, src_recv)
    (src_grad,), (tgt_recv,) = boundary([src_grad], [tgt_recv], [cross_sum, down_sum, dec_sum])
    tgt_grad = with_halo(tgt_side.dx, tgt_recv)
    boundary([tgt_grad], [], [enc_sum, down_sum, dec_sum])
    cross_out = finish(cross_sum, ids, out_shapes["cross"])
    boundary([cross_out[0]], [], [up_sum, enc_sum, dec_sum])
    up_out = finish(up_sum, ids, out_shapes["up"])
    boundary([up_out[0]], [], [enc_sum, down_sum])
    boundary([], [], [enc_sum])
    down_out = finish(down_sum, ids, out_shapes["down"])
    boundary([down_out[0]], [], [dec_sum])
    dec_out = finish(dec_sum, ids, out_shapes["dec"])
    boundary([dec_out[0]], [], [enc_sum])
    enc_out = finish(enc_sum, ids, out_shapes["enc"])

    return (
        crossed.enc,
        dec_whole,
        src_grad,
        tgt_grad,
        enc_out[0],
        enc_out[1],
        dec_out[0],
        dec_out[1],
        cross_out[0],
        cross_out[1],
        cross_out[2],
        up_out[0],
        down_out[0],
        enc_out[2],
        enc_out[3],
    )


def solution(mesh):
    in_specs = (
        P("dp", None), P("dp", None), P("dp", None), P("dp", None),
        P(None, None, "mp"), P("mp", None), P(None, None, "mp"), P("mp", None),
        P(None, "mp"), P(None, None, "mp"), P("mp", None), P(None, "mp"), P("mp", None),
        P(), P(), P(("dp", "mp"), None), P(("dp", "mp"), None),
    )
    out_specs = (
        P("dp", None), P("dp", None), P(("dp", "mp"), None), P(("dp", "mp"), None),
        P(None, None, "mp"), P("mp", None), P(None, None, "mp"), P("mp", None),
        P(None, "mp"), P(None, None, "mp"), P("mp", None), P(None, "mp"), P("mp", None),
        P(), P(),
    )
    return jax.shard_map(on_device, mesh=mesh, in_specs=in_specs, out_specs=out_specs, check_vma=False)
```

```python
import functools
import math
from types import SimpleNamespace

import jax
import jax.numpy as jnp
from jax import lax
from jax.experimental import pallas as pl
from jax.experimental.pallas import tpu as pltpu
from jax.sharding import PartitionSpec as P

HDIM = 64
SCALE = HDIM ** (-0.5)
EPSILON = 1e-05
MASKED = -1e30
BLOCK = 128
MOST = 128
QUAD = 4 * HDIM
UNITS = 4
TILE = 16
FEED = 512
SHARDS = 8
UP_BITS = ((0, 1, 2, 3), (1, 0, 2, 3))
DOWN_BITS = ((1, 0, 2, 3), (0, 1, 2, 3))
CROSS_BITS = ((0, 1, 2, 3), (1, 0, 2, 3))
DEC_BITS = ((0, 1, 2, 3), (1, 0, 2, 3))
STRIDE = HDIM + TILE
ENC_BITS = ((1, 0, 2, 3), (0, 1, 2, 3))
F32 = jnp.float32
BF16 = jnp.bfloat16
VMEM_LIMIT = 56 * 1024 * 1024
GELU_IN = math.sqrt(2.0 / math.pi)
GELU_CUBE = 0.044715


def nn(left, right):
    return jnp.dot(left, right, preferred_element_type=F32)


def nt(left, right):
    return lax.dot_general(left, right, (((1,), (1,)), ((), ())), preferred_element_type=F32)


def tn(left, right):
    return lax.dot_general(left, right, (((0,), (0,)), ((), ())), preferred_element_type=F32)


def aligned(index, size=BLOCK):
    return pl.multiple_of(index, size)


def over_rows(rows, chunk, body, carry, unroll=4):
    return lax.fori_loop(
        0,
        rows // chunk,
        lambda i, kept: body(pl.ds(aligned(i * chunk, chunk), chunk), kept),
        carry,
        unroll=min(unroll, rows // chunk),
    )


def normalize(before):
    centered = before - jnp.mean(before, axis=-1, keepdims=True)
    variance = jnp.mean(centered * centered, axis=-1, keepdims=True)
    rate = lax.rsqrt(variance + EPSILON)
    return centered * rate, rate


def norm_backward(before, upstream, gain_row):
    normed, rate = normalize(before)
    scaled = upstream * gain_row
    first = jnp.mean(scaled, axis=-1, keepdims=True)
    second = jnp.mean(scaled * normed, axis=-1, keepdims=True)
    return rate * (scaled - first - normed * second), upstream * normed


def fold_rows(block):
    return jnp.sum(block.reshape(block.shape[0] // 8, 8, block.shape[1]), axis=0)


def gelu(hidden):
    inner = GELU_IN * hidden * (1.0 + GELU_CUBE * hidden * hidden)
    return 0.5 * hidden * (1.0 + jnp.tanh(inner))


def gelu_both(hidden):
    square = hidden * hidden
    bent = jnp.tanh(GELU_IN * hidden * (1.0 + GELU_CUBE * square))
    half = 0.5 * (1.0 + bent)
    slope = half + 0.5 * hidden * (1.0 - bent * bent) * (GELU_IN * (1.0 + 3.0 * GELU_CUBE * square))
    return hidden * half, slope


def head_masks():
    lane = lax.broadcasted_iota(jnp.int32, (1, QUAD), 1)
    return [
        jnp.where((lane >= h * HDIM) & (lane < (h + 1) * HDIM), 1.0, 0.0).astype(BF16)
        for h in range(4)
    ]


def stack_heads(block, masks):
    return jnp.concatenate([block * mask for mask in masks], axis=0)


def quad(g):
    return slice(g * QUAD, (g + 1) * QUAD)


def bias_for(marks_ref, key_at, width, query_row, causal=False, key_start=0, query_start=0):
    allowed = marks_ref[pl.ds(key_at, width), :] == query_row
    if causal:
        places = key_start + lax.broadcasted_iota(jnp.int32, (width, BLOCK), 0)
        queries = query_start + lax.broadcasted_iota(jnp.int32, (width, BLOCK), 1)
        allowed = allowed & (places <= queries)
    return jnp.where(allowed, 0.0, MASKED)


def self_window(core, block, causal):
    middle = block + core
    if causal:
        return aligned(jnp.maximum(middle - 1, 0) * BLOCK), 2 * BLOCK
    return aligned(jnp.clip(middle - 1, 0, 2) * BLOCK), 3 * BLOCK


def set_self_bias(bias_ref, core, tokens, marks_ref, row_ref, causal):
    window, own = marks_ref.shape[0], row_ref.shape[1] // 2
    start = core * (tokens - window)
    spots = []
    for block in range(own // BLOCK):
        key_at, width = self_window(core, block, causal)
        first = aligned(core * own + block * BLOCK)
        bias_ref[block, :width, :] = bias_for(
            marks_ref, key_at, width, row_ref[:, pl.ds(first, BLOCK)], causal, start + key_at, first
        )
        spots.append((key_at, width))
    return spots


def soft_weights(scores, h, bias, top=None):
    one = scores[:, h * BLOCK : (h + 1) * BLOCK] + bias
    high = jnp.max(one, axis=0, keepdims=True)
    top = high if top is None else jnp.maximum(top, high)
    return top, jnp.exp((one - top).astype(BF16))


def set_values(vt_ref, values):
    turned = values.T
    for h in range(4):
        vt_ref[h * STRIDE : h * STRIDE + HDIM, :] = turned[h * HDIM : (h + 1) * HDIM]
        vt_ref[h * STRIDE + HDIM : (h + 1) * STRIDE, :] = jnp.ones((TILE, turned.shape[1]), BF16)


def quad_forward(spots, q_ref, k_ref, vt_ref, bias_ref, ot_ref, lse_ref, masks):
    def score(block):
        rows, (key_at, width) = slice(block * BLOCK, (block + 1) * BLOCK), spots[block]
        return nt(k_ref[pl.ds(key_at, width), :], stack_heads(q_ref[rows, :], masks))

    ahead = score(0)
    for block, (key_at, width) in enumerate(spots):
        rows = slice(block * BLOCK, (block + 1) * BLOCK)
        scores, ahead = ahead, score(block + 1) if block + 1 < len(spots) else None
        for h in range(4):
            top, weights = soft_weights(scores, h, bias_ref[block, :width, :])
            features = slice(h * HDIM, (h + 1) * HDIM)
            mixed = nn(vt_ref[h * STRIDE : (h + 1) * STRIDE, pl.ds(key_at, width)], weights)
            total = mixed[HDIM : HDIM + 1]
            ot_ref[features, rows] = (mixed[:HDIM] * (1.0 / total)).astype(BF16)
            lse_ref[h : h + 1, rows] = top + jnp.log(total)


def backward_scores(rows, key_at, width, masks, q_ref, k_ref, v_ref, do_ref):
    keys = pl.ds(key_at, width)
    q_stack, do_stack = stack_heads(q_ref[rows, :], masks), stack_heads(do_ref[rows, :], masks)
    return q_stack, do_stack, nt(k_ref[keys, :], q_stack), nt(v_ref[keys, :], do_stack)


def backward_sums(rows, key_at, bias, scored, kt_ref, lse_ref, delta_ref, dqt_ref, dk_ref, dv_ref, add=False):
    q_stack, do_stack, scores, prob_grads = scored
    keys = pl.ds(key_at, bias.shape[0])
    probs, score_grads = [], []
    for h in range(4):
        cols = slice(h * BLOCK, (h + 1) * BLOCK)
        prob = jnp.exp((scores[:, cols] + bias - lse_ref[h : h + 1, rows]).astype(BF16))
        probs.append(prob)
        score_grads.append(prob * (prob_grads[:, cols] - delta_ref[h : h + 1, rows]).astype(BF16))
    for h in range(4):
        features = slice(h * HDIM, (h + 1) * HDIM)
        query_grad = nn(kt_ref[features, keys], score_grads[h])
        if add:
            dqt_ref[features, rows] += query_grad
        else:
            dqt_ref[features, rows] = query_grad
    dv_ref[keys, :] += nn(jnp.concatenate(probs, axis=1), do_stack)
    dk_ref[keys, :] += nn(jnp.concatenate(score_grads, axis=1), q_stack)


def mixed_gradients(branch, ot, w_out, do_ref, delta_ref):
    do_ref[...] = nt(branch, w_out).astype(BF16)
    product = nt(w_out, branch).astype(BF16).astype(F32) * ot.astype(F32)
    for h in range(4):
        delta_ref[h : h + 1, :] = jnp.sum(product[h * HDIM : (h + 1) * HDIM, :], axis=0, keepdims=True)


def spread_marks(marks_ref, row):
    marks_ref[...] = jnp.broadcast_to(row, (marks_ref.shape[1], marks_ref.shape[0])).T


def label(bits, place):
    first, second, third = [(place >> bit) & 1 for bit in bits[:3]]
    return 4 * first + 2 * second + third


def own_label(bits, core, place):
    return jnp.where(core == 0, label(bits[0], place), label(bits[1], place))


def pack(out_ref, mark, unit, value, at=0):
    rows = value.shape[0] // 2
    for half in range(2):
        where = pl.ds(mark ^ (2 * unit + half), 1)
        out_ref[where, at : at + rows, :] = value[half * rows : (half + 1) * rows].astype(BF16)[None]


def as_unit(value):
    return jnp.concatenate([value[:, :QUAD], value[:, QUAD:]], axis=0).astype(BF16)


def pack_norms(out_ref, mark, parts):
    shards, tall, width = out_ref.shape
    halves = [part[:, half * width : (half + 1) * width] for part in parts for half in range(2)]
    each = norm_rows(shards)
    blank = jnp.zeros((1, width), F32)
    halves += [blank] * (shards * each - len(halves))
    for i in range(shards):
        block = jnp.concatenate(halves[i * each : (i + 1) * each] + [blank] * (TILE - each), axis=0)
        out_ref[pl.ds(mark ^ i, 1), tall - TILE :, :] = block.astype(BF16)[None]


def norm_rows(shards):
    return -(-20 // shards)


def prepare_quad(x_ref, w_ref, core, q_ref, k_ref, v_ref, vt_ref):
    tokens, own, window = x_ref.shape[0], q_ref.shape[0], k_ref.shape[0]
    keys = x_ref[pl.ds(aligned(core * (tokens - window)), window), :]
    q_ref[...] = (nn(x_ref[pl.ds(aligned(core * own), own), :], w_ref[0]) * SCALE).astype(BF16)
    k_ref[...] = nn(keys, w_ref[1]).astype(BF16)
    v_ref[...] = nn(keys, w_ref[2]).astype(BF16)
    set_values(vt_ref, v_ref[...])


def own_heads_kernel(r):
    core = r.ids[0]
    masks = head_masks()
    for side, causal in (("src", False), ("tgt", True)):
        x_ref, row_ref = r.get(side), r.get(side + "_row")
        k_ref = r.out(side + "_k")
        start = aligned(core * (x_ref.shape[0] - k_ref.shape[0]))
        spread_marks(r.marks, row_ref[:, pl.ds(start, k_ref.shape[0])])
        bias_ref, vt_ref = getattr(r, side + "_bias"), getattr(r, side + "_vt")
        spots = set_self_bias(bias_ref, core, x_ref.shape[0], r.marks, row_ref, causal)
        q_ref, v_ref = r.out(side + "_q"), r.out(side + "_v")
        prepare_quad(x_ref, r.get(side + "_w"), core, q_ref, k_ref, v_ref, vt_ref)
        for key in ("_q", "_k", "_v"):
            r.send(side + key)
        quad_forward(
            spots, q_ref, k_ref, vt_ref, bias_ref, r.out(side + "_ot"), r.out(side + "_lse"), masks
        )
        r.send(side + "_ot")
        r.send(side + "_lse")


def other_heads(r, causal):
    core = r.ids[0]
    x_ref, row_ref, k_ref = r.get("x"), r.get("row"), r.out("k")
    start = aligned(core * (x_ref.shape[0] - k_ref.shape[0]))
    spread_marks(r.marks, row_ref[:, pl.ds(start, k_ref.shape[0])])
    spots = set_self_bias(r.bias, core, x_ref.shape[0], r.marks, row_ref, causal)
    q_ref, v_ref, ot_ref = r.out("q"), r.out("v"), r.out("ot")
    prepare_quad(x_ref, r.get("w"), core, q_ref, k_ref, v_ref, r.vt)
    for key in ("q", "k", "v"):
        r.send(key)
    quad_forward(spots, q_ref, k_ref, r.vt, r.bias, ot_ref, r.out("lse"), head_masks())
    r.send("lse")
    r.send("ot")
    r.acc[...] = tn(r.get("ot0")[...], r.get("wo0")[...]) + tn(ot_ref[...], r.get("wo1")[...])


def norm_forward(r, at, residual, before_ref, after_ref, low_ref):
    gain, shift = r.get("gain")[at : at + 1, :], r.get("shift")[at : at + 1, :]

    def body(rows, carry):
        before = residual(rows) + r.acc[rows, :]
        if before_ref is not None:
            before_ref[rows, :] = before
        after = normalize(before)[0] * gain + shift
        if after_ref is not None:
            after_ref[rows, :] = after
        if low_ref is not None:
            low_ref[rows, :] = after.astype(BF16)
        return carry

    over_rows(r.acc.shape[0], 32, body, 0)


def own_row_reader(x_ref, core, own):
    first = core * own
    return lambda rows: x_ref[pl.ds(aligned(first + rows.start, rows.size), rows.size), :].astype(F32)


def encoder_kernel(r):
    other_heads(r, False)
    x1_low = r.out("x1_low")
    norm_forward(r, 0, own_row_reader(r.get("x"), r.ids[0], r.acc.shape[0]), r.out("z0"), r.x1, x1_low)
    r.send("z0")
    r.send("x1_low")
    feed_forward(x1_low, *feed_weights(r), (r.out("h0"), r.out("h1")), None, r.acc)
    r.send("h0")
    r.send("h1")
    norm_forward(r, 1, lambda rows: r.x1[rows, :], r.out("z1"), None, r.out("enc"))


def decoder_kernel(r):
    other_heads(r, True)
    norm_forward(r, 2, own_row_reader(r.get("x"), r.ids[0], r.acc.shape[0]), r.out("z2"), r.out("x2"), None)


def feed_weights(r):
    return (r.get("up0"), r.get("up1")), (r.get("down0"), r.get("down1"))


def feed_chunks(half):
    return [(j, slice(j * FEED, (j + 1) * FEED)) for j in range(half // FEED)]


def feed_forward(low_ref, ups, downs, h_refs, a_refs, acc_ref):
    chunks = [(g, cols) for g in range(2) for j, cols in feed_chunks(ups[0].shape[1])]
    ahead = nn(low_ref[...], ups[0][:, chunks[0][1]])
    for i, (g, cols) in enumerate(chunks):
        hidden = ahead
        if i + 1 < len(chunks):
            ahead = nn(low_ref[...], ups[chunks[i + 1][0]][:, chunks[i + 1][1]])
        hidden = hidden.astype(BF16)
        h_refs[g][:, cols] = hidden
        active = gelu(hidden)
        if a_refs is not None:
            a_refs[g][:, cols] = active
        term = nn(active, downs[g][cols, :])
        if i == 0:
            acc_ref[...] = term
        else:
            acc_ref[...] += term


def feed_backward(dy_ref, ups, downs, h_refs, dh_refs, acc_ref):
    chunks = [(g, cols) for g in range(2) for j, cols in feed_chunks(ups[0].shape[1])]
    ahead = nt(dy_ref[...], downs[0][chunks[0][1], :])
    for i, (g, cols) in enumerate(chunks):
        active_grad = ahead
        if i + 1 < len(chunks):
            ahead = nt(dy_ref[...], downs[chunks[i + 1][0]][chunks[i + 1][1], :])
        hidden_grad = active_grad.astype(BF16) * gelu_both(h_refs[g][:, cols])[1]
        dh_refs[g][:, cols] = hidden_grad
        acc_ref[...] += nt(hidden_grad, ups[g][:, cols])


def norm_back(r, gain_row, before, upstream, outs):
    def body(rows, sums):
        above = upstream(rows)
        grad, gain_terms = norm_backward(before(rows), above, gain_row)
        for ref in outs:
            ref[rows, :] = grad.astype(ref.dtype)
        return sums[0] + fold_rows(gain_terms), sums[1] + fold_rows(above)

    zeros = jnp.zeros((8, outs[0].shape[1]), F32)
    gains, shifts = over_rows(outs[0].shape[0], 32, body, (zeros, zeros))
    return jnp.sum(gains, axis=0, keepdims=True), jnp.sum(shifts, axis=0, keepdims=True)


def cross_kernel(r):
    core, place = r.ids[0], r.ids[1]
    x2_ref, enc_ref = r.get("x2"), r.out("enc")
    own, tokens = x2_ref.shape[0], enc_ref.shape[0]
    blocks = own // BLOCK
    first, second = aligned(core * own), aligned((1 - core) * own)
    width = 3 * BLOCK
    enc_ref[pl.ds(first, own), :] = r.get("enc_own")[...]
    enc_ref[pl.ds(second, own), :] = r.get("enc_other")[...]
    r.send("enc")
    spread_marks(r.marks, r.get("src_row")[...])
    steps = tokens.bit_length()

    def bound(mark, past):
        def step(i, pair):
            low, high = pair
            middle = (low + high) // 2
            value = r.src_marks[0, jnp.minimum(middle, tokens - 1)]
            below = (low < high) & ((value < mark) | (past & (value == mark)))
            above = (low < high) & jnp.logical_not(below)
            return jnp.where(below, middle + 1, low), jnp.where(above, middle, high)

        return lax.fori_loop(0, steps, step, (jnp.int32(0), jnp.int32(tokens)))[0]

    row_ref = r.get("tgt_row")
    query_rows, spots, more = [], [], []
    for block in range(blocks):
        head = first + block * BLOCK
        low = bound(r.tgt_marks[0, head], jnp.bool_(False)) // BLOCK
        high = (bound(r.tgt_marks[0, head + BLOCK - 1], jnp.bool_(True)) + BLOCK - 1) // BLOCK
        key_at = aligned(jnp.minimum(low, (tokens - width) // BLOCK) * BLOCK)
        query_rows.append(row_ref[:, pl.ds(aligned(head), BLOCK)])
        spots.append(key_at)
        more.append((key_at // BLOCK + 3, high))
        r.bias[block] = bias_for(r.marks, key_at, width, query_rows[block])
    masks = head_masks()
    x2_low = x2_ref[...].astype(BF16)
    for g in range(2):
        r.q[g] = (nn(x2_low, r.get(f"cq{g}")[...]) * SCALE).astype(BF16)
        r.k[g] = nn(enc_ref[...], r.get(f"ckv{g}")[0]).astype(BF16)
        r.v[g] = nn(enc_ref[...], r.get(f"ckv{g}")[1]).astype(BF16)
        set_values(r.vt.at[g], r.v[g])

    def weigh(g, h, scores, bias, key_at, keys_width, top):
        new_top, weights = soft_weights(scores, h, bias, top)
        mixed = nn(r.vt[g, h * STRIDE : (h + 1) * STRIDE, pl.ds(key_at, keys_width)], weights)
        features = slice(g * QUAD + h * HDIM, g * QUAD + (h + 1) * HDIM)
        return new_top, mixed[HDIM : HDIM + 1], mixed[:HDIM], features

    def score(block, g):
        rows = slice(block * BLOCK, (block + 1) * BLOCK)
        return nt(r.k[g, pl.ds(spots[block], width), :], stack_heads(r.q[g, rows, :], masks))

    tiles = [(block, g) for block in range(blocks) for g in range(2)]
    ahead = score(*tiles[0])
    for i, (block, g) in enumerate(tiles):
        rows = slice(block * BLOCK, (block + 1) * BLOCK)
        scores, ahead = ahead, score(*tiles[i + 1]) if i + 1 < len(tiles) else None
        for h in range(4):
            top, total, mixed, features = weigh(g, h, scores, r.bias[block], spots[block], width, None)
            r.mix[features, rows] = mixed
            r.tops[g * 4 + h : g * 4 + h + 1, rows] = top
            r.totals[g * 4 + h : g * 4 + h + 1, rows] = total

    for block in range(blocks):
        rows = slice(block * BLOCK, (block + 1) * BLOCK)

        def extra(i, carry, block=block, rows=rows):
            key_at = aligned(i * BLOCK)
            bias = bias_for(r.marks, key_at, BLOCK, query_rows[block])
            for g in range(2):
                scores = nt(r.k[g, pl.ds(key_at, BLOCK), :], stack_heads(r.q[g, rows, :], masks))
                for h in range(4):
                    at = slice(g * 4 + h, g * 4 + h + 1)
                    old = r.tops[at, rows]
                    top, total, mixed, features = weigh(g, h, scores, bias, key_at, BLOCK, old)
                    fade = jnp.exp(old - top)
                    r.mix[features, rows] = r.mix[features, rows] * fade + mixed
                    r.tops[at, rows] = top
                    r.totals[at, rows] = r.totals[at, rows] * fade + total
            return carry

        lax.fori_loop(*more[block], extra, 0)
    for head in range(8):
        features = slice(head * HDIM, (head + 1) * HDIM)
        at = slice(head, head + 1)
        r.ot[features, :] = (r.mix[features, :] * (1.0 / r.totals[at, :])).astype(BF16)
        r.lse[head // 4, head % 4 : head % 4 + 1, :] = r.tops[at, :] + jnp.log(r.totals[at, :])
    outs = (r.get("co0"), r.get("co1"))
    r.acc[...] = tn(r.ot[:QUAD, :], outs[0][...]) + tn(r.ot[QUAD:, :], outs[1][...])
    x3_low = r.out("x3_low")
    norm_forward(r, 3, lambda rows: x2_ref[rows, :], r.z3, r.x3, x3_low)
    r.send("x3_low")
    ups, downs = feed_weights(r)
    hs = (r.h.at[0], r.h.at[1])
    feed_forward(x3_low, ups, downs, hs, (r.out("a0"), r.out("a1")), r.acc)
    r.send("a0")
    r.send("a1")
    gain_ref, shift_ref, cot_ref, dec_ref, dy_ref = (
        r.get("gain"), r.get("shift"), r.get("cot"), r.out("dec"), r.out("dy")
    )
    last_gain, last_shift = gain_ref[4:5, :], shift_ref[4:5, :]

    def fourth_norm(rows, sums):
        before = r.x3[rows, :] + r.acc[rows, :]
        normed, rate = normalize(before)
        dec_ref[rows, :] = (normed * last_gain + last_shift).astype(BF16)
        upstream = cot_ref[rows, :].astype(F32)
        scaled = upstream * last_gain
        mean_one = jnp.mean(scaled, axis=-1, keepdims=True)
        mean_two = jnp.mean(scaled * normed, axis=-1, keepdims=True)
        grad = rate * (scaled - mean_one - normed * mean_two)
        r.z4[rows, :] = grad
        dy_ref[rows, :] = grad.astype(BF16)
        return sums[0] + fold_rows(upstream * normed), sums[1] + fold_rows(upstream)

    zeros = jnp.zeros((8, x2_ref.shape[1]), F32)
    gain_four, shift_four = over_rows(own, 32, fourth_norm, (zeros, zeros))
    r.send("dec")
    r.send("dy")
    feed_backward(dy_ref, ups, downs, hs, (r.out("dh0"), r.out("dh1")), r.z4)
    r.send("dh0")
    r.send("dh1")
    gain_three, shift_three = norm_back(
        r, gain_ref[3:4, :], lambda rows: r.z3[rows, :], lambda rows: r.z4[rows, :], (r.dz, r.low)
    )
    norms = r.out("norms")
    norms[0:1, :] = gain_three
    norms[1:2, :] = jnp.sum(gain_four, axis=0, keepdims=True)
    norms[2:3, :] = shift_three
    norms[3:4, :] = jnp.sum(shift_four, axis=0, keepdims=True)
    branch = r.low[...]
    ots = (r.ot.at[:QUAD], r.ot.at[QUAD:])
    for g in range(2):
        mixed_gradients(branch, ots[g][...], outs[g][...], r.do.at[g], r.delta.at[g])
    packs = pair_of_packs(r, CROSS_BITS)
    for g, (packed, mark) in enumerate(packs):
        pack(packed, mark, 3, as_unit(nn(ots[g][...], branch)))
        r.turn[g] = r.k[g].T
    r.dk[...] = jnp.zeros(r.dk.shape, F32)
    r.dv[...] = jnp.zeros(r.dv.shape, F32)

    def back_scores(block, g, key_at, keys_width):
        rows = slice(block * BLOCK, (block + 1) * BLOCK)
        return backward_scores(rows, key_at, keys_width, masks, r.q.at[g], r.k.at[g], r.v.at[g], r.do.at[g])

    def back_sums(block, g, key_at, bias, scored, add):
        backward_sums(
            slice(block * BLOCK, (block + 1) * BLOCK), key_at, bias, scored, r.turn.at[g], r.lse.at[g], r.delta.at[g],
            r.dqt.at[g], r.dk.at[g], r.dv.at[g], add,
        )

    ahead = back_scores(*tiles[0], spots[0], width)
    for i, (block, g) in enumerate(tiles):
        scored = ahead
        if i + 1 < len(tiles):
            ahead = back_scores(*tiles[i + 1], spots[tiles[i + 1][0]], width)
        back_sums(block, g, spots[block], r.bias[block], scored, False)
    for block in range(blocks):

        def extra_back(i, carry, block=block):
            key_at = aligned(i * BLOCK)
            bias = bias_for(r.marks, key_at, BLOCK, query_rows[block])
            for g in range(2):
                back_sums(block, g, key_at, bias, back_scores(block, g, key_at, BLOCK), True)
            return carry

        lax.fori_loop(*more[block], extra_back, 0)
    query_turned, enc_turned = x2_ref[...].astype(BF16).T, enc_ref[...].T
    query_grads = [(r.dqt[g] * SCALE).astype(BF16).T for g in range(2)]
    side_grads = [(r.dk[g].astype(BF16), r.dv[g].astype(BF16)) for g in range(2)]
    for g in (1, 0):
        packed, mark = packs[g]
        pack(packed, mark, 0, nn(query_turned, query_grads[g]))
        for i in range(2):
            pack(packed, mark, 1 + i, nn(enc_turned, side_grads[g][i]))
        r.send(f"pack{g}")
    r.denc[...] = sum(nt(side_grads[g][i], r.get(f"ckv{g}")[i]) for i in range(2) for g in range(2))
    r.out("denc_other")[...] = r.denc[pl.ds(second, own), :].astype(BF16)
    r.send("denc_other")
    r.out("denc_own")[...] = r.denc[pl.ds(first, own), :]
    r.send("denc_own")
    r.out("g2")[...] = r.dz[...] + sum(nt(query_grads[g], r.get(f"cq{g}")[...]) for g in range(2))


def pair_of_packs(r, bits, name="pack"):
    core, place = r.ids[0], r.ids[1]
    return [(r.out(f"{name}{g}"), own_label(bits, core ^ g, place)) for g in range(2)]


def key_stream_gradient(r, weights, keys=("dk", "dv")):
    return sum(nt(r.get(f"{keys[i]}{g}")[...], weights[g][i]) for i in range(2) for g in range(2))


def feed_gradients(r, g, dy_ref, acc_ref, turned):
    core, place = r.ids[0], r.ids[1]
    up_mark, down_mark = own_label(UP_BITS, core ^ g, place), own_label(DOWN_BITS, core ^ g, place)
    h_ref, dh_ref, a_ref, up_ref, down_ref = [r.get(key) for key in ("h", "dh", "a", "up", "down")]
    chunks = feed_chunks(h_ref.shape[1])
    ahead = nt(dy_ref[...], down_ref[chunks[0][1], :])
    for j, cols in chunks:
        above = ahead
        if j + 1 < len(chunks):
            ahead = nt(dy_ref[...], down_ref[chunks[j + 1][1], :])
        active, slope = gelu_both(h_ref[:, cols])
        hidden_grad = above.astype(BF16) * slope
        acc_ref[...] += nt(hidden_grad, up_ref[:, cols])
        up_grad = nn(turned[0], hidden_grad) + nn(turned[1], dh_ref[:, cols])
        down_grad = nn(turned[2], active) + nn(turned[3], a_ref[:, cols])
        for b in range(2):
            pack(r.out("up_pack"), up_mark, 2 * j + b, up_grad[:, quad(b)])
            pack(r.out("down_pack"), down_mark, 2 * j + b, down_grad[:, quad(b)])


def feed_other_kernel(r):
    cot_ref, own_ref, recv_ref, z1_ref = r.get("cot"), r.get("denc_own"), r.get("denc_recv"), r.get("z1")
    dy_ref, acc_ref, turned = r.out("dy"), r.out("g0"), r.out("turned")
    gain, shift = norm_back(
        r,
        r.get("gain")[1:2, :],
        lambda rows: z1_ref[rows, :],
        lambda rows: cot_ref[rows, :].astype(F32) + own_ref[rows, :] + recv_ref[rows, :].astype(F32),
        (acc_ref, dy_ref),
    )
    r.out("norms")[0:1, :] = gain
    r.out("norms")[1:2, :] = shift
    r.send("dy")
    for i, ref in enumerate((r.get("x1_low"), r.get("x3_low"), dy_ref, r.get("dy3"))):
        turned[i] = ref[...].T
    r.send("turned")
    feed_gradients(r, 1, dy_ref, acc_ref, turned)


def feed_own_kernel(r):
    acc_ref = r.out("g0")
    acc_ref[...] = r.get("dz")[...]
    feed_gradients(r, 0, r.get("dy"), acc_ref, r.get("turned"))


def norm_parts(norms, r):
    feed, dec, cross = r.get("feed_norms"), r.get("dec_norms"), r.get("cross_norms")
    rows = [(norms, 0), (feed, 0), (dec, 0), (cross, 0), (cross, 1)]
    rows += [(norms, 1), (feed, 1), (dec, 1), (cross, 2), (cross, 3)]
    return [ref[at : at + 1, :] for ref, at in rows]


def self_back_heads(r, causal, bits, g, branch, norms, keys_turned, query_turned):
    core, place = r.ids[0], r.ids[1]
    row_ref, window = r.get("row"), r.marks.shape[0]
    tokens = row_ref.shape[1]
    spread_marks(r.marks, row_ref[:, pl.ds(aligned(core * (tokens - window)), window)])
    spots = set_self_bias(r.bias, core, tokens, r.marks, row_ref, causal)
    ot_ref = r.get("ot")
    mixed_gradients(branch, ot_ref[...], r.get("wo")[...], r.do, r.delta)
    packed, mark = r.out("pack"), own_label(bits, core ^ g, place)
    pack(packed, mark, 3, as_unit(nn(ot_ref[...], branch)))
    if not causal:
        pack_norms(packed, mark, norm_parts(norms, r))
    r.dk[...] = jnp.zeros(r.dk.shape, F32)
    r.dv[...] = jnp.zeros(r.dv.shape, F32)
    q_ref, k_ref, v_ref, lse_ref = r.get("q"), r.get("k"), r.get("v"), r.get("lse")
    r.kt[...] = k_ref[...].T
    masks = head_masks()

    def scored(block):
        rows = slice(block * BLOCK, (block + 1) * BLOCK)
        return backward_scores(rows, *spots[block], masks, q_ref, k_ref, v_ref, r.do)

    ahead = scored(0)
    for block, (key_at, width) in enumerate(spots):
        now = ahead
        if block + 1 < len(spots):
            ahead = scored(block + 1)
        backward_sums(
            slice(block * BLOCK, (block + 1) * BLOCK), key_at, r.bias[block, :width, :], now, r.kt, lse_ref, r.delta,
            r.dqt, r.dk, r.dv,
        )
    r.out("dq")[...] = (r.dqt[...] * SCALE).astype(BF16).T
    r.out("dk")[...] = r.dk[...].astype(BF16)
    r.out("dv")[...] = r.dv[...].astype(BF16)
    for key in ("dq", "dk", "dv"):
        r.send(key)
    pack(packed, mark, 0, nn(query_turned[...], r.out("dq")[...]))
    pack(packed, mark, 1, nn(keys_turned[...], r.out("dk")[...]))
    pack(packed, mark, 2, nn(keys_turned[...], r.out("dv")[...]))


def self_back_other_kernel(causal, norm_at, bits, r):
    core = r.ids[0]
    z_ref, up_ref, x_ref = r.get("z"), r.get("up"), r.get("x")
    tokens, own, window = x_ref.shape[0], z_ref.shape[0], r.marks.shape[0]
    norms, branch = r.out("norms"), r.out("branch")
    gain, shift = norm_back(
        r,
        r.get("gain")[norm_at : norm_at + 1, :],
        lambda rows: z_ref[rows, :],
        lambda rows: up_ref[rows, :],
        (r.out("dz"), branch),
    )
    norms[0:1, :] = gain
    norms[1:2, :] = shift
    for key in ("norms", "dz", "branch"):
        r.send(key)
    keys_turned, query_turned = r.out("keys_turned"), r.out("query_turned")
    keys_turned[...] = x_ref[pl.ds(aligned(core * (tokens - window)), window), :].T
    query_turned[...] = x_ref[pl.ds(aligned(core * own), own), :].T
    r.send("keys_turned")
    r.send("query_turned")
    self_back_heads(r, causal, bits, 1, branch[...], norms, keys_turned, query_turned)


def self_back_own_kernel(causal, bits, r):
    branch = r.get("branch")[...]
    norms = None if causal else r.get("norms")
    self_back_heads(r, causal, bits, 0, branch, norms, r.get("keys_turned"), r.get("query_turned"))


def stream_gradient_kernel(r):
    core = r.ids[0]
    dz_ref, own, window = r.get("dz"), r.get("dq0").shape[0], r.get("dk0").shape[0]
    w = (r.get("w0"), r.get("w1"))
    r.near[...] = key_stream_gradient(r, [(w[g][1], w[g][2]) for g in range(2)])
    r.out("halo")[...] = r.near[pl.ds(aligned((1 - core) * own), window - own), :].astype(BF16)
    r.send("halo")
    r.out("dx")[...] = (
        dz_ref[...]
        + sum(nt(r.get(f"dq{g}")[...], w[g][0]) for g in range(2))
        + r.near[pl.ds(aligned(core * (window - own)), own), :]
    )


class Refs:
    def __init__(self, smem, ins, outs, scratch):
        for name, ref in list(smem.items()) + list(scratch.items()):
            setattr(self, name, ref)
        self.ins, self.outs = ins, outs
        self.waited, self.sent = set(), set()
        for copy, ref in ins.values():
            copy.start()

    def get(self, name):
        copy, ref = self.ins[name]
        if name not in self.waited:
            self.waited.add(name)
            copy.wait()
        return ref

    def out(self, name):
        return self.outs[name][1]

    def send(self, name):
        self.sent.add(name)
        self.outs[name][0].start()

    def close(self):
        for name in self.ins:
            self.get(name)
        for name in self.outs:
            if name not in self.sent:
                self.send(name)
        for copy, ref in self.outs.values():
            copy.wait()


def call(kernel, name, smem, ins, outs, scratch, cost):
    n_smem, n_in, n_out, n_scratch = len(smem), len(ins), len(outs), len(scratch)

    def body(*refs):
        smem_refs = refs[:n_smem]
        refs = refs[n_smem:]
        in_refs, out_refs, refs = refs[:n_in], refs[n_in : n_in + n_out], refs[n_in + n_out :]
        in_vmem, out_vmem, refs = refs[:n_in], refs[n_in : n_in + n_out], refs[n_in + n_out :]
        in_sem, out_sem = refs[-2:]
        copies_in = {
            key: (pltpu.make_async_copy(in_refs[i], in_vmem[i], in_sem.at[i]), in_vmem[i])
            for i, key in enumerate(ins)
        }
        copies_out = {
            key: (pltpu.make_async_copy(out_vmem[i], out_refs[i], out_sem.at[i]), out_vmem[i])
            for i, key in enumerate(outs)
        }
        held = Refs(dict(zip(smem, smem_refs)), copies_in, copies_out, dict(zip(scratch, refs)))
        kernel(held)
        held.close()

    results = pl.pallas_call(
        body,
        out_shape=[jax.ShapeDtypeStruct(*out) for out in outs.values()],
        in_specs=[pl.BlockSpec(memory_space=pltpu.SMEM)] * n_smem + [pl.BlockSpec(memory_space=pl.ANY)] * n_in,
        out_specs=[pl.BlockSpec(memory_space=pl.ANY)] * n_out,
        scratch_shapes=[pltpu.VMEM(array.shape, array.dtype) for array in ins.values()]
        + [pltpu.VMEM(*out) for out in outs.values()]
        + [pltpu.VMEM(*one) for one in scratch.values()]
        + [pltpu.SemaphoreType.DMA((n_in,)), pltpu.SemaphoreType.DMA((n_out,))],
        compiler_params=pltpu.CompilerParams(vmem_limit_bytes=VMEM_LIMIT),
        cost_estimate=pl.CostEstimate(flops=cost * 10**9, transcendentals=0, bytes_accessed=cost * 10**6),
        name=name,
    )(*smem.values(), *ins.values())
    return SimpleNamespace(**dict(zip(outs, results)))


def finish_kernel(kind, bits, ids_ref, *refs):
    mark = own_label(bits, ids_ref[0], ids_ref[1])
    gathered, sem = refs[-2:]
    n_outs = {"enc": 4, "dec": 2, "cross": 3, "up": 1, "down": 1}[kind]
    count = len(refs) - 2 - n_outs
    parts, outs = refs[:count], refs[count:-2]
    copies, at = [], 0
    for i, part in enumerate(parts):
        copies.append(pltpu.make_async_copy(part, gathered.at[pl.ds(at, part.shape[0])], sem.at[i]))
        at += part.shape[0]
    for copy in copies:
        copy.start()
    for copy in copies:
        copy.wait()
    for shard in range(SHARDS):
        unit, half = divmod(shard, 2)
        rows = slice(half * QUAD, (half + 1) * QUAD)
        where = pl.ds(mark ^ shard, 1)
        value = gathered[where, :QUAD, :][0].astype(F32)
        if kind == "up":
            outs[0][rows, quad(unit)] = value
        elif kind == "down":
            outs[0][quad(unit), rows] = value.T
        elif unit == 3:
            outs[2 if kind == "cross" else 1][:, quad(half)] = value
        elif kind != "cross":
            outs[0][unit, rows, :] = value
        elif unit == 0:
            outs[0][rows, :] = value
        else:
            outs[1][unit - 1, rows, :] = value
        if kind == "enc":
            norms = gathered[where, QUAD:, :][0].astype(F32)
            many = norm_rows(SHARDS)
            for i in range(many):
                row, side = divmod(shard * many + i, 2)
                if row < 10:
                    outs[2 + row // 5][row % 5 : row % 5 + 1, quad(side)] = norms[i : i + 1, :]


def finish(group, ids, outs):
    parts = group.parts
    shape = (SHARDS,) + parts[0].shape[1:]
    return pl.pallas_call(
        functools.partial(finish_kernel, group.kind, group.bits),
        out_shape=[jax.ShapeDtypeStruct(*out) for out in outs],
        in_specs=[pl.BlockSpec(memory_space=pltpu.SMEM)] + [pl.BlockSpec(memory_space=pl.ANY)] * len(parts),
        out_specs=[pl.BlockSpec(memory_space=pltpu.VMEM)] * len(outs),
        scratch_shapes=[pltpu.VMEM(shape, BF16), pltpu.SemaphoreType.DMA((len(parts),))],
        compiler_params=pltpu.CompilerParams(vmem_limit_bytes=VMEM_LIMIT),
        cost_estimate=pl.CostEstimate(flops=2 * 10**9, transcendentals=0, bytes_accessed=2 * 10**6),
        name="finish_" + group.kind,
    )(ids, *parts)


class Sum:
    def __init__(self, kind, bits, dp, mp, mine, other):
        self.kind, self.bits, self.dp, self.mp = kind, bits, dp, mp
        self.phase, self.parts, self.outgoing = -1, [mine], [other]

    def hop(self, array, step):
        pairs = []
        for place in range(self.dp):
            for core in range(self.mp):
                bit = self.bits[core][step] if step < 4 else step
                pairs.append((place * self.mp + core, (place ^ (1 << bit)) * self.mp + core))
        return lax.ppermute(array, ("dp", "mp"), pairs)

    def launch(self):
        if self.phase < 0:
            self.flying = [lax.ppermute(self.outgoing[0], "mp", [(0, 1), (1, 0)])]
        elif self.phase <= 3:
            self.flying = [self.hop(self.outgoing[0], self.last if self.phase == 3 else self.phase)]
        else:
            self.flying = [self.hop(part, 6 - self.phase) for part in self.outgoing]

    def add_up(self):
        self.phase += 1
        if self.phase <= 2:
            mine, sent = self.parts[0], self.flying[0]
            half = mine.shape[0] // 2
            self.outgoing, self.parts = [mine[half:] + sent[half:]], [mine[:half] + sent[:half]]
        elif self.phase == 3:
            part, self.last = self.parts[0] + self.flying[0], 3
            while 2 << self.last < self.dp:
                part = part + self.hop(part, self.last)
                self.last += 1
            self.parts = self.outgoing = [part]
        elif self.phase == 4:
            self.parts = self.outgoing = [self.parts[0] + self.flying[0]]
        else:
            self.parts = self.parts + self.flying
            if self.phase < 7:
                self.outgoing = self.parts if self.phase == 5 and self.kind == "enc" else [jnp.concatenate(self.parts)]
        self.flying = []


def boundary(before, after, landing, launching=()):
    before, after, landing, launching = list(before), list(after), list(landing), list(launching)
    before, landed = lax.optimization_barrier((before, [group.flying for group in landing]))
    for group, flying in zip(landing, landed):
        group.flying = flying
        group.add_up()
    moving = landing + launching
    states = [([] if group.phase < 0 else group.parts, group.outgoing) for group in moving]
    before, after, states = lax.optimization_barrier((before, after, states))
    for group, state in zip(moving, states):
        group.outgoing = list(state[1])
        if group.phase >= 0:
            group.parts = list(state[0])
        if group.phase < 7:
            group.launch()
    return before, after


def on_device(
    src_embed, tgt_embed, src_segment, tgt_segment, enc_qkv, enc_out_proj, dec_qkv, dec_out_proj, cross_query,
    cross_kv, cross_out_proj, ffn_up, ffn_down, norm_gain, norm_bias, enc_cotangent, dec_cotangent,
):
    dp, mp = lax.axis_size("dp"), lax.axis_size("mp")
    tokens, model = src_embed.shape
    own = tokens // mp
    window = own + MOST
    half = ffn_up.shape[1]
    hidden = 2 * half
    position = lax.axis_index("mp")
    ids = jnp.stack([position, lax.axis_index("dp")]).astype(jnp.int32)
    pairs = [(0, 1), (1, 0)]

    def swap(tree):
        return jax.tree.map(lambda a: lax.ppermute(a, "mp", pairs), tree)

    enc_w1, enc_o1 = swap((enc_qkv, enc_out_proj))
    up1, down1 = swap((ffn_up, ffn_down))
    dec_w1, dec_o1 = swap((dec_qkv, dec_out_proj))
    cross_q1, cross_kv1, cross_o1 = swap((cross_query, cross_kv, cross_out_proj))
    feed = {"up0": ffn_up, "up1": up1, "down0": ffn_down, "down1": down1}

    def rows(count, dtype):
        return ((count, model), dtype)

    blocks = own // BLOCK
    q_shape, k_shape, ot_shape, lse_shape = ((own, QUAD), BF16), ((window, QUAD), BF16), ((QUAD, own), BF16), ((4, own), F32)
    vt_shape, marks, bias = ((4 * STRIDE, window), BF16), ((window, BLOCK), jnp.int32), ((blocks, 3 * BLOCK, BLOCK), F32)
    heads = {"q": q_shape, "k": k_shape, "v": k_shape, "ot": ot_shape, "lse": lse_shape}
    wide = ((own, half), BF16)
    norm_in = {"gain": norm_gain, "shift": norm_bias}
    first = call(
        own_heads_kernel, "own_heads", {"ids": ids},
        {"src_row": src_segment, "src": src_embed, "src_w": enc_qkv,
         "tgt_row": tgt_segment, "tgt": tgt_embed, "tgt_w": dec_qkv},
        {f"{side}_{key}": shape for side in ("src", "tgt") for key, shape in heads.items()},
        {"marks": marks, "src_bias": bias, "tgt_bias": bias, "src_vt": vt_shape, "tgt_vt": vt_shape},
        cost=8,
    )
    encoder = call(
        encoder_kernel, "encoder_forward", {"ids": ids},
        {"row": src_segment, "x": src_embed, "w": enc_w1, "ot0": first.src_ot, "wo0": enc_out_proj, "wo1": enc_o1,
         **norm_in, "up0": ffn_up, "down0": ffn_down, "up1": up1, "down1": down1},
        {**heads, "z0": rows(own, F32), "x1_low": rows(own, BF16), "h0": wide, "h1": wide,
         "z1": rows(own, F32), "enc": rows(own, BF16)},
        {"marks": marks, "bias": bias, "vt": vt_shape, "x1": rows(own, F32), "acc": rows(own, F32)},
        cost=12,
    )
    enc_swapped = swap(encoder.enc)
    decoder = call(
        decoder_kernel, "decoder_self_forward", {"ids": ids},
        {"row": tgt_segment, "x": tgt_embed, "w": dec_w1, "ot0": first.tgt_ot, "wo0": dec_out_proj, "wo1": dec_o1,
         **norm_in},
        {**heads, "z2": rows(own, F32), "x2": rows(own, F32)},
        {"marks": marks, "bias": bias, "vt": vt_shape, "acc": rows(own, F32)}, cost=6,
    )
    packed = ((SHARDS, QUAD, QUAD), BF16)
    packed_norms = ((SHARDS, QUAD + TILE, QUAD), BF16)
    crossed = call(
        cross_kernel, "cross_and_decoder_feed",
        {"ids": ids, "src_marks": src_segment, "tgt_marks": tgt_segment},
        {"src_row": src_segment, "tgt_row": tgt_segment, "enc_own": encoder.enc, "enc_other": enc_swapped,
         "x2": decoder.x2, "cq0": cross_query, "ckv0": cross_kv, "cq1": cross_q1, "ckv1": cross_kv1,
         "co0": cross_out_proj, "co1": cross_o1, **norm_in, **feed, "cot": dec_cotangent},
        {"enc": rows(tokens, BF16), "x3_low": rows(own, BF16), "a0": wide, "a1": wide, "dec": rows(own, BF16),
         "dy": rows(own, BF16), "dh0": wide, "dh1": wide, "norms": rows(4, F32), "pack0": packed, "pack1": packed,
         "denc_other": rows(own, BF16), "denc_own": rows(own, F32), "g2": rows(own, F32)},
        {"marks": ((tokens, BLOCK), jnp.int32), "bias": bias, "q": ((2, own, QUAD), BF16),
         "k": ((2, tokens, QUAD), BF16), "v": ((2, tokens, QUAD), BF16), "turn": ((2, QUAD, tokens), BF16), "vt": ((2, 4 * STRIDE, tokens), BF16),
         "mix": ((model, own), F32), "tops": ((8, own), F32), "totals": ((8, own), F32), "lse": ((2, 4, own), F32),
         "ot": ((model, own), BF16), "acc": rows(own, F32), "x3": rows(own, F32), "z3": rows(own, F32),
         "z4": rows(own, F32), "dz": rows(own, F32), "h": ((2, own, half), BF16), "low": rows(own, BF16), "do": ((2, own, QUAD), BF16),
         "delta": ((2, 4, own), F32), "dqt": ((2, QUAD, own), F32), "dk": ((2, tokens, QUAD), F32),
         "dv": ((2, tokens, QUAD), F32), "denc": rows(tokens, F32)},
        cost=30,
    )
    def whole(mine, received):
        return jnp.where(
            position == 0, jnp.concatenate([mine, received]), jnp.concatenate([received, mine])
        )

    def group(kind, bits, mine, other):
        return Sum(kind, bits, dp, mp, mine, other)

    head_scratch = {
        "marks": marks, "bias": bias, "do": q_shape, "delta": ((4, own), F32), "kt": ((QUAD, window), BF16),
        "dqt": ((QUAD, own), F32), "dk": ((window, QUAD), F32), "dv": ((window, QUAD), F32),
    }
    turned_shapes = {"keys_turned": ((model, window), BF16), "query_turned": ((model, own), BF16)}
    head_outs = {"dq": q_shape, "dk": k_shape, "dv": k_shape}

    def self_other(causal, at, bits, name, x, row, z, up, w_out, heads_kept, pack_shape, more):
        ins = {"z": z, "up": up, "gain": norm_gain, "row": row, "x": x, "wo": w_out} | heads_kept | more
        return call(
            functools.partial(self_back_other_kernel, causal, at, bits), name, {"ids": ids}, ins,
            {"dz": rows(own, F32), "branch": rows(own, BF16), "norms": rows(2, F32), "pack": pack_shape}
            | turned_shapes | head_outs,
            head_scratch, cost=9,
        )

    def self_own(causal, bits, name, back, row, branch, w_out, heads_kept, pack_shape, more):
        ins = {"branch": branch, "row": row, "wo": w_out} | heads_kept
        ins |= {"keys_turned": back.keys_turned, "query_turned": back.query_turned} | more
        return call(
            functools.partial(self_back_own_kernel, causal, bits), name, {"ids": ids}, ins,
            {"pack": pack_shape} | head_outs, head_scratch, cost=7,
        )

    def kept_own(side):
        return {key: getattr(first, f"{side}_{key}") for key in ("ot", "k", "q", "v", "lse")}

    def kept_other(part):
        return {key: getattr(part, key) for key in ("ot", "k", "q", "v", "lse")}

    def stream_gradient(name, back, back_own, w0, w1, gate):
        ins = {"dz": gate, "w0": w0, "w1": w1}
        for key in ("dk", "dv", "dq"):
            ins |= {f"{key}0": getattr(back_own, key), f"{key}1": getattr(back, key)}
        return call(
            stream_gradient_kernel, name, {"ids": ids}, ins,
            {"halo": rows(window - own, BF16), "dx": rows(own, F32)}, {"near": rows(window, F32)}, cost=5,
        )

    def group(kind, bits, mine, other):
        return Sum(kind, bits, dp, mp, mine, other)

    halo_at = (1 - position) * (own - (window - own))

    def with_halo(grad, received):
        part = lax.dynamic_slice_in_dim(grad, halo_at, window - own, 0) + received.astype(F32)
        return lax.dynamic_update_slice_in_dim(grad, part, halo_at, 0)

    square, out_half, triple = ((model, QUAD), F32), ((QUAD, model), F32), ((3, model, QUAD), F32)
    out_shapes = {
        "cross": [square, ((2, model, QUAD), F32), out_half],
        "dec": [triple, out_half],
        "up": [((model, half), F32)],
        "down": [rows(half, F32)],
        "enc": [triple, out_half, rows(5, F32), rows(5, F32)],
    }
    cross_sum = group("cross", CROSS_BITS, crossed.pack0, crossed.pack1)
    cross_sum.launch()
    denc_recv = swap(crossed.denc_other)
    (cross_norms,), (z1, denc_recv) = boundary([crossed.norms], [encoder.z1, denc_recv], [cross_sum])
    fed = call(
        feed_other_kernel, "encoder_feed_other", {"ids": ids},
        {"cot": enc_cotangent, "denc_own": crossed.denc_own, "denc_recv": denc_recv, "z1": z1, "gain": norm_gain,
         "x1_low": encoder.x1_low, "x3_low": crossed.x3_low, "dy3": crossed.dy, "down": down1, "h": encoder.h1,
         "up": up1, "dh": crossed.dh1, "a": crossed.a1},
        {"dy": rows(own, BF16), "norms": rows(2, F32), "turned": ((4, model, own), BF16), "up_pack": packed,
         "down_pack": packed, "g0": rows(own, F32)},
        {}, cost=10,
    )
    up_sum = group("up", UP_BITS, None, fed.up_pack)
    down_sum = group("down", DOWN_BITS, None, fed.down_pack)
    (feed_norms,), (dy1,) = boundary([fed.norms], [fed.dy], [cross_sum], [up_sum, down_sum])
    fed_own = call(
        feed_own_kernel, "encoder_feed_own", {"ids": ids},
        {"dy": dy1, "down": ffn_down, "h": encoder.h0, "dz": fed.g0, "turned": fed.turned, "up": ffn_up,
         "dh": crossed.dh0, "a": crossed.a0},
        {"g0": rows(own, F32), "up_pack": packed, "down_pack": packed}, {}, cost=9,
    )
    up_sum.parts, down_sum.parts = [fed_own.up_pack], [fed_own.down_pack]
    (feed_norms,), (g2,) = boundary([feed_norms], [crossed.g2], [cross_sum, up_sum, down_sum])
    dec_back = self_other(
        True, 2, DEC_BITS, "decoder_self_other", tgt_embed, tgt_segment, decoder.z2, g2, dec_o1, kept_other(decoder),
        packed, {},
    )
    dec_sum = group("dec", DEC_BITS, None, dec_back.pack)
    (dec_norms,), (branch,) = boundary([dec_back.norms], [dec_back.branch], [cross_sum, up_sum], [dec_sum])
    dec_own = self_own(
        True, DEC_BITS, "decoder_self_own", dec_back, tgt_segment, branch, dec_out_proj, kept_own("tgt"), packed, {},
    )
    dec_sum.parts = [dec_own.pack]
    (dec_norms,), (g0,) = boundary([dec_norms], [fed_own.g0], [cross_sum, up_sum, down_sum, dec_sum])
    norms_before = {"feed_norms": feed_norms, "dec_norms": dec_norms, "cross_norms": cross_norms}
    enc_back = self_other(
        False, 0, ENC_BITS, "encoder_self_other", src_embed, src_segment, encoder.z0, g0, enc_o1, kept_other(encoder),
        packed_norms, norms_before,
    )
    enc_sum = group("enc", ENC_BITS, None, enc_back.pack)
    (enc_norms,), (branch,) = boundary(
        [enc_back.norms], [enc_back.branch], [cross_sum, up_sum, down_sum, dec_sum], [enc_sum]
    )
    enc_own = self_own(
        False, ENC_BITS, "encoder_self_own", enc_back, src_segment, branch, enc_out_proj, kept_own("src"),
        packed_norms, {"norms": enc_norms, **norms_before},
    )
    enc_sum.parts = [enc_own.pack]
    (src_dz,), () = boundary([enc_own.dq], [], [enc_sum, cross_sum, dec_sum, up_sum, down_sum])
    enc_own.dq = src_dz
    src_side = stream_gradient("src_gradient", enc_back, enc_own, enc_qkv, enc_w1, enc_back.dz)
    (src_halo,), () = boundary([src_side.halo], [], [enc_sum])
    (src_halo,), () = boundary([src_halo], [], [dec_sum])
    (src_halo,), (tgt_dz,) = boundary([src_halo], [dec_back.dz], [up_sum])
    tgt_side = stream_gradient("tgt_gradient", dec_back, dec_own, dec_qkv, dec_w1, tgt_dz)
    (tgt_halo,), () = boundary([tgt_side.halo], [], [enc_sum])
    (tgt_halo,), (dec_part, src_halo) = boundary([tgt_halo], [crossed.dec, src_halo], [down_sum, cross_sum])
    src_recv, tgt_recv, dec_swapped = swap(src_halo), swap(tgt_halo), swap(dec_part)
    (dec_swapped,), () = boundary([dec_swapped], [], [up_sum, dec_sum])
    cross_out = list(finish(cross_sum, ids, out_shapes["cross"]))
    dec_whole = whole(crossed.dec, dec_swapped)
    (dec_whole, norm_gate), (src_recv,) = boundary([dec_whole, cross_out[0]], [src_recv], [enc_sum, down_sum])
    cross_out[0] = norm_gate
    src_grad = with_halo(src_side.dx, src_recv)
    (src_grad,), (tgt_recv,) = boundary([src_grad], [tgt_recv], [up_sum, dec_sum])
    tgt_grad = with_halo(tgt_side.dx, tgt_recv)
    (tgt_grad,), () = boundary([tgt_grad], [], [enc_sum])
    (tgt_grad,), () = boundary([tgt_grad], [], [down_sum])
    (tgt_grad,), () = boundary([tgt_grad], [], [dec_sum])
    up_out = finish(up_sum, ids, out_shapes["up"])
    (up_gate,), () = boundary([up_out[0]], [], [enc_sum])
    up_out = [up_gate]
    (up_gate,), () = boundary([up_gate], [], [enc_sum])
    up_out = [up_gate]
    (up_gate,), () = boundary([up_gate], [], [down_sum])
    up_out = [up_gate]
    down_out = finish(down_sum, ids, out_shapes["down"])
    (down_gate,), () = boundary([down_out[0]], [], [dec_sum])
    down_out = [down_gate]
    dec_out = finish(dec_sum, ids, out_shapes["dec"])
    (dec_gate,), () = boundary([dec_out[0]], [], [enc_sum])
    dec_out = [dec_gate, dec_out[1]]
    enc_out = finish(enc_sum, ids, out_shapes["enc"])

    return (
        crossed.enc,
        dec_whole,
        src_grad,
        tgt_grad,
        enc_out[0],
        enc_out[1],
        dec_out[0],
        dec_out[1],
        cross_out[0],
        cross_out[1],
        cross_out[2],
        up_out[0],
        down_out[0],
        enc_out[2],
        enc_out[3],
    )


def solution(mesh):
    in_specs = (
        P("dp", None), P("dp", None), P("dp", None), P("dp", None),
        P(None, None, "mp"), P("mp", None), P(None, None, "mp"), P("mp", None),
        P(None, "mp"), P(None, None, "mp"), P("mp", None), P(None, "mp"), P("mp", None),
        P(), P(), P(("dp", "mp"), None), P(("dp", "mp"), None),
    )
    out_specs = (
        P("dp", None), P("dp", None), P(("dp", "mp"), None), P(("dp", "mp"), None),
        P(None, None, "mp"), P("mp", None), P(None, None, "mp"), P("mp", None),
        P(None, "mp"), P(None, None, "mp"), P("mp", None), P(None, "mp"), P("mp", None),
        P(), P(),
    )
    return jax.shard_map(on_device, mesh=mesh, in_specs=in_specs, out_specs=out_specs, check_vma=False)
```

```python
import functools
import math
from types import SimpleNamespace

import jax
import jax.numpy as jnp
from jax import lax
from jax.experimental import pallas as pl
from jax.experimental.pallas import tpu as pltpu
from jax.sharding import PartitionSpec as P

HDIM = 64
SCALE = HDIM ** (-0.5)
EPSILON = 1e-05
MASKED = -1e30
BLOCK = 128
MOST = 128
QUAD = 4 * HDIM
UNITS = 4
TILE = 16
FEED = 512
SHARDS = 8
UP_BITS = ((0, 1, 2, 3), (1, 0, 2, 3))
DOWN_BITS = ((1, 0, 2, 3), (0, 1, 2, 3))
CROSS_BITS = ((0, 1, 2, 3), (1, 0, 2, 3))
DEC_BITS = ((0, 1, 2, 3), (1, 0, 2, 3))
STRIDE = HDIM + TILE
ENC_BITS = ((1, 0, 2, 3), (0, 1, 2, 3))
F32 = jnp.float32
BF16 = jnp.bfloat16
FINISH_LIMIT = 10 * 1024 * 1024
SPARE = 6 * 1024 * 1024
GELU_IN = math.sqrt(2.0 / math.pi)
GELU_CUBE = 0.044715


def nn(left, right):
    return jnp.dot(left, right, preferred_element_type=F32)


def nt(left, right):
    return lax.dot_general(left, right, (((1,), (1,)), ((), ())), preferred_element_type=F32)


def tn(left, right):
    return lax.dot_general(left, right, (((0,), (0,)), ((), ())), preferred_element_type=F32)


def aligned(index, size=BLOCK):
    return pl.multiple_of(index, size)


def over_rows(rows, chunk, body, carry, unroll=4):
    return lax.fori_loop(
        0,
        rows // chunk,
        lambda i, kept: body(pl.ds(aligned(i * chunk, chunk), chunk), kept),
        carry,
        unroll=min(unroll, rows // chunk),
    )


def normalize(before):
    centered = before - jnp.mean(before, axis=-1, keepdims=True)
    variance = jnp.mean(centered * centered, axis=-1, keepdims=True)
    rate = lax.rsqrt(variance + EPSILON)
    return centered * rate, rate


def norm_backward(before, upstream, gain_row):
    normed, rate = normalize(before)
    scaled = upstream * gain_row
    first = jnp.mean(scaled, axis=-1, keepdims=True)
    second = jnp.mean(scaled * normed, axis=-1, keepdims=True)
    return rate * (scaled - first - normed * second), upstream * normed


def fold_rows(block):
    return jnp.sum(block.reshape(block.shape[0] // 8, 8, block.shape[1]), axis=0)


def gelu(hidden):
    inner = GELU_IN * hidden * (1.0 + GELU_CUBE * hidden * hidden)
    return 0.5 * hidden * (1.0 + jnp.tanh(inner))


def gelu_both(hidden):
    square = hidden * hidden
    bent = jnp.tanh(GELU_IN * hidden * (1.0 + GELU_CUBE * square))
    half = 0.5 * (1.0 + bent)
    slope = half + 0.5 * hidden * (1.0 - bent * bent) * (GELU_IN * (1.0 + 3.0 * GELU_CUBE * square))
    return hidden * half, slope


def head_masks():
    lane = lax.broadcasted_iota(jnp.int32, (1, QUAD), 1)
    return [
        jnp.where((lane >= h * HDIM) & (lane < (h + 1) * HDIM), 1.0, 0.0).astype(BF16)
        for h in range(4)
    ]


def stack_heads(block, masks):
    return jnp.concatenate([block * mask for mask in masks], axis=0)


def quad(g):
    return slice(g * QUAD, (g + 1) * QUAD)


def bias_for(marks_ref, key_at, width, query_row, causal=False, key_start=0, query_start=0):
    allowed = marks_ref[pl.ds(key_at, width), :] == query_row
    if causal:
        places = key_start + lax.broadcasted_iota(jnp.int32, (width, BLOCK), 0)
        queries = query_start + lax.broadcasted_iota(jnp.int32, (width, BLOCK), 1)
        allowed = allowed & (places <= queries)
    return jnp.where(allowed, 0.0, MASKED)


def self_window(core, block, causal):
    middle = block + core
    if causal:
        return aligned(jnp.maximum(middle - 1, 0) * BLOCK), 2 * BLOCK
    return aligned(jnp.clip(middle - 1, 0, 2) * BLOCK), 3 * BLOCK


def set_self_bias(bias_ref, core, tokens, marks_ref, row_ref, causal):
    window, own = marks_ref.shape[0], row_ref.shape[1] // 2
    start = core * (tokens - window)
    spots = []
    for block in range(own // BLOCK):
        key_at, width = self_window(core, block, causal)
        first = aligned(core * own + block * BLOCK)
        bias_ref[block, :width, :] = bias_for(
            marks_ref, key_at, width, row_ref[:, pl.ds(first, BLOCK)], causal, start + key_at, first
        )
        spots.append((key_at, width))
    return spots


def soft_weights(scores, h, bias, top=None):
    one = scores[:, h * BLOCK : (h + 1) * BLOCK] + bias
    high = jnp.max(one, axis=0, keepdims=True)
    top = high if top is None else jnp.maximum(top, high)
    return top, jnp.exp((one - top).astype(BF16))


def set_values(vt_ref, values):
    turned = values.T
    for h in range(4):
        vt_ref[h * STRIDE : h * STRIDE + HDIM, :] = turned[h * HDIM : (h + 1) * HDIM]
        vt_ref[h * STRIDE + HDIM : (h + 1) * STRIDE, :] = jnp.ones((TILE, turned.shape[1]), BF16)


def quad_forward(spots, q_ref, k_ref, vt_ref, bias_ref, ot_ref, lse_ref, masks):
    def score(block):
        rows, (key_at, width) = slice(block * BLOCK, (block + 1) * BLOCK), spots[block]
        return nt(k_ref[pl.ds(key_at, width), :], stack_heads(q_ref[rows, :], masks))

    ahead = score(0)
    for block, (key_at, width) in enumerate(spots):
        rows = slice(block * BLOCK, (block + 1) * BLOCK)
        scores, ahead = ahead, score(block + 1) if block + 1 < len(spots) else None
        for h in range(4):
            top, weights = soft_weights(scores, h, bias_ref[block, :width, :])
            features = slice(h * HDIM, (h + 1) * HDIM)
            mixed = nn(vt_ref[h * STRIDE : (h + 1) * STRIDE, pl.ds(key_at, width)], weights)
            total = mixed[HDIM : HDIM + 1]
            ot_ref[features, rows] = (mixed[:HDIM] * (1.0 / total)).astype(BF16)
            lse_ref[h : h + 1, rows] = top + jnp.log(total)


def backward_scores(rows, key_at, width, masks, q_ref, k_ref, v_ref, do_ref):
    keys = pl.ds(key_at, width)
    q_stack, do_stack = stack_heads(q_ref[rows, :], masks), stack_heads(do_ref[rows, :], masks)
    return q_stack, do_stack, nt(k_ref[keys, :], q_stack), nt(v_ref[keys, :], do_stack)


def backward_sums(rows, key_at, bias, scored, kt_ref, lse_ref, delta_ref, dqt_ref, dk_ref, dv_ref, add=False):
    q_stack, do_stack, scores, prob_grads = scored
    keys = pl.ds(key_at, bias.shape[0])
    probs, score_grads = [], []
    for h in range(4):
        cols = slice(h * BLOCK, (h + 1) * BLOCK)
        prob = jnp.exp((scores[:, cols] + bias - lse_ref[h : h + 1, rows]).astype(BF16))
        probs.append(prob)
        score_grads.append(prob * (prob_grads[:, cols] - delta_ref[h : h + 1, rows]).astype(BF16))
    for h in range(4):
        features = slice(h * HDIM, (h + 1) * HDIM)
        query_grad = nn(kt_ref[features, keys], score_grads[h])
        if add:
            dqt_ref[features, rows] += query_grad
        else:
            dqt_ref[features, rows] = query_grad
    dv_ref[keys, :] += nn(jnp.concatenate(probs, axis=1), do_stack)
    dk_ref[keys, :] += nn(jnp.concatenate(score_grads, axis=1), q_stack)


def mixed_gradients(branch, ot, w_out, do_ref, delta_ref):
    do_ref[...] = nt(branch, w_out).astype(BF16)
    product = nt(w_out, branch).astype(BF16).astype(F32) * ot.astype(F32)
    for h in range(4):
        delta_ref[h : h + 1, :] = jnp.sum(product[h * HDIM : (h + 1) * HDIM, :], axis=0, keepdims=True)


def spread_marks(marks_ref, row):
    marks_ref[...] = jnp.broadcast_to(row, (marks_ref.shape[1], marks_ref.shape[0])).T


def label(bits, place):
    first, second, third = [(place >> bit) & 1 for bit in bits[:3]]
    return 4 * first + 2 * second + third


def own_label(bits, core, place):
    return jnp.where(core == 0, label(bits[0], place), label(bits[1], place))


def pack(out_ref, mark, unit, value, at=0):
    rows = value.shape[0] // 2
    for half in range(2):
        where = pl.ds(mark ^ (2 * unit + half), 1)
        out_ref[where, at : at + rows, :] = value[half * rows : (half + 1) * rows].astype(BF16)[None]


def as_unit(value):
    return jnp.concatenate([value[:, :QUAD], value[:, QUAD:]], axis=0).astype(BF16)


def pack_norms(out_ref, mark, parts):
    shards, tall, width = out_ref.shape
    halves = [part[:, half * width : (half + 1) * width] for part in parts for half in range(2)]
    each = norm_rows(shards)
    blank = jnp.zeros((1, width), F32)
    halves += [blank] * (shards * each - len(halves))
    for i in range(shards):
        block = jnp.concatenate(halves[i * each : (i + 1) * each] + [blank] * (TILE - each), axis=0)
        out_ref[pl.ds(mark ^ i, 1), tall - TILE :, :] = block.astype(BF16)[None]


def norm_rows(shards):
    return -(-20 // shards)


def prepare_quad(x_ref, w_ref, core, q_ref, k_ref, v_ref, vt_ref):
    tokens, own, window = x_ref.shape[0], q_ref.shape[0], k_ref.shape[0]
    keys = x_ref[pl.ds(aligned(core * (tokens - window)), window), :]
    q_ref[...] = (nn(x_ref[pl.ds(aligned(core * own), own), :], w_ref[0]) * SCALE).astype(BF16)
    k_ref[...] = nn(keys, w_ref[1]).astype(BF16)
    v_ref[...] = nn(keys, w_ref[2]).astype(BF16)
    set_values(vt_ref, v_ref[...])


def own_heads_kernel(r):
    core = r.ids[0]
    masks = head_masks()
    for side, causal in (("src", False), ("tgt", True)):
        x_ref, row_ref = r.get(side), r.get(side + "_row")
        k_ref = r.out(side + "_k")
        start = aligned(core * (x_ref.shape[0] - k_ref.shape[0]))
        spread_marks(r.marks, row_ref[:, pl.ds(start, k_ref.shape[0])])
        bias_ref, vt_ref = getattr(r, side + "_bias"), getattr(r, side + "_vt")
        spots = set_self_bias(bias_ref, core, x_ref.shape[0], r.marks, row_ref, causal)
        q_ref, v_ref = r.out(side + "_q"), r.out(side + "_v")
        prepare_quad(x_ref, r.get(side + "_w"), core, q_ref, k_ref, v_ref, vt_ref)
        for key in ("_q", "_k", "_v"):
            r.send(side + key)
        quad_forward(
            spots, q_ref, k_ref, vt_ref, bias_ref, r.out(side + "_ot"), r.out(side + "_lse"), masks
        )
        r.send(side + "_ot")
        r.send(side + "_lse")


def other_heads(r, causal):
    core = r.ids[0]
    x_ref, row_ref, k_ref = r.get("x"), r.get("row"), r.out("k")
    start = aligned(core * (x_ref.shape[0] - k_ref.shape[0]))
    spread_marks(r.marks, row_ref[:, pl.ds(start, k_ref.shape[0])])
    spots = set_self_bias(r.bias, core, x_ref.shape[0], r.marks, row_ref, causal)
    q_ref, v_ref, ot_ref = r.out("q"), r.out("v"), r.out("ot")
    prepare_quad(x_ref, r.get("w"), core, q_ref, k_ref, v_ref, r.vt)
    for key in ("q", "k", "v"):
        r.send(key)
    quad_forward(spots, q_ref, k_ref, r.vt, r.bias, ot_ref, r.out("lse"), head_masks())
    r.send("lse")
    r.send("ot")
    r.acc[...] = tn(r.get("ot0")[...], r.get("wo0")[...]) + tn(ot_ref[...], r.get("wo1")[...])


def norm_forward(r, at, residual, before_ref, after_ref, low_ref):
    gain, shift = r.get("gain")[at : at + 1, :], r.get("shift")[at : at + 1, :]

    def body(rows, carry):
        before = residual(rows) + r.acc[rows, :]
        if before_ref is not None:
            before_ref[rows, :] = before
        after = normalize(before)[0] * gain + shift
        if after_ref is not None:
            after_ref[rows, :] = after
        if low_ref is not None:
            low_ref[rows, :] = after.astype(BF16)
        return carry

    over_rows(r.acc.shape[0], 32, body, 0)


def own_row_reader(x_ref, core, own):
    first = core * own
    return lambda rows: x_ref[pl.ds(aligned(first + rows.start, rows.size), rows.size), :].astype(F32)


def encoder_kernel(r):
    other_heads(r, False)
    x1_low = r.out("x1_low")
    norm_forward(r, 0, own_row_reader(r.get("x"), r.ids[0], r.acc.shape[0]), r.out("z0"), r.x1, x1_low)
    r.send("z0")
    r.send("x1_low")
    feed_forward(x1_low, *feed_weights(r), (r.out("h0"), r.out("h1")), None, r.acc)
    r.send("h0")
    r.send("h1")
    norm_forward(r, 1, lambda rows: r.x1[rows, :], r.out("z1"), None, r.out("enc"))


def decoder_kernel(r):
    other_heads(r, True)
    norm_forward(r, 2, own_row_reader(r.get("x"), r.ids[0], r.acc.shape[0]), r.out("z2"), r.out("x2"), None)


def feed_weights(r):
    return (r.get("up0"), r.get("up1")), (r.get("down0"), r.get("down1"))


def feed_chunks(half):
    return [(j, slice(j * FEED, (j + 1) * FEED)) for j in range(half // FEED)]


def feed_forward(low_ref, ups, downs, h_refs, a_refs, acc_ref):
    chunks = [(g, cols) for g in range(2) for j, cols in feed_chunks(ups[0].shape[1])]
    ahead = nn(low_ref[...], ups[0][:, chunks[0][1]])
    for i, (g, cols) in enumerate(chunks):
        hidden = ahead
        if i + 1 < len(chunks):
            ahead = nn(low_ref[...], ups[chunks[i + 1][0]][:, chunks[i + 1][1]])
        hidden = hidden.astype(BF16)
        h_refs[g][:, cols] = hidden
        active = gelu(hidden)
        if a_refs is not None:
            a_refs[g][:, cols] = active
        term = nn(active, downs[g][cols, :])
        if i == 0:
            acc_ref[...] = term
        else:
            acc_ref[...] += term


def feed_backward(dy_ref, ups, downs, h_refs, dh_refs, acc_ref):
    chunks = [(g, cols) for g in range(2) for j, cols in feed_chunks(ups[0].shape[1])]
    ahead = nt(dy_ref[...], downs[0][chunks[0][1], :])
    for i, (g, cols) in enumerate(chunks):
        active_grad = ahead
        if i + 1 < len(chunks):
            ahead = nt(dy_ref[...], downs[chunks[i + 1][0]][chunks[i + 1][1], :])
        hidden_grad = active_grad.astype(BF16) * gelu_both(h_refs[g][:, cols])[1]
        dh_refs[g][:, cols] = hidden_grad
        acc_ref[...] += nt(hidden_grad, ups[g][:, cols])


def norm_back(r, gain_row, before, upstream, outs):
    def body(rows, sums):
        above = upstream(rows)
        grad, gain_terms = norm_backward(before(rows), above, gain_row)
        for ref in outs:
            ref[rows, :] = grad.astype(ref.dtype)
        return sums[0] + fold_rows(gain_terms), sums[1] + fold_rows(above)

    zeros = jnp.zeros((8, outs[0].shape[1]), F32)
    gains, shifts = over_rows(outs[0].shape[0], 32, body, (zeros, zeros))
    return jnp.sum(gains, axis=0, keepdims=True), jnp.sum(shifts, axis=0, keepdims=True)


def cross_kernel(r):
    core, place = r.ids[0], r.ids[1]
    x2_ref, enc_ref = r.get("x2"), r.out("enc")
    own, tokens = x2_ref.shape[0], enc_ref.shape[0]
    blocks = own // BLOCK
    first, second = aligned(core * own), aligned((1 - core) * own)
    width = 3 * BLOCK
    enc_ref[pl.ds(first, own), :] = r.get("enc_own")[...]
    enc_ref[pl.ds(second, own), :] = r.get("enc_other")[...]
    r.send("enc")
    spread_marks(r.marks, r.get("src_row")[...])
    steps = tokens.bit_length()

    def bound(mark, past):
        def step(i, pair):
            low, high = pair
            middle = (low + high) // 2
            value = r.src_marks[0, jnp.minimum(middle, tokens - 1)]
            below = (low < high) & ((value < mark) | (past & (value == mark)))
            above = (low < high) & jnp.logical_not(below)
            return jnp.where(below, middle + 1, low), jnp.where(above, middle, high)

        return lax.fori_loop(0, steps, step, (jnp.int32(0), jnp.int32(tokens)))[0]

    row_ref = r.get("tgt_row")
    query_rows, spots, more = [], [], []
    for block in range(blocks):
        head = first + block * BLOCK
        low = bound(r.tgt_marks[0, head], jnp.bool_(False)) // BLOCK
        high = (bound(r.tgt_marks[0, head + BLOCK - 1], jnp.bool_(True)) + BLOCK - 1) // BLOCK
        key_at = aligned(jnp.minimum(low, (tokens - width) // BLOCK) * BLOCK)
        query_rows.append(row_ref[:, pl.ds(aligned(head), BLOCK)])
        spots.append(key_at)
        more.append((key_at // BLOCK + 3, high))
        r.bias[block] = bias_for(r.marks, key_at, width, query_rows[block])
    masks = head_masks()
    x2_low = x2_ref[...].astype(BF16)
    for g in range(2):
        r.q[g] = (nn(x2_low, r.get(f"cq{g}")[...]) * SCALE).astype(BF16)
        r.k[g] = nn(enc_ref[...], r.get(f"ckv{g}")[0]).astype(BF16)
        r.v[g] = nn(enc_ref[...], r.get(f"ckv{g}")[1]).astype(BF16)
        set_values(r.vt.at[g], r.v[g])

    def weigh(g, h, scores, bias, key_at, keys_width, top):
        new_top, weights = soft_weights(scores, h, bias, top)
        mixed = nn(r.vt[g, h * STRIDE : (h + 1) * STRIDE, pl.ds(key_at, keys_width)], weights)
        features = slice(g * QUAD + h * HDIM, g * QUAD + (h + 1) * HDIM)
        return new_top, mixed[HDIM : HDIM + 1], mixed[:HDIM], features

    def score(block, g):
        rows = slice(block * BLOCK, (block + 1) * BLOCK)
        return nt(r.k[g, pl.ds(spots[block], width), :], stack_heads(r.q[g, rows, :], masks))

    tiles = [(block, g) for block in range(blocks) for g in range(2)]
    ahead = score(*tiles[0])
    for i, (block, g) in enumerate(tiles):
        rows = slice(block * BLOCK, (block + 1) * BLOCK)
        scores, ahead = ahead, score(*tiles[i + 1]) if i + 1 < len(tiles) else None
        for h in range(4):
            top, total, mixed, features = weigh(g, h, scores, r.bias[block], spots[block], width, None)
            r.mix[features, rows] = mixed
            r.tops[g * 4 + h : g * 4 + h + 1, rows] = top
            r.totals[g * 4 + h : g * 4 + h + 1, rows] = total

    for block in range(blocks):
        rows = slice(block * BLOCK, (block + 1) * BLOCK)

        def extra(i, carry, block=block, rows=rows):
            key_at = aligned(i * BLOCK)
            bias = bias_for(r.marks, key_at, BLOCK, query_rows[block])
            for g in range(2):
                scores = nt(r.k[g, pl.ds(key_at, BLOCK), :], stack_heads(r.q[g, rows, :], masks))
                for h in range(4):
                    at = slice(g * 4 + h, g * 4 + h + 1)
                    old = r.tops[at, rows]
                    top, total, mixed, features = weigh(g, h, scores, bias, key_at, BLOCK, old)
                    fade = jnp.exp(old - top)
                    r.mix[features, rows] = r.mix[features, rows] * fade + mixed
                    r.tops[at, rows] = top
                    r.totals[at, rows] = r.totals[at, rows] * fade + total
            return carry

        lax.fori_loop(*more[block], extra, 0)
    for head in range(8):
        features = slice(head * HDIM, (head + 1) * HDIM)
        at = slice(head, head + 1)
        r.ot[features, :] = (r.mix[features, :] * (1.0 / r.totals[at, :])).astype(BF16)
        r.lse[head // 4, head % 4 : head % 4 + 1, :] = r.tops[at, :] + jnp.log(r.totals[at, :])
    outs = (r.get("co0"), r.get("co1"))
    r.acc[...] = tn(r.ot[:QUAD, :], outs[0][...]) + tn(r.ot[QUAD:, :], outs[1][...])
    x3_low = r.out("x3_low")
    norm_forward(r, 3, lambda rows: x2_ref[rows, :], r.z3, r.x3, x3_low)
    r.send("x3_low")
    ups, downs = feed_weights(r)
    hs = (r.h.at[0], r.h.at[1])
    feed_forward(x3_low, ups, downs, hs, (r.out("a0"), r.out("a1")), r.acc)
    r.send("a0")
    r.send("a1")
    gain_ref, shift_ref, cot_ref, dec_ref, dy_ref = (
        r.get("gain"), r.get("shift"), r.get("cot"), r.out("dec"), r.out("dy")
    )
    last_gain, last_shift = gain_ref[4:5, :], shift_ref[4:5, :]

    def fourth_norm(rows, sums):
        before = r.x3[rows, :] + r.acc[rows, :]
        normed, rate = normalize(before)
        dec_ref[rows, :] = (normed * last_gain + last_shift).astype(BF16)
        upstream = cot_ref[rows, :].astype(F32)
        scaled = upstream * last_gain
        mean_one = jnp.mean(scaled, axis=-1, keepdims=True)
        mean_two = jnp.mean(scaled * normed, axis=-1, keepdims=True)
        grad = rate * (scaled - mean_one - normed * mean_two)
        r.z4[rows, :] = grad
        dy_ref[rows, :] = grad.astype(BF16)
        return sums[0] + fold_rows(upstream * normed), sums[1] + fold_rows(upstream)

    zeros = jnp.zeros((8, x2_ref.shape[1]), F32)
    gain_four, shift_four = over_rows(own, 32, fourth_norm, (zeros, zeros))
    r.send("dec")
    r.send("dy")
    feed_backward(dy_ref, ups, downs, hs, (r.out("dh0"), r.out("dh1")), r.z4)
    r.send("dh0")
    r.send("dh1")
    gain_three, shift_three = norm_back(
        r, gain_ref[3:4, :], lambda rows: r.z3[rows, :], lambda rows: r.z4[rows, :], (r.dz, r.low)
    )
    norms = r.out("norms")
    norms[0:1, :] = gain_three
    norms[1:2, :] = jnp.sum(gain_four, axis=0, keepdims=True)
    norms[2:3, :] = shift_three
    norms[3:4, :] = jnp.sum(shift_four, axis=0, keepdims=True)
    branch = r.low[...]
    ots = (r.ot.at[:QUAD], r.ot.at[QUAD:])
    for g in range(2):
        mixed_gradients(branch, ots[g][...], outs[g][...], r.do.at[g], r.delta.at[g])
    packs = pair_of_packs(r, CROSS_BITS)
    for g, (packed, mark) in enumerate(packs):
        pack(packed, mark, 3, as_unit(nn(ots[g][...], branch)))
        r.turn[g] = r.k[g].T
    r.dk[...] = jnp.zeros(r.dk.shape, F32)
    r.dv[...] = jnp.zeros(r.dv.shape, F32)

    def back_scores(block, g, key_at, keys_width):
        rows = slice(block * BLOCK, (block + 1) * BLOCK)
        return backward_scores(rows, key_at, keys_width, masks, r.q.at[g], r.k.at[g], r.v.at[g], r.do.at[g])

    def back_sums(block, g, key_at, bias, scored, add):
        backward_sums(
            slice(block * BLOCK, (block + 1) * BLOCK), key_at, bias, scored, r.turn.at[g], r.lse.at[g], r.delta.at[g],
            r.dqt.at[g], r.dk.at[g], r.dv.at[g], add,
        )

    ahead = back_scores(*tiles[0], spots[0], width)
    for i, (block, g) in enumerate(tiles):
        scored = ahead
        if i + 1 < len(tiles):
            ahead = back_scores(*tiles[i + 1], spots[tiles[i + 1][0]], width)
        back_sums(block, g, spots[block], r.bias[block], scored, False)
    for block in range(blocks):

        def extra_back(i, carry, block=block):
            key_at = aligned(i * BLOCK)
            bias = bias_for(r.marks, key_at, BLOCK, query_rows[block])
            for g in range(2):
                back_sums(block, g, key_at, bias, back_scores(block, g, key_at, BLOCK), True)
            return carry

        lax.fori_loop(*more[block], extra_back, 0)
    query_turned, enc_turned = x2_ref[...].astype(BF16).T, enc_ref[...].T
    query_grads = [(r.dqt[g] * SCALE).astype(BF16).T for g in range(2)]
    side_grads = [(r.dk[g].astype(BF16), r.dv[g].astype(BF16)) for g in range(2)]
    for g in (1, 0):
        packed, mark = packs[g]
        pack(packed, mark, 0, nn(query_turned, query_grads[g]))
        for i in range(2):
            pack(packed, mark, 1 + i, nn(enc_turned, side_grads[g][i]))
        r.send(f"pack{g}")
    r.denc[...] = sum(nt(side_grads[g][i], r.get(f"ckv{g}")[i]) for i in range(2) for g in range(2))
    r.out("denc_other")[...] = r.denc[pl.ds(second, own), :].astype(BF16)
    r.send("denc_other")
    r.out("denc_own")[...] = r.denc[pl.ds(first, own), :]
    r.send("denc_own")
    r.out("g2")[...] = r.dz[...] + sum(nt(query_grads[g], r.get(f"cq{g}")[...]) for g in range(2))


def pair_of_packs(r, bits, name="pack"):
    core, place = r.ids[0], r.ids[1]
    return [(r.out(f"{name}{g}"), own_label(bits, core ^ g, place)) for g in range(2)]


def key_stream_gradient(r, weights, keys=("dk", "dv")):
    return sum(nt(r.get(f"{keys[i]}{g}")[...], weights[g][i]) for i in range(2) for g in range(2))


def feed_gradients(r, g, dy_ref, acc_ref, turned):
    core, place = r.ids[0], r.ids[1]
    up_mark, down_mark = own_label(UP_BITS, core ^ g, place), own_label(DOWN_BITS, core ^ g, place)
    h_ref, dh_ref, a_ref, up_ref, down_ref = [r.get(key) for key in ("h", "dh", "a", "up", "down")]
    chunks = feed_chunks(h_ref.shape[1])
    ahead = nt(dy_ref[...], down_ref[chunks[0][1], :])
    for j, cols in chunks:
        above = ahead
        if j + 1 < len(chunks):
            ahead = nt(dy_ref[...], down_ref[chunks[j + 1][1], :])
        active, slope = gelu_both(h_ref[:, cols])
        hidden_grad = above.astype(BF16) * slope
        acc_ref[...] += nt(hidden_grad, up_ref[:, cols])
        up_grad = nn(turned[0], hidden_grad) + nn(turned[1], dh_ref[:, cols])
        down_grad = nn(turned[2], active) + nn(turned[3], a_ref[:, cols])
        for b in range(2):
            pack(r.out("up_pack"), up_mark, 2 * j + b, up_grad[:, quad(b)])
            pack(r.out("down_pack"), down_mark, 2 * j + b, down_grad[:, quad(b)])


def feed_other_kernel(r):
    cot_ref, own_ref, recv_ref, z1_ref = r.get("cot"), r.get("denc_own"), r.get("denc_recv"), r.get("z1")
    dy_ref, acc_ref, turned = r.out("dy"), r.out("g0"), r.out("turned")
    gain, shift = norm_back(
        r,
        r.get("gain")[1:2, :],
        lambda rows: z1_ref[rows, :],
        lambda rows: cot_ref[rows, :].astype(F32) + own_ref[rows, :] + recv_ref[rows, :].astype(F32),
        (acc_ref, dy_ref),
    )
    r.out("norms")[0:1, :] = gain
    r.out("norms")[1:2, :] = shift
    r.send("dy")
    for i, ref in enumerate((r.get("x1_low"), r.get("x3_low"), dy_ref, r.get("dy3"))):
        turned[i] = ref[...].T
    r.send("turned")
    feed_gradients(r, 1, dy_ref, acc_ref, turned)


def feed_own_kernel(r):
    acc_ref = r.out("g0")
    acc_ref[...] = r.get("dz")[...]
    feed_gradients(r, 0, r.get("dy"), acc_ref, r.get("turned"))


def norm_parts(norms, r):
    feed, dec, cross = r.get("feed_norms"), r.get("dec_norms"), r.get("cross_norms")
    rows = [(norms, 0), (feed, 0), (dec, 0), (cross, 0), (cross, 1)]
    rows += [(norms, 1), (feed, 1), (dec, 1), (cross, 2), (cross, 3)]
    return [ref[at : at + 1, :] for ref, at in rows]


def self_back_heads(r, causal, bits, g, branch, norms, keys_turned, query_turned):
    core, place = r.ids[0], r.ids[1]
    row_ref, window = r.get("row"), r.marks.shape[0]
    tokens = row_ref.shape[1]
    spread_marks(r.marks, row_ref[:, pl.ds(aligned(core * (tokens - window)), window)])
    spots = set_self_bias(r.bias, core, tokens, r.marks, row_ref, causal)
    ot_ref = r.get("ot")
    mixed_gradients(branch, ot_ref[...], r.get("wo")[...], r.do, r.delta)
    packed, mark = r.out("pack"), own_label(bits, core ^ g, place)
    pack(packed, mark, 3, as_unit(nn(ot_ref[...], branch)))
    if not causal:
        pack_norms(packed, mark, norm_parts(norms, r))
    r.dk[...] = jnp.zeros(r.dk.shape, F32)
    r.dv[...] = jnp.zeros(r.dv.shape, F32)
    q_ref, k_ref, v_ref, lse_ref = r.get("q"), r.get("k"), r.get("v"), r.get("lse")
    r.kt[...] = k_ref[...].T
    masks = head_masks()

    def scored(block):
        rows = slice(block * BLOCK, (block + 1) * BLOCK)
        return backward_scores(rows, *spots[block], masks, q_ref, k_ref, v_ref, r.do)

    ahead = scored(0)
    for block, (key_at, width) in enumerate(spots):
        now = ahead
        if block + 1 < len(spots):
            ahead = scored(block + 1)
        backward_sums(
            slice(block * BLOCK, (block + 1) * BLOCK), key_at, r.bias[block, :width, :], now, r.kt, lse_ref, r.delta,
            r.dqt, r.dk, r.dv,
        )
    r.out("dq")[...] = (r.dqt[...] * SCALE).astype(BF16).T
    r.out("dk")[...] = r.dk[...].astype(BF16)
    r.out("dv")[...] = r.dv[...].astype(BF16)
    for key in ("dq", "dk", "dv"):
        r.send(key)
    pack(packed, mark, 0, nn(query_turned[...], r.out("dq")[...]))
    pack(packed, mark, 1, nn(keys_turned[...], r.out("dk")[...]))
    pack(packed, mark, 2, nn(keys_turned[...], r.out("dv")[...]))


def self_back_other_kernel(causal, norm_at, bits, r):
    core = r.ids[0]
    z_ref, up_ref, x_ref = r.get("z"), r.get("up"), r.get("x")
    tokens, own, window = x_ref.shape[0], z_ref.shape[0], r.marks.shape[0]
    norms, branch = r.out("norms"), r.out("branch")
    gain, shift = norm_back(
        r,
        r.get("gain")[norm_at : norm_at + 1, :],
        lambda rows: z_ref[rows, :],
        lambda rows: up_ref[rows, :],
        (r.out("dz"), branch),
    )
    norms[0:1, :] = gain
    norms[1:2, :] = shift
    for key in ("norms", "dz", "branch"):
        r.send(key)
    keys_turned, query_turned = r.out("keys_turned"), r.out("query_turned")
    keys_turned[...] = x_ref[pl.ds(aligned(core * (tokens - window)), window), :].T
    query_turned[...] = x_ref[pl.ds(aligned(core * own), own), :].T
    r.send("keys_turned")
    r.send("query_turned")
    self_back_heads(r, causal, bits, 1, branch[...], norms, keys_turned, query_turned)


def self_back_own_kernel(causal, bits, r):
    branch = r.get("branch")[...]
    norms = None if causal else r.get("norms")
    self_back_heads(r, causal, bits, 0, branch, norms, r.get("keys_turned"), r.get("query_turned"))


def stream_gradient_kernel(r):
    core = r.ids[0]
    dz_ref, own, window = r.get("dz"), r.get("dq0").shape[0], r.get("dk0").shape[0]
    w = (r.get("w0"), r.get("w1"))
    r.near[...] = key_stream_gradient(r, [(w[g][1], w[g][2]) for g in range(2)])
    r.out("halo")[...] = r.near[pl.ds(aligned((1 - core) * own), window - own), :].astype(BF16)
    r.send("halo")
    r.out("dx")[...] = (
        dz_ref[...]
        + sum(nt(r.get(f"dq{g}")[...], w[g][0]) for g in range(2))
        + r.near[pl.ds(aligned(core * (window - own)), own), :]
    )


class Refs:
    def __init__(self, smem, ins, outs, scratch):
        for name, ref in list(smem.items()) + list(scratch.items()):
            setattr(self, name, ref)
        self.ins, self.outs = ins, outs
        self.waited, self.sent = set(), set()
        for copy, ref in ins.values():
            copy.start()

    def get(self, name):
        copy, ref = self.ins[name]
        if name not in self.waited:
            self.waited.add(name)
            copy.wait()
        return ref

    def out(self, name):
        return self.outs[name][1]

    def send(self, name):
        self.sent.add(name)
        self.outs[name][0].start()

    def close(self):
        for name in self.ins:
            self.get(name)
        for name in self.outs:
            if name not in self.sent:
                self.send(name)
        for copy, ref in self.outs.values():
            copy.wait()


def call(kernel, name, smem, ins, outs, scratch, cost):
    n_smem, n_in, n_out, n_scratch = len(smem), len(ins), len(outs), len(scratch)

    def body(*refs):
        smem_refs = refs[:n_smem]
        refs = refs[n_smem:]
        in_refs, out_refs, refs = refs[:n_in], refs[n_in : n_in + n_out], refs[n_in + n_out :]
        in_vmem, out_vmem, refs = refs[:n_in], refs[n_in : n_in + n_out], refs[n_in + n_out :]
        in_sem, out_sem = refs[-2:]
        copies_in = {
            key: (pltpu.make_async_copy(in_refs[i], in_vmem[i], in_sem.at[i]), in_vmem[i])
            for i, key in enumerate(ins)
        }
        copies_out = {
            key: (pltpu.make_async_copy(out_vmem[i], out_refs[i], out_sem.at[i]), out_vmem[i])
            for i, key in enumerate(outs)
        }
        held = Refs(dict(zip(smem, smem_refs)), copies_in, copies_out, dict(zip(scratch, refs)))
        kernel(held)
        held.close()

    held_bytes = sum(
        math.prod(shape[:-2]) * -(-shape[-2] // 8) * 8 * shape[-1] * jnp.dtype(dtype).itemsize
        for shape, dtype in [(array.shape, array.dtype) for array in ins.values()] + list(outs.values()) + list(scratch.values())
    )
    results = pl.pallas_call(
        body,
        out_shape=[jax.ShapeDtypeStruct(*out) for out in outs.values()],
        in_specs=[pl.BlockSpec(memory_space=pltpu.SMEM)] * n_smem + [pl.BlockSpec(memory_space=pl.ANY)] * n_in,
        out_specs=[pl.BlockSpec(memory_space=pl.ANY)] * n_out,
        scratch_shapes=[pltpu.VMEM(array.shape, array.dtype) for array in ins.values()]
        + [pltpu.VMEM(*out) for out in outs.values()]
        + [pltpu.VMEM(*one) for one in scratch.values()]
        + [pltpu.SemaphoreType.DMA((n_in,)), pltpu.SemaphoreType.DMA((n_out,))],
        compiler_params=pltpu.CompilerParams(vmem_limit_bytes=held_bytes + SPARE),
        cost_estimate=pl.CostEstimate(flops=cost * 10**9, transcendentals=0, bytes_accessed=cost * 10**6),
        name=name,
    )(*smem.values(), *ins.values())
    return SimpleNamespace(**dict(zip(outs, results)))


def finish_kernel(kind, bits, ids_ref, *refs):
    mark = own_label(bits, ids_ref[0], ids_ref[1])
    gathered, sem = refs[-2:]
    n_outs = {"enc": 4, "dec": 2, "cross": 3, "up": 1, "down": 1}[kind]
    count = len(refs) - 2 - n_outs
    parts, outs = refs[:count], refs[count:-2]
    copies, at = [], 0
    for i, part in enumerate(parts):
        copies.append(pltpu.make_async_copy(part, gathered.at[pl.ds(at, part.shape[0])], sem.at[i]))
        at += part.shape[0]
    for copy in copies:
        copy.start()
    for copy in copies:
        copy.wait()
    for shard in range(SHARDS):
        unit, half = divmod(shard, 2)
        rows = slice(half * QUAD, (half + 1) * QUAD)
        where = pl.ds(mark ^ shard, 1)
        value = gathered[where, :QUAD, :][0].astype(F32)
        if kind == "up":
            outs[0][rows, quad(unit)] = value
        elif kind == "down":
            outs[0][quad(unit), rows] = value.T
        elif unit == 3:
            outs[2 if kind == "cross" else 1][:, quad(half)] = value
        elif kind != "cross":
            outs[0][unit, rows, :] = value
        elif unit == 0:
            outs[0][rows, :] = value
        else:
            outs[1][unit - 1, rows, :] = value
        if kind == "enc":
            norms = gathered[where, QUAD:, :][0].astype(F32)
            many = norm_rows(SHARDS)
            for i in range(many):
                row, side = divmod(shard * many + i, 2)
                if row < 10:
                    outs[2 + row // 5][row % 5 : row % 5 + 1, quad(side)] = norms[i : i + 1, :]


def finish(group, ids, outs):
    parts = group.parts
    shape = (SHARDS,) + parts[0].shape[1:]
    return pl.pallas_call(
        functools.partial(finish_kernel, group.kind, group.bits),
        out_shape=[jax.ShapeDtypeStruct(*out) for out in outs],
        in_specs=[pl.BlockSpec(memory_space=pltpu.SMEM)] + [pl.BlockSpec(memory_space=pl.ANY)] * len(parts),
        out_specs=[pl.BlockSpec(memory_space=pltpu.VMEM)] * len(outs),
        scratch_shapes=[pltpu.VMEM(shape, BF16), pltpu.SemaphoreType.DMA((len(parts),))],
        compiler_params=pltpu.CompilerParams(vmem_limit_bytes=FINISH_LIMIT),
        cost_estimate=pl.CostEstimate(flops=2 * 10**9, transcendentals=0, bytes_accessed=2 * 10**6),
        name="finish_" + group.kind,
    )(ids, *parts)


class Sum:
    def __init__(self, kind, bits, dp, mp, mine, other):
        self.kind, self.bits, self.dp, self.mp = kind, bits, dp, mp
        self.phase, self.parts, self.outgoing = -1, [mine], [other]

    def hop(self, array, step):
        pairs = []
        for place in range(self.dp):
            for core in range(self.mp):
                bit = self.bits[core][step] if step < 4 else step
                pairs.append((place * self.mp + core, (place ^ (1 << bit)) * self.mp + core))
        return lax.ppermute(array, ("dp", "mp"), pairs)

    def launch(self):
        if self.phase < 0:
            self.flying = [lax.ppermute(self.outgoing[0], "mp", [(0, 1), (1, 0)])]
        elif self.phase <= 3:
            self.flying = [self.hop(self.outgoing[0], self.last if self.phase == 3 else self.phase)]
        else:
            self.flying = [self.hop(part, 6 - self.phase) for part in self.outgoing]

    def add_up(self):
        self.phase += 1
        if self.phase <= 2:
            mine, sent = self.parts[0], self.flying[0]
            half = mine.shape[0] // 2
            self.outgoing, self.parts = [mine[half:] + sent[half:]], [mine[:half] + sent[:half]]
        elif self.phase == 3:
            part, self.last = self.parts[0] + self.flying[0], 3
            while 2 << self.last < self.dp:
                part = part + self.hop(part, self.last)
                self.last += 1
            self.parts = self.outgoing = [part]
        elif self.phase == 4:
            self.parts = self.outgoing = [self.parts[0] + self.flying[0]]
        else:
            self.parts = self.parts + self.flying
            if self.phase < 7:
                self.outgoing = self.parts if self.phase == 5 and self.kind == "enc" else [jnp.concatenate(self.parts)]
        self.flying = []


def boundary(before, after, landing, launching=()):
    before, after, landing, launching = list(before), list(after), list(landing), list(launching)
    before, landed = lax.optimization_barrier((before, [group.flying for group in landing]))
    for group, flying in zip(landing, landed):
        group.flying = flying
        group.add_up()
    moving = landing + launching
    states = [([] if group.phase < 0 else group.parts, group.outgoing) for group in moving]
    before, after, states = lax.optimization_barrier((before, after, states))
    for group, state in zip(moving, states):
        group.outgoing = list(state[1])
        if group.phase >= 0:
            group.parts = list(state[0])
        if group.phase < 7:
            group.launch()
    return before, after


def on_device(
    src_embed, tgt_embed, src_segment, tgt_segment, enc_qkv, enc_out_proj, dec_qkv, dec_out_proj, cross_query,
    cross_kv, cross_out_proj, ffn_up, ffn_down, norm_gain, norm_bias, enc_cotangent, dec_cotangent,
):
    dp, mp = lax.axis_size("dp"), lax.axis_size("mp")
    tokens, model = src_embed.shape
    own = tokens // mp
    window = own + MOST
    half = ffn_up.shape[1]
    hidden = 2 * half
    position = lax.axis_index("mp")
    ids = jnp.stack([position, lax.axis_index("dp")]).astype(jnp.int32)
    pairs = [(0, 1), (1, 0)]

    def swap(tree):
        return jax.tree.map(lambda a: lax.ppermute(a, "mp", pairs), tree)

    enc_w1, enc_o1 = swap((enc_qkv, enc_out_proj))
    up1, down1 = swap((ffn_up, ffn_down))
    dec_w1, dec_o1 = swap((dec_qkv, dec_out_proj))
    cross_q1, cross_kv1, cross_o1 = swap((cross_query, cross_kv, cross_out_proj))
    feed = {"up0": ffn_up, "up1": up1, "down0": ffn_down, "down1": down1}

    def rows(count, dtype):
        return ((count, model), dtype)

    blocks = own // BLOCK
    q_shape, k_shape, ot_shape, lse_shape = ((own, QUAD), BF16), ((window, QUAD), BF16), ((QUAD, own), BF16), ((4, own), F32)
    vt_shape, marks, bias = ((4 * STRIDE, window), BF16), ((window, BLOCK), jnp.int32), ((blocks, 3 * BLOCK, BLOCK), F32)
    heads = {"q": q_shape, "k": k_shape, "v": k_shape, "ot": ot_shape, "lse": lse_shape}
    wide = ((own, half), BF16)
    norm_in = {"gain": norm_gain, "shift": norm_bias}
    first = call(
        own_heads_kernel, "own_heads", {"ids": ids},
        {"src_row": src_segment, "src": src_embed, "src_w": enc_qkv,
         "tgt_row": tgt_segment, "tgt": tgt_embed, "tgt_w": dec_qkv},
        {f"{side}_{key}": shape for side in ("src", "tgt") for key, shape in heads.items()},
        {"marks": marks, "src_bias": bias, "tgt_bias": bias, "src_vt": vt_shape, "tgt_vt": vt_shape},
        cost=8,
    )
    encoder = call(
        encoder_kernel, "encoder_forward", {"ids": ids},
        {"row": src_segment, "x": src_embed, "w": enc_w1, "ot0": first.src_ot, "wo0": enc_out_proj, "wo1": enc_o1,
         **norm_in, "up0": ffn_up, "down0": ffn_down, "up1": up1, "down1": down1},
        {**heads, "z0": rows(own, F32), "x1_low": rows(own, BF16), "h0": wide, "h1": wide,
         "z1": rows(own, F32), "enc": rows(own, BF16)},
        {"marks": marks, "bias": bias, "vt": vt_shape, "x1": rows(own, F32), "acc": rows(own, F32)},
        cost=12,
    )
    enc_swapped = swap(encoder.enc)
    decoder = call(
        decoder_kernel, "decoder_self_forward", {"ids": ids},
        {"row": tgt_segment, "x": tgt_embed, "w": dec_w1, "ot0": first.tgt_ot, "wo0": dec_out_proj, "wo1": dec_o1,
         **norm_in},
        {**heads, "z2": rows(own, F32), "x2": rows(own, F32)},
        {"marks": marks, "bias": bias, "vt": vt_shape, "acc": rows(own, F32)}, cost=6,
    )
    packed = ((SHARDS, QUAD, QUAD), BF16)
    packed_norms = ((SHARDS, QUAD + TILE, QUAD), BF16)
    crossed = call(
        cross_kernel, "cross_and_decoder_feed",
        {"ids": ids, "src_marks": src_segment, "tgt_marks": tgt_segment},
        {"src_row": src_segment, "tgt_row": tgt_segment, "enc_own": encoder.enc, "enc_other": enc_swapped,
         "x2": decoder.x2, "cq0": cross_query, "ckv0": cross_kv, "cq1": cross_q1, "ckv1": cross_kv1,
         "co0": cross_out_proj, "co1": cross_o1, **norm_in, **feed, "cot": dec_cotangent},
        {"enc": rows(tokens, BF16), "x3_low": rows(own, BF16), "a0": wide, "a1": wide, "dec": rows(own, BF16),
         "dy": rows(own, BF16), "dh0": wide, "dh1": wide, "norms": rows(4, F32), "pack0": packed, "pack1": packed,
         "denc_other": rows(own, BF16), "denc_own": rows(own, F32), "g2": rows(own, F32)},
        {"marks": ((tokens, BLOCK), jnp.int32), "bias": bias, "q": ((2, own, QUAD), BF16),
         "k": ((2, tokens, QUAD), BF16), "v": ((2, tokens, QUAD), BF16), "turn": ((2, QUAD, tokens), BF16), "vt": ((2, 4 * STRIDE, tokens), BF16),
         "mix": ((model, own), F32), "tops": ((8, own), F32), "totals": ((8, own), F32), "lse": ((2, 4, own), F32),
         "ot": ((model, own), BF16), "acc": rows(own, F32), "x3": rows(own, F32), "z3": rows(own, F32),
         "z4": rows(own, F32), "dz": rows(own, F32), "h": ((2, own, half), BF16), "low": rows(own, BF16), "do": ((2, own, QUAD), BF16),
         "delta": ((2, 4, own), F32), "dqt": ((2, QUAD, own), F32), "dk": ((2, tokens, QUAD), F32),
         "dv": ((2, tokens, QUAD), F32), "denc": rows(tokens, F32)},
        cost=30,
    )
    def whole(mine, received):
        return jnp.where(
            position == 0, jnp.concatenate([mine, received]), jnp.concatenate([received, mine])
        )

    def group(kind, bits, mine, other):
        return Sum(kind, bits, dp, mp, mine, other)

    head_scratch = {
        "marks": marks, "bias": bias, "do": q_shape, "delta": ((4, own), F32), "kt": ((QUAD, window), BF16),
        "dqt": ((QUAD, own), F32), "dk": ((window, QUAD), F32), "dv": ((window, QUAD), F32),
    }
    turned_shapes = {"keys_turned": ((model, window), BF16), "query_turned": ((model, own), BF16)}
    head_outs = {"dq": q_shape, "dk": k_shape, "dv": k_shape}

    def self_other(causal, at, bits, name, x, row, z, up, w_out, heads_kept, pack_shape, more):
        ins = {"z": z, "up": up, "gain": norm_gain, "row": row, "x": x, "wo": w_out} | heads_kept | more
        return call(
            functools.partial(self_back_other_kernel, causal, at, bits), name, {"ids": ids}, ins,
            {"dz": rows(own, F32), "branch": rows(own, BF16), "norms": rows(2, F32), "pack": pack_shape}
            | turned_shapes | head_outs,
            head_scratch, cost=9,
        )

    def self_own(causal, bits, name, back, row, branch, w_out, heads_kept, pack_shape, more):
        ins = {"branch": branch, "row": row, "wo": w_out} | heads_kept
        ins |= {"keys_turned": back.keys_turned, "query_turned": back.query_turned} | more
        return call(
            functools.partial(self_back_own_kernel, causal, bits), name, {"ids": ids}, ins,
            {"pack": pack_shape} | head_outs, head_scratch, cost=7,
        )

    def kept_own(side):
        return {key: getattr(first, f"{side}_{key}") for key in ("ot", "k", "q", "v", "lse")}

    def kept_other(part):
        return {key: getattr(part, key) for key in ("ot", "k", "q", "v", "lse")}

    def stream_gradient(name, back, back_own, w0, w1, gate):
        ins = {"dz": gate, "w0": w0, "w1": w1}
        for key in ("dk", "dv", "dq"):
            ins |= {f"{key}0": getattr(back_own, key), f"{key}1": getattr(back, key)}
        return call(
            stream_gradient_kernel, name, {"ids": ids}, ins,
            {"halo": rows(window - own, BF16), "dx": rows(own, F32)}, {"near": rows(window, F32)}, cost=5,
        )

    def group(kind, bits, mine, other):
        return Sum(kind, bits, dp, mp, mine, other)

    halo_at = (1 - position) * (own - (window - own))

    def with_halo(grad, received):
        part = lax.dynamic_slice_in_dim(grad, halo_at, window - own, 0) + received.astype(F32)
        return lax.dynamic_update_slice_in_dim(grad, part, halo_at, 0)

    square, out_half, triple = ((model, QUAD), F32), ((QUAD, model), F32), ((3, model, QUAD), F32)
    out_shapes = {
        "cross": [square, ((2, model, QUAD), F32), out_half],
        "dec": [triple, out_half],
        "up": [((model, half), F32)],
        "down": [rows(half, F32)],
        "enc": [triple, out_half, rows(5, F32), rows(5, F32)],
    }
    cross_sum = group("cross", CROSS_BITS, crossed.pack0, crossed.pack1)
    cross_sum.launch()
    denc_recv = swap(crossed.denc_other)
    (cross_norms,), (z1, denc_recv) = boundary([crossed.norms], [encoder.z1, denc_recv], [cross_sum])
    fed = call(
        feed_other_kernel, "encoder_feed_other", {"ids": ids},
        {"cot": enc_cotangent, "denc_own": crossed.denc_own, "denc_recv": denc_recv, "z1": z1, "gain": norm_gain,
         "x1_low": encoder.x1_low, "x3_low": crossed.x3_low, "dy3": crossed.dy, "down": down1, "h": encoder.h1,
         "up": up1, "dh": crossed.dh1, "a": crossed.a1},
        {"dy": rows(own, BF16), "norms": rows(2, F32), "turned": ((4, model, own), BF16), "up_pack": packed,
         "down_pack": packed, "g0": rows(own, F32)},
        {}, cost=10,
    )
    up_sum = group("up", UP_BITS, None, fed.up_pack)
    down_sum = group("down", DOWN_BITS, None, fed.down_pack)
    (feed_norms,), (dy1,) = boundary([fed.norms], [fed.dy], [cross_sum], [up_sum, down_sum])
    fed_own = call(
        feed_own_kernel, "encoder_feed_own", {"ids": ids},
        {"dy": dy1, "down": ffn_down, "h": encoder.h0, "dz": fed.g0, "turned": fed.turned, "up": ffn_up,
         "dh": crossed.dh0, "a": crossed.a0},
        {"g0": rows(own, F32), "up_pack": packed, "down_pack": packed}, {}, cost=9,
    )
    up_sum.parts, down_sum.parts = [fed_own.up_pack], [fed_own.down_pack]
    (feed_norms,), (g2,) = boundary([feed_norms], [crossed.g2], [cross_sum, up_sum, down_sum])
    dec_back = self_other(
        True, 2, DEC_BITS, "decoder_self_other", tgt_embed, tgt_segment, decoder.z2, g2, dec_o1, kept_other(decoder),
        packed, {},
    )
    dec_sum = group("dec", DEC_BITS, None, dec_back.pack)
    (dec_norms,), (branch,) = boundary([dec_back.norms], [dec_back.branch], [cross_sum, up_sum], [dec_sum])
    dec_own = self_own(
        True, DEC_BITS, "decoder_self_own", dec_back, tgt_segment, branch, dec_out_proj, kept_own("tgt"), packed, {},
    )
    dec_sum.parts = [dec_own.pack]
    (dec_norms,), (g0,) = boundary([dec_norms], [fed_own.g0], [cross_sum, up_sum, down_sum, dec_sum])
    norms_before = {"feed_norms": feed_norms, "dec_norms": dec_norms, "cross_norms": cross_norms}
    enc_back = self_other(
        False, 0, ENC_BITS, "encoder_self_other", src_embed, src_segment, encoder.z0, g0, enc_o1, kept_other(encoder),
        packed_norms, norms_before,
    )
    enc_sum = group("enc", ENC_BITS, None, enc_back.pack)
    (enc_norms,), (branch,) = boundary(
        [enc_back.norms], [enc_back.branch], [cross_sum, up_sum, down_sum, dec_sum], [enc_sum]
    )
    enc_own = self_own(
        False, ENC_BITS, "encoder_self_own", enc_back, src_segment, branch, enc_out_proj, kept_own("src"),
        packed_norms, {"norms": enc_norms, **norms_before},
    )
    enc_sum.parts = [enc_own.pack]
    (src_dz,), () = boundary([enc_own.dq], [], [enc_sum, cross_sum, dec_sum, up_sum, down_sum])
    enc_own.dq = src_dz
    src_side = stream_gradient("src_gradient", enc_back, enc_own, enc_qkv, enc_w1, enc_back.dz)
    (src_halo,), () = boundary([src_side.halo], [], [enc_sum])
    (src_halo,), () = boundary([src_halo], [], [dec_sum])
    (src_halo,), (tgt_dz,) = boundary([src_halo], [dec_back.dz], [up_sum])
    tgt_side = stream_gradient("tgt_gradient", dec_back, dec_own, dec_qkv, dec_w1, tgt_dz)
    (tgt_halo,), () = boundary([tgt_side.halo], [], [enc_sum])
    (tgt_halo,), (dec_part, src_halo) = boundary([tgt_halo], [crossed.dec, src_halo], [down_sum, cross_sum])
    src_recv, tgt_recv, dec_swapped = swap(src_halo), swap(tgt_halo), swap(dec_part)
    (dec_swapped,), () = boundary([dec_swapped], [], [up_sum, dec_sum])
    cross_out = list(finish(cross_sum, ids, out_shapes["cross"]))
    dec_whole = whole(crossed.dec, dec_swapped)
    (dec_whole, norm_gate), (src_recv,) = boundary([dec_whole, cross_out[0]], [src_recv], [enc_sum, down_sum])
    cross_out[0] = norm_gate
    src_grad = with_halo(src_side.dx, src_recv)
    (src_grad,), (tgt_recv,) = boundary([src_grad], [tgt_recv], [up_sum, dec_sum])
    tgt_grad = with_halo(tgt_side.dx, tgt_recv)
    (tgt_grad,), () = boundary([tgt_grad], [], [enc_sum])
    (tgt_grad,), () = boundary([tgt_grad], [], [down_sum])
    (tgt_grad,), () = boundary([tgt_grad], [], [dec_sum])
    up_out = finish(up_sum, ids, out_shapes["up"])
    (up_gate,), () = boundary([up_out[0]], [], [enc_sum])
    up_out = [up_gate]
    (up_gate,), () = boundary([up_gate], [], [enc_sum])
    up_out = [up_gate]
    (up_gate,), () = boundary([up_gate], [], [down_sum])
    up_out = [up_gate]
    down_out = finish(down_sum, ids, out_shapes["down"])
    (down_gate,), () = boundary([down_out[0]], [], [dec_sum])
    down_out = [down_gate]
    dec_out = finish(dec_sum, ids, out_shapes["dec"])
    (dec_gate,), () = boundary([dec_out[0]], [], [enc_sum])
    dec_out = [dec_gate, dec_out[1]]
    enc_out = finish(enc_sum, ids, out_shapes["enc"])

    return (
        crossed.enc,
        dec_whole,
        src_grad,
        tgt_grad,
        enc_out[0],
        enc_out[1],
        dec_out[0],
        dec_out[1],
        cross_out[0],
        cross_out[1],
        cross_out[2],
        up_out[0],
        down_out[0],
        enc_out[2],
        enc_out[3],
    )


def solution(mesh):
    in_specs = (
        P("dp", None), P("dp", None), P("dp", None), P("dp", None),
        P(None, None, "mp"), P("mp", None), P(None, None, "mp"), P("mp", None),
        P(None, "mp"), P(None, None, "mp"), P("mp", None), P(None, "mp"), P("mp", None),
        P(), P(), P(("dp", "mp"), None), P(("dp", "mp"), None),
    )
    out_specs = (
        P("dp", None), P("dp", None), P(("dp", "mp"), None), P(("dp", "mp"), None),
        P(None, None, "mp"), P("mp", None), P(None, None, "mp"), P("mp", None),
        P(None, "mp"), P(None, None, "mp"), P("mp", None), P(None, "mp"), P("mp", None),
        P(), P(),
    )
    return jax.shard_map(on_device, mesh=mesh, in_specs=in_specs, out_specs=out_specs, check_vma=False)
```

```python
import functools
import math
from types import SimpleNamespace

import jax
import jax.numpy as jnp
from jax import lax
from jax.experimental import pallas as pl
from jax.experimental.pallas import tpu as pltpu
from jax.sharding import PartitionSpec as P

HDIM = 64
SCALE = HDIM ** (-0.5)
EPSILON = 1e-05
MASKED = -1e30
BLOCK = 128
MOST = 128
QUAD = 4 * HDIM
UNITS = 4
TILE = 16
FEED = 512
SHARDS = 8
UP_BITS = ((0, 1, 2, 3), (1, 0, 2, 3))
DOWN_BITS = ((1, 0, 2, 3), (0, 1, 2, 3))
CROSS_BITS = ((0, 1, 2, 3), (1, 0, 2, 3))
DEC_BITS = ((0, 1, 2, 3), (1, 0, 2, 3))
STRIDE = HDIM + TILE
ENC_BITS = ((1, 0, 2, 3), (0, 1, 2, 3))
F32 = jnp.float32
BF16 = jnp.bfloat16
VMEM_LIMIT = 56 * 1024 * 1024
FINISH_LIMIT = 10 * 1024 * 1024
SPARE = 6 * 1024 * 1024
GELU_IN = math.sqrt(2.0 / math.pi)
GELU_CUBE = 0.044715


def nn(left, right):
    return jnp.dot(left, right, preferred_element_type=F32)


def nt(left, right):
    return lax.dot_general(left, right, (((1,), (1,)), ((), ())), preferred_element_type=F32)


def tn(left, right):
    return lax.dot_general(left, right, (((0,), (0,)), ((), ())), preferred_element_type=F32)


def aligned(index, size=BLOCK):
    return pl.multiple_of(index, size)


def over_rows(rows, chunk, body, carry, unroll=4):
    return lax.fori_loop(
        0,
        rows // chunk,
        lambda i, kept: body(pl.ds(aligned(i * chunk, chunk), chunk), kept),
        carry,
        unroll=min(unroll, rows // chunk),
    )


def normalize(before):
    centered = before - jnp.mean(before, axis=-1, keepdims=True)
    variance = jnp.mean(centered * centered, axis=-1, keepdims=True)
    rate = lax.rsqrt(variance + EPSILON)
    return centered * rate, rate


def norm_backward(before, upstream, gain_row):
    normed, rate = normalize(before)
    scaled = upstream * gain_row
    first = jnp.mean(scaled, axis=-1, keepdims=True)
    second = jnp.mean(scaled * normed, axis=-1, keepdims=True)
    return rate * (scaled - first - normed * second), upstream * normed


def fold_rows(block):
    return jnp.sum(block.reshape(block.shape[0] // 8, 8, block.shape[1]), axis=0)


def gelu(hidden):
    inner = GELU_IN * hidden * (1.0 + GELU_CUBE * hidden * hidden)
    return 0.5 * hidden * (1.0 + jnp.tanh(inner))


def gelu_both(hidden):
    square = hidden * hidden
    bent = jnp.tanh(GELU_IN * hidden * (1.0 + GELU_CUBE * square))
    half = 0.5 * (1.0 + bent)
    slope = half + 0.5 * hidden * (1.0 - bent * bent) * (GELU_IN * (1.0 + 3.0 * GELU_CUBE * square))
    return hidden * half, slope


def head_masks():
    lane = lax.broadcasted_iota(jnp.int32, (1, QUAD), 1)
    return [
        jnp.where((lane >= h * HDIM) & (lane < (h + 1) * HDIM), 1.0, 0.0).astype(BF16)
        for h in range(4)
    ]


def stack_heads(block, masks):
    return jnp.concatenate([block * mask for mask in masks], axis=0)


def quad(g):
    return slice(g * QUAD, (g + 1) * QUAD)


def bias_for(marks_ref, key_at, width, query_row, causal=False, key_start=0, query_start=0):
    allowed = marks_ref[pl.ds(key_at, width), :] == query_row
    if causal:
        places = key_start + lax.broadcasted_iota(jnp.int32, (width, BLOCK), 0)
        queries = query_start + lax.broadcasted_iota(jnp.int32, (width, BLOCK), 1)
        allowed = allowed & (places <= queries)
    return jnp.where(allowed, 0.0, MASKED)


def self_window(core, block, causal):
    middle = block + core
    if causal:
        return aligned(jnp.maximum(middle - 1, 0) * BLOCK), 2 * BLOCK
    return aligned(jnp.clip(middle - 1, 0, 2) * BLOCK), 3 * BLOCK


def set_self_bias(bias_ref, core, tokens, marks_ref, row_ref, causal):
    window, own = marks_ref.shape[0], row_ref.shape[1] // 2
    start = core * (tokens - window)
    spots = []
    for block in range(own // BLOCK):
        key_at, width = self_window(core, block, causal)
        first = aligned(core * own + block * BLOCK)
        bias_ref[block, :width, :] = bias_for(
            marks_ref, key_at, width, row_ref[:, pl.ds(first, BLOCK)], causal, start + key_at, first
        )
        spots.append((key_at, width))
    return spots


def soft_weights(scores, h, bias, top=None):
    one = scores[:, h * BLOCK : (h + 1) * BLOCK] + bias
    high = jnp.max(one, axis=0, keepdims=True)
    top = high if top is None else jnp.maximum(top, high)
    return top, jnp.exp((one - top).astype(BF16))


def set_values(vt_ref, values):
    turned = values.T
    for h in range(4):
        vt_ref[h * STRIDE : h * STRIDE + HDIM, :] = turned[h * HDIM : (h + 1) * HDIM]
        vt_ref[h * STRIDE + HDIM : (h + 1) * STRIDE, :] = jnp.ones((TILE, turned.shape[1]), BF16)


def quad_forward(spots, q_ref, k_ref, vt_ref, bias_ref, ot_ref, lse_ref, masks):
    def score(block):
        rows, (key_at, width) = slice(block * BLOCK, (block + 1) * BLOCK), spots[block]
        return nt(k_ref[pl.ds(key_at, width), :], stack_heads(q_ref[rows, :], masks))

    ahead = score(0)
    for block, (key_at, width) in enumerate(spots):
        rows = slice(block * BLOCK, (block + 1) * BLOCK)
        scores, ahead = ahead, score(block + 1) if block + 1 < len(spots) else None
        for h in range(4):
            top, weights = soft_weights(scores, h, bias_ref[block, :width, :])
            features = slice(h * HDIM, (h + 1) * HDIM)
            mixed = nn(vt_ref[h * STRIDE : (h + 1) * STRIDE, pl.ds(key_at, width)], weights)
            total = mixed[HDIM : HDIM + 1]
            ot_ref[features, rows] = (mixed[:HDIM] * (1.0 / total)).astype(BF16)
            lse_ref[h : h + 1, rows] = top + jnp.log(total)


def backward_scores(rows, key_at, width, masks, q_ref, k_ref, v_ref, do_ref):
    keys = pl.ds(key_at, width)
    q_stack, do_stack = stack_heads(q_ref[rows, :], masks), stack_heads(do_ref[rows, :], masks)
    return q_stack, do_stack, nt(k_ref[keys, :], q_stack), nt(v_ref[keys, :], do_stack)


def backward_sums(rows, key_at, bias, scored, kt_ref, lse_ref, delta_ref, dqt_ref, dk_ref, dv_ref, add=False):
    q_stack, do_stack, scores, prob_grads = scored
    keys = pl.ds(key_at, bias.shape[0])
    probs, score_grads = [], []
    for h in range(4):
        cols = slice(h * BLOCK, (h + 1) * BLOCK)
        prob = jnp.exp((scores[:, cols] + bias - lse_ref[h : h + 1, rows]).astype(BF16))
        probs.append(prob)
        score_grads.append(prob * (prob_grads[:, cols] - delta_ref[h : h + 1, rows]).astype(BF16))
    for h in range(4):
        features = slice(h * HDIM, (h + 1) * HDIM)
        query_grad = nn(kt_ref[features, keys], score_grads[h])
        if add:
            dqt_ref[features, rows] += query_grad
        else:
            dqt_ref[features, rows] = query_grad
    dv_ref[keys, :] += nn(jnp.concatenate(probs, axis=1), do_stack)
    dk_ref[keys, :] += nn(jnp.concatenate(score_grads, axis=1), q_stack)


def mixed_gradients(branch, ot, w_out, do_ref, delta_ref):
    do_ref[...] = nt(branch, w_out).astype(BF16)
    product = nt(w_out, branch).astype(BF16).astype(F32) * ot.astype(F32)
    for h in range(4):
        delta_ref[h : h + 1, :] = jnp.sum(product[h * HDIM : (h + 1) * HDIM, :], axis=0, keepdims=True)


def spread_marks(marks_ref, row):
    marks_ref[...] = jnp.broadcast_to(row, (marks_ref.shape[1], marks_ref.shape[0])).T


def label(bits, place):
    first, second, third = [(place >> bit) & 1 for bit in bits[:3]]
    return 4 * first + 2 * second + third


def own_label(bits, core, place):
    return jnp.where(core == 0, label(bits[0], place), label(bits[1], place))


def pack(out_ref, mark, unit, value, at=0):
    rows = value.shape[0] // 2
    for half in range(2):
        where = pl.ds(mark ^ (2 * unit + half), 1)
        out_ref[where, at : at + rows, :] = value[half * rows : (half + 1) * rows].astype(BF16)[None]


def as_unit(value):
    return jnp.concatenate([value[:, :QUAD], value[:, QUAD:]], axis=0).astype(BF16)


def pack_norms(out_ref, mark, parts):
    shards, tall, width = out_ref.shape
    halves = [part[:, half * width : (half + 1) * width] for part in parts for half in range(2)]
    each = norm_rows(shards)
    blank = jnp.zeros((1, width), F32)
    halves += [blank] * (shards * each - len(halves))
    for i in range(shards):
        block = jnp.concatenate(halves[i * each : (i + 1) * each] + [blank] * (TILE - each), axis=0)
        out_ref[pl.ds(mark ^ i, 1), tall - TILE :, :] = block.astype(BF16)[None]


def norm_rows(shards):
    return -(-20 // shards)


def prepare_quad(x_ref, w_ref, core, q_ref, k_ref, v_ref, vt_ref):
    tokens, own, window = x_ref.shape[0], q_ref.shape[0], k_ref.shape[0]
    keys = x_ref[pl.ds(aligned(core * (tokens - window)), window), :]
    q_ref[...] = (nn(x_ref[pl.ds(aligned(core * own), own), :], w_ref[0]) * SCALE).astype(BF16)
    k_ref[...] = nn(keys, w_ref[1]).astype(BF16)
    v_ref[...] = nn(keys, w_ref[2]).astype(BF16)
    set_values(vt_ref, v_ref[...])


def own_heads_kernel(r):
    core = r.ids[0]
    masks = head_masks()
    for side, causal in (("src", False), ("tgt", True)):
        x_ref, row_ref = r.get(side), r.get(side + "_row")
        k_ref = r.out(side + "_k")
        start = aligned(core * (x_ref.shape[0] - k_ref.shape[0]))
        spread_marks(r.marks, row_ref[:, pl.ds(start, k_ref.shape[0])])
        bias_ref, vt_ref = getattr(r, side + "_bias"), getattr(r, side + "_vt")
        spots = set_self_bias(bias_ref, core, x_ref.shape[0], r.marks, row_ref, causal)
        q_ref, v_ref = r.out(side + "_q"), r.out(side + "_v")
        prepare_quad(x_ref, r.get(side + "_w"), core, q_ref, k_ref, v_ref, vt_ref)
        for key in ("_q", "_k", "_v"):
            r.send(side + key)
        quad_forward(
            spots, q_ref, k_ref, vt_ref, bias_ref, r.out(side + "_ot"), r.out(side + "_lse"), masks
        )
        r.send(side + "_ot")
        r.send(side + "_lse")


def other_heads(r, causal):
    core = r.ids[0]
    x_ref, row_ref, k_ref = r.get("x"), r.get("row"), r.out("k")
    start = aligned(core * (x_ref.shape[0] - k_ref.shape[0]))
    spread_marks(r.marks, row_ref[:, pl.ds(start, k_ref.shape[0])])
    spots = set_self_bias(r.bias, core, x_ref.shape[0], r.marks, row_ref, causal)
    q_ref, v_ref, ot_ref = r.out("q"), r.out("v"), r.out("ot")
    prepare_quad(x_ref, r.get("w"), core, q_ref, k_ref, v_ref, r.vt)
    for key in ("q", "k", "v"):
        r.send(key)
    quad_forward(spots, q_ref, k_ref, r.vt, r.bias, ot_ref, r.out("lse"), head_masks())
    r.send("lse")
    r.send("ot")
    r.acc[...] = tn(r.get("ot0")[...], r.get("wo0")[...]) + tn(ot_ref[...], r.get("wo1")[...])


def norm_forward(r, at, residual, before_ref, after_ref, low_ref):
    gain, shift = r.get("gain")[at : at + 1, :], r.get("shift")[at : at + 1, :]

    def body(rows, carry):
        before = residual(rows) + r.acc[rows, :]
        if before_ref is not None:
            before_ref[rows, :] = before
        after = normalize(before)[0] * gain + shift
        if after_ref is not None:
            after_ref[rows, :] = after
        if low_ref is not None:
            low_ref[rows, :] = after.astype(BF16)
        return carry

    over_rows(r.acc.shape[0], 32, body, 0)


def own_row_reader(x_ref, core, own):
    first = core * own
    return lambda rows: x_ref[pl.ds(aligned(first + rows.start, rows.size), rows.size), :].astype(F32)


def encoder_kernel(r):
    other_heads(r, False)
    x1_low = r.out("x1_low")
    norm_forward(r, 0, own_row_reader(r.get("x"), r.ids[0], r.acc.shape[0]), r.out("z0"), r.x1, x1_low)
    r.send("z0")
    r.send("x1_low")
    feed_forward(x1_low, *feed_weights(r), (r.out("h0"), r.out("h1")), None, r.acc)
    r.send("h0")
    r.send("h1")
    norm_forward(r, 1, lambda rows: r.x1[rows, :], r.out("z1"), None, r.out("enc"))


def decoder_kernel(r):
    other_heads(r, True)
    norm_forward(r, 2, own_row_reader(r.get("x"), r.ids[0], r.acc.shape[0]), r.out("z2"), r.out("x2"), None)


def feed_weights(r):
    return (r.get("up0"), r.get("up1")), (r.get("down0"), r.get("down1"))


def feed_chunks(half):
    return [(j, slice(j * FEED, (j + 1) * FEED)) for j in range(half // FEED)]


def feed_forward(low_ref, ups, downs, h_refs, a_refs, acc_ref):
    chunks = [(g, cols) for g in range(2) for j, cols in feed_chunks(ups[0].shape[1])]
    ahead = nn(low_ref[...], ups[0][:, chunks[0][1]])
    for i, (g, cols) in enumerate(chunks):
        hidden = ahead
        if i + 1 < len(chunks):
            ahead = nn(low_ref[...], ups[chunks[i + 1][0]][:, chunks[i + 1][1]])
        hidden = hidden.astype(BF16)
        h_refs[g][:, cols] = hidden
        active = gelu(hidden)
        if a_refs is not None:
            a_refs[g][:, cols] = active
        term = nn(active, downs[g][cols, :])
        if i == 0:
            acc_ref[...] = term
        else:
            acc_ref[...] += term


def feed_backward(dy_ref, ups, downs, h_refs, dh_refs, acc_ref):
    chunks = [(g, cols) for g in range(2) for j, cols in feed_chunks(ups[0].shape[1])]
    ahead = nt(dy_ref[...], downs[0][chunks[0][1], :])
    for i, (g, cols) in enumerate(chunks):
        active_grad = ahead
        if i + 1 < len(chunks):
            ahead = nt(dy_ref[...], downs[chunks[i + 1][0]][chunks[i + 1][1], :])
        hidden_grad = active_grad.astype(BF16) * gelu_both(h_refs[g][:, cols])[1]
        dh_refs[g][:, cols] = hidden_grad
        acc_ref[...] += nt(hidden_grad, ups[g][:, cols])


def norm_back(r, gain_row, before, upstream, outs):
    def body(rows, sums):
        above = upstream(rows)
        grad, gain_terms = norm_backward(before(rows), above, gain_row)
        for ref in outs:
            ref[rows, :] = grad.astype(ref.dtype)
        return sums[0] + fold_rows(gain_terms), sums[1] + fold_rows(above)

    zeros = jnp.zeros((8, outs[0].shape[1]), F32)
    gains, shifts = over_rows(outs[0].shape[0], 32, body, (zeros, zeros))
    return jnp.sum(gains, axis=0, keepdims=True), jnp.sum(shifts, axis=0, keepdims=True)


def cross_kernel(r):
    core, place = r.ids[0], r.ids[1]
    x2_ref, enc_ref = r.get("x2"), r.out("enc")
    own, tokens = x2_ref.shape[0], enc_ref.shape[0]
    blocks = own // BLOCK
    first, second = aligned(core * own), aligned((1 - core) * own)
    width = 3 * BLOCK
    enc_ref[pl.ds(first, own), :] = r.get("enc_own")[...]
    enc_ref[pl.ds(second, own), :] = r.get("enc_other")[...]
    r.send("enc")
    spread_marks(r.marks, r.get("src_row")[...])
    steps = tokens.bit_length()

    def bound(mark, past):
        def step(i, pair):
            low, high = pair
            middle = (low + high) // 2
            value = r.src_marks[0, jnp.minimum(middle, tokens - 1)]
            below = (low < high) & ((value < mark) | (past & (value == mark)))
            above = (low < high) & jnp.logical_not(below)
            return jnp.where(below, middle + 1, low), jnp.where(above, middle, high)

        return lax.fori_loop(0, steps, step, (jnp.int32(0), jnp.int32(tokens)))[0]

    row_ref = r.get("tgt_row")
    query_rows, spots, more = [], [], []
    for block in range(blocks):
        head = first + block * BLOCK
        low = bound(r.tgt_marks[0, head], jnp.bool_(False)) // BLOCK
        high = (bound(r.tgt_marks[0, head + BLOCK - 1], jnp.bool_(True)) + BLOCK - 1) // BLOCK
        key_at = aligned(jnp.minimum(low, (tokens - width) // BLOCK) * BLOCK)
        query_rows.append(row_ref[:, pl.ds(aligned(head), BLOCK)])
        spots.append(key_at)
        more.append((key_at // BLOCK + 3, high))
        r.bias[block] = bias_for(r.marks, key_at, width, query_rows[block])
    masks = head_masks()
    x2_low = x2_ref[...].astype(BF16)
    for g in range(2):
        r.q[g] = (nn(x2_low, r.get(f"cq{g}")[...]) * SCALE).astype(BF16)
        r.k[g] = nn(enc_ref[...], r.get(f"ckv{g}")[0]).astype(BF16)
        r.v[g] = nn(enc_ref[...], r.get(f"ckv{g}")[1]).astype(BF16)
        set_values(r.vt.at[g], r.v[g])

    def weigh(g, h, scores, bias, key_at, keys_width, top):
        new_top, weights = soft_weights(scores, h, bias, top)
        mixed = nn(r.vt[g, h * STRIDE : (h + 1) * STRIDE, pl.ds(key_at, keys_width)], weights)
        features = slice(g * QUAD + h * HDIM, g * QUAD + (h + 1) * HDIM)
        return new_top, mixed[HDIM : HDIM + 1], mixed[:HDIM], features

    def score(block, g):
        rows = slice(block * BLOCK, (block + 1) * BLOCK)
        return nt(r.k[g, pl.ds(spots[block], width), :], stack_heads(r.q[g, rows, :], masks))

    tiles = [(block, g) for block in range(blocks) for g in range(2)]
    ahead = score(*tiles[0])
    for i, (block, g) in enumerate(tiles):
        rows = slice(block * BLOCK, (block + 1) * BLOCK)
        scores, ahead = ahead, score(*tiles[i + 1]) if i + 1 < len(tiles) else None
        for h in range(4):
            top, total, mixed, features = weigh(g, h, scores, r.bias[block], spots[block], width, None)
            r.mix[features, rows] = mixed
            r.tops[g * 4 + h : g * 4 + h + 1, rows] = top
            r.totals[g * 4 + h : g * 4 + h + 1, rows] = total

    for block in range(blocks):
        rows = slice(block * BLOCK, (block + 1) * BLOCK)

        def extra(i, carry, block=block, rows=rows):
            key_at = aligned(i * BLOCK)
            bias = bias_for(r.marks, key_at, BLOCK, query_rows[block])
            for g in range(2):
                scores = nt(r.k[g, pl.ds(key_at, BLOCK), :], stack_heads(r.q[g, rows, :], masks))
                for h in range(4):
                    at = slice(g * 4 + h, g * 4 + h + 1)
                    old = r.tops[at, rows]
                    top, total, mixed, features = weigh(g, h, scores, bias, key_at, BLOCK, old)
                    fade = jnp.exp(old - top)
                    r.mix[features, rows] = r.mix[features, rows] * fade + mixed
                    r.tops[at, rows] = top
                    r.totals[at, rows] = r.totals[at, rows] * fade + total
            return carry

        lax.fori_loop(*more[block], extra, 0)
    for head in range(8):
        features = slice(head * HDIM, (head + 1) * HDIM)
        at = slice(head, head + 1)
        r.ot[features, :] = (r.mix[features, :] * (1.0 / r.totals[at, :])).astype(BF16)
        r.lse[head // 4, head % 4 : head % 4 + 1, :] = r.tops[at, :] + jnp.log(r.totals[at, :])
    outs = (r.get("co0"), r.get("co1"))
    r.acc[...] = tn(r.ot[:QUAD, :], outs[0][...]) + tn(r.ot[QUAD:, :], outs[1][...])
    x3_low = r.out("x3_low")
    norm_forward(r, 3, lambda rows: x2_ref[rows, :], r.z3, r.x3, x3_low)
    r.send("x3_low")
    ups, downs = feed_weights(r)
    hs = (r.h.at[0], r.h.at[1])
    feed_forward(x3_low, ups, downs, hs, (r.out("a0"), r.out("a1")), r.acc)
    r.send("a0")
    r.send("a1")
    gain_ref, shift_ref, cot_ref, dec_ref, dy_ref = (
        r.get("gain"), r.get("shift"), r.get("cot"), r.out("dec"), r.out("dy")
    )
    last_gain, last_shift = gain_ref[4:5, :], shift_ref[4:5, :]

    def fourth_norm(rows, sums):
        before = r.x3[rows, :] + r.acc[rows, :]
        normed, rate = normalize(before)
        dec_ref[rows, :] = (normed * last_gain + last_shift).astype(BF16)
        upstream = cot_ref[rows, :].astype(F32)
        scaled = upstream * last_gain
        mean_one = jnp.mean(scaled, axis=-1, keepdims=True)
        mean_two = jnp.mean(scaled * normed, axis=-1, keepdims=True)
        grad = rate * (scaled - mean_one - normed * mean_two)
        r.z4[rows, :] = grad
        dy_ref[rows, :] = grad.astype(BF16)
        return sums[0] + fold_rows(upstream * normed), sums[1] + fold_rows(upstream)

    zeros = jnp.zeros((8, x2_ref.shape[1]), F32)
    gain_four, shift_four = over_rows(own, 32, fourth_norm, (zeros, zeros))
    r.send("dec")
    r.send("dy")
    feed_backward(dy_ref, ups, downs, hs, (r.out("dh0"), r.out("dh1")), r.z4)
    r.send("dh0")
    r.send("dh1")
    gain_three, shift_three = norm_back(
        r, gain_ref[3:4, :], lambda rows: r.z3[rows, :], lambda rows: r.z4[rows, :], (r.dz, r.low)
    )
    norms = r.out("norms")
    norms[0:1, :] = gain_three
    norms[1:2, :] = jnp.sum(gain_four, axis=0, keepdims=True)
    norms[2:3, :] = shift_three
    norms[3:4, :] = jnp.sum(shift_four, axis=0, keepdims=True)
    branch = r.low[...]
    ots = (r.ot.at[:QUAD], r.ot.at[QUAD:])
    for g in range(2):
        mixed_gradients(branch, ots[g][...], outs[g][...], r.do.at[g], r.delta.at[g])
    packs = pair_of_packs(r, CROSS_BITS)
    for g, (packed, mark) in enumerate(packs):
        pack(packed, mark, 3, as_unit(nn(ots[g][...], branch)))
        r.turn[g] = r.k[g].T
    r.dk[...] = jnp.zeros(r.dk.shape, F32)
    r.dv[...] = jnp.zeros(r.dv.shape, F32)

    def back_scores(block, g, key_at, keys_width):
        rows = slice(block * BLOCK, (block + 1) * BLOCK)
        return backward_scores(rows, key_at, keys_width, masks, r.q.at[g], r.k.at[g], r.v.at[g], r.do.at[g])

    def back_sums(block, g, key_at, bias, scored, add):
        backward_sums(
            slice(block * BLOCK, (block + 1) * BLOCK), key_at, bias, scored, r.turn.at[g], r.lse.at[g], r.delta.at[g],
            r.dqt.at[g], r.dk.at[g], r.dv.at[g], add,
        )

    ahead = back_scores(*tiles[0], spots[0], width)
    for i, (block, g) in enumerate(tiles):
        scored = ahead
        if i + 1 < len(tiles):
            ahead = back_scores(*tiles[i + 1], spots[tiles[i + 1][0]], width)
        back_sums(block, g, spots[block], r.bias[block], scored, False)
    for block in range(blocks):

        def extra_back(i, carry, block=block):
            key_at = aligned(i * BLOCK)
            bias = bias_for(r.marks, key_at, BLOCK, query_rows[block])
            for g in range(2):
                back_sums(block, g, key_at, bias, back_scores(block, g, key_at, BLOCK), True)
            return carry

        lax.fori_loop(*more[block], extra_back, 0)
    query_turned, enc_turned = x2_ref[...].astype(BF16).T, enc_ref[...].T
    query_grads = [(r.dqt[g] * SCALE).astype(BF16).T for g in range(2)]
    side_grads = [(r.dk[g].astype(BF16), r.dv[g].astype(BF16)) for g in range(2)]
    for g in (1, 0):
        packed, mark = packs[g]
        pack(packed, mark, 0, nn(query_turned, query_grads[g]))
        for i in range(2):
            pack(packed, mark, 1 + i, nn(enc_turned, side_grads[g][i]))
        r.send(f"pack{g}")
    r.denc[...] = sum(nt(side_grads[g][i], r.get(f"ckv{g}")[i]) for i in range(2) for g in range(2))
    r.out("denc_other")[...] = r.denc[pl.ds(second, own), :].astype(BF16)
    r.send("denc_other")
    r.out("denc_own")[...] = r.denc[pl.ds(first, own), :]
    r.send("denc_own")
    r.out("g2")[...] = r.dz[...] + sum(nt(query_grads[g], r.get(f"cq{g}")[...]) for g in range(2))


def pair_of_packs(r, bits, name="pack"):
    core, place = r.ids[0], r.ids[1]
    return [(r.out(f"{name}{g}"), own_label(bits, core ^ g, place)) for g in range(2)]


def key_stream_gradient(r, weights, keys=("dk", "dv")):
    return sum(nt(r.get(f"{keys[i]}{g}")[...], weights[g][i]) for i in range(2) for g in range(2))


def feed_gradients(r, g, dy_ref, acc_ref, turned):
    core, place = r.ids[0], r.ids[1]
    up_mark, down_mark = own_label(UP_BITS, core ^ g, place), own_label(DOWN_BITS, core ^ g, place)
    h_ref, dh_ref, a_ref, up_ref, down_ref = [r.get(key) for key in ("h", "dh", "a", "up", "down")]
    chunks = feed_chunks(h_ref.shape[1])
    ahead = nt(dy_ref[...], down_ref[chunks[0][1], :])
    for j, cols in chunks:
        above = ahead
        if j + 1 < len(chunks):
            ahead = nt(dy_ref[...], down_ref[chunks[j + 1][1], :])
        active, slope = gelu_both(h_ref[:, cols])
        hidden_grad = above.astype(BF16) * slope
        acc_ref[...] += nt(hidden_grad, up_ref[:, cols])
        up_grad = nn(turned[0], hidden_grad) + nn(turned[1], dh_ref[:, cols])
        down_grad = nn(turned[2], active) + nn(turned[3], a_ref[:, cols])
        for b in range(2):
            pack(r.out("up_pack"), up_mark, 2 * j + b, up_grad[:, quad(b)])
            pack(r.out("down_pack"), down_mark, 2 * j + b, down_grad[:, quad(b)])


def feed_other_kernel(r):
    cot_ref, own_ref, recv_ref, z1_ref = r.get("cot"), r.get("denc_own"), r.get("denc_recv"), r.get("z1")
    dy_ref, acc_ref, turned = r.out("dy"), r.out("g0"), r.out("turned")
    gain, shift = norm_back(
        r,
        r.get("gain")[1:2, :],
        lambda rows: z1_ref[rows, :],
        lambda rows: cot_ref[rows, :].astype(F32) + own_ref[rows, :] + recv_ref[rows, :].astype(F32),
        (acc_ref, dy_ref),
    )
    r.out("norms")[0:1, :] = gain
    r.out("norms")[1:2, :] = shift
    r.send("dy")
    for i, ref in enumerate((r.get("x1_low"), r.get("x3_low"), dy_ref, r.get("dy3"))):
        turned[i] = ref[...].T
    r.send("turned")
    feed_gradients(r, 1, dy_ref, acc_ref, turned)


def feed_own_kernel(r):
    acc_ref = r.out("g0")
    acc_ref[...] = r.get("dz")[...]
    feed_gradients(r, 0, r.get("dy"), acc_ref, r.get("turned"))


def norm_parts(norms, r):
    feed, dec, cross = r.get("feed_norms"), r.get("dec_norms"), r.get("cross_norms")
    rows = [(norms, 0), (feed, 0), (dec, 0), (cross, 0), (cross, 1)]
    rows += [(norms, 1), (feed, 1), (dec, 1), (cross, 2), (cross, 3)]
    return [ref[at : at + 1, :] for ref, at in rows]


def self_back_heads(r, causal, bits, g, branch, norms, keys_turned, query_turned):
    core, place = r.ids[0], r.ids[1]
    row_ref, window = r.get("row"), r.marks.shape[0]
    tokens = row_ref.shape[1]
    spread_marks(r.marks, row_ref[:, pl.ds(aligned(core * (tokens - window)), window)])
    spots = set_self_bias(r.bias, core, tokens, r.marks, row_ref, causal)
    ot_ref = r.get("ot")
    mixed_gradients(branch, ot_ref[...], r.get("wo")[...], r.do, r.delta)
    packed, mark = r.out("pack"), own_label(bits, core ^ g, place)
    pack(packed, mark, 3, as_unit(nn(ot_ref[...], branch)))
    if not causal:
        pack_norms(packed, mark, norm_parts(norms, r))
    r.dk[...] = jnp.zeros(r.dk.shape, F32)
    r.dv[...] = jnp.zeros(r.dv.shape, F32)
    q_ref, k_ref, v_ref, lse_ref = r.get("q"), r.get("k"), r.get("v"), r.get("lse")
    r.kt[...] = k_ref[...].T
    masks = head_masks()

    def scored(block):
        rows = slice(block * BLOCK, (block + 1) * BLOCK)
        return backward_scores(rows, *spots[block], masks, q_ref, k_ref, v_ref, r.do)

    ahead = scored(0)
    for block, (key_at, width) in enumerate(spots):
        now = ahead
        if block + 1 < len(spots):
            ahead = scored(block + 1)
        backward_sums(
            slice(block * BLOCK, (block + 1) * BLOCK), key_at, r.bias[block, :width, :], now, r.kt, lse_ref, r.delta,
            r.dqt, r.dk, r.dv,
        )
    r.out("dq")[...] = (r.dqt[...] * SCALE).astype(BF16).T
    r.out("dk")[...] = r.dk[...].astype(BF16)
    r.out("dv")[...] = r.dv[...].astype(BF16)
    for key in ("dq", "dk", "dv"):
        r.send(key)
    pack(packed, mark, 0, nn(query_turned[...], r.out("dq")[...]))
    pack(packed, mark, 1, nn(keys_turned[...], r.out("dk")[...]))
    pack(packed, mark, 2, nn(keys_turned[...], r.out("dv")[...]))


def self_back_other_kernel(causal, norm_at, bits, r):
    core = r.ids[0]
    z_ref, up_ref, x_ref = r.get("z"), r.get("up"), r.get("x")
    tokens, own, window = x_ref.shape[0], z_ref.shape[0], r.marks.shape[0]
    norms, branch = r.out("norms"), r.out("branch")
    gain, shift = norm_back(
        r,
        r.get("gain")[norm_at : norm_at + 1, :],
        lambda rows: z_ref[rows, :],
        lambda rows: up_ref[rows, :],
        (r.out("dz"), branch),
    )
    norms[0:1, :] = gain
    norms[1:2, :] = shift
    for key in ("norms", "dz", "branch"):
        r.send(key)
    keys_turned, query_turned = r.out("keys_turned"), r.out("query_turned")
    keys_turned[...] = x_ref[pl.ds(aligned(core * (tokens - window)), window), :].T
    query_turned[...] = x_ref[pl.ds(aligned(core * own), own), :].T
    r.send("keys_turned")
    r.send("query_turned")
    self_back_heads(r, causal, bits, 1, branch[...], norms, keys_turned, query_turned)


def self_back_own_kernel(causal, bits, r):
    branch = r.get("branch")[...]
    norms = None if causal else r.get("norms")
    self_back_heads(r, causal, bits, 0, branch, norms, r.get("keys_turned"), r.get("query_turned"))


def stream_gradient_kernel(r):
    core = r.ids[0]
    dz_ref, own, window = r.get("dz"), r.get("dq0").shape[0], r.get("dk0").shape[0]
    w = (r.get("w0"), r.get("w1"))
    r.near[...] = key_stream_gradient(r, [(w[g][1], w[g][2]) for g in range(2)])
    r.out("halo")[...] = r.near[pl.ds(aligned((1 - core) * own), window - own), :].astype(BF16)
    r.send("halo")
    r.out("dx")[...] = (
        dz_ref[...]
        + sum(nt(r.get(f"dq{g}")[...], w[g][0]) for g in range(2))
        + r.near[pl.ds(aligned(core * (window - own)), own), :]
    )


class Refs:
    def __init__(self, smem, ins, outs, scratch):
        for name, ref in list(smem.items()) + list(scratch.items()):
            setattr(self, name, ref)
        self.ins, self.outs = ins, outs
        self.waited, self.sent = set(), set()
        for copy, ref in ins.values():
            copy.start()

    def get(self, name):
        copy, ref = self.ins[name]
        if name not in self.waited:
            self.waited.add(name)
            copy.wait()
        return ref

    def out(self, name):
        return self.outs[name][1]

    def send(self, name):
        self.sent.add(name)
        self.outs[name][0].start()

    def close(self):
        for name in self.ins:
            self.get(name)
        for name in self.outs:
            if name not in self.sent:
                self.send(name)
        for copy, ref in self.outs.values():
            copy.wait()


def call(kernel, name, smem, ins, outs, scratch, cost, near=False):
    n_smem, n_in, n_out, n_scratch = len(smem), len(ins), len(outs), len(scratch)

    def body(*refs):
        smem_refs = refs[:n_smem]
        refs = refs[n_smem:]
        in_refs, out_refs, refs = refs[:n_in], refs[n_in : n_in + n_out], refs[n_in + n_out :]
        in_vmem, out_vmem, refs = refs[:n_in], refs[n_in : n_in + n_out], refs[n_in + n_out :]
        in_sem, out_sem = refs[-2:]
        copies_in = {
            key: (pltpu.make_async_copy(in_refs[i], in_vmem[i], in_sem.at[i]), in_vmem[i])
            for i, key in enumerate(ins)
        }
        copies_out = {
            key: (pltpu.make_async_copy(out_vmem[i], out_refs[i], out_sem.at[i]), out_vmem[i])
            for i, key in enumerate(outs)
        }
        held = Refs(dict(zip(smem, smem_refs)), copies_in, copies_out, dict(zip(scratch, refs)))
        kernel(held)
        held.close()

    held_bytes = sum(
        math.prod(shape[:-2]) * -(-shape[-2] // 8) * 8 * shape[-1] * jnp.dtype(dtype).itemsize
        for shape, dtype in [(array.shape, array.dtype) for array in ins.values()] + list(outs.values()) + list(scratch.values())
    )
    results = pl.pallas_call(
        body,
        out_shape=[jax.ShapeDtypeStruct(*out) for out in outs.values()],
        in_specs=[pl.BlockSpec(memory_space=pltpu.SMEM)] * n_smem + [pl.BlockSpec(memory_space=pl.ANY)] * n_in,
        out_specs=[pl.BlockSpec(memory_space=pl.ANY)] * n_out,
        scratch_shapes=[pltpu.VMEM(array.shape, array.dtype) for array in ins.values()]
        + [pltpu.VMEM(*out) for out in outs.values()]
        + [pltpu.VMEM(*one) for one in scratch.values()]
        + [pltpu.SemaphoreType.DMA((n_in,)), pltpu.SemaphoreType.DMA((n_out,))],
        compiler_params=pltpu.CompilerParams(vmem_limit_bytes=held_bytes + SPARE if near else VMEM_LIMIT),
        cost_estimate=pl.CostEstimate(flops=cost * 10**9, transcendentals=0, bytes_accessed=cost * 10**6),
        name=name,
    )(*smem.values(), *ins.values())
    return SimpleNamespace(**dict(zip(outs, results)))


def finish_kernel(kind, bits, ids_ref, *refs):
    mark = own_label(bits, ids_ref[0], ids_ref[1])
    gathered, sem = refs[-2:]
    n_outs = {"enc": 4, "dec": 2, "cross": 3, "up": 1, "down": 1}[kind]
    count = len(refs) - 2 - n_outs
    parts, outs = refs[:count], refs[count:-2]
    copies, at = [], 0
    for i, part in enumerate(parts):
        copies.append(pltpu.make_async_copy(part, gathered.at[pl.ds(at, part.shape[0])], sem.at[i]))
        at += part.shape[0]
    for copy in copies:
        copy.start()
    for copy in copies:
        copy.wait()
    for shard in range(SHARDS):
        unit, half = divmod(shard, 2)
        rows = slice(half * QUAD, (half + 1) * QUAD)
        where = pl.ds(mark ^ shard, 1)
        value = gathered[where, :QUAD, :][0].astype(F32)
        if kind == "up":
            outs[0][rows, quad(unit)] = value
        elif kind == "down":
            outs[0][quad(unit), rows] = value.T
        elif unit == 3:
            outs[2 if kind == "cross" else 1][:, quad(half)] = value
        elif kind != "cross":
            outs[0][unit, rows, :] = value
        elif unit == 0:
            outs[0][rows, :] = value
        else:
            outs[1][unit - 1, rows, :] = value
        if kind == "enc":
            norms = gathered[where, QUAD:, :][0].astype(F32)
            many = norm_rows(SHARDS)
            for i in range(many):
                row, side = divmod(shard * many + i, 2)
                if row < 10:
                    outs[2 + row // 5][row % 5 : row % 5 + 1, quad(side)] = norms[i : i + 1, :]


def finish(group, ids, outs):
    parts = group.parts
    shape = (SHARDS,) + parts[0].shape[1:]
    return pl.pallas_call(
        functools.partial(finish_kernel, group.kind, group.bits),
        out_shape=[jax.ShapeDtypeStruct(*out) for out in outs],
        in_specs=[pl.BlockSpec(memory_space=pltpu.SMEM)] + [pl.BlockSpec(memory_space=pl.ANY)] * len(parts),
        out_specs=[pl.BlockSpec(memory_space=pltpu.VMEM)] * len(outs),
        scratch_shapes=[pltpu.VMEM(shape, BF16), pltpu.SemaphoreType.DMA((len(parts),))],
        compiler_params=pltpu.CompilerParams(vmem_limit_bytes=FINISH_LIMIT),
        cost_estimate=pl.CostEstimate(flops=2 * 10**9, transcendentals=0, bytes_accessed=2 * 10**6),
        name="finish_" + group.kind,
    )(ids, *parts)


class Sum:
    def __init__(self, kind, bits, dp, mp, mine, other):
        self.kind, self.bits, self.dp, self.mp = kind, bits, dp, mp
        self.phase, self.parts, self.outgoing = -1, [mine], [other]

    def hop(self, array, step):
        pairs = []
        for place in range(self.dp):
            for core in range(self.mp):
                bit = self.bits[core][step] if step < 4 else step
                pairs.append((place * self.mp + core, (place ^ (1 << bit)) * self.mp + core))
        return lax.ppermute(array, ("dp", "mp"), pairs)

    def launch(self):
        if self.phase < 0:
            self.flying = [lax.ppermute(self.outgoing[0], "mp", [(0, 1), (1, 0)])]
        elif self.phase <= 3:
            self.flying = [self.hop(self.outgoing[0], self.last if self.phase == 3 else self.phase)]
        else:
            self.flying = [self.hop(part, 6 - self.phase) for part in self.outgoing]

    def add_up(self):
        self.phase += 1
        if self.phase <= 2:
            mine, sent = self.parts[0], self.flying[0]
            half = mine.shape[0] // 2
            self.outgoing, self.parts = [mine[half:] + sent[half:]], [mine[:half] + sent[:half]]
        elif self.phase == 3:
            part, self.last = self.parts[0] + self.flying[0], 3
            while 2 << self.last < self.dp:
                part = part + self.hop(part, self.last)
                self.last += 1
            self.parts = self.outgoing = [part]
        elif self.phase == 4:
            self.parts = self.outgoing = [self.parts[0] + self.flying[0]]
        else:
            self.parts = self.parts + self.flying
            if self.phase < 7:
                self.outgoing = self.parts if self.phase == 5 and self.kind == "enc" else [jnp.concatenate(self.parts)]
        self.flying = []


def boundary(before, after, landing, launching=()):
    before, after, landing, launching = list(before), list(after), list(landing), list(launching)
    before, landed = lax.optimization_barrier((before, [group.flying for group in landing]))
    for group, flying in zip(landing, landed):
        group.flying = flying
        group.add_up()
    moving = landing + launching
    states = [([] if group.phase < 0 else group.parts, group.outgoing) for group in moving]
    before, after, states = lax.optimization_barrier((before, after, states))
    for group, state in zip(moving, states):
        group.outgoing = list(state[1])
        if group.phase >= 0:
            group.parts = list(state[0])
        if group.phase < 7:
            group.launch()
    return before, after


def on_device(
    src_embed, tgt_embed, src_segment, tgt_segment, enc_qkv, enc_out_proj, dec_qkv, dec_out_proj, cross_query,
    cross_kv, cross_out_proj, ffn_up, ffn_down, norm_gain, norm_bias, enc_cotangent, dec_cotangent,
):
    dp, mp = lax.axis_size("dp"), lax.axis_size("mp")
    tokens, model = src_embed.shape
    own = tokens // mp
    window = own + MOST
    half = ffn_up.shape[1]
    hidden = 2 * half
    position = lax.axis_index("mp")
    ids = jnp.stack([position, lax.axis_index("dp")]).astype(jnp.int32)
    pairs = [(0, 1), (1, 0)]

    def swap(tree):
        return jax.tree.map(lambda a: lax.ppermute(a, "mp", pairs), tree)

    enc_w1, enc_o1 = swap((enc_qkv, enc_out_proj))
    up1, down1 = swap((ffn_up, ffn_down))
    dec_w1, dec_o1 = swap((dec_qkv, dec_out_proj))
    cross_q1, cross_kv1, cross_o1 = swap((cross_query, cross_kv, cross_out_proj))
    feed = {"up0": ffn_up, "up1": up1, "down0": ffn_down, "down1": down1}

    def rows(count, dtype):
        return ((count, model), dtype)

    blocks = own // BLOCK
    q_shape, k_shape, ot_shape, lse_shape = ((own, QUAD), BF16), ((window, QUAD), BF16), ((QUAD, own), BF16), ((4, own), F32)
    vt_shape, marks, bias = ((4 * STRIDE, window), BF16), ((window, BLOCK), jnp.int32), ((blocks, 3 * BLOCK, BLOCK), F32)
    heads = {"q": q_shape, "k": k_shape, "v": k_shape, "ot": ot_shape, "lse": lse_shape}
    wide = ((own, half), BF16)
    norm_in = {"gain": norm_gain, "shift": norm_bias}
    first = call(
        own_heads_kernel, "own_heads", {"ids": ids},
        {"src_row": src_segment, "src": src_embed, "src_w": enc_qkv,
         "tgt_row": tgt_segment, "tgt": tgt_embed, "tgt_w": dec_qkv},
        {f"{side}_{key}": shape for side in ("src", "tgt") for key, shape in heads.items()},
        {"marks": marks, "src_bias": bias, "tgt_bias": bias, "src_vt": vt_shape, "tgt_vt": vt_shape},
        cost=8,
    )
    encoder = call(
        encoder_kernel, "encoder_forward", {"ids": ids},
        {"row": src_segment, "x": src_embed, "w": enc_w1, "ot0": first.src_ot, "wo0": enc_out_proj, "wo1": enc_o1,
         **norm_in, "up0": ffn_up, "down0": ffn_down, "up1": up1, "down1": down1},
        {**heads, "z0": rows(own, F32), "x1_low": rows(own, BF16), "h0": wide, "h1": wide,
         "z1": rows(own, F32), "enc": rows(own, BF16)},
        {"marks": marks, "bias": bias, "vt": vt_shape, "x1": rows(own, F32), "acc": rows(own, F32)},
        cost=12,
    )
    enc_swapped = swap(encoder.enc)
    decoder = call(
        decoder_kernel, "decoder_self_forward", {"ids": ids},
        {"row": tgt_segment, "x": tgt_embed, "w": dec_w1, "ot0": first.tgt_ot, "wo0": dec_out_proj, "wo1": dec_o1,
         **norm_in},
        {**heads, "z2": rows(own, F32), "x2": rows(own, F32)},
        {"marks": marks, "bias": bias, "vt": vt_shape, "acc": rows(own, F32)}, cost=6,
    )
    packed = ((SHARDS, QUAD, QUAD), BF16)
    packed_norms = ((SHARDS, QUAD + TILE, QUAD), BF16)
    crossed = call(
        cross_kernel, "cross_and_decoder_feed",
        {"ids": ids, "src_marks": src_segment, "tgt_marks": tgt_segment},
        {"src_row": src_segment, "tgt_row": tgt_segment, "enc_own": encoder.enc, "enc_other": enc_swapped,
         "x2": decoder.x2, "cq0": cross_query, "ckv0": cross_kv, "cq1": cross_q1, "ckv1": cross_kv1,
         "co0": cross_out_proj, "co1": cross_o1, **norm_in, **feed, "cot": dec_cotangent},
        {"enc": rows(tokens, BF16), "x3_low": rows(own, BF16), "a0": wide, "a1": wide, "dec": rows(own, BF16),
         "dy": rows(own, BF16), "dh0": wide, "dh1": wide, "norms": rows(4, F32), "pack0": packed, "pack1": packed,
         "denc_other": rows(own, BF16), "denc_own": rows(own, F32), "g2": rows(own, F32)},
        {"marks": ((tokens, BLOCK), jnp.int32), "bias": bias, "q": ((2, own, QUAD), BF16),
         "k": ((2, tokens, QUAD), BF16), "v": ((2, tokens, QUAD), BF16), "turn": ((2, QUAD, tokens), BF16), "vt": ((2, 4 * STRIDE, tokens), BF16),
         "mix": ((model, own), F32), "tops": ((8, own), F32), "totals": ((8, own), F32), "lse": ((2, 4, own), F32),
         "ot": ((model, own), BF16), "acc": rows(own, F32), "x3": rows(own, F32), "z3": rows(own, F32),
         "z4": rows(own, F32), "dz": rows(own, F32), "h": ((2, own, half), BF16), "low": rows(own, BF16), "do": ((2, own, QUAD), BF16),
         "delta": ((2, 4, own), F32), "dqt": ((2, QUAD, own), F32), "dk": ((2, tokens, QUAD), F32),
         "dv": ((2, tokens, QUAD), F32), "denc": rows(tokens, F32)},
        cost=30,
    )
    def whole(mine, received):
        return jnp.where(
            position == 0, jnp.concatenate([mine, received]), jnp.concatenate([received, mine])
        )

    def group(kind, bits, mine, other):
        return Sum(kind, bits, dp, mp, mine, other)

    head_scratch = {
        "marks": marks, "bias": bias, "do": q_shape, "delta": ((4, own), F32), "kt": ((QUAD, window), BF16),
        "dqt": ((QUAD, own), F32), "dk": ((window, QUAD), F32), "dv": ((window, QUAD), F32),
    }
    turned_shapes = {"keys_turned": ((model, window), BF16), "query_turned": ((model, own), BF16)}
    head_outs = {"dq": q_shape, "dk": k_shape, "dv": k_shape}

    def self_other(causal, at, bits, name, x, row, z, up, w_out, heads_kept, pack_shape, more):
        ins = {"z": z, "up": up, "gain": norm_gain, "row": row, "x": x, "wo": w_out} | heads_kept | more
        return call(
            functools.partial(self_back_other_kernel, causal, at, bits), name, {"ids": ids}, ins,
            {"dz": rows(own, F32), "branch": rows(own, BF16), "norms": rows(2, F32), "pack": pack_shape}
            | turned_shapes | head_outs,
            head_scratch, cost=9, near=True,
        )

    def self_own(causal, bits, name, back, row, branch, w_out, heads_kept, pack_shape, more):
        ins = {"branch": branch, "row": row, "wo": w_out} | heads_kept
        ins |= {"keys_turned": back.keys_turned, "query_turned": back.query_turned} | more
        return call(
            functools.partial(self_back_own_kernel, causal, bits), name, {"ids": ids}, ins,
            {"pack": pack_shape} | head_outs, head_scratch, cost=7, near=True,
        )

    def kept_own(side):
        return {key: getattr(first, f"{side}_{key}") for key in ("ot", "k", "q", "v", "lse")}

    def kept_other(part):
        return {key: getattr(part, key) for key in ("ot", "k", "q", "v", "lse")}

    def stream_gradient(name, back, back_own, w0, w1, gate):
        ins = {"dz": gate, "w0": w0, "w1": w1}
        for key in ("dk", "dv", "dq"):
            ins |= {f"{key}0": getattr(back_own, key), f"{key}1": getattr(back, key)}
        return call(
            stream_gradient_kernel, name, {"ids": ids}, ins,
            {"halo": rows(window - own, BF16), "dx": rows(own, F32)}, {"near": rows(window, F32)}, cost=5, near=True,
        )

    def group(kind, bits, mine, other):
        return Sum(kind, bits, dp, mp, mine, other)

    halo_at = (1 - position) * (own - (window - own))

    def with_halo(grad, received):
        part = lax.dynamic_slice_in_dim(grad, halo_at, window - own, 0) + received.astype(F32)
        return lax.dynamic_update_slice_in_dim(grad, part, halo_at, 0)

    square, out_half, triple = ((model, QUAD), F32), ((QUAD, model), F32), ((3, model, QUAD), F32)
    out_shapes = {
        "cross": [square, ((2, model, QUAD), F32), out_half],
        "dec": [triple, out_half],
        "up": [((model, half), F32)],
        "down": [rows(half, F32)],
        "enc": [triple, out_half, rows(5, F32), rows(5, F32)],
    }
    cross_sum = group("cross", CROSS_BITS, crossed.pack0, crossed.pack1)
    cross_sum.launch()
    denc_recv = swap(crossed.denc_other)
    (cross_norms,), (z1, denc_recv) = boundary([crossed.norms], [encoder.z1, denc_recv], [cross_sum])
    fed = call(
        feed_other_kernel, "encoder_feed_other", {"ids": ids},
        {"cot": enc_cotangent, "denc_own": crossed.denc_own, "denc_recv": denc_recv, "z1": z1, "gain": norm_gain,
         "x1_low": encoder.x1_low, "x3_low": crossed.x3_low, "dy3": crossed.dy, "down": down1, "h": encoder.h1,
         "up": up1, "dh": crossed.dh1, "a": crossed.a1},
        {"dy": rows(own, BF16), "norms": rows(2, F32), "turned": ((4, model, own), BF16), "up_pack": packed,
         "down_pack": packed, "g0": rows(own, F32)},
        {}, cost=10, near=True,
    )
    up_sum = group("up", UP_BITS, None, fed.up_pack)
    down_sum = group("down", DOWN_BITS, None, fed.down_pack)
    (feed_norms,), (dy1,) = boundary([fed.norms], [fed.dy], [cross_sum], [up_sum, down_sum])
    fed_own = call(
        feed_own_kernel, "encoder_feed_own", {"ids": ids},
        {"dy": dy1, "down": ffn_down, "h": encoder.h0, "dz": fed.g0, "turned": fed.turned, "up": ffn_up,
         "dh": crossed.dh0, "a": crossed.a0},
        {"g0": rows(own, F32), "up_pack": packed, "down_pack": packed}, {}, cost=9, near=True,
    )
    up_sum.parts, down_sum.parts = [fed_own.up_pack], [fed_own.down_pack]
    (feed_norms,), (g2,) = boundary([feed_norms], [crossed.g2], [cross_sum, up_sum, down_sum])
    dec_back = self_other(
        True, 2, DEC_BITS, "decoder_self_other", tgt_embed, tgt_segment, decoder.z2, g2, dec_o1, kept_other(decoder),
        packed, {},
    )
    dec_sum = group("dec", DEC_BITS, None, dec_back.pack)
    (dec_norms,), (branch,) = boundary([dec_back.norms], [dec_back.branch], [cross_sum, up_sum], [dec_sum])
    dec_own = self_own(
        True, DEC_BITS, "decoder_self_own", dec_back, tgt_segment, branch, dec_out_proj, kept_own("tgt"), packed, {},
    )
    dec_sum.parts = [dec_own.pack]
    (dec_norms,), (g0,) = boundary([dec_norms], [fed_own.g0], [cross_sum, up_sum, down_sum, dec_sum])
    norms_before = {"feed_norms": feed_norms, "dec_norms": dec_norms, "cross_norms": cross_norms}
    enc_back = self_other(
        False, 0, ENC_BITS, "encoder_self_other", src_embed, src_segment, encoder.z0, g0, enc_o1, kept_other(encoder),
        packed_norms, norms_before,
    )
    enc_sum = group("enc", ENC_BITS, None, enc_back.pack)
    (enc_norms,), (branch,) = boundary(
        [enc_back.norms], [enc_back.branch], [cross_sum, up_sum, down_sum, dec_sum], [enc_sum]
    )
    enc_own = self_own(
        False, ENC_BITS, "encoder_self_own", enc_back, src_segment, branch, enc_out_proj, kept_own("src"),
        packed_norms, {"norms": enc_norms, **norms_before},
    )
    enc_sum.parts = [enc_own.pack]
    (src_dz,), () = boundary([enc_own.dq], [], [enc_sum, cross_sum, dec_sum, up_sum, down_sum])
    enc_own.dq = src_dz
    src_side = stream_gradient("src_gradient", enc_back, enc_own, enc_qkv, enc_w1, enc_back.dz)
    (src_halo,), () = boundary([src_side.halo], [], [enc_sum])
    (src_halo,), () = boundary([src_halo], [], [dec_sum])
    (src_halo,), (tgt_dz,) = boundary([src_halo], [dec_back.dz], [up_sum])
    tgt_side = stream_gradient("tgt_gradient", dec_back, dec_own, dec_qkv, dec_w1, tgt_dz)
    (tgt_halo,), () = boundary([tgt_side.halo], [], [enc_sum])
    (tgt_halo,), (dec_part, src_halo) = boundary([tgt_halo], [crossed.dec, src_halo], [down_sum, cross_sum])
    src_recv, tgt_recv, dec_swapped = swap(src_halo), swap(tgt_halo), swap(dec_part)
    (dec_swapped,), () = boundary([dec_swapped], [], [up_sum, dec_sum])
    cross_out = list(finish(cross_sum, ids, out_shapes["cross"]))
    dec_whole = whole(crossed.dec, dec_swapped)
    (dec_whole, norm_gate), (src_recv,) = boundary([dec_whole, cross_out[0]], [src_recv], [enc_sum, down_sum])
    cross_out[0] = norm_gate
    src_grad = with_halo(src_side.dx, src_recv)
    (src_grad,), (tgt_recv,) = boundary([src_grad], [tgt_recv], [up_sum, dec_sum])
    tgt_grad = with_halo(tgt_side.dx, tgt_recv)
    (tgt_grad,), () = boundary([tgt_grad], [], [enc_sum])
    (tgt_grad,), () = boundary([tgt_grad], [], [down_sum])
    (tgt_grad,), () = boundary([tgt_grad], [], [dec_sum])
    up_out = finish(up_sum, ids, out_shapes["up"])
    (up_gate,), () = boundary([up_out[0]], [], [enc_sum])
    up_out = [up_gate]
    (up_gate,), () = boundary([up_gate], [], [enc_sum])
    up_out = [up_gate]
    (up_gate,), () = boundary([up_gate], [], [down_sum])
    up_out = [up_gate]
    down_out = finish(down_sum, ids, out_shapes["down"])
    (down_gate,), () = boundary([down_out[0]], [], [dec_sum])
    down_out = [down_gate]
    dec_out = finish(dec_sum, ids, out_shapes["dec"])
    (dec_gate,), () = boundary([dec_out[0]], [], [enc_sum])
    dec_out = [dec_gate, dec_out[1]]
    enc_out = finish(enc_sum, ids, out_shapes["enc"])

    return (
        crossed.enc,
        dec_whole,
        src_grad,
        tgt_grad,
        enc_out[0],
        enc_out[1],
        dec_out[0],
        dec_out[1],
        cross_out[0],
        cross_out[1],
        cross_out[2],
        up_out[0],
        down_out[0],
        enc_out[2],
        enc_out[3],
    )


def solution(mesh):
    in_specs = (
        P("dp", None), P("dp", None), P("dp", None), P("dp", None),
        P(None, None, "mp"), P("mp", None), P(None, None, "mp"), P("mp", None),
        P(None, "mp"), P(None, None, "mp"), P("mp", None), P(None, "mp"), P("mp", None),
        P(), P(), P(("dp", "mp"), None), P(("dp", "mp"), None),
    )
    out_specs = (
        P("dp", None), P("dp", None), P(("dp", "mp"), None), P(("dp", "mp"), None),
        P(None, None, "mp"), P("mp", None), P(None, None, "mp"), P("mp", None),
        P(None, "mp"), P(None, None, "mp"), P("mp", None), P(None, "mp"), P("mp", None),
        P(), P(),
    )
    return jax.shard_map(on_device, mesh=mesh, in_specs=in_specs, out_specs=out_specs, check_vma=False)
```

```python
import functools
import math
from types import SimpleNamespace

import jax
import jax.numpy as jnp
from jax import lax
from jax.experimental import pallas as pl
from jax.experimental.pallas import tpu as pltpu
from jax.sharding import PartitionSpec as P

HDIM = 64
SCALE = HDIM ** (-0.5)
EPSILON = 1e-05
MASKED = -1e30
BLOCK = 128
MOST = 128
QUAD = 4 * HDIM
UNITS = 4
TILE = 16
FEED = 512
SHARDS = 8
UP_BITS = ((0, 1, 2, 3), (1, 0, 2, 3))
DOWN_BITS = ((1, 0, 2, 3), (0, 1, 2, 3))
CROSS_BITS = ((0, 1, 2, 3), (1, 0, 2, 3))
DEC_BITS = ((0, 1, 2, 3), (1, 0, 2, 3))
STRIDE = HDIM + TILE
ENC_BITS = ((1, 0, 2, 3), (0, 1, 2, 3))
F32 = jnp.float32
BF16 = jnp.bfloat16
VMEM_LIMIT = 56 * 1024 * 1024
FEED_LIMIT = 44 * 1024 * 1024
FINISH_LIMIT = 10 * 1024 * 1024
SPARE = 6 * 1024 * 1024
GELU_IN = math.sqrt(2.0 / math.pi)
GELU_CUBE = 0.044715


def nn(left, right):
    return jnp.dot(left, right, preferred_element_type=F32)


def nt(left, right):
    return lax.dot_general(left, right, (((1,), (1,)), ((), ())), preferred_element_type=F32)


def tn(left, right):
    return lax.dot_general(left, right, (((0,), (0,)), ((), ())), preferred_element_type=F32)


def aligned(index, size=BLOCK):
    return pl.multiple_of(index, size)


def over_rows(rows, chunk, body, carry, unroll=4):
    return lax.fori_loop(
        0,
        rows // chunk,
        lambda i, kept: body(pl.ds(aligned(i * chunk, chunk), chunk), kept),
        carry,
        unroll=min(unroll, rows // chunk),
    )


def normalize(before):
    centered = before - jnp.mean(before, axis=-1, keepdims=True)
    variance = jnp.mean(centered * centered, axis=-1, keepdims=True)
    rate = lax.rsqrt(variance + EPSILON)
    return centered * rate, rate


def norm_backward(before, upstream, gain_row):
    normed, rate = normalize(before)
    scaled = upstream * gain_row
    first = jnp.mean(scaled, axis=-1, keepdims=True)
    second = jnp.mean(scaled * normed, axis=-1, keepdims=True)
    return rate * (scaled - first - normed * second), upstream * normed


def fold_rows(block):
    return jnp.sum(block.reshape(block.shape[0] // 8, 8, block.shape[1]), axis=0)


def gelu(hidden):
    inner = GELU_IN * hidden * (1.0 + GELU_CUBE * hidden * hidden)
    return 0.5 * hidden * (1.0 + jnp.tanh(inner))


def gelu_both(hidden):
    square = hidden * hidden
    bent = jnp.tanh(GELU_IN * hidden * (1.0 + GELU_CUBE * square))
    half = 0.5 * (1.0 + bent)
    slope = half + 0.5 * hidden * (1.0 - bent * bent) * (GELU_IN * (1.0 + 3.0 * GELU_CUBE * square))
    return hidden * half, slope


def head_masks():
    lane = lax.broadcasted_iota(jnp.int32, (1, QUAD), 1)
    return [
        jnp.where((lane >= h * HDIM) & (lane < (h + 1) * HDIM), 1.0, 0.0).astype(BF16)
        for h in range(4)
    ]


def stack_heads(block, masks):
    return jnp.concatenate([block * mask for mask in masks], axis=0)


def quad(g):
    return slice(g * QUAD, (g + 1) * QUAD)


def bias_for(marks_ref, key_at, width, query_row, causal=False, key_start=0, query_start=0):
    allowed = marks_ref[pl.ds(key_at, width), :] == query_row
    if causal:
        places = key_start + lax.broadcasted_iota(jnp.int32, (width, BLOCK), 0)
        queries = query_start + lax.broadcasted_iota(jnp.int32, (width, BLOCK), 1)
        allowed = allowed & (places <= queries)
    return jnp.where(allowed, 0.0, MASKED)


def self_window(core, block, causal):
    middle = block + core
    if causal:
        return aligned(jnp.maximum(middle - 1, 0) * BLOCK), 2 * BLOCK
    return aligned(jnp.clip(middle - 1, 0, 2) * BLOCK), 3 * BLOCK


def set_self_bias(bias_ref, core, tokens, marks_ref, row_ref, causal):
    window, own = marks_ref.shape[0], row_ref.shape[1] // 2
    start = core * (tokens - window)
    spots = []
    for block in range(own // BLOCK):
        key_at, width = self_window(core, block, causal)
        first = aligned(core * own + block * BLOCK)
        bias_ref[block, :width, :] = bias_for(
            marks_ref, key_at, width, row_ref[:, pl.ds(first, BLOCK)], causal, start + key_at, first
        )
        spots.append((key_at, width))
    return spots


def soft_weights(scores, h, bias, top=None):
    one = scores[:, h * BLOCK : (h + 1) * BLOCK] + bias
    high = jnp.max(one, axis=0, keepdims=True)
    top = high if top is None else jnp.maximum(top, high)
    return top, jnp.exp((one - top).astype(BF16))


def set_values(vt_ref, values):
    turned = values.T
    for h in range(4):
        vt_ref[h * STRIDE : h * STRIDE + HDIM, :] = turned[h * HDIM : (h + 1) * HDIM]
        vt_ref[h * STRIDE + HDIM : (h + 1) * STRIDE, :] = jnp.ones((TILE, turned.shape[1]), BF16)


def quad_forward(spots, q_ref, k_ref, vt_ref, bias_ref, ot_ref, lse_ref, masks):
    def score(block):
        rows, (key_at, width) = slice(block * BLOCK, (block + 1) * BLOCK), spots[block]
        return nt(k_ref[pl.ds(key_at, width), :], stack_heads(q_ref[rows, :], masks))

    ahead = score(0)
    for block, (key_at, width) in enumerate(spots):
        rows = slice(block * BLOCK, (block + 1) * BLOCK)
        scores, ahead = ahead, score(block + 1) if block + 1 < len(spots) else None
        for h in range(4):
            top, weights = soft_weights(scores, h, bias_ref[block, :width, :])
            features = slice(h * HDIM, (h + 1) * HDIM)
            mixed = nn(vt_ref[h * STRIDE : (h + 1) * STRIDE, pl.ds(key_at, width)], weights)
            total = mixed[HDIM : HDIM + 1]
            ot_ref[features, rows] = (mixed[:HDIM] * (1.0 / total)).astype(BF16)
            lse_ref[h : h + 1, rows] = top + jnp.log(total)


def backward_scores(rows, key_at, width, masks, q_ref, k_ref, v_ref, do_ref):
    keys = pl.ds(key_at, width)
    q_stack, do_stack = stack_heads(q_ref[rows, :], masks), stack_heads(do_ref[rows, :], masks)
    return q_stack, do_stack, nt(k_ref[keys, :], q_stack), nt(v_ref[keys, :], do_stack)


def backward_sums(rows, key_at, bias, scored, kt_ref, lse_ref, delta_ref, dqt_ref, dk_ref, dv_ref, add=False):
    q_stack, do_stack, scores, prob_grads = scored
    keys = pl.ds(key_at, bias.shape[0])
    probs, score_grads = [], []
    for h in range(4):
        cols = slice(h * BLOCK, (h + 1) * BLOCK)
        prob = jnp.exp((scores[:, cols] + bias - lse_ref[h : h + 1, rows]).astype(BF16))
        probs.append(prob)
        score_grads.append(prob * (prob_grads[:, cols] - delta_ref[h : h + 1, rows]).astype(BF16))
    for h in range(4):
        features = slice(h * HDIM, (h + 1) * HDIM)
        query_grad = nn(kt_ref[features, keys], score_grads[h])
        if add:
            dqt_ref[features, rows] += query_grad
        else:
            dqt_ref[features, rows] = query_grad
    dv_ref[keys, :] += nn(jnp.concatenate(probs, axis=1), do_stack)
    dk_ref[keys, :] += nn(jnp.concatenate(score_grads, axis=1), q_stack)


def mixed_gradients(branch, ot, w_out, do_ref, delta_ref):
    do_ref[...] = nt(branch, w_out).astype(BF16)
    product = nt(w_out, branch).astype(BF16).astype(F32) * ot.astype(F32)
    for h in range(4):
        delta_ref[h : h + 1, :] = jnp.sum(product[h * HDIM : (h + 1) * HDIM, :], axis=0, keepdims=True)


def spread_marks(marks_ref, row):
    marks_ref[...] = jnp.broadcast_to(row, (marks_ref.shape[1], marks_ref.shape[0])).T


def label(bits, place):
    first, second, third = [(place >> bit) & 1 for bit in bits[:3]]
    return 4 * first + 2 * second + third


def own_label(bits, core, place):
    return jnp.where(core == 0, label(bits[0], place), label(bits[1], place))


def pack(out_ref, mark, unit, value, at=0):
    rows = value.shape[0] // 2
    for half in range(2):
        where = pl.ds(mark ^ (2 * unit + half), 1)
        out_ref[where, at : at + rows, :] = value[half * rows : (half + 1) * rows].astype(BF16)[None]


def as_unit(value):
    return jnp.concatenate([value[:, :QUAD], value[:, QUAD:]], axis=0).astype(BF16)


def pack_norms(out_ref, mark, parts):
    shards, tall, width = out_ref.shape
    halves = [part[:, half * width : (half + 1) * width] for part in parts for half in range(2)]
    each = norm_rows(shards)
    blank = jnp.zeros((1, width), F32)
    halves += [blank] * (shards * each - len(halves))
    for i in range(shards):
        block = jnp.concatenate(halves[i * each : (i + 1) * each] + [blank] * (TILE - each), axis=0)
        out_ref[pl.ds(mark ^ i, 1), tall - TILE :, :] = block.astype(BF16)[None]


def norm_rows(shards):
    return -(-20 // shards)


def prepare_quad(x_ref, w_ref, core, q_ref, k_ref, v_ref, vt_ref):
    tokens, own, window = x_ref.shape[0], q_ref.shape[0], k_ref.shape[0]
    keys = x_ref[pl.ds(aligned(core * (tokens - window)), window), :]
    q_ref[...] = (nn(x_ref[pl.ds(aligned(core * own), own), :], w_ref[0]) * SCALE).astype(BF16)
    k_ref[...] = nn(keys, w_ref[1]).astype(BF16)
    v_ref[...] = nn(keys, w_ref[2]).astype(BF16)
    set_values(vt_ref, v_ref[...])


def own_heads_kernel(r):
    core = r.ids[0]
    masks = head_masks()
    for side, causal in (("src", False), ("tgt", True)):
        x_ref, row_ref = r.get(side), r.get(side + "_row")
        k_ref = r.out(side + "_k")
        start = aligned(core * (x_ref.shape[0] - k_ref.shape[0]))
        spread_marks(r.marks, row_ref[:, pl.ds(start, k_ref.shape[0])])
        bias_ref, vt_ref = getattr(r, side + "_bias"), getattr(r, side + "_vt")
        spots = set_self_bias(bias_ref, core, x_ref.shape[0], r.marks, row_ref, causal)
        q_ref, v_ref = r.out(side + "_q"), r.out(side + "_v")
        prepare_quad(x_ref, r.get(side + "_w"), core, q_ref, k_ref, v_ref, vt_ref)
        for key in ("_q", "_k", "_v"):
            r.send(side + key)
        quad_forward(
            spots, q_ref, k_ref, vt_ref, bias_ref, r.out(side + "_ot"), r.out(side + "_lse"), masks
        )
        r.send(side + "_ot")
        r.send(side + "_lse")


def other_heads(r, causal):
    core = r.ids[0]
    x_ref, row_ref, k_ref = r.get("x"), r.get("row"), r.out("k")
    start = aligned(core * (x_ref.shape[0] - k_ref.shape[0]))
    spread_marks(r.marks, row_ref[:, pl.ds(start, k_ref.shape[0])])
    spots = set_self_bias(r.bias, core, x_ref.shape[0], r.marks, row_ref, causal)
    q_ref, v_ref, ot_ref = r.out("q"), r.out("v"), r.out("ot")
    prepare_quad(x_ref, r.get("w"), core, q_ref, k_ref, v_ref, r.vt)
    for key in ("q", "k", "v"):
        r.send(key)
    quad_forward(spots, q_ref, k_ref, r.vt, r.bias, ot_ref, r.out("lse"), head_masks())
    r.send("lse")
    r.send("ot")
    r.acc[...] = tn(r.get("ot0")[...], r.get("wo0")[...]) + tn(ot_ref[...], r.get("wo1")[...])


def norm_forward(r, at, residual, before_ref, after_ref, low_ref):
    gain, shift = r.get("gain")[at : at + 1, :], r.get("shift")[at : at + 1, :]

    def body(rows, carry):
        before = residual(rows) + r.acc[rows, :]
        if before_ref is not None:
            before_ref[rows, :] = before
        after = normalize(before)[0] * gain + shift
        if after_ref is not None:
            after_ref[rows, :] = after
        if low_ref is not None:
            low_ref[rows, :] = after.astype(BF16)
        return carry

    over_rows(r.acc.shape[0], 32, body, 0)


def own_row_reader(x_ref, core, own):
    first = core * own
    return lambda rows: x_ref[pl.ds(aligned(first + rows.start, rows.size), rows.size), :].astype(F32)


def encoder_kernel(r):
    other_heads(r, False)
    x1_low = r.out("x1_low")
    norm_forward(r, 0, own_row_reader(r.get("x"), r.ids[0], r.acc.shape[0]), r.out("z0"), r.x1, x1_low)
    r.send("z0")
    r.send("x1_low")
    feed_forward(x1_low, *feed_weights(r), (r.out("h0"), r.out("h1")), None, r.acc)
    r.send("h0")
    r.send("h1")
    norm_forward(r, 1, lambda rows: r.x1[rows, :], r.out("z1"), None, r.out("enc"))


def decoder_kernel(r):
    other_heads(r, True)
    norm_forward(r, 2, own_row_reader(r.get("x"), r.ids[0], r.acc.shape[0]), r.out("z2"), r.out("x2"), None)


def feed_weights(r):
    return (r.get("up0"), r.get("up1")), (r.get("down0"), r.get("down1"))


def feed_chunks(half):
    return [(j, slice(j * FEED, (j + 1) * FEED)) for j in range(half // FEED)]


def feed_forward(low_ref, ups, downs, h_refs, a_refs, acc_ref):
    chunks = [(g, cols) for g in range(2) for j, cols in feed_chunks(ups[0].shape[1])]
    ahead = nn(low_ref[...], ups[0][:, chunks[0][1]])
    for i, (g, cols) in enumerate(chunks):
        hidden = ahead
        if i + 1 < len(chunks):
            ahead = nn(low_ref[...], ups[chunks[i + 1][0]][:, chunks[i + 1][1]])
        hidden = hidden.astype(BF16)
        h_refs[g][:, cols] = hidden
        active = gelu(hidden)
        if a_refs is not None:
            a_refs[g][:, cols] = active
        term = nn(active, downs[g][cols, :])
        if i == 0:
            acc_ref[...] = term
        else:
            acc_ref[...] += term


def feed_backward(dy_ref, ups, downs, h_refs, dh_refs, acc_ref):
    chunks = [(g, cols) for g in range(2) for j, cols in feed_chunks(ups[0].shape[1])]
    ahead = nt(dy_ref[...], downs[0][chunks[0][1], :])
    for i, (g, cols) in enumerate(chunks):
        active_grad = ahead
        if i + 1 < len(chunks):
            ahead = nt(dy_ref[...], downs[chunks[i + 1][0]][chunks[i + 1][1], :])
        hidden_grad = active_grad.astype(BF16) * gelu_both(h_refs[g][:, cols])[1]
        dh_refs[g][:, cols] = hidden_grad
        acc_ref[...] += nt(hidden_grad, ups[g][:, cols])


def norm_back(r, gain_row, before, upstream, outs):
    def body(rows, sums):
        above = upstream(rows)
        grad, gain_terms = norm_backward(before(rows), above, gain_row)
        for ref in outs:
            ref[rows, :] = grad.astype(ref.dtype)
        return sums[0] + fold_rows(gain_terms), sums[1] + fold_rows(above)

    zeros = jnp.zeros((8, outs[0].shape[1]), F32)
    gains, shifts = over_rows(outs[0].shape[0], 32, body, (zeros, zeros))
    return jnp.sum(gains, axis=0, keepdims=True), jnp.sum(shifts, axis=0, keepdims=True)


def cross_kernel(r):
    core, place = r.ids[0], r.ids[1]
    x2_ref, enc_ref = r.get("x2"), r.out("enc")
    own, tokens = x2_ref.shape[0], enc_ref.shape[0]
    blocks = own // BLOCK
    first, second = aligned(core * own), aligned((1 - core) * own)
    width = 3 * BLOCK
    enc_ref[pl.ds(first, own), :] = r.get("enc_own")[...]
    enc_ref[pl.ds(second, own), :] = r.get("enc_other")[...]
    r.send("enc")
    spread_marks(r.marks, r.get("src_row")[...])
    steps = tokens.bit_length()

    def bound(mark, past):
        def step(i, pair):
            low, high = pair
            middle = (low + high) // 2
            value = r.src_marks[0, jnp.minimum(middle, tokens - 1)]
            below = (low < high) & ((value < mark) | (past & (value == mark)))
            above = (low < high) & jnp.logical_not(below)
            return jnp.where(below, middle + 1, low), jnp.where(above, middle, high)

        return lax.fori_loop(0, steps, step, (jnp.int32(0), jnp.int32(tokens)))[0]

    row_ref = r.get("tgt_row")
    query_rows, spots, more = [], [], []
    for block in range(blocks):
        head = first + block * BLOCK
        low = bound(r.tgt_marks[0, head], jnp.bool_(False)) // BLOCK
        high = (bound(r.tgt_marks[0, head + BLOCK - 1], jnp.bool_(True)) + BLOCK - 1) // BLOCK
        key_at = aligned(jnp.minimum(low, (tokens - width) // BLOCK) * BLOCK)
        query_rows.append(row_ref[:, pl.ds(aligned(head), BLOCK)])
        spots.append(key_at)
        more.append((key_at // BLOCK + 3, high))
        r.bias[block] = bias_for(r.marks, key_at, width, query_rows[block])
    masks = head_masks()
    x2_low = x2_ref[...].astype(BF16)
    for g in range(2):
        r.q[g] = (nn(x2_low, r.get(f"cq{g}")[...]) * SCALE).astype(BF16)
        r.k[g] = nn(enc_ref[...], r.get(f"ckv{g}")[0]).astype(BF16)
        r.v[g] = nn(enc_ref[...], r.get(f"ckv{g}")[1]).astype(BF16)
        set_values(r.vt.at[g], r.v[g])

    def weigh(g, h, scores, bias, key_at, keys_width, top):
        new_top, weights = soft_weights(scores, h, bias, top)
        mixed = nn(r.vt[g, h * STRIDE : (h + 1) * STRIDE, pl.ds(key_at, keys_width)], weights)
        features = slice(g * QUAD + h * HDIM, g * QUAD + (h + 1) * HDIM)
        return new_top, mixed[HDIM : HDIM + 1], mixed[:HDIM], features

    def score(block, g):
        rows = slice(block * BLOCK, (block + 1) * BLOCK)
        return nt(r.k[g, pl.ds(spots[block], width), :], stack_heads(r.q[g, rows, :], masks))

    tiles = [(block, g) for block in range(blocks) for g in range(2)]
    ahead = score(*tiles[0])
    for i, (block, g) in enumerate(tiles):
        rows = slice(block * BLOCK, (block + 1) * BLOCK)
        scores, ahead = ahead, score(*tiles[i + 1]) if i + 1 < len(tiles) else None
        for h in range(4):
            top, total, mixed, features = weigh(g, h, scores, r.bias[block], spots[block], width, None)
            r.mix[features, rows] = mixed
            r.tops[g * 4 + h : g * 4 + h + 1, rows] = top
            r.totals[g * 4 + h : g * 4 + h + 1, rows] = total

    for block in range(blocks):
        rows = slice(block * BLOCK, (block + 1) * BLOCK)

        def extra(i, carry, block=block, rows=rows):
            key_at = aligned(i * BLOCK)
            bias = bias_for(r.marks, key_at, BLOCK, query_rows[block])
            for g in range(2):
                scores = nt(r.k[g, pl.ds(key_at, BLOCK), :], stack_heads(r.q[g, rows, :], masks))
                for h in range(4):
                    at = slice(g * 4 + h, g * 4 + h + 1)
                    old = r.tops[at, rows]
                    top, total, mixed, features = weigh(g, h, scores, bias, key_at, BLOCK, old)
                    fade = jnp.exp(old - top)
                    r.mix[features, rows] = r.mix[features, rows] * fade + mixed
                    r.tops[at, rows] = top
                    r.totals[at, rows] = r.totals[at, rows] * fade + total
            return carry

        lax.fori_loop(*more[block], extra, 0)
    for head in range(8):
        features = slice(head * HDIM, (head + 1) * HDIM)
        at = slice(head, head + 1)
        r.ot[features, :] = (r.mix[features, :] * (1.0 / r.totals[at, :])).astype(BF16)
        r.lse[head // 4, head % 4 : head % 4 + 1, :] = r.tops[at, :] + jnp.log(r.totals[at, :])
    outs = (r.get("co0"), r.get("co1"))
    r.acc[...] = tn(r.ot[:QUAD, :], outs[0][...]) + tn(r.ot[QUAD:, :], outs[1][...])
    x3_low = r.out("x3_low")
    norm_forward(r, 3, lambda rows: x2_ref[rows, :], r.z3, r.x3, x3_low)
    r.send("x3_low")
    ups, downs = feed_weights(r)
    hs = (r.h.at[0], r.h.at[1])
    feed_forward(x3_low, ups, downs, hs, (r.out("a0"), r.out("a1")), r.acc)
    r.send("a0")
    r.send("a1")
    gain_ref, shift_ref, cot_ref, dec_ref, dy_ref = (
        r.get("gain"), r.get("shift"), r.get("cot"), r.out("dec"), r.out("dy")
    )
    last_gain, last_shift = gain_ref[4:5, :], shift_ref[4:5, :]

    def fourth_norm(rows, sums):
        before = r.x3[rows, :] + r.acc[rows, :]
        normed, rate = normalize(before)
        dec_ref[rows, :] = (normed * last_gain + last_shift).astype(BF16)
        upstream = cot_ref[rows, :].astype(F32)
        scaled = upstream * last_gain
        mean_one = jnp.mean(scaled, axis=-1, keepdims=True)
        mean_two = jnp.mean(scaled * normed, axis=-1, keepdims=True)
        grad = rate * (scaled - mean_one - normed * mean_two)
        r.z4[rows, :] = grad
        dy_ref[rows, :] = grad.astype(BF16)
        return sums[0] + fold_rows(upstream * normed), sums[1] + fold_rows(upstream)

    zeros = jnp.zeros((8, x2_ref.shape[1]), F32)
    gain_four, shift_four = over_rows(own, 32, fourth_norm, (zeros, zeros))
    r.send("dec")
    r.send("dy")
    feed_backward(dy_ref, ups, downs, hs, (r.out("dh0"), r.out("dh1")), r.z4)
    r.send("dh0")
    r.send("dh1")
    gain_three, shift_three = norm_back(
        r, gain_ref[3:4, :], lambda rows: r.z3[rows, :], lambda rows: r.z4[rows, :], (r.dz, r.low)
    )
    norms = r.out("norms")
    norms[0:1, :] = gain_three
    norms[1:2, :] = jnp.sum(gain_four, axis=0, keepdims=True)
    norms[2:3, :] = shift_three
    norms[3:4, :] = jnp.sum(shift_four, axis=0, keepdims=True)
    branch = r.low[...]
    ots = (r.ot.at[:QUAD], r.ot.at[QUAD:])
    for g in range(2):
        mixed_gradients(branch, ots[g][...], outs[g][...], r.do.at[g], r.delta.at[g])
    packs = pair_of_packs(r, CROSS_BITS)
    for g, (packed, mark) in enumerate(packs):
        pack(packed, mark, 3, as_unit(nn(ots[g][...], branch)))
        r.turn[g] = r.k[g].T
    r.dk[...] = jnp.zeros(r.dk.shape, F32)
    r.dv[...] = jnp.zeros(r.dv.shape, F32)

    def back_scores(block, g, key_at, keys_width):
        rows = slice(block * BLOCK, (block + 1) * BLOCK)
        return backward_scores(rows, key_at, keys_width, masks, r.q.at[g], r.k.at[g], r.v.at[g], r.do.at[g])

    def back_sums(block, g, key_at, bias, scored, add):
        backward_sums(
            slice(block * BLOCK, (block + 1) * BLOCK), key_at, bias, scored, r.turn.at[g], r.lse.at[g], r.delta.at[g],
            r.dqt.at[g], r.dk.at[g], r.dv.at[g], add,
        )

    ahead = back_scores(*tiles[0], spots[0], width)
    for i, (block, g) in enumerate(tiles):
        scored = ahead
        if i + 1 < len(tiles):
            ahead = back_scores(*tiles[i + 1], spots[tiles[i + 1][0]], width)
        back_sums(block, g, spots[block], r.bias[block], scored, False)
    for block in range(blocks):

        def extra_back(i, carry, block=block):
            key_at = aligned(i * BLOCK)
            bias = bias_for(r.marks, key_at, BLOCK, query_rows[block])
            for g in range(2):
                back_sums(block, g, key_at, bias, back_scores(block, g, key_at, BLOCK), True)
            return carry

        lax.fori_loop(*more[block], extra_back, 0)
    query_turned, enc_turned = x2_ref[...].astype(BF16).T, enc_ref[...].T
    query_grads = [(r.dqt[g] * SCALE).astype(BF16).T for g in range(2)]
    side_grads = [(r.dk[g].astype(BF16), r.dv[g].astype(BF16)) for g in range(2)]
    for g in (1, 0):
        packed, mark = packs[g]
        pack(packed, mark, 0, nn(query_turned, query_grads[g]))
        for i in range(2):
            pack(packed, mark, 1 + i, nn(enc_turned, side_grads[g][i]))
        r.send(f"pack{g}")
    r.denc[...] = sum(nt(side_grads[g][i], r.get(f"ckv{g}")[i]) for i in range(2) for g in range(2))
    r.out("denc_other")[...] = r.denc[pl.ds(second, own), :].astype(BF16)
    r.send("denc_other")
    r.out("denc_own")[...] = r.denc[pl.ds(first, own), :]
    r.send("denc_own")
    r.out("g2")[...] = r.dz[...] + sum(nt(query_grads[g], r.get(f"cq{g}")[...]) for g in range(2))


def pair_of_packs(r, bits, name="pack"):
    core, place = r.ids[0], r.ids[1]
    return [(r.out(f"{name}{g}"), own_label(bits, core ^ g, place)) for g in range(2)]


def key_stream_gradient(r, weights, keys=("dk", "dv")):
    return sum(nt(r.get(f"{keys[i]}{g}")[...], weights[g][i]) for i in range(2) for g in range(2))


def feed_gradients(r, g, dy_ref, acc_ref, turned):
    core, place = r.ids[0], r.ids[1]
    up_mark, down_mark = own_label(UP_BITS, core ^ g, place), own_label(DOWN_BITS, core ^ g, place)
    h_ref, dh_ref, a_ref, up_ref, down_ref = [r.get(key) for key in ("h", "dh", "a", "up", "down")]
    chunks = feed_chunks(h_ref.shape[1])
    ahead = nt(dy_ref[...], down_ref[chunks[0][1], :])
    for j, cols in chunks:
        above = ahead
        if j + 1 < len(chunks):
            ahead = nt(dy_ref[...], down_ref[chunks[j + 1][1], :])
        active, slope = gelu_both(h_ref[:, cols])
        hidden_grad = above.astype(BF16) * slope
        acc_ref[...] += nt(hidden_grad, up_ref[:, cols])
        up_grad = nn(turned[0][...], hidden_grad) + nn(turned[1][...], dh_ref[:, cols])
        down_grad = nn(turned[2][...], active) + nn(turned[3][...], a_ref[:, cols])
        for b in range(2):
            pack(r.out("up_pack"), up_mark, 2 * j + b, up_grad[:, quad(b)])
            pack(r.out("down_pack"), down_mark, 2 * j + b, down_grad[:, quad(b)])


def feed_other_kernel(r):
    cot_ref, own_ref, recv_ref, z1_ref = r.get("cot"), r.get("denc_own"), r.get("denc_recv"), r.get("z1")
    dy_ref, acc_ref, turned = r.out("dy"), r.out("g0"), [r.out(f"turned{i}") for i in range(4)]
    gain, shift = norm_back(
        r,
        r.get("gain")[1:2, :],
        lambda rows: z1_ref[rows, :],
        lambda rows: cot_ref[rows, :].astype(F32) + own_ref[rows, :] + recv_ref[rows, :].astype(F32),
        (acc_ref, dy_ref),
    )
    r.out("norms")[0:1, :] = gain
    r.out("norms")[1:2, :] = shift
    r.send("dy")
    for i, ref in enumerate((r.get("x1_low"), r.get("x3_low"), dy_ref, r.get("dy3"))):
        turned[i][...] = ref[...].T
        r.send(f"turned{i}")
    feed_gradients(r, 1, dy_ref, acc_ref, turned)


def feed_own_kernel(r):
    acc_ref = r.out("g0")
    acc_ref[...] = r.get("dz")[...]
    feed_gradients(r, 0, r.get("dy"), acc_ref, [r.get(f"turned{i}") for i in range(4)])


def norm_parts(norms, r):
    feed, dec, cross = r.get("feed_norms"), r.get("dec_norms"), r.get("cross_norms")
    rows = [(norms, 0), (feed, 0), (dec, 0), (cross, 0), (cross, 1)]
    rows += [(norms, 1), (feed, 1), (dec, 1), (cross, 2), (cross, 3)]
    return [ref[at : at + 1, :] for ref, at in rows]


def self_back_heads(r, causal, bits, g, branch, norms, keys_turned, query_turned):
    core, place = r.ids[0], r.ids[1]
    row_ref, window = r.get("row"), r.marks.shape[0]
    tokens = row_ref.shape[1]
    spread_marks(r.marks, row_ref[:, pl.ds(aligned(core * (tokens - window)), window)])
    spots = set_self_bias(r.bias, core, tokens, r.marks, row_ref, causal)
    ot_ref = r.get("ot")
    mixed_gradients(branch, ot_ref[...], r.get("wo")[...], r.do, r.delta)
    packed, mark = r.out("pack"), own_label(bits, core ^ g, place)
    pack(packed, mark, 3, as_unit(nn(ot_ref[...], branch)))
    if not causal:
        pack_norms(packed, mark, norm_parts(norms, r))
    r.dk[...] = jnp.zeros(r.dk.shape, F32)
    r.dv[...] = jnp.zeros(r.dv.shape, F32)
    q_ref, k_ref, v_ref, lse_ref = r.get("q"), r.get("k"), r.get("v"), r.get("lse")
    r.kt[...] = k_ref[...].T
    masks = head_masks()

    def scored(block):
        rows = slice(block * BLOCK, (block + 1) * BLOCK)
        return backward_scores(rows, *spots[block], masks, q_ref, k_ref, v_ref, r.do)

    ahead = scored(0)
    for block, (key_at, width) in enumerate(spots):
        now = ahead
        if block + 1 < len(spots):
            ahead = scored(block + 1)
        backward_sums(
            slice(block * BLOCK, (block + 1) * BLOCK), key_at, r.bias[block, :width, :], now, r.kt, lse_ref, r.delta,
            r.dqt, r.dk, r.dv,
        )
    r.out("dq")[...] = (r.dqt[...] * SCALE).astype(BF16).T
    r.out("dk")[...] = r.dk[...].astype(BF16)
    r.out("dv")[...] = r.dv[...].astype(BF16)
    for key in ("dq", "dk", "dv"):
        r.send(key)
    pack(packed, mark, 0, nn(query_turned[...], r.out("dq")[...]))
    pack(packed, mark, 1, nn(keys_turned[...], r.out("dk")[...]))
    pack(packed, mark, 2, nn(keys_turned[...], r.out("dv")[...]))


def self_back_other_kernel(causal, norm_at, bits, r):
    core = r.ids[0]
    z_ref, up_ref, x_ref = r.get("z"), r.get("up"), r.get("x")
    tokens, own, window = x_ref.shape[0], z_ref.shape[0], r.marks.shape[0]
    norms, branch = r.out("norms"), r.out("branch")
    gain, shift = norm_back(
        r,
        r.get("gain")[norm_at : norm_at + 1, :],
        lambda rows: z_ref[rows, :],
        lambda rows: up_ref[rows, :],
        (r.out("dz"), branch),
    )
    norms[0:1, :] = gain
    norms[1:2, :] = shift
    for key in ("norms", "dz", "branch"):
        r.send(key)
    keys_turned, query_turned = r.out("keys_turned"), r.out("query_turned")
    keys_turned[...] = x_ref[pl.ds(aligned(core * (tokens - window)), window), :].T
    query_turned[...] = x_ref[pl.ds(aligned(core * own), own), :].T
    r.send("keys_turned")
    r.send("query_turned")
    self_back_heads(r, causal, bits, 1, branch[...], norms, keys_turned, query_turned)


def self_back_own_kernel(causal, bits, r):
    branch = r.get("branch")[...]
    norms = None if causal else r.get("norms")
    self_back_heads(r, causal, bits, 0, branch, norms, r.get("keys_turned"), r.get("query_turned"))


def stream_gradient_kernel(r):
    core = r.ids[0]
    dz_ref, own, window = r.get("dz"), r.get("dq0").shape[0], r.get("dk0").shape[0]
    w = (r.get("w0"), r.get("w1"))
    r.near[...] = key_stream_gradient(r, [(w[g][1], w[g][2]) for g in range(2)])
    r.out("halo")[...] = r.near[pl.ds(aligned((1 - core) * own), window - own), :].astype(BF16)
    r.send("halo")
    r.out("dx")[...] = (
        dz_ref[...]
        + sum(nt(r.get(f"dq{g}")[...], w[g][0]) for g in range(2))
        + r.near[pl.ds(aligned(core * (window - own)), own), :]
    )


class Refs:
    def __init__(self, smem, ins, outs, scratch):
        for name, ref in list(smem.items()) + list(scratch.items()):
            setattr(self, name, ref)
        self.ins, self.outs = ins, outs
        self.waited, self.sent = set(), set()
        for copy, ref in ins.values():
            copy.start()

    def get(self, name):
        copy, ref = self.ins[name]
        if name not in self.waited:
            self.waited.add(name)
            copy.wait()
        return ref

    def out(self, name):
        return self.outs[name][1]

    def send(self, name):
        self.sent.add(name)
        self.outs[name][0].start()

    def close(self):
        for name in self.ins:
            self.get(name)
        for name in self.outs:
            if name not in self.sent:
                self.send(name)
        for copy, ref in self.outs.values():
            copy.wait()


def call(kernel, name, smem, ins, outs, scratch, cost, limit=VMEM_LIMIT):
    n_smem, n_in, n_out, n_scratch = len(smem), len(ins), len(outs), len(scratch)

    def body(*refs):
        smem_refs = refs[:n_smem]
        refs = refs[n_smem:]
        in_refs, out_refs, refs = refs[:n_in], refs[n_in : n_in + n_out], refs[n_in + n_out :]
        in_vmem, out_vmem, refs = refs[:n_in], refs[n_in : n_in + n_out], refs[n_in + n_out :]
        in_sem, out_sem = refs[-2:]
        copies_in = {
            key: (pltpu.make_async_copy(in_refs[i], in_vmem[i], in_sem.at[i]), in_vmem[i])
            for i, key in enumerate(ins)
        }
        copies_out = {
            key: (pltpu.make_async_copy(out_vmem[i], out_refs[i], out_sem.at[i]), out_vmem[i])
            for i, key in enumerate(outs)
        }
        held = Refs(dict(zip(smem, smem_refs)), copies_in, copies_out, dict(zip(scratch, refs)))
        kernel(held)
        held.close()

    held_bytes = sum(
        math.prod(shape[:-2]) * -(-shape[-2] // 8) * 8 * shape[-1] * jnp.dtype(dtype).itemsize
        for shape, dtype in [(array.shape, array.dtype) for array in ins.values()] + list(outs.values()) + list(scratch.values())
    )
    results = pl.pallas_call(
        body,
        out_shape=[jax.ShapeDtypeStruct(*out) for out in outs.values()],
        in_specs=[pl.BlockSpec(memory_space=pltpu.SMEM)] * n_smem + [pl.BlockSpec(memory_space=pl.ANY)] * n_in,
        out_specs=[pl.BlockSpec(memory_space=pl.ANY)] * n_out,
        scratch_shapes=[pltpu.VMEM(array.shape, array.dtype) for array in ins.values()]
        + [pltpu.VMEM(*out) for out in outs.values()]
        + [pltpu.VMEM(*one) for one in scratch.values()]
        + [pltpu.SemaphoreType.DMA((n_in,)), pltpu.SemaphoreType.DMA((n_out,))],
        compiler_params=pltpu.CompilerParams(vmem_limit_bytes=max(held_bytes + SPARE, limit)),
        cost_estimate=pl.CostEstimate(flops=cost * 10**9, transcendentals=0, bytes_accessed=cost * 10**6),
        name=name,
    )(*smem.values(), *ins.values())
    return SimpleNamespace(**dict(zip(outs, results)))


def finish_kernel(kind, bits, ids_ref, *refs):
    mark = own_label(bits, ids_ref[0], ids_ref[1])
    gathered, sem = refs[-2:]
    n_outs = {"enc": 4, "dec": 2, "cross": 3, "up": 1, "down": 1}[kind]
    count = len(refs) - 2 - n_outs
    parts, outs = refs[:count], refs[count:-2]
    copies, at = [], 0
    for i, part in enumerate(parts):
        copies.append(pltpu.make_async_copy(part, gathered.at[pl.ds(at, part.shape[0])], sem.at[i]))
        at += part.shape[0]
    for copy in copies:
        copy.start()
    for copy in copies:
        copy.wait()
    for shard in range(SHARDS):
        unit, half = divmod(shard, 2)
        rows = slice(half * QUAD, (half + 1) * QUAD)
        where = pl.ds(mark ^ shard, 1)
        value = gathered[where, :QUAD, :][0].astype(F32)
        if kind == "up":
            outs[0][rows, quad(unit)] = value
        elif kind == "down":
            outs[0][quad(unit), rows] = value.T
        elif unit == 3:
            outs[2 if kind == "cross" else 1][:, quad(half)] = value
        elif kind != "cross":
            outs[0][unit, rows, :] = value
        elif unit == 0:
            outs[0][rows, :] = value
        else:
            outs[1][unit - 1, rows, :] = value
        if kind == "enc":
            norms = gathered[where, QUAD:, :][0].astype(F32)
            many = norm_rows(SHARDS)
            for i in range(many):
                row, side = divmod(shard * many + i, 2)
                if row < 10:
                    outs[2 + row // 5][row % 5 : row % 5 + 1, quad(side)] = norms[i : i + 1, :]


def finish(group, ids, outs):
    parts = group.parts
    shape = (SHARDS,) + parts[0].shape[1:]
    return pl.pallas_call(
        functools.partial(finish_kernel, group.kind, group.bits),
        out_shape=[jax.ShapeDtypeStruct(*out) for out in outs],
        in_specs=[pl.BlockSpec(memory_space=pltpu.SMEM)] + [pl.BlockSpec(memory_space=pl.ANY)] * len(parts),
        out_specs=[pl.BlockSpec(memory_space=pltpu.VMEM)] * len(outs),
        scratch_shapes=[pltpu.VMEM(shape, BF16), pltpu.SemaphoreType.DMA((len(parts),))],
        compiler_params=pltpu.CompilerParams(vmem_limit_bytes=FINISH_LIMIT),
        cost_estimate=pl.CostEstimate(flops=2 * 10**9, transcendentals=0, bytes_accessed=2 * 10**6),
        name="finish_" + group.kind,
    )(ids, *parts)


class Sum:
    def __init__(self, kind, bits, dp, mp, mine, other):
        self.kind, self.bits, self.dp, self.mp = kind, bits, dp, mp
        self.phase, self.parts, self.outgoing = -1, [mine], [other]

    def hop(self, array, step):
        pairs = []
        for place in range(self.dp):
            for core in range(self.mp):
                bit = self.bits[core][step] if step < 4 else step
                pairs.append((place * self.mp + core, (place ^ (1 << bit)) * self.mp + core))
        return lax.ppermute(array, ("dp", "mp"), pairs)

    def launch(self):
        if self.phase < 0:
            self.flying = [lax.ppermute(self.outgoing[0], "mp", [(0, 1), (1, 0)])]
        elif self.phase <= 3:
            self.flying = [self.hop(self.outgoing[0], self.last if self.phase == 3 else self.phase)]
        else:
            self.flying = [self.hop(part, 6 - self.phase) for part in self.outgoing]

    def add_up(self):
        self.phase += 1
        if self.phase <= 2:
            mine, sent = self.parts[0], self.flying[0]
            half = mine.shape[0] // 2
            self.outgoing, self.parts = [mine[half:] + sent[half:]], [mine[:half] + sent[:half]]
        elif self.phase == 3:
            part, self.last = self.parts[0] + self.flying[0], 3
            while 2 << self.last < self.dp:
                part = part + self.hop(part, self.last)
                self.last += 1
            self.parts = self.outgoing = [part]
        elif self.phase == 4:
            self.parts = self.outgoing = [self.parts[0] + self.flying[0]]
        else:
            self.parts = self.parts + self.flying
            if self.phase < 7:
                self.outgoing = self.parts if self.phase == 5 and self.kind == "enc" else [jnp.concatenate(self.parts)]
        self.flying = []


def boundary(before, after, landing, launching=()):
    before, after, landing, launching = list(before), list(after), list(landing), list(launching)
    before, landed = lax.optimization_barrier((before, [group.flying for group in landing]))
    for group, flying in zip(landing, landed):
        group.flying = flying
        group.add_up()
    moving = landing + launching
    states = [([] if group.phase < 0 else group.parts, group.outgoing) for group in moving]
    before, after, states = lax.optimization_barrier((before, after, states))
    for group, state in zip(moving, states):
        group.outgoing = list(state[1])
        if group.phase >= 0:
            group.parts = list(state[0])
        if group.phase < 7:
            group.launch()
    return before, after


def on_device(
    src_embed, tgt_embed, src_segment, tgt_segment, enc_qkv, enc_out_proj, dec_qkv, dec_out_proj, cross_query,
    cross_kv, cross_out_proj, ffn_up, ffn_down, norm_gain, norm_bias, enc_cotangent, dec_cotangent,
):
    dp, mp = lax.axis_size("dp"), lax.axis_size("mp")
    tokens, model = src_embed.shape
    own = tokens // mp
    window = own + MOST
    half = ffn_up.shape[1]
    hidden = 2 * half
    position = lax.axis_index("mp")
    ids = jnp.stack([position, lax.axis_index("dp")]).astype(jnp.int32)
    pairs = [(0, 1), (1, 0)]

    def swap(tree):
        return jax.tree.map(lambda a: lax.ppermute(a, "mp", pairs), tree)

    enc_w1, enc_o1 = swap((enc_qkv, enc_out_proj))
    up1, down1 = swap((ffn_up, ffn_down))
    dec_w1, dec_o1 = swap((dec_qkv, dec_out_proj))
    cross_q1, cross_kv1, cross_o1 = swap((cross_query, cross_kv, cross_out_proj))
    feed = {"up0": ffn_up, "up1": up1, "down0": ffn_down, "down1": down1}

    def rows(count, dtype):
        return ((count, model), dtype)

    blocks = own // BLOCK
    q_shape, k_shape, ot_shape, lse_shape = ((own, QUAD), BF16), ((window, QUAD), BF16), ((QUAD, own), BF16), ((4, own), F32)
    vt_shape, marks, bias = ((4 * STRIDE, window), BF16), ((window, BLOCK), jnp.int32), ((blocks, 3 * BLOCK, BLOCK), F32)
    heads = {"q": q_shape, "k": k_shape, "v": k_shape, "ot": ot_shape, "lse": lse_shape}
    wide = ((own, half), BF16)
    norm_in = {"gain": norm_gain, "shift": norm_bias}
    first = call(
        own_heads_kernel, "own_heads", {"ids": ids},
        {"src_row": src_segment, "src": src_embed, "src_w": enc_qkv,
         "tgt_row": tgt_segment, "tgt": tgt_embed, "tgt_w": dec_qkv},
        {f"{side}_{key}": shape for side in ("src", "tgt") for key, shape in heads.items()},
        {"marks": marks, "src_bias": bias, "tgt_bias": bias, "src_vt": vt_shape, "tgt_vt": vt_shape},
        cost=8,
    )
    encoder = call(
        encoder_kernel, "encoder_forward", {"ids": ids},
        {"row": src_segment, "x": src_embed, "w": enc_w1, "ot0": first.src_ot, "wo0": enc_out_proj, "wo1": enc_o1,
         **norm_in, "up0": ffn_up, "down0": ffn_down, "up1": up1, "down1": down1},
        {**heads, "z0": rows(own, F32), "x1_low": rows(own, BF16), "h0": wide, "h1": wide,
         "z1": rows(own, F32), "enc": rows(own, BF16)},
        {"marks": marks, "bias": bias, "vt": vt_shape, "x1": rows(own, F32), "acc": rows(own, F32)},
        cost=12,
    )
    enc_swapped = swap(encoder.enc)
    decoder = call(
        decoder_kernel, "decoder_self_forward", {"ids": ids},
        {"row": tgt_segment, "x": tgt_embed, "w": dec_w1, "ot0": first.tgt_ot, "wo0": dec_out_proj, "wo1": dec_o1,
         **norm_in},
        {**heads, "z2": rows(own, F32), "x2": rows(own, F32)},
        {"marks": marks, "bias": bias, "vt": vt_shape, "acc": rows(own, F32)}, cost=6,
    )
    packed = ((SHARDS, QUAD, QUAD), BF16)
    packed_norms = ((SHARDS, QUAD + TILE, QUAD), BF16)
    crossed = call(
        cross_kernel, "cross_and_decoder_feed",
        {"ids": ids, "src_marks": src_segment, "tgt_marks": tgt_segment},
        {"src_row": src_segment, "tgt_row": tgt_segment, "enc_own": encoder.enc, "enc_other": enc_swapped,
         "x2": decoder.x2, "cq0": cross_query, "ckv0": cross_kv, "cq1": cross_q1, "ckv1": cross_kv1,
         "co0": cross_out_proj, "co1": cross_o1, **norm_in, **feed, "cot": dec_cotangent},
        {"enc": rows(tokens, BF16), "x3_low": rows(own, BF16), "a0": wide, "a1": wide, "dec": rows(own, BF16),
         "dy": rows(own, BF16), "dh0": wide, "dh1": wide, "norms": rows(4, F32), "pack0": packed, "pack1": packed,
         "denc_other": rows(own, BF16), "denc_own": rows(own, F32), "g2": rows(own, F32)},
        {"marks": ((tokens, BLOCK), jnp.int32), "bias": bias, "q": ((2, own, QUAD), BF16),
         "k": ((2, tokens, QUAD), BF16), "v": ((2, tokens, QUAD), BF16), "turn": ((2, QUAD, tokens), BF16), "vt": ((2, 4 * STRIDE, tokens), BF16),
         "mix": ((model, own), F32), "tops": ((8, own), F32), "totals": ((8, own), F32), "lse": ((2, 4, own), F32),
         "ot": ((model, own), BF16), "acc": rows(own, F32), "x3": rows(own, F32), "z3": rows(own, F32),
         "z4": rows(own, F32), "dz": rows(own, F32), "h": ((2, own, half), BF16), "low": rows(own, BF16), "do": ((2, own, QUAD), BF16),
         "delta": ((2, 4, own), F32), "dqt": ((2, QUAD, own), F32), "dk": ((2, tokens, QUAD), F32),
         "dv": ((2, tokens, QUAD), F32), "denc": rows(tokens, F32)},
        cost=30,
    )
    def whole(mine, received):
        return jnp.where(
            position == 0, jnp.concatenate([mine, received]), jnp.concatenate([received, mine])
        )

    def group(kind, bits, mine, other):
        return Sum(kind, bits, dp, mp, mine, other)

    head_scratch = {
        "marks": marks, "bias": bias, "do": q_shape, "delta": ((4, own), F32), "kt": ((QUAD, window), BF16),
        "dqt": ((QUAD, own), F32), "dk": ((window, QUAD), F32), "dv": ((window, QUAD), F32),
    }
    turned_shapes = {"keys_turned": ((model, window), BF16), "query_turned": ((model, own), BF16)}
    head_outs = {"dq": q_shape, "dk": k_shape, "dv": k_shape}

    def self_other(causal, at, bits, name, x, row, z, up, w_out, heads_kept, pack_shape, more):
        ins = {"z": z, "up": up, "gain": norm_gain, "row": row, "x": x, "wo": w_out} | heads_kept | more
        return call(
            functools.partial(self_back_other_kernel, causal, at, bits), name, {"ids": ids}, ins,
            {"dz": rows(own, F32), "branch": rows(own, BF16), "norms": rows(2, F32), "pack": pack_shape}
            | turned_shapes | head_outs,
            head_scratch, cost=9, limit=0,
        )

    def self_own(causal, bits, name, back, row, branch, w_out, heads_kept, pack_shape, more):
        ins = {"branch": branch, "row": row, "wo": w_out} | heads_kept
        ins |= {"keys_turned": back.keys_turned, "query_turned": back.query_turned} | more
        return call(
            functools.partial(self_back_own_kernel, causal, bits), name, {"ids": ids}, ins,
            {"pack": pack_shape} | head_outs, head_scratch, cost=7, limit=0,
        )

    def kept_own(side):
        return {key: getattr(first, f"{side}_{key}") for key in ("ot", "k", "q", "v", "lse")}

    def kept_other(part):
        return {key: getattr(part, key) for key in ("ot", "k", "q", "v", "lse")}

    def stream_gradient(name, back, back_own, w0, w1, ids):
        ins = {"dz": back.dz, "w0": w0, "w1": w1}
        for key in ("dk", "dv", "dq"):
            ins |= {f"{key}0": getattr(back_own, key), f"{key}1": getattr(back, key)}
        return call(
            stream_gradient_kernel, name, {"ids": ids}, ins,
            {"halo": rows(window - own, BF16), "dx": rows(own, F32)}, {"near": rows(window, F32)}, cost=5, limit=0,
        )

    def group(kind, bits, mine, other):
        return Sum(kind, bits, dp, mp, mine, other)

    halo_at = (1 - position) * (own - (window - own))

    def with_halo(grad, received):
        part = lax.dynamic_slice_in_dim(grad, halo_at, window - own, 0) + received.astype(F32)
        return lax.dynamic_update_slice_in_dim(grad, part, halo_at, 0)

    square, out_half, triple = ((model, QUAD), F32), ((QUAD, model), F32), ((3, model, QUAD), F32)
    out_shapes = {
        "cross": [square, ((2, model, QUAD), F32), out_half],
        "dec": [triple, out_half],
        "up": [((model, half), F32)],
        "down": [rows(half, F32)],
        "enc": [triple, out_half, rows(5, F32), rows(5, F32)],
    }
    cross_sum = group("cross", CROSS_BITS, crossed.pack0, crossed.pack1)
    cross_sum.launch()
    denc_recv = swap(crossed.denc_other)
    (cross_norms,), (z1, denc_recv) = boundary([crossed.norms], [encoder.z1, denc_recv], [cross_sum])
    fed = call(
        feed_other_kernel, "encoder_feed_other", {"ids": ids},
        {"cot": enc_cotangent, "denc_own": crossed.denc_own, "denc_recv": denc_recv, "z1": z1, "gain": norm_gain,
         "x1_low": encoder.x1_low, "x3_low": crossed.x3_low, "dy3": crossed.dy, "down": down1, "h": encoder.h1,
         "up": up1, "dh": crossed.dh1, "a": crossed.a1},
        {"dy": rows(own, BF16), "norms": rows(2, F32), **{f"turned{i}": ((model, own), BF16) for i in range(4)}, "up_pack": packed,
         "down_pack": packed, "g0": rows(own, F32)},
        {}, cost=10, limit=FEED_LIMIT,
    )
    up_sum = group("up", UP_BITS, None, fed.up_pack)
    down_sum = group("down", DOWN_BITS, None, fed.down_pack)
    (feed_norms,), (dy1,) = boundary([fed.norms], [fed.dy], [cross_sum], [up_sum, down_sum])
    fed_own = call(
        feed_own_kernel, "encoder_feed_own", {"ids": ids},
        {"dy": dy1, "down": ffn_down, "h": encoder.h0, "dz": fed.g0, **{f"turned{i}": getattr(fed, f"turned{i}") for i in range(4)}, "up": ffn_up,
         "dh": crossed.dh0, "a": crossed.a0},
        {"g0": rows(own, F32), "up_pack": packed, "down_pack": packed}, {}, cost=9, limit=0,
    )
    up_sum.parts, down_sum.parts = [fed_own.up_pack], [fed_own.down_pack]
    (feed_norms,), (g2,) = boundary([feed_norms], [crossed.g2], [cross_sum, up_sum, down_sum])
    dec_back = self_other(
        True, 2, DEC_BITS, "decoder_self_other", tgt_embed, tgt_segment, decoder.z2, g2, dec_o1, kept_other(decoder),
        packed, {},
    )
    dec_sum = group("dec", DEC_BITS, None, dec_back.pack)
    (dec_norms,), (branch,) = boundary([dec_back.norms], [dec_back.branch], [cross_sum, up_sum], [dec_sum])
    dec_own = self_own(
        True, DEC_BITS, "decoder_self_own", dec_back, tgt_segment, branch, dec_out_proj, kept_own("tgt"), packed, {},
    )
    dec_sum.parts = [dec_own.pack]
    (dec_norms,), (g0,) = boundary([dec_norms], [fed_own.g0], [cross_sum, up_sum, down_sum, dec_sum])
    norms_before = {"feed_norms": feed_norms, "dec_norms": dec_norms, "cross_norms": cross_norms}
    enc_back = self_other(
        False, 0, ENC_BITS, "encoder_self_other", src_embed, src_segment, encoder.z0, g0, enc_o1, kept_other(encoder),
        packed_norms, norms_before,
    )
    enc_sum = group("enc", ENC_BITS, None, enc_back.pack)
    (enc_norms,), (branch,) = boundary(
        [enc_back.norms], [enc_back.branch], [cross_sum, up_sum, down_sum, dec_sum], [enc_sum]
    )
    enc_own = self_own(
        False, ENC_BITS, "encoder_self_own", enc_back, src_segment, branch, enc_out_proj, kept_own("src"),
        packed_norms, {"norms": enc_norms, **norms_before},
    )
    enc_sum.parts = [enc_own.pack]
    order = ids

    def step(*landing, after=()):
        nonlocal order
        (order, *after), () = boundary([order, *after], [], landing)
        return after

    (enc_own.dq,) = step(enc_sum, after=[enc_own.dq])
    step(up_sum, down_sum, dec_sum)
    src_side = stream_gradient("src_gradient", enc_back, enc_own, enc_qkv, enc_w1, order)
    (src_halo,) = step(enc_sum, after=[src_side.halo])
    tgt_side = stream_gradient("tgt_gradient", dec_back, dec_own, dec_qkv, dec_w1, order)
    (tgt_halo,) = step(up_sum, dec_sum, cross_sum, after=[tgt_side.halo])
    step(enc_sum)
    dec_part, src_halo, tgt_halo = step(down_sum, after=[crossed.dec, src_halo, tgt_halo])
    src_recv, tgt_recv, dec_swapped = swap(src_halo), swap(tgt_halo), swap(dec_part)
    (dec_swapped,) = step(up_sum, after=[dec_swapped])
    dec_whole = whole(crossed.dec, dec_swapped)
    (dec_whole,) = step(enc_sum, after=[dec_whole])
    step(down_sum)
    step(dec_sum, cross_sum)
    cross_out = list(finish(cross_sum, order, out_shapes["cross"]))
    (cross_out[0],) = step(down_sum, after=[cross_out[0]])
    step(enc_sum)
    (src_recv,) = step(dec_sum, after=[src_recv])
    src_grad = with_halo(src_side.dx, src_recv)
    (src_grad,) = step(enc_sum, after=[src_grad])
    (tgt_recv,) = step(dec_sum, up_sum, after=[tgt_recv])
    up_out = list(finish(up_sum, order, out_shapes["up"]))
    (up_out[0],) = step(enc_sum, after=[up_out[0]])
    tgt_grad = with_halo(tgt_side.dx, tgt_recv)
    (tgt_grad,) = step(down_sum, after=[tgt_grad])
    down_out = list(finish(down_sum, order, out_shapes["down"]))
    (down_out[0],) = step(dec_sum, after=[down_out[0]])
    dec_out = list(finish(dec_sum, order, out_shapes["dec"]))
    (dec_out[0],) = step(enc_sum, after=[dec_out[0]])
    enc_out = finish(enc_sum, order, out_shapes["enc"])

    return (
        crossed.enc,
        dec_whole,
        src_grad,
        tgt_grad,
        enc_out[0],
        enc_out[1],
        dec_out[0],
        dec_out[1],
        cross_out[0],
        cross_out[1],
        cross_out[2],
        up_out[0],
        down_out[0],
        enc_out[2],
        enc_out[3],
    )


def solution(mesh):
    in_specs = (
        P("dp", None), P("dp", None), P("dp", None), P("dp", None),
        P(None, None, "mp"), P("mp", None), P(None, None, "mp"), P("mp", None),
        P(None, "mp"), P(None, None, "mp"), P("mp", None), P(None, "mp"), P("mp", None),
        P(), P(), P(("dp", "mp"), None), P(("dp", "mp"), None),
    )
    out_specs = (
        P("dp", None), P("dp", None), P(("dp", "mp"), None), P(("dp", "mp"), None),
        P(None, None, "mp"), P("mp", None), P(None, None, "mp"), P("mp", None),
        P(None, "mp"), P(None, None, "mp"), P("mp", None), P(None, "mp"), P("mp", None),
        P(), P(),
    )
    return jax.shard_map(on_device, mesh=mesh, in_specs=in_specs, out_specs=out_specs, check_vma=False)
```

```python
import functools
import math
from types import SimpleNamespace

import jax
import jax.numpy as jnp
from jax import lax
from jax.experimental import pallas as pl
from jax.experimental.pallas import tpu as pltpu
from jax.sharding import PartitionSpec as P

HDIM = 64
SCALE = HDIM ** (-0.5)
EPSILON = 1e-05
MASKED = -1e30
BLOCK = 128
MOST = 128
QUAD = 4 * HDIM
UNITS = 4
TILE = 16
FEED = 512
SHARDS = 8
UP_BITS = ((0, 1, 2, 3), (1, 0, 2, 3))
DOWN_BITS = ((1, 0, 2, 3), (0, 1, 2, 3))
CROSS_BITS = ((0, 1, 2, 3), (1, 0, 2, 3))
DEC_BITS = ((0, 1, 2, 3), (1, 0, 2, 3))
STRIDE = HDIM + TILE
ENC_BITS = ((1, 0, 2, 3), (0, 1, 2, 3))
F32 = jnp.float32
BF16 = jnp.bfloat16
VMEM_LIMIT = 56 * 1024 * 1024
FEED_LIMIT = 44 * 1024 * 1024
FINISH_LIMIT = 10 * 1024 * 1024
SPARE = 6 * 1024 * 1024
GELU_IN = math.sqrt(2.0 / math.pi)
GELU_CUBE = 0.044715


def nn(left, right):
    return jnp.dot(left, right, preferred_element_type=F32)


def nt(left, right):
    return lax.dot_general(left, right, (((1,), (1,)), ((), ())), preferred_element_type=F32)


def tn(left, right):
    return lax.dot_general(left, right, (((0,), (0,)), ((), ())), preferred_element_type=F32)


def aligned(index, size=BLOCK):
    return pl.multiple_of(index, size)


def over_rows(rows, chunk, body, carry, unroll=4):
    return lax.fori_loop(
        0,
        rows // chunk,
        lambda i, kept: body(pl.ds(aligned(i * chunk, chunk), chunk), kept),
        carry,
        unroll=min(unroll, rows // chunk),
    )


def normalize(before):
    centered = before - jnp.mean(before, axis=-1, keepdims=True)
    variance = jnp.mean(centered * centered, axis=-1, keepdims=True)
    rate = lax.rsqrt(variance + EPSILON)
    return centered * rate, rate


def norm_backward(before, upstream, gain_row):
    normed, rate = normalize(before)
    scaled = upstream * gain_row
    first = jnp.mean(scaled, axis=-1, keepdims=True)
    second = jnp.mean(scaled * normed, axis=-1, keepdims=True)
    return rate * (scaled - first - normed * second), upstream * normed


def fold_rows(block):
    return jnp.sum(block.reshape(block.shape[0] // 8, 8, block.shape[1]), axis=0)


def gelu(hidden):
    inner = GELU_IN * hidden * (1.0 + GELU_CUBE * hidden * hidden)
    return 0.5 * hidden * (1.0 + jnp.tanh(inner))


def gelu_both(hidden):
    square = hidden * hidden
    bent = jnp.tanh(GELU_IN * hidden * (1.0 + GELU_CUBE * square))
    half = 0.5 * (1.0 + bent)
    slope = half + 0.5 * hidden * (1.0 - bent * bent) * (GELU_IN * (1.0 + 3.0 * GELU_CUBE * square))
    return hidden * half, slope


def head_masks():
    lane = lax.broadcasted_iota(jnp.int32, (1, QUAD), 1)
    return [
        jnp.where((lane >= h * HDIM) & (lane < (h + 1) * HDIM), 1.0, 0.0).astype(BF16)
        for h in range(4)
    ]


def stack_heads(block, masks):
    return jnp.concatenate([block * mask for mask in masks], axis=0)


def quad(g):
    return slice(g * QUAD, (g + 1) * QUAD)


def bias_for(marks_ref, key_at, width, query_row, causal=False, key_start=0, query_start=0):
    allowed = marks_ref[pl.ds(key_at, width), :] == query_row
    if causal:
        places = key_start + lax.broadcasted_iota(jnp.int32, (width, BLOCK), 0)
        queries = query_start + lax.broadcasted_iota(jnp.int32, (width, BLOCK), 1)
        allowed = allowed & (places <= queries)
    return jnp.where(allowed, 0.0, MASKED)


def self_window(core, block, causal):
    middle = block + core
    if causal:
        return aligned(jnp.maximum(middle - 1, 0) * BLOCK), 2 * BLOCK
    return aligned(jnp.clip(middle - 1, 0, 2) * BLOCK), 3 * BLOCK


def set_self_bias(bias_ref, core, tokens, marks_ref, row_ref, causal):
    window, own = marks_ref.shape[0], row_ref.shape[1] // 2
    start = core * (tokens - window)
    spots = []
    for block in range(own // BLOCK):
        key_at, width = self_window(core, block, causal)
        first = aligned(core * own + block * BLOCK)
        bias_ref[block, :width, :] = bias_for(
            marks_ref, key_at, width, row_ref[:, pl.ds(first, BLOCK)], causal, start + key_at, first
        )
        spots.append((key_at, width))
    return spots


def soft_weights(scores, h, bias, top=None):
    one = scores[:, h * BLOCK : (h + 1) * BLOCK] + bias
    high = jnp.max(one, axis=0, keepdims=True)
    top = high if top is None else jnp.maximum(top, high)
    return top, jnp.exp((one - top).astype(BF16))


def set_values(vt_ref, values):
    turned = values.T
    for h in range(4):
        vt_ref[h * STRIDE : h * STRIDE + HDIM, :] = turned[h * HDIM : (h + 1) * HDIM]
        vt_ref[h * STRIDE + HDIM : (h + 1) * STRIDE, :] = jnp.ones((TILE, turned.shape[1]), BF16)


def quad_forward(spots, q_ref, k_ref, vt_ref, bias_ref, ot_ref, lse_ref, masks):
    def score(block):
        rows, (key_at, width) = slice(block * BLOCK, (block + 1) * BLOCK), spots[block]
        return nt(k_ref[pl.ds(key_at, width), :], stack_heads(q_ref[rows, :], masks))

    ahead = score(0)
    for block, (key_at, width) in enumerate(spots):
        rows = slice(block * BLOCK, (block + 1) * BLOCK)
        scores, ahead = ahead, score(block + 1) if block + 1 < len(spots) else None
        for h in range(4):
            top, weights = soft_weights(scores, h, bias_ref[block, :width, :])
            features = slice(h * HDIM, (h + 1) * HDIM)
            mixed = nn(vt_ref[h * STRIDE : (h + 1) * STRIDE, pl.ds(key_at, width)], weights)
            total = mixed[HDIM : HDIM + 1]
            ot_ref[features, rows] = (mixed[:HDIM] * (1.0 / total)).astype(BF16)
            lse_ref[h : h + 1, rows] = top + jnp.log(total)


def backward_scores(rows, key_at, width, masks, q_ref, k_ref, v_ref, do_ref):
    keys = pl.ds(key_at, width)
    q_stack, do_stack = stack_heads(q_ref[rows, :], masks), stack_heads(do_ref[rows, :], masks)
    return q_stack, do_stack, nt(k_ref[keys, :], q_stack), nt(v_ref[keys, :], do_stack)


def backward_sums(rows, key_at, bias, scored, kt_ref, lse_ref, delta_ref, dqt_ref, dk_ref, dv_ref, add=False):
    q_stack, do_stack, scores, prob_grads = scored
    keys = pl.ds(key_at, bias.shape[0])
    probs, score_grads = [], []
    for h in range(4):
        cols = slice(h * BLOCK, (h + 1) * BLOCK)
        prob = jnp.exp((scores[:, cols] + bias - lse_ref[h : h + 1, rows]).astype(BF16))
        probs.append(prob)
        score_grads.append(prob * (prob_grads[:, cols] - delta_ref[h : h + 1, rows]).astype(BF16))
    for h in range(4):
        features = slice(h * HDIM, (h + 1) * HDIM)
        query_grad = nn(kt_ref[features, keys], score_grads[h])
        if add:
            dqt_ref[features, rows] += query_grad
        else:
            dqt_ref[features, rows] = query_grad
    dv_ref[keys, :] += nn(jnp.concatenate(probs, axis=1), do_stack)
    dk_ref[keys, :] += nn(jnp.concatenate(score_grads, axis=1), q_stack)


def mixed_gradients(branch, ot, w_out, do_ref, delta_ref):
    do_ref[...] = nt(branch, w_out).astype(BF16)
    product = nt(w_out, branch).astype(BF16).astype(F32) * ot.astype(F32)
    for h in range(4):
        delta_ref[h : h + 1, :] = jnp.sum(product[h * HDIM : (h + 1) * HDIM, :], axis=0, keepdims=True)


def spread_marks(marks_ref, row):
    marks_ref[...] = jnp.broadcast_to(row, (marks_ref.shape[1], marks_ref.shape[0])).T


def label(bits, place):
    first, second, third = [(place >> bit) & 1 for bit in bits[:3]]
    return 4 * first + 2 * second + third


def own_label(bits, core, place):
    return jnp.where(core == 0, label(bits[0], place), label(bits[1], place))


def pack(out_ref, mark, unit, value, at=0):
    rows = value.shape[0] // 2
    for half in range(2):
        where = pl.ds(mark ^ (2 * unit + half), 1)
        out_ref[where, at : at + rows, :] = value[half * rows : (half + 1) * rows].astype(BF16)[None]


def as_unit(value):
    return jnp.concatenate([value[:, :QUAD], value[:, QUAD:]], axis=0).astype(BF16)


def pack_norms(out_ref, mark, parts):
    shards, tall, width = out_ref.shape
    halves = [part[:, half * width : (half + 1) * width] for part in parts for half in range(2)]
    each = norm_rows(shards)
    blank = jnp.zeros((1, width), F32)
    halves += [blank] * (shards * each - len(halves))
    for i in range(shards):
        block = jnp.concatenate(halves[i * each : (i + 1) * each] + [blank] * (TILE - each), axis=0)
        out_ref[pl.ds(mark ^ i, 1), tall - TILE :, :] = block.astype(BF16)[None]


def norm_rows(shards):
    return -(-20 // shards)


def prepare_quad(x_ref, w_ref, core, q_ref, k_ref, v_ref, vt_ref):
    tokens, own, window = x_ref.shape[0], q_ref.shape[0], k_ref.shape[0]
    keys = x_ref[pl.ds(aligned(core * (tokens - window)), window), :]
    q_ref[...] = (nn(x_ref[pl.ds(aligned(core * own), own), :], w_ref[0]) * SCALE).astype(BF16)
    k_ref[...] = nn(keys, w_ref[1]).astype(BF16)
    v_ref[...] = nn(keys, w_ref[2]).astype(BF16)
    set_values(vt_ref, v_ref[...])


def own_heads_kernel(r):
    core = r.ids[0]
    masks = head_masks()
    for side, causal in (("src", False), ("tgt", True)):
        x_ref, row_ref = r.get(side), r.get(side + "_row")
        k_ref = r.out(side + "_k")
        start = aligned(core * (x_ref.shape[0] - k_ref.shape[0]))
        spread_marks(r.marks, row_ref[:, pl.ds(start, k_ref.shape[0])])
        bias_ref, vt_ref = getattr(r, side + "_bias"), getattr(r, side + "_vt")
        spots = set_self_bias(bias_ref, core, x_ref.shape[0], r.marks, row_ref, causal)
        q_ref, v_ref = r.out(side + "_q"), r.out(side + "_v")
        prepare_quad(x_ref, r.get(side + "_w"), core, q_ref, k_ref, v_ref, vt_ref)
        for key in ("_q", "_k", "_v"):
            r.send(side + key)
        quad_forward(
            spots, q_ref, k_ref, vt_ref, bias_ref, r.out(side + "_ot"), r.out(side + "_lse"), masks
        )
        r.send(side + "_ot")
        r.send(side + "_lse")


def other_heads(r, causal):
    core = r.ids[0]
    x_ref, row_ref, k_ref = r.get("x"), r.get("row"), r.out("k")
    start = aligned(core * (x_ref.shape[0] - k_ref.shape[0]))
    spread_marks(r.marks, row_ref[:, pl.ds(start, k_ref.shape[0])])
    spots = set_self_bias(r.bias, core, x_ref.shape[0], r.marks, row_ref, causal)
    q_ref, v_ref, ot_ref = r.out("q"), r.out("v"), r.out("ot")
    prepare_quad(x_ref, r.get("w"), core, q_ref, k_ref, v_ref, r.vt)
    for key in ("q", "k", "v"):
        r.send(key)
    quad_forward(spots, q_ref, k_ref, r.vt, r.bias, ot_ref, r.out("lse"), head_masks())
    r.send("lse")
    r.send("ot")
    r.acc[...] = tn(r.get("ot0")[...], r.get("wo0")[...]) + tn(ot_ref[...], r.get("wo1")[...])


def norm_forward(r, at, residual, before_ref, after_ref, low_ref):
    gain, shift = r.get("gain")[at : at + 1, :], r.get("shift")[at : at + 1, :]

    def body(rows, carry):
        before = residual(rows) + r.acc[rows, :]
        if before_ref is not None:
            before_ref[rows, :] = before
        after = normalize(before)[0] * gain + shift
        if after_ref is not None:
            after_ref[rows, :] = after
        if low_ref is not None:
            low_ref[rows, :] = after.astype(BF16)
        return carry

    over_rows(r.acc.shape[0], 32, body, 0)


def own_row_reader(x_ref, core, own):
    first = core * own
    return lambda rows: x_ref[pl.ds(aligned(first + rows.start, rows.size), rows.size), :].astype(F32)


def encoder_kernel(r):
    other_heads(r, False)
    x1_low = r.out("x1_low")
    norm_forward(r, 0, own_row_reader(r.get("x"), r.ids[0], r.acc.shape[0]), r.out("z0"), r.x1, x1_low)
    r.send("z0")
    r.send("x1_low")
    feed_forward(x1_low, *feed_weights(r), (r.out("h0"), r.out("h1")), None, r.acc)
    r.send("h0")
    r.send("h1")
    norm_forward(r, 1, lambda rows: r.x1[rows, :], r.out("z1"), None, r.out("enc"))


def decoder_kernel(r):
    other_heads(r, True)
    norm_forward(r, 2, own_row_reader(r.get("x"), r.ids[0], r.acc.shape[0]), r.out("z2"), r.out("x2"), None)


def feed_weights(r):
    return (r.get("up0"), r.get("up1")), (r.get("down0"), r.get("down1"))


def feed_chunks(half):
    return [(j, slice(j * FEED, (j + 1) * FEED)) for j in range(half // FEED)]


def feed_forward(low_ref, ups, downs, h_refs, a_refs, acc_ref):
    chunks = [(g, cols) for g in range(2) for j, cols in feed_chunks(ups[0].shape[1])]
    ahead = nn(low_ref[...], ups[0][:, chunks[0][1]])
    for i, (g, cols) in enumerate(chunks):
        hidden = ahead
        if i + 1 < len(chunks):
            ahead = nn(low_ref[...], ups[chunks[i + 1][0]][:, chunks[i + 1][1]])
        hidden = hidden.astype(BF16)
        h_refs[g][:, cols] = hidden
        active = gelu(hidden)
        if a_refs is not None:
            a_refs[g][:, cols] = active
        term = nn(active, downs[g][cols, :])
        if i == 0:
            acc_ref[...] = term
        else:
            acc_ref[...] += term


def feed_backward(dy_ref, ups, downs, h_refs, dh_refs, acc_ref):
    chunks = [(g, cols) for g in range(2) for j, cols in feed_chunks(ups[0].shape[1])]
    ahead = nt(dy_ref[...], downs[0][chunks[0][1], :])
    for i, (g, cols) in enumerate(chunks):
        active_grad = ahead
        if i + 1 < len(chunks):
            ahead = nt(dy_ref[...], downs[chunks[i + 1][0]][chunks[i + 1][1], :])
        hidden_grad = active_grad.astype(BF16) * gelu_both(h_refs[g][:, cols])[1]
        dh_refs[g][:, cols] = hidden_grad
        acc_ref[...] += nt(hidden_grad, ups[g][:, cols])


def norm_back(r, gain_row, before, upstream, outs):
    def body(rows, sums):
        above = upstream(rows)
        grad, gain_terms = norm_backward(before(rows), above, gain_row)
        for ref in outs:
            ref[rows, :] = grad.astype(ref.dtype)
        return sums[0] + fold_rows(gain_terms), sums[1] + fold_rows(above)

    zeros = jnp.zeros((8, outs[0].shape[1]), F32)
    gains, shifts = over_rows(outs[0].shape[0], 32, body, (zeros, zeros))
    return jnp.sum(gains, axis=0, keepdims=True), jnp.sum(shifts, axis=0, keepdims=True)


def cross_kernel(r):
    core, place = r.ids[0], r.ids[1]
    x2_ref, enc_ref = r.get("x2"), r.out("enc")
    own, tokens = x2_ref.shape[0], enc_ref.shape[0]
    blocks = own // BLOCK
    first, second = aligned(core * own), aligned((1 - core) * own)
    width = 3 * BLOCK
    enc_ref[pl.ds(first, own), :] = r.get("enc_own")[...]
    enc_ref[pl.ds(second, own), :] = r.get("enc_other")[...]
    r.send("enc")
    spread_marks(r.marks, r.get("src_row")[...])
    steps = tokens.bit_length()

    def bound(mark, past):
        def step(i, pair):
            low, high = pair
            middle = (low + high) // 2
            value = r.src_marks[0, jnp.minimum(middle, tokens - 1)]
            below = (low < high) & ((value < mark) | (past & (value == mark)))
            above = (low < high) & jnp.logical_not(below)
            return jnp.where(below, middle + 1, low), jnp.where(above, middle, high)

        return lax.fori_loop(0, steps, step, (jnp.int32(0), jnp.int32(tokens)))[0]

    row_ref = r.get("tgt_row")
    query_rows, spots, more = [], [], []
    for block in range(blocks):
        head = first + block * BLOCK
        low = bound(r.tgt_marks[0, head], jnp.bool_(False)) // BLOCK
        high = (bound(r.tgt_marks[0, head + BLOCK - 1], jnp.bool_(True)) + BLOCK - 1) // BLOCK
        key_at = aligned(jnp.minimum(low, (tokens - width) // BLOCK) * BLOCK)
        query_rows.append(row_ref[:, pl.ds(aligned(head), BLOCK)])
        spots.append(key_at)
        more.append((key_at // BLOCK + 3, high))
        r.bias[block] = bias_for(r.marks, key_at, width, query_rows[block])
    masks = head_masks()
    x2_low = x2_ref[...].astype(BF16)
    for g in range(2):
        r.q[g] = (nn(x2_low, r.get(f"cq{g}")[...]) * SCALE).astype(BF16)
        r.k[g] = nn(enc_ref[...], r.get(f"ckv{g}")[0]).astype(BF16)
        r.v[g] = nn(enc_ref[...], r.get(f"ckv{g}")[1]).astype(BF16)
        set_values(r.vt.at[g], r.v[g])

    def weigh(g, h, scores, bias, key_at, keys_width, top):
        new_top, weights = soft_weights(scores, h, bias, top)
        mixed = nn(r.vt[g, h * STRIDE : (h + 1) * STRIDE, pl.ds(key_at, keys_width)], weights)
        features = slice(g * QUAD + h * HDIM, g * QUAD + (h + 1) * HDIM)
        return new_top, mixed[HDIM : HDIM + 1], mixed[:HDIM], features

    def score(block, g):
        rows = slice(block * BLOCK, (block + 1) * BLOCK)
        return nt(r.k[g, pl.ds(spots[block], width), :], stack_heads(r.q[g, rows, :], masks))

    tiles = [(block, g) for block in range(blocks) for g in range(2)]
    ahead = score(*tiles[0])
    for i, (block, g) in enumerate(tiles):
        rows = slice(block * BLOCK, (block + 1) * BLOCK)
        scores, ahead = ahead, score(*tiles[i + 1]) if i + 1 < len(tiles) else None
        for h in range(4):
            top, total, mixed, features = weigh(g, h, scores, r.bias[block], spots[block], width, None)
            r.mix[features, rows] = mixed
            r.tops[g * 4 + h : g * 4 + h + 1, rows] = top
            r.totals[g * 4 + h : g * 4 + h + 1, rows] = total

    for block in range(blocks):
        rows = slice(block * BLOCK, (block + 1) * BLOCK)

        def extra(i, carry, block=block, rows=rows):
            key_at = aligned(i * BLOCK)
            bias = bias_for(r.marks, key_at, BLOCK, query_rows[block])
            for g in range(2):
                scores = nt(r.k[g, pl.ds(key_at, BLOCK), :], stack_heads(r.q[g, rows, :], masks))
                for h in range(4):
                    at = slice(g * 4 + h, g * 4 + h + 1)
                    old = r.tops[at, rows]
                    top, total, mixed, features = weigh(g, h, scores, bias, key_at, BLOCK, old)
                    fade = jnp.exp(old - top)
                    r.mix[features, rows] = r.mix[features, rows] * fade + mixed
                    r.tops[at, rows] = top
                    r.totals[at, rows] = r.totals[at, rows] * fade + total
            return carry

        lax.fori_loop(*more[block], extra, 0)
    for head in range(8):
        features = slice(head * HDIM, (head + 1) * HDIM)
        at = slice(head, head + 1)
        r.ot[features, :] = (r.mix[features, :] * (1.0 / r.totals[at, :])).astype(BF16)
        r.lse[head // 4, head % 4 : head % 4 + 1, :] = r.tops[at, :] + jnp.log(r.totals[at, :])
    outs = (r.get("co0"), r.get("co1"))
    r.acc[...] = tn(r.ot[:QUAD, :], outs[0][...]) + tn(r.ot[QUAD:, :], outs[1][...])
    x3_low = r.out("x3_low")
    norm_forward(r, 3, lambda rows: x2_ref[rows, :], r.z3, r.x3, x3_low)
    r.send("x3_low")
    ups, downs = feed_weights(r)
    hs = (r.h.at[0], r.h.at[1])
    feed_forward(x3_low, ups, downs, hs, (r.out("a0"), r.out("a1")), r.acc)
    r.send("a0")
    r.send("a1")
    gain_ref, shift_ref, cot_ref, dec_ref, dy_ref = (
        r.get("gain"), r.get("shift"), r.get("cot"), r.out("dec"), r.out("dy")
    )
    last_gain, last_shift = gain_ref[4:5, :], shift_ref[4:5, :]

    def fourth_norm(rows, sums):
        before = r.x3[rows, :] + r.acc[rows, :]
        normed, rate = normalize(before)
        dec_ref[rows, :] = (normed * last_gain + last_shift).astype(BF16)
        upstream = cot_ref[rows, :].astype(F32)
        scaled = upstream * last_gain
        mean_one = jnp.mean(scaled, axis=-1, keepdims=True)
        mean_two = jnp.mean(scaled * normed, axis=-1, keepdims=True)
        grad = rate * (scaled - mean_one - normed * mean_two)
        r.z4[rows, :] = grad
        dy_ref[rows, :] = grad.astype(BF16)
        return sums[0] + fold_rows(upstream * normed), sums[1] + fold_rows(upstream)

    zeros = jnp.zeros((8, x2_ref.shape[1]), F32)
    gain_four, shift_four = over_rows(own, 32, fourth_norm, (zeros, zeros))
    r.send("dec")
    r.send("dy")
    feed_backward(dy_ref, ups, downs, hs, (r.out("dh0"), r.out("dh1")), r.z4)
    r.send("dh0")
    r.send("dh1")
    gain_three, shift_three = norm_back(
        r, gain_ref[3:4, :], lambda rows: r.z3[rows, :], lambda rows: r.z4[rows, :], (r.dz, r.low)
    )
    norms = r.out("norms")
    norms[0:1, :] = gain_three
    norms[1:2, :] = jnp.sum(gain_four, axis=0, keepdims=True)
    norms[2:3, :] = shift_three
    norms[3:4, :] = jnp.sum(shift_four, axis=0, keepdims=True)
    branch = r.low[...]
    ots = (r.ot.at[:QUAD], r.ot.at[QUAD:])
    for g in range(2):
        mixed_gradients(branch, ots[g][...], outs[g][...], r.do.at[g], r.delta.at[g])
    packs = pair_of_packs(r, CROSS_BITS)
    for g, (packed, mark) in enumerate(packs):
        pack(packed, mark, 3, as_unit(nn(ots[g][...], branch)))
        r.turn[g] = r.k[g].T
    r.dk[...] = jnp.zeros(r.dk.shape, F32)
    r.dv[...] = jnp.zeros(r.dv.shape, F32)

    def back_scores(block, g, key_at, keys_width):
        rows = slice(block * BLOCK, (block + 1) * BLOCK)
        return backward_scores(rows, key_at, keys_width, masks, r.q.at[g], r.k.at[g], r.v.at[g], r.do.at[g])

    def back_sums(block, g, key_at, bias, scored, add):
        backward_sums(
            slice(block * BLOCK, (block + 1) * BLOCK), key_at, bias, scored, r.turn.at[g], r.lse.at[g], r.delta.at[g],
            r.dqt.at[g], r.dk.at[g], r.dv.at[g], add,
        )

    ahead = back_scores(*tiles[0], spots[0], width)
    for i, (block, g) in enumerate(tiles):
        scored = ahead
        if i + 1 < len(tiles):
            ahead = back_scores(*tiles[i + 1], spots[tiles[i + 1][0]], width)
        back_sums(block, g, spots[block], r.bias[block], scored, False)
    for block in range(blocks):

        def extra_back(i, carry, block=block):
            key_at = aligned(i * BLOCK)
            bias = bias_for(r.marks, key_at, BLOCK, query_rows[block])
            for g in range(2):
                back_sums(block, g, key_at, bias, back_scores(block, g, key_at, BLOCK), True)
            return carry

        lax.fori_loop(*more[block], extra_back, 0)
    query_turned, enc_turned = x2_ref[...].astype(BF16).T, enc_ref[...].T
    query_grads = [(r.dqt[g] * SCALE).astype(BF16).T for g in range(2)]
    side_grads = [(r.dk[g].astype(BF16), r.dv[g].astype(BF16)) for g in range(2)]
    for g in (1, 0):
        packed, mark = packs[g]
        pack(packed, mark, 0, nn(query_turned, query_grads[g]))
        for i in range(2):
            pack(packed, mark, 1 + i, nn(enc_turned, side_grads[g][i]))
        r.send(f"pack{g}")
    r.denc[...] = sum(nt(side_grads[g][i], r.get(f"ckv{g}")[i]) for i in range(2) for g in range(2))
    r.out("denc_other")[...] = r.denc[pl.ds(second, own), :].astype(BF16)
    r.send("denc_other")
    r.out("denc_own")[...] = r.denc[pl.ds(first, own), :]
    r.send("denc_own")
    r.out("g2")[...] = r.dz[...] + sum(nt(query_grads[g], r.get(f"cq{g}")[...]) for g in range(2))


def pair_of_packs(r, bits, name="pack"):
    core, place = r.ids[0], r.ids[1]
    return [(r.out(f"{name}{g}"), own_label(bits, core ^ g, place)) for g in range(2)]


def key_stream_gradient(r, weights, keys=("dk", "dv")):
    return sum(nt(r.get(f"{keys[i]}{g}")[...], weights[g][i]) for i in range(2) for g in range(2))


def feed_gradients(r, g, dy_ref, acc_ref, turned):
    core, place = r.ids[0], r.ids[1]
    up_mark, down_mark = own_label(UP_BITS, core ^ g, place), own_label(DOWN_BITS, core ^ g, place)
    h_ref, dh_ref, a_ref, up_ref, down_ref = [r.get(key) for key in ("h", "dh", "a", "up", "down")]
    chunks = feed_chunks(h_ref.shape[1])
    ahead = nt(dy_ref[...], down_ref[chunks[0][1], :])
    for j, cols in chunks:
        above = ahead
        if j + 1 < len(chunks):
            ahead = nt(dy_ref[...], down_ref[chunks[j + 1][1], :])
        active, slope = gelu_both(h_ref[:, cols])
        hidden_grad = above.astype(BF16) * slope
        acc_ref[...] += nt(hidden_grad, up_ref[:, cols])
        up_grad = nn(turned[0][...], hidden_grad) + nn(turned[1][...], dh_ref[:, cols])
        down_grad = nn(turned[2][...], active) + nn(turned[3][...], a_ref[:, cols])
        for b in range(2):
            pack(r.out("up_pack"), up_mark, 2 * j + b, up_grad[:, quad(b)])
            pack(r.out("down_pack"), down_mark, 2 * j + b, down_grad[:, quad(b)])


def feed_other_kernel(r):
    cot_ref, own_ref, recv_ref, z1_ref = r.get("cot"), r.get("denc_own"), r.get("denc_recv"), r.get("z1")
    dy_ref, acc_ref, turned = r.out("dy"), r.out("g0"), [r.out(f"turned{i}") for i in range(4)]
    gain, shift = norm_back(
        r,
        r.get("gain")[1:2, :],
        lambda rows: z1_ref[rows, :],
        lambda rows: cot_ref[rows, :].astype(F32) + own_ref[rows, :] + recv_ref[rows, :].astype(F32),
        (acc_ref, dy_ref),
    )
    r.out("norms")[0:1, :] = gain
    r.out("norms")[1:2, :] = shift
    r.send("dy")
    for i, ref in enumerate((r.get("x1_low"), r.get("x3_low"), dy_ref, r.get("dy3"))):
        turned[i][...] = ref[...].T
        r.send(f"turned{i}")
    feed_gradients(r, 1, dy_ref, acc_ref, turned)


def feed_own_kernel(r):
    acc_ref = r.out("g0")
    acc_ref[...] = r.get("dz")[...]
    feed_gradients(r, 0, r.get("dy"), acc_ref, [r.get(f"turned{i}") for i in range(4)])


def norm_parts(norms, r):
    feed, dec, cross = r.get("feed_norms"), r.get("dec_norms"), r.get("cross_norms")
    rows = [(norms, 0), (feed, 0), (dec, 0), (cross, 0), (cross, 1)]
    rows += [(norms, 1), (feed, 1), (dec, 1), (cross, 2), (cross, 3)]
    return [ref[at : at + 1, :] for ref, at in rows]


def self_back_heads(r, causal, bits, g, branch, norms, keys_turned, query_turned):
    core, place = r.ids[0], r.ids[1]
    row_ref, window = r.get("row"), r.marks.shape[0]
    tokens = row_ref.shape[1]
    spread_marks(r.marks, row_ref[:, pl.ds(aligned(core * (tokens - window)), window)])
    spots = set_self_bias(r.bias, core, tokens, r.marks, row_ref, causal)
    ot_ref = r.get("ot")
    mixed_gradients(branch, ot_ref[...], r.get("wo")[...], r.do, r.delta)
    packed, mark = r.out("pack"), own_label(bits, core ^ g, place)
    pack(packed, mark, 3, as_unit(nn(ot_ref[...], branch)))
    if not causal:
        pack_norms(packed, mark, norm_parts(norms, r))
    r.dk[...] = jnp.zeros(r.dk.shape, F32)
    r.dv[...] = jnp.zeros(r.dv.shape, F32)
    q_ref, k_ref, v_ref, lse_ref = r.get("q"), r.get("k"), r.get("v"), r.get("lse")
    r.kt[...] = k_ref[...].T
    masks = head_masks()

    def scored(block):
        rows = slice(block * BLOCK, (block + 1) * BLOCK)
        return backward_scores(rows, *spots[block], masks, q_ref, k_ref, v_ref, r.do)

    ahead = scored(0)
    for block, (key_at, width) in enumerate(spots):
        now = ahead
        if block + 1 < len(spots):
            ahead = scored(block + 1)
        backward_sums(
            slice(block * BLOCK, (block + 1) * BLOCK), key_at, r.bias[block, :width, :], now, r.kt, lse_ref, r.delta,
            r.dqt, r.dk, r.dv,
        )
    r.out("dq")[...] = (r.dqt[...] * SCALE).astype(BF16).T
    r.out("dk")[...] = r.dk[...].astype(BF16)
    r.out("dv")[...] = r.dv[...].astype(BF16)
    for key in ("dq", "dk", "dv"):
        r.send(key)
    pack(packed, mark, 0, nn(query_turned[...], r.out("dq")[...]))
    pack(packed, mark, 1, nn(keys_turned[...], r.out("dk")[...]))
    pack(packed, mark, 2, nn(keys_turned[...], r.out("dv")[...]))


def self_back_other_kernel(causal, norm_at, bits, r):
    core = r.ids[0]
    z_ref, up_ref, x_ref = r.get("z"), r.get("up"), r.get("x")
    tokens, own, window = x_ref.shape[0], z_ref.shape[0], r.marks.shape[0]
    norms, branch = r.out("norms"), r.out("branch")
    gain, shift = norm_back(
        r,
        r.get("gain")[norm_at : norm_at + 1, :],
        lambda rows: z_ref[rows, :],
        lambda rows: up_ref[rows, :],
        (r.out("dz"), branch),
    )
    norms[0:1, :] = gain
    norms[1:2, :] = shift
    for key in ("norms", "dz", "branch"):
        r.send(key)
    keys_turned, query_turned = r.out("keys_turned"), r.out("query_turned")
    keys_turned[...] = x_ref[pl.ds(aligned(core * (tokens - window)), window), :].T
    query_turned[...] = x_ref[pl.ds(aligned(core * own), own), :].T
    r.send("keys_turned")
    r.send("query_turned")
    self_back_heads(r, causal, bits, 1, branch[...], norms, keys_turned, query_turned)


def self_back_own_kernel(causal, bits, r):
    branch = r.get("branch")[...]
    norms = None if causal else r.get("norms")
    self_back_heads(r, causal, bits, 0, branch, norms, r.get("keys_turned"), r.get("query_turned"))


def stream_gradient_kernel(r):
    core = r.ids[0]
    dz_ref, own, window = r.get("dz"), r.get("dq0").shape[0], r.get("dk0").shape[0]
    w = (r.get("w0"), r.get("w1"))
    r.near[...] = key_stream_gradient(r, [(w[g][1], w[g][2]) for g in range(2)])
    r.out("halo")[...] = r.near[pl.ds(aligned((1 - core) * own), window - own), :].astype(BF16)
    r.send("halo")
    r.out("dx")[...] = (
        dz_ref[...]
        + sum(nt(r.get(f"dq{g}")[...], w[g][0]) for g in range(2))
        + r.near[pl.ds(aligned(core * (window - own)), own), :]
    )


class Refs:
    def __init__(self, smem, ins, outs, scratch):
        for name, ref in list(smem.items()) + list(scratch.items()):
            setattr(self, name, ref)
        self.ins, self.outs = ins, outs
        self.waited, self.sent = set(), set()
        for copy, ref in ins.values():
            copy.start()

    def get(self, name):
        copy, ref = self.ins[name]
        if name not in self.waited:
            self.waited.add(name)
            copy.wait()
        return ref

    def out(self, name):
        return self.outs[name][1]

    def send(self, name):
        self.sent.add(name)
        self.outs[name][0].start()

    def close(self):
        for name in self.ins:
            self.get(name)
        for name in self.outs:
            if name not in self.sent:
                self.send(name)
        for copy, ref in self.outs.values():
            copy.wait()


def call(kernel, name, smem, ins, outs, scratch, cost, limit=VMEM_LIMIT):
    n_smem, n_in, n_out, n_scratch = len(smem), len(ins), len(outs), len(scratch)

    def body(*refs):
        smem_refs = refs[:n_smem]
        refs = refs[n_smem:]
        in_refs, out_refs, refs = refs[:n_in], refs[n_in : n_in + n_out], refs[n_in + n_out :]
        in_vmem, out_vmem, refs = refs[:n_in], refs[n_in : n_in + n_out], refs[n_in + n_out :]
        in_sem, out_sem = refs[-2:]
        copies_in = {
            key: (pltpu.make_async_copy(in_refs[i], in_vmem[i], in_sem.at[i]), in_vmem[i])
            for i, key in enumerate(ins)
        }
        copies_out = {
            key: (pltpu.make_async_copy(out_vmem[i], out_refs[i], out_sem.at[i]), out_vmem[i])
            for i, key in enumerate(outs)
        }
        held = Refs(dict(zip(smem, smem_refs)), copies_in, copies_out, dict(zip(scratch, refs)))
        kernel(held)
        held.close()

    held_bytes = sum(
        math.prod(shape[:-2]) * -(-shape[-2] // 8) * 8 * shape[-1] * jnp.dtype(dtype).itemsize
        for shape, dtype in [(array.shape, array.dtype) for array in ins.values()] + list(outs.values()) + list(scratch.values())
    )
    results = pl.pallas_call(
        body,
        out_shape=[jax.ShapeDtypeStruct(*out) for out in outs.values()],
        in_specs=[pl.BlockSpec(memory_space=pltpu.SMEM)] * n_smem + [pl.BlockSpec(memory_space=pl.ANY)] * n_in,
        out_specs=[pl.BlockSpec(memory_space=pl.ANY)] * n_out,
        scratch_shapes=[pltpu.VMEM(array.shape, array.dtype) for array in ins.values()]
        + [pltpu.VMEM(*out) for out in outs.values()]
        + [pltpu.VMEM(*one) for one in scratch.values()]
        + [pltpu.SemaphoreType.DMA((n_in,)), pltpu.SemaphoreType.DMA((n_out,))],
        compiler_params=pltpu.CompilerParams(vmem_limit_bytes=max(held_bytes + SPARE, limit)),
        cost_estimate=pl.CostEstimate(flops=cost * 10**9, transcendentals=0, bytes_accessed=cost * 10**6),
        name=name,
    )(*smem.values(), *ins.values())
    return SimpleNamespace(**dict(zip(outs, results)))


def finish_kernel(kind, bits, ids_ref, *refs):
    mark = own_label(bits, ids_ref[0], ids_ref[1])
    gathered, sem = refs[-2:]
    n_outs = {"enc": 4, "dec": 2, "cross": 3, "up": 1, "down": 1}[kind]
    count = len(refs) - 2 - n_outs
    parts, outs = refs[:count], refs[count:-2]
    copies, at = [], 0
    for i, part in enumerate(parts):
        copies.append(pltpu.make_async_copy(part, gathered.at[pl.ds(at, part.shape[0])], sem.at[i]))
        at += part.shape[0]
    for copy in copies:
        copy.start()
    for copy in copies:
        copy.wait()
    for shard in range(SHARDS):
        unit, half = divmod(shard, 2)
        rows = slice(half * QUAD, (half + 1) * QUAD)
        where = pl.ds(mark ^ shard, 1)
        value = gathered[where, :QUAD, :][0].astype(F32)
        if kind == "up":
            outs[0][rows, quad(unit)] = value
        elif kind == "down":
            outs[0][quad(unit), rows] = value.T
        elif unit == 3:
            outs[2 if kind == "cross" else 1][:, quad(half)] = value
        elif kind != "cross":
            outs[0][unit, rows, :] = value
        elif unit == 0:
            outs[0][rows, :] = value
        else:
            outs[1][unit - 1, rows, :] = value
        if kind == "enc":
            norms = gathered[where, QUAD:, :][0].astype(F32)
            many = norm_rows(SHARDS)
            for i in range(many):
                row, side = divmod(shard * many + i, 2)
                if row < 10:
                    outs[2 + row // 5][row % 5 : row % 5 + 1, quad(side)] = norms[i : i + 1, :]


def finish(group, ids, outs):
    parts = group.parts
    shape = (SHARDS,) + parts[0].shape[1:]
    return pl.pallas_call(
        functools.partial(finish_kernel, group.kind, group.bits),
        out_shape=[jax.ShapeDtypeStruct(*out) for out in outs],
        in_specs=[pl.BlockSpec(memory_space=pltpu.SMEM)] + [pl.BlockSpec(memory_space=pl.ANY)] * len(parts),
        out_specs=[pl.BlockSpec(memory_space=pltpu.VMEM)] * len(outs),
        scratch_shapes=[pltpu.VMEM(shape, BF16), pltpu.SemaphoreType.DMA((len(parts),))],
        compiler_params=pltpu.CompilerParams(vmem_limit_bytes=FINISH_LIMIT),
        cost_estimate=pl.CostEstimate(flops=2 * 10**9, transcendentals=0, bytes_accessed=2 * 10**6),
        name="finish_" + group.kind,
    )(ids, *parts)


class Sum:
    def __init__(self, kind, bits, dp, mp, mine, other):
        self.kind, self.bits, self.dp, self.mp = kind, bits, dp, mp
        self.phase, self.parts, self.outgoing = -1, [mine], [other]

    def hop(self, array, step):
        pairs = []
        for place in range(self.dp):
            for core in range(self.mp):
                bit = self.bits[core][step] if step < 4 else step
                pairs.append((place * self.mp + core, (place ^ (1 << bit)) * self.mp + core))
        return lax.ppermute(array, ("dp", "mp"), pairs)

    def launch(self):
        if self.phase < 0:
            self.flying = [lax.ppermute(self.outgoing[0], "mp", [(0, 1), (1, 0)])]
        elif self.phase <= 3:
            self.flying = [self.hop(self.outgoing[0], self.last if self.phase == 3 else self.phase)]
        else:
            self.flying = [self.hop(part, 6 - self.phase) for part in self.outgoing]

    def add_up(self):
        self.phase += 1
        if self.phase <= 2:
            mine, sent = self.parts[0], self.flying[0]
            half = mine.shape[0] // 2
            self.outgoing, self.parts = [mine[half:] + sent[half:]], [mine[:half] + sent[:half]]
        elif self.phase == 3:
            part, self.last = self.parts[0] + self.flying[0], 3
            while 2 << self.last < self.dp:
                part = part + self.hop(part, self.last)
                self.last += 1
            self.parts = self.outgoing = [part]
        elif self.phase == 4:
            self.parts = self.outgoing = [self.parts[0] + self.flying[0]]
        else:
            self.parts = self.parts + self.flying
            if self.phase < 7:
                self.outgoing = self.parts if self.phase == 5 and self.kind == "enc" else [jnp.concatenate(self.parts)]
        self.flying = []


def boundary(before, after, landing, launching=()):
    before, after, landing, launching = list(before), list(after), list(landing), list(launching)
    before, landed = lax.optimization_barrier((before, [group.flying for group in landing]))
    for group, flying in zip(landing, landed):
        group.flying = flying
        group.add_up()
    moving = landing + launching
    states = [([] if group.phase < 0 else group.parts, group.outgoing) for group in moving]
    before, after, states = lax.optimization_barrier((before, after, states))
    for group, state in zip(moving, states):
        group.outgoing = list(state[1])
        if group.phase >= 0:
            group.parts = list(state[0])
        if group.phase < 7:
            group.launch()
    return before, after


def on_device(
    src_embed, tgt_embed, src_segment, tgt_segment, enc_qkv, enc_out_proj, dec_qkv, dec_out_proj, cross_query,
    cross_kv, cross_out_proj, ffn_up, ffn_down, norm_gain, norm_bias, enc_cotangent, dec_cotangent,
):
    dp, mp = lax.axis_size("dp"), lax.axis_size("mp")
    tokens, model = src_embed.shape
    own = tokens // mp
    window = own + MOST
    half = ffn_up.shape[1]
    hidden = 2 * half
    position = lax.axis_index("mp")
    ids = jnp.stack([position, lax.axis_index("dp")]).astype(jnp.int32)
    pairs = [(0, 1), (1, 0)]

    def swap(tree):
        return jax.tree.map(lambda a: lax.ppermute(a, "mp", pairs), tree)

    enc_w1, enc_o1 = swap((enc_qkv, enc_out_proj))
    up1, down1 = swap((ffn_up, ffn_down))
    dec_w1, dec_o1 = swap((dec_qkv, dec_out_proj))
    cross_q1, cross_kv1, cross_o1 = swap((cross_query, cross_kv, cross_out_proj))
    feed = {"up0": ffn_up, "up1": up1, "down0": ffn_down, "down1": down1}

    def rows(count, dtype):
        return ((count, model), dtype)

    blocks = own // BLOCK
    q_shape, k_shape, ot_shape, lse_shape = ((own, QUAD), BF16), ((window, QUAD), BF16), ((QUAD, own), BF16), ((4, own), F32)
    vt_shape, marks, bias = ((4 * STRIDE, window), BF16), ((window, BLOCK), jnp.int32), ((blocks, 3 * BLOCK, BLOCK), F32)
    heads = {"q": q_shape, "k": k_shape, "v": k_shape, "ot": ot_shape, "lse": lse_shape}
    wide = ((own, half), BF16)
    norm_in = {"gain": norm_gain, "shift": norm_bias}
    first = call(
        own_heads_kernel, "own_heads", {"ids": ids},
        {"src_row": src_segment, "src": src_embed, "src_w": enc_qkv,
         "tgt_row": tgt_segment, "tgt": tgt_embed, "tgt_w": dec_qkv},
        {f"{side}_{key}": shape for side in ("src", "tgt") for key, shape in heads.items()},
        {"marks": marks, "src_bias": bias, "tgt_bias": bias, "src_vt": vt_shape, "tgt_vt": vt_shape},
        cost=8,
    )
    encoder = call(
        encoder_kernel, "encoder_forward", {"ids": ids},
        {"row": src_segment, "x": src_embed, "w": enc_w1, "ot0": first.src_ot, "wo0": enc_out_proj, "wo1": enc_o1,
         **norm_in, "up0": ffn_up, "down0": ffn_down, "up1": up1, "down1": down1},
        {**heads, "z0": rows(own, F32), "x1_low": rows(own, BF16), "h0": wide, "h1": wide,
         "z1": rows(own, F32), "enc": rows(own, BF16)},
        {"marks": marks, "bias": bias, "vt": vt_shape, "x1": rows(own, F32), "acc": rows(own, F32)},
        cost=12,
    )
    enc_swapped = swap(encoder.enc)
    decoder = call(
        decoder_kernel, "decoder_self_forward", {"ids": ids},
        {"row": tgt_segment, "x": tgt_embed, "w": dec_w1, "ot0": first.tgt_ot, "wo0": dec_out_proj, "wo1": dec_o1,
         **norm_in},
        {**heads, "z2": rows(own, F32), "x2": rows(own, F32)},
        {"marks": marks, "bias": bias, "vt": vt_shape, "acc": rows(own, F32)}, cost=6,
    )
    packed = ((SHARDS, QUAD, QUAD), BF16)
    packed_norms = ((SHARDS, QUAD + TILE, QUAD), BF16)
    crossed = call(
        cross_kernel, "cross_and_decoder_feed",
        {"ids": ids, "src_marks": src_segment, "tgt_marks": tgt_segment},
        {"src_row": src_segment, "tgt_row": tgt_segment, "enc_own": encoder.enc, "enc_other": enc_swapped,
         "x2": decoder.x2, "cq0": cross_query, "ckv0": cross_kv, "cq1": cross_q1, "ckv1": cross_kv1,
         "co0": cross_out_proj, "co1": cross_o1, **norm_in, **feed, "cot": dec_cotangent},
        {"enc": rows(tokens, BF16), "x3_low": rows(own, BF16), "a0": wide, "a1": wide, "dec": rows(own, BF16),
         "dy": rows(own, BF16), "dh0": wide, "dh1": wide, "norms": rows(4, F32), "pack0": packed, "pack1": packed,
         "denc_other": rows(own, BF16), "denc_own": rows(own, F32), "g2": rows(own, F32)},
        {"marks": ((tokens, BLOCK), jnp.int32), "bias": bias, "q": ((2, own, QUAD), BF16),
         "k": ((2, tokens, QUAD), BF16), "v": ((2, tokens, QUAD), BF16), "turn": ((2, QUAD, tokens), BF16), "vt": ((2, 4 * STRIDE, tokens), BF16),
         "mix": ((model, own), F32), "tops": ((8, own), F32), "totals": ((8, own), F32), "lse": ((2, 4, own), F32),
         "ot": ((model, own), BF16), "acc": rows(own, F32), "x3": rows(own, F32), "z3": rows(own, F32),
         "z4": rows(own, F32), "dz": rows(own, F32), "h": ((2, own, half), BF16), "low": rows(own, BF16), "do": ((2, own, QUAD), BF16),
         "delta": ((2, 4, own), F32), "dqt": ((2, QUAD, own), F32), "dk": ((2, tokens, QUAD), F32),
         "dv": ((2, tokens, QUAD), F32), "denc": rows(tokens, F32)},
        cost=30,
    )
    def whole(mine, received):
        return jnp.where(
            position == 0, jnp.concatenate([mine, received]), jnp.concatenate([received, mine])
        )

    def group(kind, bits, mine, other):
        return Sum(kind, bits, dp, mp, mine, other)

    head_scratch = {
        "marks": marks, "bias": bias, "do": q_shape, "delta": ((4, own), F32), "kt": ((QUAD, window), BF16),
        "dqt": ((QUAD, own), F32), "dk": ((window, QUAD), F32), "dv": ((window, QUAD), F32),
    }
    turned_shapes = {"keys_turned": ((model, window), BF16), "query_turned": ((model, own), BF16)}
    head_outs = {"dq": q_shape, "dk": k_shape, "dv": k_shape}

    def self_other(causal, at, bits, name, x, row, z, up, w_out, heads_kept, pack_shape, more):
        ins = {"z": z, "up": up, "gain": norm_gain, "row": row, "x": x, "wo": w_out} | heads_kept | more
        return call(
            functools.partial(self_back_other_kernel, causal, at, bits), name, {"ids": ids}, ins,
            {"dz": rows(own, F32), "branch": rows(own, BF16), "norms": rows(2, F32), "pack": pack_shape}
            | turned_shapes | head_outs,
            head_scratch, cost=9, limit=0,
        )

    def self_own(causal, bits, name, back, row, branch, w_out, heads_kept, pack_shape, more):
        ins = {"branch": branch, "row": row, "wo": w_out} | heads_kept
        ins |= {"keys_turned": back.keys_turned, "query_turned": back.query_turned} | more
        return call(
            functools.partial(self_back_own_kernel, causal, bits), name, {"ids": ids}, ins,
            {"pack": pack_shape} | head_outs, head_scratch, cost=7, limit=0,
        )

    def kept_own(side):
        return {key: getattr(first, f"{side}_{key}") for key in ("ot", "k", "q", "v", "lse")}

    def kept_other(part):
        return {key: getattr(part, key) for key in ("ot", "k", "q", "v", "lse")}

    def stream_gradient(name, back, back_own, w0, w1, ids):
        ins = {"dz": back.dz, "w0": w0, "w1": w1}
        for key in ("dk", "dv", "dq"):
            ins |= {f"{key}0": getattr(back_own, key), f"{key}1": getattr(back, key)}
        return call(
            stream_gradient_kernel, name, {"ids": ids}, ins,
            {"halo": rows(window - own, BF16), "dx": rows(own, F32)}, {"near": rows(window, F32)}, cost=5, limit=0,
        )

    def group(kind, bits, mine, other):
        return Sum(kind, bits, dp, mp, mine, other)

    halo_at = (1 - position) * (own - (window - own))

    def with_halo(grad, received):
        part = lax.dynamic_slice_in_dim(grad, halo_at, window - own, 0) + received.astype(F32)
        return lax.dynamic_update_slice_in_dim(grad, part, halo_at, 0)

    square, out_half, triple = ((model, QUAD), F32), ((QUAD, model), F32), ((3, model, QUAD), F32)
    out_shapes = {
        "cross": [square, ((2, model, QUAD), F32), out_half],
        "dec": [triple, out_half],
        "up": [((model, half), F32)],
        "down": [rows(half, F32)],
        "enc": [triple, out_half, rows(5, F32), rows(5, F32)],
    }
    cross_sum = group("cross", CROSS_BITS, crossed.pack0, crossed.pack1)
    cross_sum.launch()
    denc_recv = swap(crossed.denc_other)
    (cross_norms,), (z1, denc_recv) = boundary([crossed.norms], [encoder.z1, denc_recv], [cross_sum])
    fed = call(
        feed_other_kernel, "encoder_feed_other", {"ids": ids},
        {"cot": enc_cotangent, "denc_own": crossed.denc_own, "denc_recv": denc_recv, "z1": z1, "gain": norm_gain,
         "x1_low": encoder.x1_low, "x3_low": crossed.x3_low, "dy3": crossed.dy, "down": down1, "h": encoder.h1,
         "up": up1, "dh": crossed.dh1, "a": crossed.a1},
        {"dy": rows(own, BF16), "norms": rows(2, F32), **{f"turned{i}": ((model, own), BF16) for i in range(4)}, "up_pack": packed,
         "down_pack": packed, "g0": rows(own, F32)},
        {}, cost=10, limit=FEED_LIMIT,
    )
    up_sum = group("up", UP_BITS, None, fed.up_pack)
    down_sum = group("down", DOWN_BITS, None, fed.down_pack)
    (feed_norms,), (dy1,) = boundary([fed.norms], [fed.dy], [cross_sum], [up_sum, down_sum])
    fed_own = call(
        feed_own_kernel, "encoder_feed_own", {"ids": ids},
        {"dy": dy1, "down": ffn_down, "h": encoder.h0, "dz": fed.g0, **{f"turned{i}": getattr(fed, f"turned{i}") for i in range(4)}, "up": ffn_up,
         "dh": crossed.dh0, "a": crossed.a0},
        {"g0": rows(own, F32), "up_pack": packed, "down_pack": packed}, {}, cost=9, limit=0,
    )
    up_sum.parts, down_sum.parts = [fed_own.up_pack], [fed_own.down_pack]
    (feed_norms,), (g2,) = boundary([feed_norms], [crossed.g2], [cross_sum, up_sum, down_sum])
    dec_back = self_other(
        True, 2, DEC_BITS, "decoder_self_other", tgt_embed, tgt_segment, decoder.z2, g2, dec_o1, kept_other(decoder),
        packed, {},
    )
    dec_sum = group("dec", DEC_BITS, None, dec_back.pack)
    (dec_norms,), (branch,) = boundary([dec_back.norms], [dec_back.branch], [cross_sum, up_sum], [dec_sum])
    dec_own = self_own(
        True, DEC_BITS, "decoder_self_own", dec_back, tgt_segment, branch, dec_out_proj, kept_own("tgt"), packed, {},
    )
    dec_sum.parts = [dec_own.pack]
    (dec_norms,), (g0,) = boundary([dec_norms], [fed_own.g0], [cross_sum, up_sum, down_sum, dec_sum])
    norms_before = {"feed_norms": feed_norms, "dec_norms": dec_norms, "cross_norms": cross_norms}
    enc_back = self_other(
        False, 0, ENC_BITS, "encoder_self_other", src_embed, src_segment, encoder.z0, g0, enc_o1, kept_other(encoder),
        packed_norms, norms_before,
    )
    enc_sum = group("enc", ENC_BITS, None, enc_back.pack)
    (enc_norms,), (branch,) = boundary(
        [enc_back.norms], [enc_back.branch], [cross_sum, up_sum, down_sum, dec_sum], [enc_sum]
    )
    enc_own = self_own(
        False, ENC_BITS, "encoder_self_own", enc_back, src_segment, branch, enc_out_proj, kept_own("src"),
        packed_norms, {"norms": enc_norms, **norms_before},
    )
    enc_sum.parts = [enc_own.pack]
    order = ids

    def step(*landing, after=()):
        nonlocal order
        (order, *after), () = boundary([order, *after], [], landing)
        return after

    (enc_own.dq,) = step(enc_sum, after=[enc_own.dq])
    step(up_sum, down_sum, dec_sum)
    src_side = stream_gradient("src_gradient", enc_back, enc_own, enc_qkv, enc_w1, order)
    (src_halo,) = step(enc_sum, after=[src_side.halo])
    tgt_side = stream_gradient("tgt_gradient", dec_back, dec_own, dec_qkv, dec_w1, order)
    (tgt_halo,) = step(up_sum, dec_sum, cross_sum, after=[tgt_side.halo])
    step(enc_sum)
    dec_part, src_halo, tgt_halo = step(down_sum, after=[crossed.dec, src_halo, tgt_halo])
    src_recv, tgt_recv, dec_swapped = swap(src_halo), swap(tgt_halo), swap(dec_part)
    (dec_swapped,) = step(up_sum, after=[dec_swapped])
    step(enc_sum)
    step(down_sum)
    step(dec_sum, cross_sum)
    cross_out = list(finish(cross_sum, order, out_shapes["cross"]))
    (cross_out[0],) = step(down_sum, after=[cross_out[0]])
    step(enc_sum)
    (src_recv,) = step(dec_sum, after=[src_recv])
    src_grad = with_halo(src_side.dx, src_recv)
    (src_grad,) = step(enc_sum, after=[src_grad])
    (tgt_recv,) = step(dec_sum, up_sum, after=[tgt_recv])
    up_out = list(finish(up_sum, order, out_shapes["up"]))
    (up_out[0],) = step(enc_sum, after=[up_out[0]])
    tgt_grad = with_halo(tgt_side.dx, tgt_recv)
    (tgt_grad,) = step(down_sum, after=[tgt_grad])
    down_out = list(finish(down_sum, order, out_shapes["down"]))
    down_out[0], dec_swapped = step(dec_sum, after=[down_out[0], dec_swapped])
    dec_whole = whole(crossed.dec, dec_swapped)
    dec_out = list(finish(dec_sum, order, out_shapes["dec"]))
    dec_out[0], dec_whole = step(enc_sum, after=[dec_out[0], dec_whole])
    enc_out = finish(enc_sum, order, out_shapes["enc"])

    return (
        crossed.enc,
        dec_whole,
        src_grad,
        tgt_grad,
        enc_out[0],
        enc_out[1],
        dec_out[0],
        dec_out[1],
        cross_out[0],
        cross_out[1],
        cross_out[2],
        up_out[0],
        down_out[0],
        enc_out[2],
        enc_out[3],
    )


def solution(mesh):
    in_specs = (
        P("dp", None), P("dp", None), P("dp", None), P("dp", None),
        P(None, None, "mp"), P("mp", None), P(None, None, "mp"), P("mp", None),
        P(None, "mp"), P(None, None, "mp"), P("mp", None), P(None, "mp"), P("mp", None),
        P(), P(), P(("dp", "mp"), None), P(("dp", "mp"), None),
    )
    out_specs = (
        P("dp", None), P("dp", None), P(("dp", "mp"), None), P(("dp", "mp"), None),
        P(None, None, "mp"), P("mp", None), P(None, None, "mp"), P("mp", None),
        P(None, "mp"), P(None, None, "mp"), P("mp", None), P(None, "mp"), P("mp", None),
        P(), P(),
    )
    return jax.shard_map(on_device, mesh=mesh, in_specs=in_specs, out_specs=out_specs, check_vma=False)
```
